32 devices in a mesh: req: 8 (over z, y), tp: 4 (over x, core).
Axes of the slice: x: 2, y: 2, z: 4, core: 2. Of those that a mesh axis runs over, the one named last changes fastest.
Arguments:
- resid: bfloat16 [256, 1536], P('req', 'tp'), may hold values from -2.5 to 2.5
- queries: bfloat16 [256, 1536], P('req', 'tp'), may hold values from -250 to 250
- new_keys: bfloat16 [256, 512], P('req', 'tp'), may hold values from -6 to 6
- new_values: bfloat16 [256, 512], P('req', 'tp'), may hold values from -6 to 6
- k_cache: bfloat16 [256, 128, 512], P('req', None, 'tp'), may hold values from -6.5 to 6.5
- v_cache: bfloat16 [256, 128, 512], P('req', None, 'tp'), may hold values from -6 to 6
- lengths: int32 [256], P('req'), may hold values from 2 to 128, as said below
- w_out: bfloat16 [1536, 1536], P('tp'), may hold values from -0.15625 to 0.15625
- norm_gain: float32 [1536], P('tp'), may hold values from 0.1 to 1.9
- w_router: float32 [1536, 16], P('tp'), may hold values from -0.08125 to 0.08125
- routes: int32 [256, 2], P('req'), may hold values from 0 to 15, as said below
- w_gate: bfloat16 [16, 1536, 1024], P('req', 'tp'), may hold values from -0.15625 to 0.15625
- w_up: bfloat16 [16, 1536, 1024], P('req', 'tp'), may hold values from -0.15625 to 0.15625
- w_down: bfloat16 [16, 1024, 1536], P('req', None, 'tp'), may hold values from -0.46875 to 0.46875
Outputs:
- attended: bfloat16 [256, 1536], P('req', 'tp')
- layer_out: bfloat16 [256, 1536], P('req', 'tp')
The draws below stay inside these ranges and needn't reach their ends.
Inputs may be any that keep to these rules, and one draw needn't show every extreme that they name: A request reads the first lengths[b] positions of its cache; some request has exactly 128, and some request exactly 2. `routes`: each request names two different experts; among the 32 requests of one device, at most 8 name the same expert, and on every device some expert is named exactly 8 times.
All inputs are finite; a program needn't handle non-finite values.
Results may differ from the reference program's by a relative error of at most 0.01.
Values may be sent and summed in bfloat16 or wider, within the bound.
No kernel may reach another device: no remote copies, remote signals or barrier semaphores. Data moves between devices by JAX's collectives and lax.ppermute only.
A program may use at most 64 MiB of HBM per device.

```python
import math
import jax
import jax.numpy as jnp
from jax import lax

D = 1536
HEADS = 24
KV_HEADS = 8
HEAD_DIM = 64
FF = 1024
EXPERTS = 16
TOP = 2
REQ_DEV = 32
LMAX = 128
REQS = 256
CAP = 8
SHARDS = 1
SLOTS = 16
FF_SH = 1024
N_REQ = 8


def leading_keys(key):
    first_keys = jnp.clip(jax.random.normal(jax.random.fold_in(key, 11), (REQS, KV_HEADS * HEAD_DIM), jnp.float32), -6.0, 6.0)
    second_keys = jnp.clip(jax.random.normal(jax.random.fold_in(key, 12), (REQS, KV_HEADS * HEAD_DIM), jnp.float32), -6.0, 6.0)
    return (first_keys, second_keys)


def draw_k_cache(key, part):
    first_keys, second_keys = leading_keys(key)
    remaining = jnp.clip(jax.random.normal(jax.random.fold_in(key, 14), (REQS, LMAX - 2, KV_HEADS * HEAD_DIM), jnp.float32), -6.0, 6.0)
    stacked = jnp.concatenate([first_keys[:, None, :], second_keys[:, None, :], remaining], axis=1)
    return stacked.astype(jnp.bfloat16)


def draw_queries(key, part):
    drawn = jnp.clip(jax.random.normal(jax.random.fold_in(key, 21), (REQS, HEADS * HEAD_DIM), jnp.float32), -6.0, 6.0)
    return drawn.astype(jnp.bfloat16)


def column_profile():
    return jnp.exp(jnp.log(3.0) * jnp.arange(D, dtype=jnp.float32) / D)


def shared_direction(key):
    return jnp.clip(jax.random.normal(jax.random.fold_in(key, 61), (D,), jnp.float32), -4.0, 4.0)


def expert_levels(key):
    level_key = jax.random.fold_in(key, 71)
    ranking = jax.random.permutation(jax.random.fold_in(level_key, 1), EXPERTS)
    lower = ranking < EXPERTS // 4
    jitter = jax.random.uniform(jax.random.fold_in(level_key, 2), (EXPERTS,), jnp.float32, -0.25, 0.25)
    offset = jnp.where(lower, 0.0, 3.7) + jitter
    size_jitter = jax.random.uniform(jax.random.fold_in(level_key, 3), (EXPERTS,), jnp.float32, -0.2, 0.2)
    level = jnp.where(lower, 3.0, 0.12) * jnp.exp(size_jitter)
    return (offset, level)


def draw_resid(key, part):
    column_scale = column_profile()
    direction = shared_direction(key)
    noise_field = jnp.clip(jax.random.normal(jax.random.fold_in(key, 51), (REQS, D), jnp.float32), -6.0, 6.0)
    field = 0.12 * column_scale[None, :] * (direction[None, :] + 0.5 * noise_field)
    return jnp.clip(field, -2.5, 2.5).astype(jnp.bfloat16)


def draw_w_router(key, part):
    column_scale = column_profile()
    direction = shared_direction(key)
    offset, level = expert_levels(key)
    noise_part = jnp.clip(0.01 * jax.random.normal(jax.random.fold_in(key, 81), (D, EXPERTS), jnp.float32), -0.05, 0.05)
    aligned = (direction * column_scale)[:, None] * offset[None, :] / D
    return (noise_part + aligned).astype(jnp.float32)


def draw_w_down(key, part):
    offset, level = expert_levels(key)
    slot_expert = jnp.arange(SLOTS, dtype=jnp.int32) // SHARDS
    slot_scale = jnp.take(level, slot_expert) * FF ** (-0.5)
    base = jnp.clip(jax.random.normal(jax.random.fold_in(key, 91), (SLOTS, FF_SH, D), jnp.float32), -4.0, 4.0)
    return (base * slot_scale[:, None, None]).astype(jnp.bfloat16)


def draw_lengths(key, part):
    device_count = REQS // REQ_DEV
    halved_cap = jax.random.randint(jax.random.fold_in(key, 31), (device_count,), 0, 2)
    length_cap = jnp.repeat(jnp.where(halved_cap == 1, LMAX // 2, LMAX), REQ_DEV)
    lowest = jnp.maximum(length_cap // 4, 2)
    drawn_len = jax.random.randint(jax.random.fold_in(key, 32), (REQS,), lowest, length_cap + 1)
    chosen = jax.random.randint(jax.random.fold_in(key, 33), (), 0, REQS)
    offset = jax.random.randint(jax.random.fold_in(key, 34), (), 1, REQS)
    shortest = (chosen + offset) % REQS
    position = jnp.arange(REQS)
    drawn_len = jnp.where(position == shortest, 2, drawn_len)
    return jnp.where(position == chosen, LMAX, drawn_len).astype(jnp.int32)


def block_order(sub_key):
    return jax.random.permutation(sub_key, EXPERTS - 1)


def token_order(sub_key):
    return jax.random.permutation(sub_key, REQ_DEV)


def draw_routes(key, part):
    block_count = REQS // REQ_DEV
    route_count = REQ_DEV * TOP
    hot_expert = jax.random.randint(jax.random.fold_in(key, 41), (), 0, EXPERTS)
    orders = jax.vmap(block_order)(jax.random.split(jax.random.fold_in(key, 42), block_count)).astype(jnp.int32)
    others = orders + (orders >= hot_expert).astype(jnp.int32)
    ranked = jnp.concatenate([jnp.full((block_count, 1), hot_expert, jnp.int32), others], axis=1)
    full_count = jax.random.randint(jax.random.fold_in(key, 45), (block_count,), 2, 4).astype(jnp.int32)
    rank = jnp.arange(EXPERTS, dtype=jnp.int32)
    rest = route_count - full_count * CAP
    light_count = EXPERTS - full_count
    base = rest // light_count
    extra = rest % light_count
    beyond = rank[None, :] - full_count[:, None]
    counts = jnp.where(rank[None, :] < full_count[:, None], CAP, base[:, None] + (beyond < extra[:, None]).astype(jnp.int32))
    ends = jnp.cumsum(counts, axis=1)
    position = jnp.arange(route_count, dtype=jnp.int32)
    which = jnp.sum((position[None, :, None] >= ends[:, None, :]).astype(jnp.int32), axis=2)
    sequence = jnp.take_along_axis(ranked, which, axis=1)
    paired = jnp.stack([sequence[:, :REQ_DEV], sequence[:, REQ_DEV:]], axis=-1)
    flipped = jax.random.randint(jax.random.fold_in(key, 43), (block_count, REQ_DEV), 0, 2)
    paired = jnp.where(flipped[..., None] == 1, paired[..., ::-1], paired)
    shuffles = jax.vmap(token_order)(jax.random.split(jax.random.fold_in(key, 44), block_count)).astype(jnp.int32)
    paired = jnp.take_along_axis(paired, shuffles[..., None], axis=1)
    return paired.reshape(REQS, TOP).astype(jnp.int32)


def block_levels(rng, shape, pieces, least, top_value):
    level, own = 1.0, jax.random.fold_in(rng, 6)
    for dim, shards_of in pieces:
        draws = jnp.exp(jax.random.uniform(jax.random.fold_in(own, dim), (shards_of,), jnp.float32, least / len(pieces), top_value / len(pieces)))
        level = level * jnp.repeat(draws, shape[dim] // shards_of).reshape([-1 if axis == dim else 1 for axis in range(len(shape))])
    return level


def noise(own_key, extent, spread, most, cuts=(), kind=jnp.bfloat16):
    values = jax.random.normal(own_key, extent, jnp.float32) * spread
    if len(cuts) > 0:
        values = block_levels(own_key, extent, cuts, -0.22, 0.18) * values
    return jnp.clip(values, min=-most, max=most).astype(kind)


def setup_inputs(seed: int = 0) -> dict:
    keys = jax.random.split(jax.random.key(seed), 15)
    resid = draw_resid(jax.random.fold_in(keys[14], 71), 0)
    queries = draw_queries(jax.random.fold_in(keys[14], 71), 0)
    new_keys = noise(keys[2], (REQS, KV_HEADS * HEAD_DIM), 1.0, 6.0, ((0, 8), (1, 4)))
    new_values = noise(keys[3], (REQS, KV_HEADS * HEAD_DIM), 1.0, 6.0, ((0, 8), (1, 4)))
    k_cache = draw_k_cache(jax.random.fold_in(keys[14], 71), 0)
    v_cache = noise(keys[5], (REQS, LMAX, KV_HEADS * HEAD_DIM), 1.0, 6.0, ((0, 8), (2, 4)))
    lengths = draw_lengths(jax.random.fold_in(keys[14], 71), 0)
    w_out = noise(keys[7], (HEADS * HEAD_DIM, D), (HEADS * HEAD_DIM) ** -0.5, 0.15625, ((0, 4),))
    norm_gain = jnp.clip(1.0 + 0.18 * jax.random.normal(keys[8], (D,), jnp.float32), 0.1, 1.9)
    w_router = draw_w_router(jax.random.fold_in(keys[14], 71), 0)
    routes = draw_routes(jax.random.fold_in(keys[14], 71), 0)
    w_gate = noise(keys[11], (SLOTS, D, FF_SH), D ** -0.5, 0.15625, ((0, 8), (1, 4)))
    w_up = noise(keys[12], (SLOTS, D, FF_SH), D ** -0.5, 0.15625, ((0, 8), (1, 4)))
    w_down = draw_w_down(jax.random.fold_in(keys[14], 71), 0)
    return {"resid": resid, "queries": queries, "new_keys": new_keys, "new_values": new_values, "k_cache": k_cache, "v_cache": v_cache, "lengths": lengths, "w_out": w_out, "norm_gain": norm_gain, "w_router": w_router, "routes": routes, "w_gate": w_gate, "w_up": w_up, "w_down": w_down}


def attend_block(block_items):
    query_block, key_new, value_new, key_block, value_block, length_block = block_items
    row_count = query_block.shape[0]
    group_size = HEADS // KV_HEADS
    score_scale = 1.0 / math.sqrt(HEAD_DIM)
    query = query_block.astype(jnp.float32).reshape(row_count, KV_HEADS, group_size, HEAD_DIM)
    keys_all = key_block.astype(jnp.float32).reshape(row_count, LMAX, KV_HEADS, HEAD_DIM)
    values_all = value_block.astype(jnp.float32).reshape(row_count, LMAX, KV_HEADS, HEAD_DIM)
    scores = jnp.einsum('bgqd,blgd->bgql', query, keys_all) * score_scale
    self_score = jnp.einsum('bgqd,bgd->bgq', query, key_new.astype(jnp.float32).reshape(row_count, KV_HEADS, HEAD_DIM)) * score_scale
    valid_mask = (jnp.arange(LMAX, dtype=jnp.int32)[None, :] < length_block[:, None])[:, None, None, :]
    peak_score = jnp.maximum(lax.optimization_barrier(jnp.max(jnp.where(valid_mask, scores, -1e+30), axis=-1)), self_score)
    exp_terms = jnp.where(valid_mask, jnp.exp(scores - peak_score[..., None]), 0.0)
    self_exp = jnp.exp(self_score - peak_score)
    denom_sum = lax.optimization_barrier(jnp.sum(exp_terms, axis=-1)) + self_exp
    weights = (exp_terms / denom_sum[..., None]).astype(jnp.bfloat16)
    self_weight = (self_exp / denom_sum).astype(jnp.bfloat16)
    value_self = value_new.astype(jnp.float32).reshape(row_count, KV_HEADS, 1, HEAD_DIM)
    mixed = jnp.einsum('bgql,blgd->bgqd', weights.astype(jnp.float32), values_all) + self_weight.astype(jnp.float32)[..., None] * value_self
    return mixed.astype(jnp.bfloat16).reshape(row_count, HEADS * HEAD_DIM)

def reference(resid, queries, new_keys, new_values, k_cache, v_cache, lengths, w_out, norm_gain, w_router, routes, w_gate, w_up, w_down):
    block_count = REQS // REQ_DEV
    block_items = (queries.reshape(block_count, REQ_DEV, HEADS * HEAD_DIM), new_keys.reshape(block_count, REQ_DEV, KV_HEADS * HEAD_DIM), new_values.reshape(block_count, REQ_DEV, KV_HEADS * HEAD_DIM), k_cache.reshape(block_count, REQ_DEV, LMAX, KV_HEADS * HEAD_DIM), v_cache.reshape(block_count, REQ_DEV, LMAX, KV_HEADS * HEAD_DIM), lengths.reshape(block_count, REQ_DEV))
    attention = lax.map(attend_block, block_items).reshape(REQS, HEADS * HEAD_DIM)
    projected = jnp.dot(attention, w_out, preferred_element_type=jnp.float32)
    attended = (resid.astype(jnp.float32) + projected).astype(jnp.bfloat16)
    attended_f = attended.astype(jnp.float32)
    inv_rms = 1.0 / jnp.sqrt(lax.optimization_barrier(jnp.sum(attended_f * attended_f, axis=1)) / D + 1e-06)
    scaled = attended_f * norm_gain
    normed = (scaled * inv_rms[:, None]).astype(jnp.bfloat16)
    logits = jnp.dot(scaled, w_router, precision=lax.Precision.HIGHEST) * inv_rms[:, None]
    first_logit = jnp.take_along_axis(logits, routes[:, 0:1], axis=1)[:, 0]
    second_logit = jnp.take_along_axis(logits, routes[:, 1:2], axis=1)[:, 0]
    first_weight = jax.nn.sigmoid(first_logit - second_logit)
    second_weight = 1.0 - first_weight
    route_share = jnp.stack([first_weight, second_weight], axis=-1)
    gate_all = w_gate.reshape(EXPERTS, SHARDS, D, FF_SH).transpose(0, 2, 1, 3).reshape(EXPERTS, D, FF)
    up_all = w_up.reshape(EXPERTS, SHARDS, D, FF_SH).transpose(0, 2, 1, 3).reshape(EXPERTS, D, FF)
    down_all = w_down.reshape(EXPERTS, FF, D)
    most_rows = N_REQ * CAP

    def one_expert(accumulator, expert_items):
        gate_e, up_e, down_e, expert_index = expert_items
        matched = routes == expert_index
        share = lax.optimization_barrier(jnp.sum(jnp.where(matched, route_share, 0.0), axis=1))
        used_rows = jnp.any(matched, axis=1)
        used_count = jnp.sum(used_rows.astype(jnp.int32))
        picked = jnp.nonzero(used_rows, size=most_rows, fill_value=0)[0].astype(jnp.int32)
        picked_rows = normed[picked]
        gate_pre = jnp.dot(picked_rows, gate_e, preferred_element_type=jnp.float32)
        up_pre = jnp.dot(picked_rows, up_e, preferred_element_type=jnp.float32)
        hidden = (jax.nn.silu(gate_pre) * up_pre).astype(jnp.bfloat16)
        expert_out = jnp.dot(hidden, down_e, preferred_element_type=jnp.float32)
        keep_rows = jnp.arange(most_rows, dtype=jnp.int32) < used_count
        contrib = jnp.where(keep_rows[:, None], expert_out * share[picked][:, None], 0.0)
        return (accumulator.at[picked].add(contrib), None)
    moe, _unused = lax.scan(one_expert, jnp.zeros((REQS, D), jnp.float32), (gate_all, up_all, down_all, jnp.arange(EXPERTS, dtype=jnp.int32)))
    layer_out = (attended_f + moe).astype(jnp.bfloat16)
    return (attended, layer_out)
```

```python
import math

import jax
import jax.numpy as jnp
from jax import lax
from jax.sharding import PartitionSpec as P

D = 1536
HEAD_DIM = 64
EXPERTS = 16
TOP = 2
CAP = 8


def attend_local(queries, new_keys, new_values, k_cache, v_cache, lengths):
    row_count = queries.shape[0]
    kv_local = new_keys.shape[1] // HEAD_DIM
    group_size = queries.shape[1] // HEAD_DIM // kv_local
    cache_len = k_cache.shape[1]
    score_scale = 1.0 / math.sqrt(HEAD_DIM)
    query = queries.reshape(row_count, kv_local, group_size, HEAD_DIM)
    keys_all = k_cache.reshape(row_count, cache_len, kv_local, HEAD_DIM)
    values_all = v_cache.reshape(row_count, cache_len, kv_local, HEAD_DIM)
    scores = (
        jnp.einsum("bgqd,blgd->bgql", query, keys_all, preferred_element_type=jnp.float32)
        * score_scale
    )
    self_score = (
        jnp.einsum(
            "bgqd,bgd->bgq",
            query,
            new_keys.reshape(row_count, kv_local, HEAD_DIM),
            preferred_element_type=jnp.float32,
        )
        * score_scale
    )
    valid_mask = (jnp.arange(cache_len, dtype=jnp.int32)[None, :] < lengths[:, None])[
        :, None, None, :
    ]
    peak_score = jnp.maximum(jnp.max(jnp.where(valid_mask, scores, -1e30), axis=-1), self_score)
    exp_terms = jnp.where(valid_mask, jnp.exp(scores - peak_score[..., None]), 0.0)
    self_exp = jnp.exp(self_score - peak_score)
    denom_sum = jnp.sum(exp_terms, axis=-1) + self_exp
    weights = (exp_terms / denom_sum[..., None]).astype(jnp.bfloat16)
    self_weight = (self_exp / denom_sum).astype(jnp.bfloat16)
    value_self = new_values.astype(jnp.float32).reshape(row_count, kv_local, 1, HEAD_DIM)
    mixed = (
        jnp.einsum("bgql,blgd->bgqd", weights, values_all, preferred_element_type=jnp.float32)
        + self_weight.astype(jnp.float32)[..., None] * value_self
    )
    return mixed.astype(jnp.bfloat16).reshape(row_count, kv_local * group_size * HEAD_DIM)


def exchange(blocks, axis):
    count = lax.axis_size(axis)
    return [
        lax.ppermute(block, axis, [(i, (i + shift) % count) for i in range(count)])
        for shift, block in enumerate(blocks, 1)
    ]


def blocks_by_shift(array, axis, dim):
    count = lax.axis_size(axis)
    index = lax.axis_index(axis)
    size = array.shape[dim] // count
    blocks = [
        lax.dynamic_slice_in_dim(array, ((index + shift) % count) * size, size, axis=dim)
        for shift in range(count)
    ]
    return blocks[0], blocks[1:]


def all_to_all(array, axis):
    count = lax.axis_size(axis)
    if count > 8:
        return lax.all_to_all(array, axis, split_axis=0, concat_axis=0, tiled=True)
    index = lax.axis_index(axis)
    own_block, sent_blocks = blocks_by_shift(array, axis, 0)
    result = jnp.zeros_like(array)
    for shift, piece in enumerate([own_block] + exchange(sent_blocks, axis)):
        result = lax.dynamic_update_slice_in_dim(result, piece, (index - shift) % count, axis=0)
    return result


def shards(
    resid,
    queries,
    new_keys,
    new_values,
    k_cache,
    v_cache,
    lengths,
    w_out,
    norm_gain,
    w_router,
    routes,
    w_gate,
    w_up,
    w_down,
):
    req_dev = resid.shape[0]
    width_local = resid.shape[1]
    slot_dev = w_gate.shape[0]
    req_count = lax.axis_size("req")
    shard_count = max(1, req_count // EXPERTS)
    attention = attend_local(queries, new_keys, new_values, k_cache, v_cache, lengths)
    partial_value = jnp.dot(attention, w_out, preferred_element_type=jnp.float32)
    tp_count = lax.axis_size("tp")
    tp_index = lax.axis_index("tp")
    own_block, sent_blocks = blocks_by_shift(partial_value, "tp", 1)
    projected = own_block
    for block in exchange(sent_blocks, "tp"):
        projected = projected + block
    attended = (resid.astype(jnp.float32) + projected).astype(jnp.bfloat16)
    attended_f = attended.astype(jnp.float32)
    expert_ids = jnp.arange(EXPERTS, dtype=jnp.int32)
    flat_routes = routes.reshape(req_dev * TOP)
    one_hot = (flat_routes[None, :] == expert_ids[:, None]).astype(jnp.int32)
    rank_in = jnp.cumsum(one_hot, axis=1) - one_hot
    slot_ids = jnp.arange(CAP, dtype=jnp.int32)
    chosen = (one_hot[:, None, :] == 1) & (rank_in[:, None, :] == slot_ids[None, :, None])
    token_pick = jnp.sum(
        chosen.reshape(EXPERTS, CAP, req_dev, TOP).astype(jnp.int32), axis=-1
    ).astype(jnp.bfloat16)
    per_expert = jnp.einsum(
        "ecb,bd->ecd", token_pick, attended, preferred_element_type=jnp.float32
    ).astype(jnp.bfloat16)
    outgoing = jnp.broadcast_to(
        per_expert[:, None], (EXPERTS, shard_count, CAP, width_local)
    ).reshape(req_count, slot_dev, CAP, width_local)
    incoming = all_to_all(outgoing, "req")
    scaled = attended_f * norm_gain[None, :]
    logit_part = jnp.dot(scaled, w_router, precision=lax.Precision.HIGHEST)
    square_part = jnp.sum(attended_f * attended_f, axis=1, keepdims=True)
    stats_part = jnp.concatenate([logit_part, square_part], axis=1)
    stats = stats_part
    for other in exchange([stats_part] * (tp_count - 1), "tp"):
        stats = stats + other
    inv_rms = 1.0 / jnp.sqrt(stats[:, EXPERTS] / D + 1e-06)
    logits = stats[:, :EXPERTS] * inv_rms[:, None]
    first_logit = jnp.sum(jnp.where(routes[:, 0:1] == expert_ids[None, :], logits, 0.0), axis=1)
    second_logit = jnp.sum(jnp.where(routes[:, 1:2] == expert_ids[None, :], logits, 0.0), axis=1)
    first_weight = jax.nn.sigmoid(first_logit - second_logit)
    second_weight = 1.0 - first_weight
    incoming_f = incoming.astype(jnp.float32)
    rows = (incoming_f * norm_gain).astype(jnp.bfloat16)
    row_square = jnp.sum(incoming_f * incoming_f, axis=-1, keepdims=True)
    gate_pre = jnp.einsum("nscd,sdf->nscf", rows, w_gate, preferred_element_type=jnp.float32)
    up_pre = jnp.einsum("nscd,sdf->nscf", rows, w_up, preferred_element_type=jnp.float32)
    square_high = row_square.astype(jnp.bfloat16)
    square_low = (row_square - square_high.astype(jnp.float32)).astype(jnp.bfloat16)
    pre = jnp.concatenate(
        [gate_pre.astype(jnp.bfloat16), up_pre.astype(jnp.bfloat16), square_high, square_low], axis=-1
    )
    own_block, sent_blocks = blocks_by_shift(pre, "tp", 0)
    sums = own_block.astype(jnp.float32)
    for block in exchange(sent_blocks, "tp"):
        sums = sums + block.astype(jnp.float32)
    width = w_gate.shape[2]
    row_inv = 1.0 / jnp.sqrt((sums[..., 2 * width :].sum(axis=-1, keepdims=True)) / D + 1e-06)
    hidden_part = (
        jax.nn.silu(sums[..., :width] * row_inv) * (sums[..., width : 2 * width] * row_inv)
    ).astype(jnp.bfloat16)
    hidden = jnp.zeros((req_count, slot_dev, CAP, width), jnp.bfloat16)
    step = req_count // tp_count
    pieces = [hidden_part] + exchange([hidden_part] * (tp_count - 1), "tp")
    for shift, piece in enumerate(pieces):
        hidden = lax.dynamic_update_slice_in_dim(
            hidden, piece, ((tp_index - shift) % tp_count) * step, axis=0
        )
    computed = jnp.einsum("nscf,sfd->nscd", hidden, w_down, preferred_element_type=jnp.float32)
    returned = all_to_all(computed, "req")
    combined = jnp.sum(returned.reshape(EXPERTS, shard_count, CAP, width_local), axis=1)
    route_out = jnp.einsum(
        "ecr,ecd->rd", chosen.astype(jnp.float32), combined, precision=lax.Precision.HIGHEST
    ).reshape(req_dev, TOP, width_local)
    moe = first_weight[:, None] * route_out[:, 0] + second_weight[:, None] * route_out[:, 1]
    layer_out = (attended_f + moe).astype(jnp.bfloat16)
    return (attended, layer_out)


def solution(mesh):
    placed = (
        P("req", "tp"),
        P("req", "tp"),
        P("req", "tp"),
        P("req", "tp"),
        P("req", None, "tp"),
        P("req", None, "tp"),
        P("req"),
        P("tp", None),
        P("tp"),
        P("tp", None),
        P("req", None),
        P("req", "tp", None),
        P("req", "tp", None),
        P("req", None, "tp"),
    )
    return jax.shard_map(
        shards,
        mesh=mesh,
        in_specs=placed,
        out_specs=(P("req", "tp"), P("req", "tp")),
        check_vma=False,
    )
```

```python
import functools
import math

import jax
import jax.numpy as jnp
from jax import lax
from jax.experimental import pallas as pl
from jax.experimental.pallas import tpu as pltpu
from jax.sharding import PartitionSpec as P

D = 1536
HEAD_DIM = 64
EXPERTS = 16
TOP = 2
CAP = 8


def attend_local(queries, new_keys, new_values, k_cache, v_cache, lengths):
    row_count = queries.shape[0]
    kv_local = new_keys.shape[1] // HEAD_DIM
    group_size = queries.shape[1] // HEAD_DIM // kv_local
    cache_len = k_cache.shape[1]
    score_scale = 1.0 / math.sqrt(HEAD_DIM)
    query = queries.reshape(row_count, kv_local, group_size, HEAD_DIM)
    keys_all = k_cache.reshape(row_count, cache_len, kv_local, HEAD_DIM)
    values_all = v_cache.reshape(row_count, cache_len, kv_local, HEAD_DIM)
    scores = (
        jnp.einsum("bgqd,blgd->bgql", query, keys_all, preferred_element_type=jnp.float32)
        * score_scale
    )
    self_score = (
        jnp.einsum(
            "bgqd,bgd->bgq",
            query,
            new_keys.reshape(row_count, kv_local, HEAD_DIM),
            preferred_element_type=jnp.float32,
        )
        * score_scale
    )
    valid_mask = (jnp.arange(cache_len, dtype=jnp.int32)[None, :] < lengths[:, None])[
        :, None, None, :
    ]
    peak_score = jnp.maximum(jnp.max(jnp.where(valid_mask, scores, -1e30), axis=-1), self_score)
    exp_terms = jnp.where(valid_mask, jnp.exp(scores - peak_score[..., None]), 0.0)
    self_exp = jnp.exp(self_score - peak_score)
    denom_sum = jnp.sum(exp_terms, axis=-1) + self_exp
    weights = (exp_terms / denom_sum[..., None]).astype(jnp.bfloat16)
    self_weight = (self_exp / denom_sum).astype(jnp.bfloat16)
    value_self = new_values.astype(jnp.float32).reshape(row_count, kv_local, 1, HEAD_DIM)
    mixed = (
        jnp.einsum("bgql,blgd->bgqd", weights, values_all, preferred_element_type=jnp.float32)
        + self_weight.astype(jnp.float32)[..., None] * value_self
    )
    return mixed.astype(jnp.bfloat16).reshape(row_count, kv_local * group_size * HEAD_DIM)


def shards_general(
    resid,
    queries,
    new_keys,
    new_values,
    k_cache,
    v_cache,
    lengths,
    w_out,
    norm_gain,
    w_router,
    routes,
    w_gate,
    w_up,
    w_down,
):
    req_dev = resid.shape[0]
    width_local = resid.shape[1]
    slot_dev = w_gate.shape[0]
    req_count = lax.axis_size("req")
    shard_count = max(1, req_count // EXPERTS)
    attention = attend_local(queries, new_keys, new_values, k_cache, v_cache, lengths)
    partial_value = jnp.dot(attention, w_out, preferred_element_type=jnp.float32)
    projected = lax.psum_scatter(partial_value, "tp", scatter_dimension=1, tiled=True)
    attended = (resid.astype(jnp.float32) + projected).astype(jnp.bfloat16)
    attended_f = attended.astype(jnp.float32)
    scaled = attended_f * norm_gain[None, :]
    square_sum, logit_part = lax.psum(
        (
            jnp.sum(attended_f * attended_f, axis=1),
            jnp.dot(scaled, w_router, precision=lax.Precision.HIGHEST),
        ),
        "tp",
    )
    inv_rms = 1.0 / jnp.sqrt(square_sum / D + 1e-06)
    normed = (scaled * inv_rms[:, None]).astype(jnp.bfloat16)
    logits = logit_part * inv_rms[:, None]
    expert_ids = jnp.arange(EXPERTS, dtype=jnp.int32)
    first_logit = jnp.sum(jnp.where(routes[:, 0:1] == expert_ids[None, :], logits, 0.0), axis=1)
    second_logit = jnp.sum(jnp.where(routes[:, 1:2] == expert_ids[None, :], logits, 0.0), axis=1)
    first_weight = jax.nn.sigmoid(first_logit - second_logit)
    second_weight = 1.0 - first_weight
    flat_routes = routes.reshape(req_dev * TOP)
    one_hot = (flat_routes[None, :] == expert_ids[:, None]).astype(jnp.int32)
    rank_in = jnp.cumsum(one_hot, axis=1) - one_hot
    slot_ids = jnp.arange(CAP, dtype=jnp.int32)
    chosen = (one_hot[:, None, :] == 1) & (rank_in[:, None, :] == slot_ids[None, :, None])
    token_pick = jnp.sum(
        chosen.reshape(EXPERTS, CAP, req_dev, TOP).astype(jnp.int32), axis=-1
    ).astype(jnp.bfloat16)
    per_expert = jnp.einsum(
        "ecb,bd->ecd", token_pick, normed, preferred_element_type=jnp.float32
    ).astype(jnp.bfloat16)
    outgoing = jnp.broadcast_to(
        per_expert[:, None], (EXPERTS, shard_count, CAP, width_local)
    ).reshape(req_count, slot_dev, CAP, width_local)
    incoming = lax.all_to_all(outgoing, "req", split_axis=0, concat_axis=0, tiled=True)
    gate_pre = jnp.einsum("nscd,sdf->nscf", incoming, w_gate, preferred_element_type=jnp.float32)
    up_pre = jnp.einsum("nscd,sdf->nscf", incoming, w_up, preferred_element_type=jnp.float32)
    gate_sum, up_sum = lax.psum((gate_pre, up_pre), "tp")
    hidden = (jax.nn.silu(gate_sum) * up_sum).astype(jnp.bfloat16)
    computed = jnp.einsum("nscf,sfd->nscd", hidden, w_down, preferred_element_type=jnp.float32)
    returned = lax.all_to_all(computed, "req", split_axis=0, concat_axis=0, tiled=True)
    combined = jnp.sum(returned.reshape(EXPERTS, shard_count, CAP, width_local), axis=1)
    route_out = jnp.einsum(
        "ecr,ecd->rd", chosen.astype(jnp.float32), combined, precision=lax.Precision.HIGHEST
    ).reshape(req_dev, TOP, width_local)
    moe = first_weight[:, None] * route_out[:, 0] + second_weight[:, None] * route_out[:, 1]
    layer_out = (attended_f + moe).astype(jnp.bfloat16)
    return (attended, layer_out)


def spec(space=pltpu.VMEM):
    return pl.BlockSpec(memory_space=space)


def call(kernel, outs, ins, operands, scratch=(), mebibytes=8, flops=100_000, moved=100_000):
    return pl.pallas_call(
        kernel,
        out_shape=[jax.ShapeDtypeStruct(shape, dtype) for shape, dtype in outs],
        in_specs=ins,
        out_specs=[spec() for _ in outs],
        scratch_shapes=scratch,
        compiler_params=pltpu.CompilerParams(vmem_limit_bytes=mebibytes << 20),
        cost_estimate=pl.CostEstimate(flops=flops, bytes_accessed=moved, transcendentals=0),
    )(*operands)


def partner_permute(block, axis, distance):
    count = lax.axis_size(axis)
    return lax.ppermute(block, axis, [(i, i ^ distance) for i in range(count)])


def attend_kernel(
    lengths, routes, queries, new_keys, new_values, w_router, k_hbm, v_hbm, w_hbm,
    own, sent1, sent2, sent3, pick0, pick1, pick_rows, router_rows,
    k_buf, v_buf, w_buf, query_s, self_s, score_s, weight_s, sems,
):
    row_count = queries.shape[0]
    width = own.shape[1]
    lanes = 2 * HEAD_DIM
    cache_len = k_hbm.shape[1]
    chunks = 4
    per_chunk = row_count // chunks
    copies = []
    for index, (source, target) in enumerate(((k_hbm, k_buf), (v_hbm, v_buf))):
        for chunk in range(chunks):
            part = pl.ds(chunk * per_chunk, per_chunk)
            copies.append(
                pltpu.make_async_copy(source.at[part], target.at[part], sems.at[index * chunks + chunk])
            )
    copies.append(pltpu.make_async_copy(w_hbm, w_buf, sems.at[2 * chunks]))
    for copy in copies:
        copy.start()

    route0, route1 = routes[:, 0:1], routes[:, 1:2]
    lane = lax.broadcasted_iota(jnp.int32, (row_count, lanes), 1)
    named0, named1 = lane == route0, lane == route1
    named = jnp.where(named0 | named1, 1.0, 0.0).astype(jnp.bfloat16)
    row_of = lax.broadcasted_iota(jnp.int32, (row_count, row_count), 0)
    col_of = lax.broadcasted_iota(jnp.int32, (row_count, row_count), 1)
    earlier = jnp.where(col_of < row_of, 1.0, 0.0).astype(jnp.bfloat16)
    before = jnp.dot(earlier, named, preferred_element_type=jnp.float32)
    rank0 = jnp.sum(jnp.where(named0, before, 0.0), axis=1, keepdims=True).astype(jnp.int32)
    rank1 = jnp.sum(jnp.where(named1, before, 0.0), axis=1, keepdims=True).astype(jnp.int32)
    first = jnp.where(lane == route0 * CAP + rank0, 1.0, 0.0)
    second = jnp.where(lane == route1 * CAP + rank1, 1.0, 0.0)
    pick0[...] = first.astype(jnp.bfloat16)
    pick1[...] = second.astype(jnp.bfloat16)
    pick_rows[...] = jnp.transpose(first + second).astype(jnp.bfloat16)
    signed = jnp.where(named0, 1.0, 0.0) - jnp.where(named1, 1.0, 0.0)
    router_rows[...] = lax.dot_general(
        signed[:, :EXPERTS], w_router[...], (((1,), (1,)), ((), ())),
        precision=lax.Precision.HIGHEST, preferred_element_type=jnp.float32,
    )

    low = lane < HEAD_DIM
    tiles = [queries[:, i * lanes : (i + 1) * lanes].astype(jnp.float32) for i in range(3)]
    heads = [
        jnp.where(low, tiles[0], 0.0),
        jnp.where(low, pltpu.roll(tiles[0], HEAD_DIM, 1), 0.0),
        jnp.where(low, tiles[1], 0.0),
        jnp.where(low, 0.0, tiles[1]),
        jnp.where(low, 0.0, pltpu.roll(tiles[2], HEAD_DIM, 1)),
        jnp.where(low, 0.0, tiles[2]),
    ]
    scale = 1.0 / math.sqrt(HEAD_DIM)
    keys_new = new_keys[...].astype(jnp.float32)
    zeros = jnp.zeros((row_count, lanes), jnp.float32)
    for head in range(8):
        rows = pl.ds(head, row_count, stride=8)
        if head < 6:
            own_score = jnp.sum(heads[head] * keys_new, axis=1, keepdims=True) * scale
            query_s[rows, :] = heads[head]
            self_s[rows, :] = jnp.broadcast_to(own_score, zeros.shape)
        else:
            query_s[rows, :] = zeros
            self_s[rows, :] = zeros

    pair_row = lax.broadcasted_iota(jnp.int32, (16, 2 * cache_len), 0)
    pair_lane = lax.broadcasted_iota(jnp.int32, (16, 2 * cache_len), 1)
    upper = pair_row < 8
    place = jnp.where(upper, pair_lane, pair_lane - cache_len)
    place = jnp.where(place < 0, cache_len, place)
    for pair in range(row_count // 2):
        if pair % (per_chunk // 2) == 0:
            copies[pair // (per_chunk // 2)].wait()
        pair_rows = slice(16 * pair, 16 * pair + 16)
        keys = k_buf[2 * pair : 2 * pair + 2].reshape(2 * cache_len, lanes)
        raw = lax.dot_general(
            query_s[pair_rows, :].astype(jnp.bfloat16), keys, (((1,), (1,)), ((), ())),
            preferred_element_type=jnp.float32,
        )
        limit = jnp.where(upper, lengths[2 * pair], lengths[2 * pair + 1])
        score_s[pair_rows, :] = jnp.where(place < limit, raw * scale, -1e30)

    own_score = self_s[:, 0:1]
    scores = score_s[...]
    peak = jnp.maximum(jnp.max(scores, axis=1, keepdims=True), own_score)
    terms = jnp.exp(scores - peak)
    own_term = jnp.exp(own_score - peak)
    inverse = 1.0 / (jnp.sum(terms, axis=1, keepdims=True) + own_term)
    weight_s[...] = (terms * inverse).astype(jnp.bfloat16)
    own_weight = (own_term * inverse).astype(jnp.bfloat16).astype(jnp.float32)
    self_s[...] = jnp.broadcast_to(own_weight, self_s.shape)
    for pair in range(row_count // 2):
        if pair % (per_chunk // 2) == 0:
            copies[chunks + pair // (per_chunk // 2)].wait()
        pair_rows = slice(16 * pair, 16 * pair + 16)
        values = v_buf[2 * pair : 2 * pair + 2].reshape(2 * cache_len, lanes)
        query_s[pair_rows, :] = jnp.dot(
            weight_s[pair_rows, :], values, preferred_element_type=jnp.float32
        )

    values_new = new_values[...].astype(jnp.float32)
    mixed = []
    for head in range(6):
        rows = pl.ds(head, row_count, stride=8)
        mixed.append(query_s[rows, :] + self_s[rows, :] * values_new)
    attention = jnp.concatenate(
        [
            jnp.where(low, mixed[0], pltpu.roll(mixed[1], HEAD_DIM, 1)),
            jnp.where(low, mixed[2], mixed[3]),
            jnp.where(low, pltpu.roll(mixed[4], HEAD_DIM, 1), mixed[5]),
        ],
        axis=1,
    ).astype(jnp.bfloat16)
    copies[2 * chunks].wait()
    place_tp = lax.axis_index("tp")
    for shift, out in enumerate((own, sent1, sent2, sent3)):
        columns = pl.ds(pl.multiple_of((place_tp ^ shift) * width, width), width)
        out[...] = jnp.dot(
            attention, w_buf[:, columns], preferred_element_type=jnp.float32
        ).astype(out.dtype)


def pack_kernel(own, part1, part2, part3, resid, pick_rows, attended, packed):
    total = own[...]
    for part in (part1, part2, part3):
        total = total + part[...].astype(jnp.float32)
    rows = (resid[...].astype(jnp.float32) + total).astype(jnp.bfloat16)
    attended[...] = rows
    packed[...] = jnp.dot(pick_rows[...], rows, preferred_element_type=jnp.float32).astype(
        jnp.bfloat16
    )


def stats_kernel(attended, gain, router_rows, stats):
    rows = attended[...].astype(jnp.float32)
    square = jnp.sum(rows * rows, axis=1, keepdims=True)
    logit = jnp.sum(rows * gain[...] * router_rows[...], axis=1, keepdims=True)
    lane = lax.broadcasted_iota(jnp.int32, stats.shape, 1)
    stats[...] = jnp.where(lane == 0, square, jnp.where(lane == 1, logit, 0.0))


def slot_masks(row_count, slot_dev):
    slot = lax.rem(lax.broadcasted_iota(jnp.int32, (row_count, 1), 0) // CAP, slot_dev)
    return [slot == index for index in range(slot_dev)]


def gate_kernel(
    slot_dev, incoming, gain, stats, w_gate, w_up, own, sent1, sent2, sent3, lhs
):
    quarter = own.shape[0]
    width = incoming.shape[1]
    hidden = w_gate.shape[1]
    place_tp = lax.axis_index("tp")
    masks = slot_masks(quarter, slot_dev)
    lane = lax.broadcasted_iota(jnp.int32, (quarter, 128), 1)
    extras = []
    for shift in range(4):
        rows = incoming[
            pl.ds(pl.multiple_of((place_tp ^ shift) * quarter, quarter), quarter), :
        ].astype(jnp.float32)
        columns = [
            jnp.sum(rows * rows, axis=1, keepdims=True),
            stats[:, 0:1],
            stats[:, 1:2],
        ]
        extra = jnp.zeros((quarter, 128), jnp.float32)
        for index, column in enumerate(columns):
            high = column.astype(jnp.bfloat16).astype(jnp.float32)
            extra = jnp.where(lane == 2 * index, high, extra)
            extra = jnp.where(lane == 2 * index + 1, column - high, extra)
        extras.append(extra)
        scaled = rows * gain[...]
        for index, mask in enumerate(masks):
            lhs[shift * quarter : (shift + 1) * quarter, index * width : (index + 1) * width] = (
                jnp.where(mask, scaled, 0.0).astype(jnp.bfloat16)
            )
    left = lhs[...]
    outs = (own, sent1, sent2, sent3)
    for first, weight in ((0, w_gate), (hidden, w_up)):
        product = jnp.dot(left, weight[...], preferred_element_type=jnp.float32)
        for shift, out in enumerate(outs):
            out[:, first : first + hidden] = product[
                shift * quarter : (shift + 1) * quarter
            ].astype(out.dtype)
    for extra, out in zip(extras, outs):
        out[:, 2 * hidden :] = extra.astype(out.dtype)


def hidden_kernel(own, part1, part2, part3, hidden, first_weight):
    width = hidden.shape[1]

    def total(first, size):
        columns = slice(first, first + size)
        result = own[:, columns]
        for part in (part1, part2, part3):
            result = result + part[:, columns].astype(jnp.float32)
        return result

    extra = total(2 * width, 128)
    row_inv = 1.0 / jnp.sqrt((extra[:, 0:1] + extra[:, 1:2]) / D + 1e-06)
    gate = total(0, width) * row_inv
    up = total(width, width) * row_inv
    hidden[...] = (gate / (1.0 + jnp.exp(-gate)) * up).astype(jnp.bfloat16)
    inv_rms = 1.0 / jnp.sqrt((extra[:, 2:3] + extra[:, 3:4]) / D + 1e-06)
    logit = (extra[:, 4:5] + extra[:, 5:6]) * inv_rms
    first_weight[...] = jnp.broadcast_to(1.0 / (1.0 + jnp.exp(-logit)), first_weight.shape)


def down_kernel(slot_dev, own, part1, part2, part3, w_down, computed, lhs):
    quarter, width = own.shape
    place_tp = lax.axis_index("tp")
    masks = slot_masks(quarter, slot_dev)
    for shift, part in enumerate((own, part1, part2, part3)):
        rows = part[...].astype(jnp.float32)
        place = pl.ds(pl.multiple_of((place_tp ^ shift) * quarter, quarter), quarter)
        for index, mask in enumerate(masks):
            lhs[place, index * width : (index + 1) * width] = jnp.where(mask, rows, 0.0).astype(
                jnp.bfloat16
            )
    computed[...] = jnp.dot(lhs[...], w_down[...], preferred_element_type=jnp.float32).astype(
        computed.dtype
    )


def combine_kernel(returned, pick0, pick1, first_weight, attended, layer_out):
    rows = returned[...]
    out0 = jnp.dot(pick0[...], rows, preferred_element_type=jnp.float32)
    out1 = jnp.dot(pick1[...], rows, preferred_element_type=jnp.float32)
    weight = first_weight[:, 0:1]
    moe = weight * out0 + (1.0 - weight) * out1
    layer_out[...] = (attended[...].astype(jnp.float32) + moe).astype(jnp.bfloat16)


def shards(
    resid,
    queries,
    new_keys,
    new_values,
    k_cache,
    v_cache,
    lengths,
    w_out,
    norm_gain,
    w_router,
    routes,
    w_gate,
    w_up,
    w_down,
):
    row_count, width = resid.shape
    slot_dev, _, hidden = w_gate.shape
    cache_len, lanes = k_cache.shape[1:]
    packed_count = EXPERTS * CAP
    quarter = packed_count // lax.axis_size("tp")
    if not (
        lax.axis_size("tp") == 4
        and lax.axis_size("req") * slot_dev == EXPERTS
        and row_count == quarter
        and lanes == 2 * HEAD_DIM
        and queries.shape[1] == 6 * HEAD_DIM
    ):
        return shards_general(
            resid, queries, new_keys, new_values, k_cache, v_cache, lengths, w_out,
            norm_gain, w_router, routes, w_gate, w_up, w_down,
        )
    bf16, f32 = jnp.bfloat16, jnp.float32
    gain = norm_gain.reshape(1, width)
    own, sent1, sent2, sent3, pick0, pick1, pick_rows, router_rows = call(
        attend_kernel,
        [
            ((row_count, width), f32),
            ((row_count, width), bf16),
            ((row_count, width), bf16),
            ((row_count, width), bf16),
            ((row_count, packed_count), bf16),
            ((row_count, packed_count), bf16),
            ((packed_count, row_count), bf16),
            ((row_count, width), f32),
        ],
        [spec(pltpu.SMEM)] + [spec()] * 5 + [spec(pl.ANY)] * 3,
        (lengths, routes, queries, new_keys, new_values, w_router, k_cache, v_cache, w_out),
        scratch=[
            pltpu.VMEM(k_cache.shape, bf16),
            pltpu.VMEM(v_cache.shape, bf16),
            pltpu.VMEM(w_out.shape, bf16),
            pltpu.VMEM((8 * row_count, lanes), f32),
            pltpu.VMEM((8 * row_count, lanes), f32),
            pltpu.VMEM((8 * row_count, 2 * cache_len), f32),
            pltpu.VMEM((8 * row_count, 2 * cache_len), bf16),
            pltpu.SemaphoreType.DMA((9,)),
        ],
        mebibytes=12,
        flops=200_000_000,
        moved=3_400_000,
    )
    parts = [partner_permute(block, "tp", k) for k, block in enumerate((sent1, sent2, sent3), 1)]
    attended, packed = call(
        pack_kernel,
        [((row_count, width), bf16), ((packed_count, width), bf16)],
        [spec()] * 6,
        (own, *parts, resid, pick_rows),
    )
    incoming = lax.all_to_all(packed, "req", split_axis=0, concat_axis=0, tiled=True)
    (stats,) = call(
        stats_kernel, [((row_count, 128), f32)], [spec()] * 3, (attended, gain, router_rows)
    )
    message = (quarter, 2 * hidden + 128)
    own, sent1, sent2, sent3 = call(
        functools.partial(gate_kernel, slot_dev),
        [(message, f32), (message, bf16), (message, bf16), (message, bf16)],
        [spec()] * 5,
        (
            incoming,
            gain,
            stats,
            w_gate.reshape(slot_dev * width, hidden),
            w_up.reshape(slot_dev * width, hidden),
        ),
        scratch=[pltpu.VMEM((packed_count, slot_dev * width), bf16)],
        mebibytes=12,
        flops=800_000_000,
        moved=4_000_000,
    )
    parts = [partner_permute(block, "tp", k) for k, block in enumerate((sent1, sent2, sent3), 1)]
    own, first_weight = call(
        hidden_kernel,
        [((quarter, hidden), bf16), ((row_count, 128), f32)],
        [spec()] * 4,
        (own, *parts),
    )
    parts = [partner_permute(own, "tp", k) for k in (1, 2, 3)]
    (computed,) = call(
        functools.partial(down_kernel, slot_dev),
        [((packed_count, width), bf16)],
        [spec()] * 5,
        (own, *parts, w_down.reshape(slot_dev * hidden, width)),
        scratch=[pltpu.VMEM((packed_count, slot_dev * hidden), bf16)],
        flops=200_000_000,
        moved=2_000_000,
    )
    returned = lax.all_to_all(computed, "req", split_axis=0, concat_axis=0, tiled=True)
    (layer_out,) = call(
        combine_kernel,
        [((row_count, width), bf16)],
        [spec()] * 5,
        (returned, pick0, pick1, first_weight, attended),
    )
    return (attended, layer_out)


def solution(mesh):
    placed = (
        P("req", "tp"),
        P("req", "tp"),
        P("req", "tp"),
        P("req", "tp"),
        P("req", None, "tp"),
        P("req", None, "tp"),
        P("req"),
        P("tp", None),
        P("tp"),
        P("tp", None),
        P("req", None),
        P("req", "tp", None),
        P("req", "tp", None),
        P("req", None, "tp"),
    )
    return jax.shard_map(
        shards,
        mesh=mesh,
        in_specs=placed,
        out_specs=(P("req", "tp"), P("req", "tp")),
        check_vma=False,
    )
```

```python
import functools
import math

import jax
import jax.numpy as jnp
from jax import lax
from jax.experimental import pallas as pl
from jax.experimental.pallas import tpu as pltpu
from jax.sharding import PartitionSpec as P

D = 1536
HEAD_DIM = 64
EXPERTS = 16
TOP = 2
CAP = 8


def attend_local(queries, new_keys, new_values, k_cache, v_cache, lengths):
    row_count = queries.shape[0]
    kv_local = new_keys.shape[1] // HEAD_DIM
    group_size = queries.shape[1] // HEAD_DIM // kv_local
    cache_len = k_cache.shape[1]
    score_scale = 1.0 / math.sqrt(HEAD_DIM)
    query = queries.reshape(row_count, kv_local, group_size, HEAD_DIM)
    keys_all = k_cache.reshape(row_count, cache_len, kv_local, HEAD_DIM)
    values_all = v_cache.reshape(row_count, cache_len, kv_local, HEAD_DIM)
    scores = (
        jnp.einsum("bgqd,blgd->bgql", query, keys_all, preferred_element_type=jnp.float32)
        * score_scale
    )
    self_score = (
        jnp.einsum(
            "bgqd,bgd->bgq",
            query,
            new_keys.reshape(row_count, kv_local, HEAD_DIM),
            preferred_element_type=jnp.float32,
        )
        * score_scale
    )
    valid_mask = (jnp.arange(cache_len, dtype=jnp.int32)[None, :] < lengths[:, None])[
        :, None, None, :
    ]
    peak_score = jnp.maximum(jnp.max(jnp.where(valid_mask, scores, -1e30), axis=-1), self_score)
    exp_terms = jnp.where(valid_mask, jnp.exp(scores - peak_score[..., None]), 0.0)
    self_exp = jnp.exp(self_score - peak_score)
    denom_sum = jnp.sum(exp_terms, axis=-1) + self_exp
    weights = (exp_terms / denom_sum[..., None]).astype(jnp.bfloat16)
    self_weight = (self_exp / denom_sum).astype(jnp.bfloat16)
    value_self = new_values.astype(jnp.float32).reshape(row_count, kv_local, 1, HEAD_DIM)
    mixed = (
        jnp.einsum("bgql,blgd->bgqd", weights, values_all, preferred_element_type=jnp.float32)
        + self_weight.astype(jnp.float32)[..., None] * value_self
    )
    return mixed.astype(jnp.bfloat16).reshape(row_count, kv_local * group_size * HEAD_DIM)


def shards_general(
    resid,
    queries,
    new_keys,
    new_values,
    k_cache,
    v_cache,
    lengths,
    w_out,
    norm_gain,
    w_router,
    routes,
    w_gate,
    w_up,
    w_down,
):
    req_dev = resid.shape[0]
    width_local = resid.shape[1]
    slot_dev = w_gate.shape[0]
    req_count = lax.axis_size("req")
    shard_count = max(1, req_count // EXPERTS)
    attention = attend_local(queries, new_keys, new_values, k_cache, v_cache, lengths)
    partial_value = jnp.dot(attention, w_out, preferred_element_type=jnp.float32)
    projected = lax.psum_scatter(partial_value, "tp", scatter_dimension=1, tiled=True)
    attended = (resid.astype(jnp.float32) + projected).astype(jnp.bfloat16)
    attended_f = attended.astype(jnp.float32)
    scaled = attended_f * norm_gain[None, :]
    square_sum, logit_part = lax.psum(
        (
            jnp.sum(attended_f * attended_f, axis=1),
            jnp.dot(scaled, w_router, precision=lax.Precision.HIGHEST),
        ),
        "tp",
    )
    inv_rms = 1.0 / jnp.sqrt(square_sum / D + 1e-06)
    normed = (scaled * inv_rms[:, None]).astype(jnp.bfloat16)
    logits = logit_part * inv_rms[:, None]
    expert_ids = jnp.arange(EXPERTS, dtype=jnp.int32)
    first_logit = jnp.sum(jnp.where(routes[:, 0:1] == expert_ids[None, :], logits, 0.0), axis=1)
    second_logit = jnp.sum(jnp.where(routes[:, 1:2] == expert_ids[None, :], logits, 0.0), axis=1)
    first_weight = jax.nn.sigmoid(first_logit - second_logit)
    second_weight = 1.0 - first_weight
    flat_routes = routes.reshape(req_dev * TOP)
    one_hot = (flat_routes[None, :] == expert_ids[:, None]).astype(jnp.int32)
    rank_in = jnp.cumsum(one_hot, axis=1) - one_hot
    slot_ids = jnp.arange(CAP, dtype=jnp.int32)
    chosen = (one_hot[:, None, :] == 1) & (rank_in[:, None, :] == slot_ids[None, :, None])
    token_pick = jnp.sum(
        chosen.reshape(EXPERTS, CAP, req_dev, TOP).astype(jnp.int32), axis=-1
    ).astype(jnp.bfloat16)
    per_expert = jnp.einsum(
        "ecb,bd->ecd", token_pick, normed, preferred_element_type=jnp.float32
    ).astype(jnp.bfloat16)
    outgoing = jnp.broadcast_to(
        per_expert[:, None], (EXPERTS, shard_count, CAP, width_local)
    ).reshape(req_count, slot_dev, CAP, width_local)
    incoming = lax.all_to_all(outgoing, "req", split_axis=0, concat_axis=0, tiled=True)
    gate_pre = jnp.einsum("nscd,sdf->nscf", incoming, w_gate, preferred_element_type=jnp.float32)
    up_pre = jnp.einsum("nscd,sdf->nscf", incoming, w_up, preferred_element_type=jnp.float32)
    gate_sum, up_sum = lax.psum((gate_pre, up_pre), "tp")
    hidden = (jax.nn.silu(gate_sum) * up_sum).astype(jnp.bfloat16)
    computed = jnp.einsum("nscf,sfd->nscd", hidden, w_down, preferred_element_type=jnp.float32)
    returned = lax.all_to_all(computed, "req", split_axis=0, concat_axis=0, tiled=True)
    combined = jnp.sum(returned.reshape(EXPERTS, shard_count, CAP, width_local), axis=1)
    route_out = jnp.einsum(
        "ecr,ecd->rd", chosen.astype(jnp.float32), combined, precision=lax.Precision.HIGHEST
    ).reshape(req_dev, TOP, width_local)
    moe = first_weight[:, None] * route_out[:, 0] + second_weight[:, None] * route_out[:, 1]
    layer_out = (attended_f + moe).astype(jnp.bfloat16)
    return (attended, layer_out)


def spec(space=pltpu.VMEM):
    return pl.BlockSpec(memory_space=space)


def call(kernel, outs, ins, operands, scratch=(), mebibytes=8, flops=100_000, moved=100_000):
    return pl.pallas_call(
        kernel,
        out_shape=[jax.ShapeDtypeStruct(shape, dtype) for shape, dtype in outs],
        in_specs=ins,
        out_specs=[spec() for _ in outs],
        scratch_shapes=scratch,
        compiler_params=pltpu.CompilerParams(vmem_limit_bytes=mebibytes << 20),
        cost_estimate=pl.CostEstimate(flops=flops, bytes_accessed=moved, transcendentals=0),
    )(*operands)


def partner_permute(block, axis, distance):
    count = lax.axis_size(axis)
    return lax.ppermute(block, axis, [(i, i ^ distance) for i in range(count)])


def attend_kernel(
    slot_dev, lengths_hbm, routes_hbm, queries_hbm, keys_hbm, values_hbm, router_hbm, k_hbm, v_hbm,
    w_hbm, own, sent1, sent2, sent3, pick0, pick1, pick_rows, router_rows,
    lengths, routes, queries, new_keys, new_values, w_router, k_buf, v_buf, w_buf,
    query_s, self_s, score_s, weight_s, small_sems, sems,
):
    row_count = queries.shape[0]
    width = own.shape[1]
    lanes = 2 * HEAD_DIM
    cache_len = k_hbm.shape[1]
    packed_count = pick0.shape[1]
    chunks = 4
    small = [
        pltpu.make_async_copy(source, target, small_sems.at[index])
        for index, (source, target) in enumerate(
            (
                (routes_hbm, routes),
                (router_hbm, w_router),
                (queries_hbm, queries),
                (keys_hbm, new_keys),
                (values_hbm, new_values),
                (lengths_hbm, lengths),
            )
        )
    ]
    copies = []
    for source, target in ((k_hbm, k_buf), (v_hbm, v_buf), (w_hbm, w_buf)):
        size = source.shape[0] // chunks
        for chunk in range(chunks):
            part = pl.ds(chunk * size, size)
            copies.append(
                pltpu.make_async_copy(source.at[part], target.at[part], sems.at[len(copies)])
            )
    for copy in small + copies:
        copy.start()
    per_chunk = row_count // chunks

    small[0].wait()
    route0, route1 = routes[0:1, :], routes[1:2, :]
    place = lax.broadcasted_iota(jnp.int32, (packed_count, row_count), 0)
    named0 = jnp.where(place == route0, 1.0, 0.0)
    named1 = jnp.where(place == route1, 1.0, 0.0)
    row_of = lax.broadcasted_iota(jnp.int32, (row_count, row_count), 0)
    col_of = lax.broadcasted_iota(jnp.int32, (row_count, row_count), 1)
    earlier = jnp.where(row_of < col_of, 1.0, 0.0).astype(jnp.bfloat16)
    before = jnp.dot(
        (named0 + named1).astype(jnp.bfloat16), earlier, preferred_element_type=jnp.float32
    )
    place_req = lax.axis_index("req")

    def pick(route, named):
        rank = jnp.sum(named * before, axis=0, keepdims=True).astype(jnp.int32)
        block = ((route // slot_dev) ^ place_req) * slot_dev + lax.rem(route, slot_dev)
        return jnp.where(place == block * CAP + rank, 1.0, 0.0)

    first, second = pick(route0, named0), pick(route1, named1)
    pick_rows[...] = (first + second).astype(jnp.bfloat16)
    pick0[...] = jnp.transpose(first).astype(jnp.bfloat16)
    pick1[...] = jnp.transpose(second).astype(jnp.bfloat16)
    signed = jnp.transpose(named0 - named1)
    small[1].wait()
    router_rows[...] = jnp.dot(
        signed[:, :EXPERTS], w_router[...],
        precision=lax.Precision.HIGHEST, preferred_element_type=jnp.float32,
    )
    for copy in small[2:]:
        copy.wait()

    low = lax.broadcasted_iota(jnp.int32, (row_count, lanes), 1) < HEAD_DIM
    tiles = [queries[:, i * lanes : (i + 1) * lanes].astype(jnp.float32) for i in range(3)]
    heads = [
        jnp.where(low, tiles[0], 0.0),
        jnp.where(low, pltpu.roll(tiles[0], HEAD_DIM, 1), 0.0),
        jnp.where(low, tiles[1], 0.0),
        jnp.where(low, 0.0, tiles[1]),
        jnp.where(low, 0.0, pltpu.roll(tiles[2], HEAD_DIM, 1)),
        jnp.where(low, 0.0, tiles[2]),
    ]
    scale = 1.0 / math.sqrt(HEAD_DIM)
    keys_new = new_keys[...].astype(jnp.float32)
    zeros = jnp.zeros((row_count, lanes), jnp.float32)
    for head in range(8):
        rows = pl.ds(head, row_count, stride=8)
        if head < 6:
            own_score = jnp.sum(heads[head] * keys_new, axis=1, keepdims=True) * scale
            query_s[rows, :] = heads[head]
            self_s[rows, :] = jnp.broadcast_to(own_score, zeros.shape)
        else:
            query_s[rows, :] = zeros
            self_s[rows, :] = zeros

    pair_row = lax.broadcasted_iota(jnp.int32, (16, 2 * cache_len), 0)
    pair_lane = lax.broadcasted_iota(jnp.int32, (16, 2 * cache_len), 1)
    upper = pair_row < 8
    place = jnp.where(upper, pair_lane, pair_lane - cache_len)
    place = jnp.where(place < 0, cache_len, place)
    for pair in range(row_count // 2):
        if pair % (per_chunk // 2) == 0:
            copies[pair // (per_chunk // 2)].wait()
        pair_rows = slice(16 * pair, 16 * pair + 16)
        keys = k_buf[2 * pair : 2 * pair + 2].reshape(2 * cache_len, lanes)
        raw = lax.dot_general(
            query_s[pair_rows, :].astype(jnp.bfloat16), keys, (((1,), (1,)), ((), ())),
            preferred_element_type=jnp.float32,
        )
        limit = jnp.where(upper, lengths[2 * pair], lengths[2 * pair + 1])
        score_s[pair_rows, :] = jnp.where(place < limit, raw * scale, -1e30)

    own_score = self_s[:, 0:1]
    scores = score_s[...]
    peak = jnp.maximum(jnp.max(scores, axis=1, keepdims=True), own_score)
    terms = jnp.exp(scores - peak)
    own_term = jnp.exp(own_score - peak)
    inverse = 1.0 / (jnp.sum(terms, axis=1, keepdims=True) + own_term)
    weight_s[...] = (terms * inverse).astype(jnp.bfloat16)
    own_weight = (own_term * inverse).astype(jnp.bfloat16).astype(jnp.float32)
    self_s[...] = jnp.broadcast_to(own_weight, self_s.shape)
    for pair in range(row_count // 2):
        if pair % (per_chunk // 2) == 0:
            copies[chunks + pair // (per_chunk // 2)].wait()
        pair_rows = slice(16 * pair, 16 * pair + 16)
        values = v_buf[2 * pair : 2 * pair + 2].reshape(2 * cache_len, lanes)
        query_s[pair_rows, :] = jnp.dot(
            weight_s[pair_rows, :], values, preferred_element_type=jnp.float32
        )

    values_new = new_values[...].astype(jnp.float32)
    mixed = []
    for head in range(6):
        rows = pl.ds(head, row_count, stride=8)
        mixed.append(query_s[rows, :] + self_s[rows, :] * values_new)
    attention = jnp.concatenate(
        [
            jnp.where(low, mixed[0], pltpu.roll(mixed[1], HEAD_DIM, 1)),
            jnp.where(low, mixed[2], mixed[3]),
            jnp.where(low, pltpu.roll(mixed[4], HEAD_DIM, 1), mixed[5]),
        ],
        axis=1,
    ).astype(jnp.bfloat16)
    for copy in copies[2 * chunks :]:
        copy.wait()
    place_tp = lax.axis_index("tp")
    for shift, out in enumerate((own, sent1, sent2, sent3)):
        columns = pl.ds(pl.multiple_of((place_tp ^ shift) * width, width), width)
        out[...] = jnp.dot(
            attention, w_buf[:, columns], preferred_element_type=jnp.float32
        ).astype(out.dtype)


def store_blocks(rows, home, sent1, sent2, sent3):
    size = home.shape[0]
    for distance, out in enumerate((home, sent1, sent2, sent3)):
        out[...] = rows[distance * size : (distance + 1) * size].astype(out.dtype)


def pack_kernel(own, part1, part2, part3, resid, pick_rows, attended, home, sent1, sent2, sent3):
    total = own[...]
    for part in (part1, part2, part3):
        total = total + part[...].astype(jnp.float32)
    rows = (resid[...].astype(jnp.float32) + total).astype(jnp.bfloat16)
    attended[...] = rows
    packed = jnp.dot(pick_rows[...], rows, preferred_element_type=jnp.float32)
    store_blocks(packed, home, sent1, sent2, sent3)


def stats_kernel(attended, gain, router_rows, stats, result):
    result[...] = attended[...]
    rows = attended[...].astype(jnp.float32)
    square = jnp.sum(rows * rows, axis=1, keepdims=True)
    logit = jnp.sum(rows * gain[...] * router_rows[...], axis=1, keepdims=True)
    lane = lax.broadcasted_iota(jnp.int32, stats.shape, 1)
    stats[...] = jnp.where(lane == 0, square, jnp.where(lane == 1, logit, 0.0))


def turn_kernel(home, part1, part2, part3, along):
    half = home.shape[0] // 2
    for index, part in enumerate((home, part1, part2, part3)):
        along[index * half : (index + 1) * half, :] = part[half:, :]


def two_hop(home, sents):
    parts = [partner_permute(block, "req", 2 * k) for k, block in enumerate(sents, 1)]
    (along,) = call(
        turn_kernel,
        [((2 * home.shape[0], home.shape[1]), home.dtype)],
        [spec()] * 4,
        (home, *parts),
    )
    return (home, *parts, partner_permute(along, "req", 1))


def gather_blocks(refs, target):
    *first_hop, second_hop = refs
    half = first_hop[0].shape[0] // 2
    for index, part in enumerate(first_hop):
        start = 2 * index * half
        target[start : start + half, :] = part[:half, :].astype(target.dtype)
        target[start + half : start + 2 * half, :] = second_hop[
            index * half : (index + 1) * half, :
        ].astype(target.dtype)


def slot_masks(row_count, slot_dev):
    slot = lax.rem(lax.broadcasted_iota(jnp.int32, (row_count, 1), 0) // CAP, slot_dev)
    return [slot == index for index in range(slot_dev)]


def gate_kernel(
    slot_dev, in0, in1, in2, in3, in4, gain, stats, w_gate, w_up,
    own, sent1, sent2, sent3, incoming, lhs
):
    gather_blocks((in0, in1, in2, in3, in4), incoming)
    quarter = own.shape[0]
    width = incoming.shape[1]
    hidden = w_gate.shape[1]
    place_tp = lax.axis_index("tp")
    masks = slot_masks(quarter, slot_dev)
    lane = lax.broadcasted_iota(jnp.int32, (quarter, 128), 1)
    extras = []
    for shift in range(4):
        rows = incoming[
            pl.ds(pl.multiple_of((place_tp ^ shift) * quarter, quarter), quarter), :
        ].astype(jnp.float32)
        columns = [
            jnp.sum(rows * rows, axis=1, keepdims=True),
            stats[:, 0:1],
            stats[:, 1:2],
        ]
        extra = jnp.zeros((quarter, 128), jnp.float32)
        for index, column in enumerate(columns):
            high = column.astype(jnp.bfloat16).astype(jnp.float32)
            extra = jnp.where(lane == 2 * index, high, extra)
            extra = jnp.where(lane == 2 * index + 1, column - high, extra)
        extras.append(extra)
        scaled = rows * gain[...]
        for index, mask in enumerate(masks):
            lhs[shift * quarter : (shift + 1) * quarter, index * width : (index + 1) * width] = (
                jnp.where(mask, scaled, 0.0).astype(jnp.bfloat16)
            )
    left = lhs[...]
    outs = (own, sent1, sent2, sent3)
    for first, weight in ((0, w_gate), (hidden, w_up)):
        product = jnp.dot(left, weight[...], preferred_element_type=jnp.float32)
        for shift, out in enumerate(outs):
            out[:, first : first + hidden] = product[
                shift * quarter : (shift + 1) * quarter
            ].astype(out.dtype)
    for extra, out in zip(extras, outs):
        out[:, 2 * hidden :] = extra.astype(out.dtype)


def hidden_kernel(own, part1, part2, part3, hidden, first_weight):
    width = hidden.shape[1]

    def total(first, size):
        columns = slice(first, first + size)
        result = own[:, columns]
        for part in (part1, part2, part3):
            result = result + part[:, columns].astype(jnp.float32)
        return result

    extra = total(2 * width, 128)
    row_inv = 1.0 / jnp.sqrt((extra[:, 0:1] + extra[:, 1:2]) / D + 1e-06)
    gate = total(0, width) * row_inv
    up = total(width, width) * row_inv
    hidden[...] = (gate / (1.0 + jnp.exp(-gate)) * up).astype(jnp.bfloat16)
    inv_rms = 1.0 / jnp.sqrt((extra[:, 2:3] + extra[:, 3:4]) / D + 1e-06)
    logit = (extra[:, 4:5] + extra[:, 5:6]) * inv_rms
    first_weight[...] = jnp.broadcast_to(1.0 / (1.0 + jnp.exp(-logit)), first_weight.shape)


def down_kernel(slot_dev, own, part1, part2, part3, w_down, home, sent1, sent2, sent3, lhs):
    quarter, width = own.shape
    place_tp = lax.axis_index("tp")
    masks = slot_masks(quarter, slot_dev)
    for shift, part in enumerate((own, part1, part2, part3)):
        rows = part[...].astype(jnp.float32)
        place = pl.ds(pl.multiple_of((place_tp ^ shift) * quarter, quarter), quarter)
        for index, mask in enumerate(masks):
            lhs[place, index * width : (index + 1) * width] = jnp.where(mask, rows, 0.0).astype(
                jnp.bfloat16
            )
    computed = jnp.dot(lhs[...], w_down[...], preferred_element_type=jnp.float32)
    store_blocks(computed, home, sent1, sent2, sent3)


def combine_kernel(
    in0, in1, in2, in3, in4, pick0, pick1, first_weight, attended, layer_out, returned
):
    gather_blocks((in0, in1, in2, in3, in4), returned)
    rows = returned[...]
    out0 = jnp.dot(pick0[...], rows, preferred_element_type=jnp.float32)
    out1 = jnp.dot(pick1[...], rows, preferred_element_type=jnp.float32)
    weight = first_weight[:, 0:1]
    moe = weight * out0 + (1.0 - weight) * out1
    layer_out[...] = (attended[...].astype(jnp.float32) + moe).astype(jnp.bfloat16)


def shards(
    resid,
    queries,
    new_keys,
    new_values,
    k_cache,
    v_cache,
    lengths,
    w_out,
    norm_gain,
    w_router,
    routes,
    w_gate,
    w_up,
    w_down,
):
    row_count, width = resid.shape
    slot_dev, _, hidden = w_gate.shape
    cache_len, lanes = k_cache.shape[1:]
    packed_count = EXPERTS * CAP
    quarter = packed_count // lax.axis_size("tp")
    if not (
        lax.axis_size("tp") == 4
        and lax.axis_size("req") == 8
        and 8 * slot_dev == EXPERTS
        and row_count == quarter
        and lanes == 2 * HEAD_DIM
        and queries.shape[1] == 6 * HEAD_DIM
    ):
        return shards_general(
            resid, queries, new_keys, new_values, k_cache, v_cache, lengths, w_out,
            norm_gain, w_router, routes, w_gate, w_up, w_down,
        )
    bf16, f32 = jnp.bfloat16, jnp.float32
    gain = norm_gain.reshape(1, width)
    own, sent1, sent2, sent3, pick0, pick1, pick_rows, router_rows = call(
        functools.partial(attend_kernel, slot_dev),
        [
            ((row_count, width), f32),
            ((row_count, width), bf16),
            ((row_count, width), bf16),
            ((row_count, width), bf16),
            ((row_count, packed_count), bf16),
            ((row_count, packed_count), bf16),
            ((packed_count, row_count), bf16),
            ((row_count, width), f32),
        ],
        [spec(pl.ANY)] * 9,
        (
            lengths, routes.T, queries, new_keys, new_values, w_router.T, k_cache, v_cache, w_out,
        ),
        scratch=[
            pltpu.SMEM(lengths.shape, jnp.int32),
            pltpu.VMEM(routes.shape[::-1], jnp.int32),
            pltpu.VMEM(queries.shape, bf16),
            pltpu.VMEM(new_keys.shape, bf16),
            pltpu.VMEM(new_values.shape, bf16),
            pltpu.VMEM(w_router.shape[::-1], f32),
            pltpu.VMEM(k_cache.shape, bf16),
            pltpu.VMEM(v_cache.shape, bf16),
            pltpu.VMEM(w_out.shape, bf16),
            pltpu.VMEM((8 * row_count, lanes), f32),
            pltpu.VMEM((8 * row_count, lanes), f32),
            pltpu.VMEM((8 * row_count, 2 * cache_len), f32),
            pltpu.VMEM((8 * row_count, 2 * cache_len), bf16),
            pltpu.SemaphoreType.DMA((6,)),
            pltpu.SemaphoreType.DMA((12,)),
        ],
        mebibytes=56,
        flops=200_000_000,
        moved=3_400_000,
    )
    parts = [partner_permute(block, "tp", k) for k, block in enumerate((sent1, sent2, sent3), 1)]
    block = ((quarter, width), bf16)
    attended, home, *sents = call(
        pack_kernel,
        [((row_count, width), bf16)] + [block] * 4,
        [spec()] * 6,
        (own, *parts, resid, pick_rows),
    )
    stats, result = call(
        stats_kernel,
        [((row_count, 128), f32), ((row_count, width), bf16)],
        [spec()] * 3,
        (attended, gain, router_rows),
    )
    message = (quarter, 2 * hidden + 128)
    own, sent1, sent2, sent3 = call(
        functools.partial(gate_kernel, slot_dev),
        [(message, f32), (message, bf16), (message, bf16), (message, bf16)],
        [spec()] * 9,
        (
            *two_hop(home, sents),
            gain,
            stats,
            w_gate.reshape(slot_dev * width, hidden),
            w_up.reshape(slot_dev * width, hidden),
        ),
        scratch=[
            pltpu.VMEM((packed_count, width), bf16),
            pltpu.VMEM((packed_count, slot_dev * width), bf16),
        ],
        mebibytes=12,
        flops=800_000_000,
        moved=4_000_000,
    )
    parts = [partner_permute(block, "tp", k) for k, block in enumerate((sent1, sent2, sent3), 1)]
    own, first_weight = call(
        hidden_kernel,
        [((quarter, hidden), bf16), ((row_count, 128), f32)],
        [spec()] * 4,
        (own, *parts),
    )
    parts = [partner_permute(own, "tp", k) for k in (1, 2, 3)]
    home, *sents = call(
        functools.partial(down_kernel, slot_dev),
        [block] * 4,
        [spec()] * 5,
        (own, *parts, w_down.reshape(slot_dev * hidden, width)),
        scratch=[pltpu.VMEM((packed_count, slot_dev * hidden), bf16)],
        flops=200_000_000,
        moved=2_000_000,
    )
    (layer_out,) = call(
        combine_kernel,
        [((row_count, width), bf16)],
        [spec()] * 9,
        (*two_hop(home, sents), pick0, pick1, first_weight, attended),
        scratch=[pltpu.VMEM((packed_count, width), bf16)],
    )
    return (result, layer_out)


def solution(mesh):
    placed = (
        P("req", "tp"),
        P("req", "tp"),
        P("req", "tp"),
        P("req", "tp"),
        P("req", None, "tp"),
        P("req", None, "tp"),
        P("req"),
        P("tp", None),
        P("tp"),
        P("tp", None),
        P("req", None),
        P("req", "tp", None),
        P("req", "tp", None),
        P("req", None, "tp"),
    )
    return jax.shard_map(
        shards,
        mesh=mesh,
        in_specs=placed,
        out_specs=(P("req", "tp"), P("req", "tp")),
        check_vma=False,
    )
```

```python
import functools
import math

import jax
import jax.numpy as jnp
from jax import lax
from jax.experimental import pallas as pl
from jax.experimental.pallas import tpu as pltpu
from jax.sharding import PartitionSpec as P

D = 1536
HEAD_DIM = 64
EXPERTS = 16
TOP = 2
CAP = 8


def attend_local(queries, new_keys, new_values, k_cache, v_cache, lengths):
    row_count = queries.shape[0]
    kv_local = new_keys.shape[1] // HEAD_DIM
    group_size = queries.shape[1] // HEAD_DIM // kv_local
    cache_len = k_cache.shape[1]
    score_scale = 1.0 / math.sqrt(HEAD_DIM)
    query = queries.reshape(row_count, kv_local, group_size, HEAD_DIM)
    keys_all = k_cache.reshape(row_count, cache_len, kv_local, HEAD_DIM)
    values_all = v_cache.reshape(row_count, cache_len, kv_local, HEAD_DIM)
    scores = (
        jnp.einsum("bgqd,blgd->bgql", query, keys_all, preferred_element_type=jnp.float32)
        * score_scale
    )
    self_score = (
        jnp.einsum(
            "bgqd,bgd->bgq",
            query,
            new_keys.reshape(row_count, kv_local, HEAD_DIM),
            preferred_element_type=jnp.float32,
        )
        * score_scale
    )
    valid_mask = (jnp.arange(cache_len, dtype=jnp.int32)[None, :] < lengths[:, None])[
        :, None, None, :
    ]
    peak_score = jnp.maximum(jnp.max(jnp.where(valid_mask, scores, -1e30), axis=-1), self_score)
    exp_terms = jnp.where(valid_mask, jnp.exp(scores - peak_score[..., None]), 0.0)
    self_exp = jnp.exp(self_score - peak_score)
    denom_sum = jnp.sum(exp_terms, axis=-1) + self_exp
    weights = (exp_terms / denom_sum[..., None]).astype(jnp.bfloat16)
    self_weight = (self_exp / denom_sum).astype(jnp.bfloat16)
    value_self = new_values.astype(jnp.float32).reshape(row_count, kv_local, 1, HEAD_DIM)
    mixed = (
        jnp.einsum("bgql,blgd->bgqd", weights, values_all, preferred_element_type=jnp.float32)
        + self_weight.astype(jnp.float32)[..., None] * value_self
    )
    return mixed.astype(jnp.bfloat16).reshape(row_count, kv_local * group_size * HEAD_DIM)


def shards_general(
    resid,
    queries,
    new_keys,
    new_values,
    k_cache,
    v_cache,
    lengths,
    w_out,
    norm_gain,
    w_router,
    routes,
    w_gate,
    w_up,
    w_down,
):
    req_dev = resid.shape[0]
    width_local = resid.shape[1]
    slot_dev = w_gate.shape[0]
    req_count = lax.axis_size("req")
    shard_count = max(1, req_count // EXPERTS)
    attention = attend_local(queries, new_keys, new_values, k_cache, v_cache, lengths)
    partial_value = jnp.dot(attention, w_out, preferred_element_type=jnp.float32)
    projected = lax.psum_scatter(partial_value, "tp", scatter_dimension=1, tiled=True)
    attended = (resid.astype(jnp.float32) + projected).astype(jnp.bfloat16)
    attended_f = attended.astype(jnp.float32)
    scaled = attended_f * norm_gain[None, :]
    square_sum, logit_part = lax.psum(
        (
            jnp.sum(attended_f * attended_f, axis=1),
            jnp.dot(scaled, w_router, precision=lax.Precision.HIGHEST),
        ),
        "tp",
    )
    inv_rms = 1.0 / jnp.sqrt(square_sum / D + 1e-06)
    normed = (scaled * inv_rms[:, None]).astype(jnp.bfloat16)
    logits = logit_part * inv_rms[:, None]
    expert_ids = jnp.arange(EXPERTS, dtype=jnp.int32)
    first_logit = jnp.sum(jnp.where(routes[:, 0:1] == expert_ids[None, :], logits, 0.0), axis=1)
    second_logit = jnp.sum(jnp.where(routes[:, 1:2] == expert_ids[None, :], logits, 0.0), axis=1)
    first_weight = jax.nn.sigmoid(first_logit - second_logit)
    second_weight = 1.0 - first_weight
    flat_routes = routes.reshape(req_dev * TOP)
    one_hot = (flat_routes[None, :] == expert_ids[:, None]).astype(jnp.int32)
    rank_in = jnp.cumsum(one_hot, axis=1) - one_hot
    slot_ids = jnp.arange(CAP, dtype=jnp.int32)
    chosen = (one_hot[:, None, :] == 1) & (rank_in[:, None, :] == slot_ids[None, :, None])
    token_pick = jnp.sum(
        chosen.reshape(EXPERTS, CAP, req_dev, TOP).astype(jnp.int32), axis=-1
    ).astype(jnp.bfloat16)
    per_expert = jnp.einsum(
        "ecb,bd->ecd", token_pick, normed, preferred_element_type=jnp.float32
    ).astype(jnp.bfloat16)
    outgoing = jnp.broadcast_to(
        per_expert[:, None], (EXPERTS, shard_count, CAP, width_local)
    ).reshape(req_count, slot_dev, CAP, width_local)
    incoming = lax.all_to_all(outgoing, "req", split_axis=0, concat_axis=0, tiled=True)
    gate_pre = jnp.einsum("nscd,sdf->nscf", incoming, w_gate, preferred_element_type=jnp.float32)
    up_pre = jnp.einsum("nscd,sdf->nscf", incoming, w_up, preferred_element_type=jnp.float32)
    gate_sum, up_sum = lax.psum((gate_pre, up_pre), "tp")
    hidden = (jax.nn.silu(gate_sum) * up_sum).astype(jnp.bfloat16)
    computed = jnp.einsum("nscf,sfd->nscd", hidden, w_down, preferred_element_type=jnp.float32)
    returned = lax.all_to_all(computed, "req", split_axis=0, concat_axis=0, tiled=True)
    combined = jnp.sum(returned.reshape(EXPERTS, shard_count, CAP, width_local), axis=1)
    route_out = jnp.einsum(
        "ecr,ecd->rd", chosen.astype(jnp.float32), combined, precision=lax.Precision.HIGHEST
    ).reshape(req_dev, TOP, width_local)
    moe = first_weight[:, None] * route_out[:, 0] + second_weight[:, None] * route_out[:, 1]
    layer_out = (attended_f + moe).astype(jnp.bfloat16)
    return (attended, layer_out)


TP_ORDER = (0, 2, 3, 1)


def spec(space=pltpu.VMEM):
    return pl.BlockSpec(memory_space=space)


def call(kernel, outs, ins, operands, scratch=(), mebibytes=8, flops=100_000, moved=100_000):
    return pl.pallas_call(
        kernel,
        out_shape=[jax.ShapeDtypeStruct(shape, dtype) for shape, dtype in outs],
        in_specs=ins,
        out_specs=[spec() for _ in outs],
        scratch_shapes=scratch,
        compiler_params=pltpu.CompilerParams(vmem_limit_bytes=mebibytes << 20),
        cost_estimate=pl.CostEstimate(flops=flops, bytes_accessed=moved, transcendentals=0),
    )(*operands)


def partner_permute(block, axis, distance):
    count = lax.axis_size(axis)
    return lax.ppermute(block, axis, [(i, i ^ distance) for i in range(count)])


def attend_kernel(
    slot_dev, lengths_hbm, routes_hbm, queries_hbm, keys_hbm, values_hbm, router_hbm, k_hbm, v_hbm,
    w_hbm, own, sent1, sent2, sent3, pick0, pick1, pick_rows, router_rows,
    lengths, routes, queries, new_keys, new_values, w_router, k_buf, v_buf, w_buf,
    query_s, self_s, score_s, weight_s, small_sems, sems,
):
    row_count = queries.shape[0]
    width = own.shape[1]
    lanes = 2 * HEAD_DIM
    cache_len = k_hbm.shape[1]
    packed_count = pick0.shape[1]
    chunks = 4
    small = [
        pltpu.make_async_copy(source, target, small_sems.at[index])
        for index, (source, target) in enumerate(
            (
                (routes_hbm, routes),
                (router_hbm, w_router),
                (queries_hbm, queries),
                (keys_hbm, new_keys),
                (values_hbm, new_values),
                (lengths_hbm, lengths),
            )
        )
    ]
    copies = []
    for source, target in ((k_hbm, k_buf), (v_hbm, v_buf), (w_hbm, w_buf)):
        size = source.shape[0] // chunks
        for chunk in range(chunks):
            part = pl.ds(chunk * size, size)
            copies.append(
                pltpu.make_async_copy(source.at[part], target.at[part], sems.at[len(copies)])
            )
    for copy in small + copies:
        copy.start()
    per_chunk = row_count // chunks

    small[0].wait()
    route0, route1 = routes[0:1, :], routes[1:2, :]
    place = lax.broadcasted_iota(jnp.int32, (packed_count, row_count), 0)
    named0 = jnp.where(place == route0, 1.0, 0.0)
    named1 = jnp.where(place == route1, 1.0, 0.0)
    row_of = lax.broadcasted_iota(jnp.int32, (row_count, row_count), 0)
    col_of = lax.broadcasted_iota(jnp.int32, (row_count, row_count), 1)
    earlier = jnp.where(row_of < col_of, 1.0, 0.0).astype(jnp.bfloat16)
    before = jnp.dot(
        (named0 + named1).astype(jnp.bfloat16), earlier, preferred_element_type=jnp.float32
    )
    place_req = lax.axis_index("req")

    def pick(route, named, mine):
        rank = jnp.sum(named * before, axis=0, keepdims=True).astype(jnp.int32)
        block = ((route // slot_dev) ^ mine) * slot_dev + lax.rem(route, slot_dev)
        return jnp.where(place == block * CAP + rank, 1.0, 0.0)

    sent_rows = pick(route0, named0, place_req) + pick(route1, named1, place_req)
    pick_rows[...] = sent_rows.astype(jnp.bfloat16)
    pick0[...] = jnp.transpose(pick(route0, named0, 0)).astype(jnp.bfloat16)
    pick1[...] = jnp.transpose(pick(route1, named1, 0)).astype(jnp.bfloat16)
    signed = jnp.transpose(named0 - named1)
    small[1].wait()
    router_rows[...] = jnp.dot(
        signed[:, :EXPERTS], w_router[...],
        precision=lax.Precision.HIGHEST, preferred_element_type=jnp.float32,
    )
    for copy in small[2:]:
        copy.wait()

    low = lax.broadcasted_iota(jnp.int32, (row_count, lanes), 1) < HEAD_DIM
    tiles = [queries[:, i * lanes : (i + 1) * lanes].astype(jnp.float32) for i in range(3)]
    heads = [
        jnp.where(low, tiles[0], 0.0),
        jnp.where(low, pltpu.roll(tiles[0], HEAD_DIM, 1), 0.0),
        jnp.where(low, tiles[1], 0.0),
        jnp.where(low, 0.0, tiles[1]),
        jnp.where(low, 0.0, pltpu.roll(tiles[2], HEAD_DIM, 1)),
        jnp.where(low, 0.0, tiles[2]),
    ]
    scale = 1.0 / math.sqrt(HEAD_DIM)
    keys_new = new_keys[...].astype(jnp.float32)
    zeros = jnp.zeros((row_count, lanes), jnp.float32)
    for head in range(8):
        rows = pl.ds(head, row_count, stride=8)
        if head < 6:
            own_score = jnp.sum(heads[head] * keys_new, axis=1, keepdims=True) * scale
            query_s[rows, :] = heads[head]
            self_s[rows, :] = jnp.broadcast_to(own_score, zeros.shape)
        else:
            query_s[rows, :] = zeros
            self_s[rows, :] = zeros

    pair_row = lax.broadcasted_iota(jnp.int32, (16, 2 * cache_len), 0)
    pair_lane = lax.broadcasted_iota(jnp.int32, (16, 2 * cache_len), 1)
    upper = pair_row < 8
    place = jnp.where(upper, pair_lane, pair_lane - cache_len)
    place = jnp.where(place < 0, cache_len, place)
    for pair in range(row_count // 2):
        if pair % (per_chunk // 2) == 0:
            copies[pair // (per_chunk // 2)].wait()
        pair_rows = slice(16 * pair, 16 * pair + 16)
        keys = k_buf[2 * pair : 2 * pair + 2].reshape(2 * cache_len, lanes)
        raw = lax.dot_general(
            query_s[pair_rows, :].astype(jnp.bfloat16), keys, (((1,), (1,)), ((), ())),
            preferred_element_type=jnp.float32,
        )
        limit = jnp.where(upper, lengths[2 * pair], lengths[2 * pair + 1])
        score_s[pair_rows, :] = jnp.where(place < limit, raw * scale, -1e30)

    own_score = self_s[:, 0:1]
    scores = score_s[...]
    peak = jnp.maximum(jnp.max(scores, axis=1, keepdims=True), own_score)
    terms = jnp.exp(scores - peak)
    own_term = jnp.exp(own_score - peak)
    inverse = 1.0 / (jnp.sum(terms, axis=1, keepdims=True) + own_term)
    weight_s[...] = (terms * inverse).astype(jnp.bfloat16)
    own_weight = (own_term * inverse).astype(jnp.bfloat16).astype(jnp.float32)
    self_s[...] = jnp.broadcast_to(own_weight, self_s.shape)
    for pair in range(row_count // 2):
        if pair % (per_chunk // 2) == 0:
            copies[chunks + pair // (per_chunk // 2)].wait()
        pair_rows = slice(16 * pair, 16 * pair + 16)
        values = v_buf[2 * pair : 2 * pair + 2].reshape(2 * cache_len, lanes)
        query_s[pair_rows, :] = jnp.dot(
            weight_s[pair_rows, :], values, preferred_element_type=jnp.float32
        )

    values_new = new_values[...].astype(jnp.float32)
    mixed = []
    for head in range(6):
        rows = pl.ds(head, row_count, stride=8)
        mixed.append(query_s[rows, :] + self_s[rows, :] * values_new)
    attention = jnp.concatenate(
        [
            jnp.where(low, mixed[0], pltpu.roll(mixed[1], HEAD_DIM, 1)),
            jnp.where(low, mixed[2], mixed[3]),
            jnp.where(low, pltpu.roll(mixed[4], HEAD_DIM, 1), mixed[5]),
        ],
        axis=1,
    ).astype(jnp.bfloat16)
    for copy in copies[2 * chunks :]:
        copy.wait()
    place_tp = lax.axis_index("tp")
    for shift, out in zip(TP_ORDER, (own, sent1, sent2, sent3)):
        columns = pl.ds(pl.multiple_of((place_tp ^ shift) * width, width), width)
        out[...] = jnp.dot(
            attention, w_buf[:, columns], preferred_element_type=jnp.float32
        ).astype(out.dtype)


def ready_kernel(own, resid, pick_rows, base, pick_near):
    base[...] = own[...] + resid[...].astype(jnp.float32)
    pick_near[...] = pick_rows[...]


def pack_kernel(base, part1, part2, part3, pick_rows, attended, home, sent1, sent2, sent3):
    total = base[...]
    for part in (part1, part2, part3):
        total = total + part[...].astype(jnp.float32)
    rows = total.astype(jnp.bfloat16)
    attended[...] = rows
    packed = jnp.dot(pick_rows[...], rows, preferred_element_type=jnp.float32)
    size = home.shape[0]
    for distance, out in enumerate((home, sent1, sent2, sent3)):
        out[...] = packed[distance * size : (distance + 1) * size].astype(out.dtype)


def stats_kernel(attended, gain, router_rows, stats, result):
    result[...] = attended[...]
    rows = attended[...].astype(jnp.float32)
    square = jnp.sum(rows * rows, axis=1, keepdims=True)
    logit = jnp.sum(rows * gain[...] * router_rows[...], axis=1, keepdims=True)
    lane = lax.broadcasted_iota(jnp.int32, stats.shape, 1)
    stats[...] = jnp.where(lane == 0, square, jnp.where(lane == 1, logit, 0.0))


def turn_kernel(home, part1, part2, part3, along):
    half = home.shape[0] // 2
    for index, part in enumerate((home, part1, part2, part3)):
        along[index * half : (index + 1) * half, :] = part[half:, :]


def slot_masks(row_count, slot_dev):
    slot = lax.rem(lax.broadcasted_iota(jnp.int32, (row_count, 1), 0) // CAP, slot_dev)
    return [slot == index for index in range(slot_dev)]


def split_high(column):
    high = column.astype(jnp.bfloat16).astype(jnp.float32)
    return high, column - high


def gate_terms(slot_dev, blocks, gain, stats, w_gate, w_up, outs, lhs):
    size = outs[0].shape[0]
    width = blocks.shape[1]
    hidden = w_gate.shape[1]
    place_tp = lax.axis_index("tp")
    masks = slot_masks(size, slot_dev)
    lane = lax.broadcasted_iota(jnp.int32, (size, 128), 1)
    for order, (shift, out) in enumerate(zip(TP_ORDER, outs)):
        rows = blocks[
            pl.ds(pl.multiple_of((place_tp ^ shift) * size, size), size), :
        ].astype(jnp.float32)
        columns = [jnp.sum(rows * rows, axis=1, keepdims=True)]
        if stats is not None:
            for first in range(0, stats.shape[0], size):
                columns += [stats[first : first + size, 0:1], stats[first : first + size, 1:2]]
        extra = jnp.zeros((size, 128), jnp.float32)
        for index, column in enumerate(columns):
            high, low = split_high(column)
            extra = jnp.where(lane == 2 * index, high, extra)
            extra = jnp.where(lane == 2 * index + 1, low, extra)
        out[:, 2 * hidden :] = extra.astype(out.dtype)
        scaled = rows * gain[...]
        for index, mask in enumerate(masks):
            lhs[order * size : (order + 1) * size, index * width : (index + 1) * width] = (
                jnp.where(mask, scaled, 0.0).astype(jnp.bfloat16)
            )
    left = lhs[...]
    for first, weight in ((0, w_gate), (hidden, w_up)):
        product = jnp.dot(left, weight[...], preferred_element_type=jnp.float32)
        for order, out in enumerate(outs):
            out[:, first : first + hidden] = product[order * size : (order + 1) * size].astype(
                out.dtype
            )


def early_kernel(slot_dev, in0, in1, in2, in3, gain, w_gate, w_up, *refs):
    *outs, blocks, lhs = refs
    half = outs[0].shape[0]
    for index, part in enumerate((in0, in1, in2, in3)):
        blocks[index * half : (index + 1) * half, :] = part[:half, :]
    gate_terms(slot_dev, blocks, gain, None, w_gate, w_up, outs, lhs)


def late_kernel(slot_dev, blocks, gain, stats, w_gate, w_up, *refs):
    *outs, lhs = refs
    gate_terms(slot_dev, blocks, gain, stats, w_gate, w_up, outs, lhs)


def hidden_kernel(*refs):
    early, late, (hidden, first_weight) = refs[:4], refs[4:8], refs[8:]
    width = hidden.shape[1]
    half = hidden.shape[0] // 2

    def total(parts, columns):
        result = parts[0][:, columns]
        for part in parts[1:]:
            result = result + part[:, columns].astype(jnp.float32)
        return result

    def inverse_rms(columns, index):
        square = columns[:, index : index + 1] + columns[:, index + 1 : index + 2]
        return 1.0 / jnp.sqrt(square / D + 1e-06)

    for index, parts in enumerate((early, late)):
        extra = total(parts, slice(2 * width, 2 * width + 128))
        row_inv = inverse_rms(extra, 0)
        gate = total(parts, slice(0, width)) * row_inv
        up = total(parts, slice(width, 2 * width)) * row_inv
        hidden[index * half : (index + 1) * half, :] = (
            gate / (1.0 + jnp.exp(-gate)) * up
        ).astype(jnp.bfloat16)
    for index in range(first_weight.shape[0] // half):
        place = 2 + 4 * index
        logit = extra[:, place + 2 : place + 3] + extra[:, place + 3 : place + 4]
        weight = 1.0 / (1.0 + jnp.exp(-logit * inverse_rms(extra, place)))
        first_weight[index * half : (index + 1) * half, :] = jnp.broadcast_to(weight, (half, 128))


def down_kernel(slot_dev, own, part1, part2, part3, w_down, computed, lhs):
    quarter, width = own.shape
    block = computed.shape[1]
    place_tp = lax.axis_index("tp")
    place_req = lax.axis_index("req")
    masks = slot_masks(quarter, slot_dev)
    for shift, part in enumerate((own, part1, part2, part3)):
        rows = part[...].astype(jnp.float32)
        place = pl.ds(pl.multiple_of((place_tp ^ shift) * quarter, quarter), quarter)
        for index, mask in enumerate(masks):
            lhs[place, index * width : (index + 1) * width] = jnp.where(mask, rows, 0.0).astype(
                jnp.bfloat16
            )
    product = jnp.dot(lhs[...], w_down[...], preferred_element_type=jnp.float32)
    for index in range(computed.shape[0]):
        computed[place_req ^ index] = product[index * block : (index + 1) * block].astype(
            computed.dtype
        )


def combine_kernel(returned, pick0, pick1, first_weight, attended, layer_out):
    rows = returned[...]
    out0 = jnp.dot(pick0[...], rows, preferred_element_type=jnp.float32)
    out1 = jnp.dot(pick1[...], rows, preferred_element_type=jnp.float32)
    weight = first_weight[:, 0:1]
    moe = weight * out0 + (1.0 - weight) * out1
    layer_out[...] = (attended[...].astype(jnp.float32) + moe).astype(jnp.bfloat16)


def shards(
    resid,
    queries,
    new_keys,
    new_values,
    k_cache,
    v_cache,
    lengths,
    w_out,
    norm_gain,
    w_router,
    routes,
    w_gate,
    w_up,
    w_down,
):
    row_count, width = resid.shape
    slot_dev, _, hidden = w_gate.shape
    cache_len, lanes = k_cache.shape[1:]
    packed_count = EXPERTS * CAP
    quarter = packed_count // lax.axis_size("tp")
    if not (
        lax.axis_size("tp") == 4
        and lax.axis_size("req") == 8
        and 8 * slot_dev == EXPERTS
        and row_count == quarter
        and lanes == 2 * HEAD_DIM
        and queries.shape[1] == 6 * HEAD_DIM
    ):
        return shards_general(
            resid, queries, new_keys, new_values, k_cache, v_cache, lengths, w_out,
            norm_gain, w_router, routes, w_gate, w_up, w_down,
        )
    bf16, f32 = jnp.bfloat16, jnp.float32
    gain = norm_gain.reshape(1, width)
    own, sent1, sent2, sent3, pick0, pick1, pick_rows, router_rows = call(
        functools.partial(attend_kernel, slot_dev),
        [
            ((row_count, width), f32),
            ((row_count, width), bf16),
            ((row_count, width), bf16),
            ((row_count, width), bf16),
            ((row_count, packed_count), bf16),
            ((row_count, packed_count), bf16),
            ((packed_count, row_count), bf16),
            ((row_count, width), f32),
        ],
        [spec(pl.ANY)] * 9,
        (
            lengths, routes.T, queries, new_keys, new_values, w_router.T, k_cache, v_cache, w_out,
        ),
        scratch=[
            pltpu.SMEM(lengths.shape, jnp.int32),
            pltpu.VMEM(routes.shape[::-1], jnp.int32),
            pltpu.VMEM(queries.shape, bf16),
            pltpu.VMEM(new_keys.shape, bf16),
            pltpu.VMEM(new_values.shape, bf16),
            pltpu.VMEM(w_router.shape[::-1], f32),
            pltpu.VMEM(k_cache.shape, bf16),
            pltpu.VMEM(v_cache.shape, bf16),
            pltpu.VMEM(w_out.shape, bf16),
            pltpu.VMEM((8 * row_count, lanes), f32),
            pltpu.VMEM((8 * row_count, lanes), f32),
            pltpu.VMEM((8 * row_count, 2 * cache_len), f32),
            pltpu.VMEM((8 * row_count, 2 * cache_len), bf16),
            pltpu.SemaphoreType.DMA((6,)),
            pltpu.SemaphoreType.DMA((12,)),
        ],
        mebibytes=56,
        flops=200_000_000,
        moved=3_400_000,
    )
    def sum_exchange(sents):
        return [partner_permute(block, "tp", k) for k, block in zip(TP_ORDER[1:], sents)]

    parts = sum_exchange((sent1, sent2, sent3))
    base, pick_near = call(
        ready_kernel,
        [((row_count, width), f32), ((packed_count, row_count), bf16)],
        [spec()] * 3,
        (own, resid, pick_rows),
    )
    attended, home, *sents = call(
        pack_kernel,
        [((row_count, width), bf16)] + [((quarter, width), bf16)] * 4,
        [spec()] * 5,
        (base, *parts, pick_near),
    )
    stats, result = call(
        stats_kernel,
        [((row_count, 128), f32), ((row_count, width), bf16)],
        [spec()] * 3,
        (attended, gain, router_rows),
    )
    parts = [partner_permute(block, "req", 2 * k) for k, block in enumerate(sents, 1)]
    (along,) = call(
        turn_kernel, [((2 * quarter, width), bf16)], [spec()] * 4, (home, *parts)
    )
    along = partner_permute(along, "req", 1)
    weights = (w_gate.reshape(slot_dev * width, hidden), w_up.reshape(slot_dev * width, hidden))
    half = quarter // 2
    message = (half, 2 * hidden + 128)
    messages = [(message, f32)] + [(message, bf16)] * 3
    lhs = pltpu.VMEM((packed_count // 2, slot_dev * width), bf16)
    early, *sents = call(
        functools.partial(early_kernel, slot_dev),
        messages,
        [spec()] * 7,
        (home, *parts, gain, *weights),
        scratch=[pltpu.VMEM((2 * quarter, width), bf16), lhs],
        flops=400_000_000,
        moved=3_500_000,
    )
    early = (early, *sum_exchange(sents))
    late, *sents = call(
        functools.partial(late_kernel, slot_dev),
        messages,
        [spec()] * 5,
        (along, gain, stats, *weights),
        scratch=[lhs],
        flops=400_000_000,
        moved=3_500_000,
    )
    late = (late, *sum_exchange(sents))
    own, first_weight = call(
        hidden_kernel,
        [((quarter, hidden), bf16), ((row_count, 128), f32)],
        [spec()] * 8,
        (*early, *late),
    )
    parts = [partner_permute(own, "tp", k) for k in (1, 2, 3)]
    (computed,) = call(
        functools.partial(down_kernel, slot_dev),
        [((8, packed_count // 8, width), bf16)],
        [spec()] * 5,
        (own, *parts, w_down.reshape(slot_dev * hidden, width)),
        scratch=[pltpu.VMEM((packed_count, slot_dev * hidden), bf16)],
        flops=200_000_000,
        moved=2_000_000,
    )
    returned = lax.all_to_all(computed, "req", split_axis=0, concat_axis=0, tiled=True)
    (layer_out,) = call(
        combine_kernel,
        [((row_count, width), bf16)],
        [spec()] * 5,
        (returned.reshape(packed_count, width), pick0, pick1, first_weight, attended),
    )
    return (result, layer_out)


def solution(mesh):
    placed = (
        P("req", "tp"),
        P("req", "tp"),
        P("req", "tp"),
        P("req", "tp"),
        P("req", None, "tp"),
        P("req", None, "tp"),
        P("req"),
        P("tp", None),
        P("tp"),
        P("tp", None),
        P("req", None),
        P("req", "tp", None),
        P("req", "tp", None),
        P("req", None, "tp"),
    )
    return jax.shard_map(
        shards,
        mesh=mesh,
        in_specs=placed,
        out_specs=(P("req", "tp"), P("req", "tp")),
        check_vma=False,
    )
```

```python
import functools
import math

import jax
import jax.numpy as jnp
from jax import lax
from jax.experimental import pallas as pl
from jax.experimental.pallas import tpu as pltpu
from jax.sharding import PartitionSpec as P

D = 1536
HEAD_DIM = 64
EXPERTS = 16
TOP = 2
CAP = 8


def attend_local(queries, new_keys, new_values, k_cache, v_cache, lengths):
    row_count = queries.shape[0]
    kv_local = new_keys.shape[1] // HEAD_DIM
    group_size = queries.shape[1] // HEAD_DIM // kv_local
    cache_len = k_cache.shape[1]
    score_scale = 1.0 / math.sqrt(HEAD_DIM)
    query = queries.reshape(row_count, kv_local, group_size, HEAD_DIM)
    keys_all = k_cache.reshape(row_count, cache_len, kv_local, HEAD_DIM)
    values_all = v_cache.reshape(row_count, cache_len, kv_local, HEAD_DIM)
    scores = (
        jnp.einsum("bgqd,blgd->bgql", query, keys_all, preferred_element_type=jnp.float32)
        * score_scale
    )
    self_score = (
        jnp.einsum(
            "bgqd,bgd->bgq",
            query,
            new_keys.reshape(row_count, kv_local, HEAD_DIM),
            preferred_element_type=jnp.float32,
        )
        * score_scale
    )
    valid_mask = (jnp.arange(cache_len, dtype=jnp.int32)[None, :] < lengths[:, None])[
        :, None, None, :
    ]
    peak_score = jnp.maximum(jnp.max(jnp.where(valid_mask, scores, -1e30), axis=-1), self_score)
    exp_terms = jnp.where(valid_mask, jnp.exp(scores - peak_score[..., None]), 0.0)
    self_exp = jnp.exp(self_score - peak_score)
    denom_sum = jnp.sum(exp_terms, axis=-1) + self_exp
    weights = (exp_terms / denom_sum[..., None]).astype(jnp.bfloat16)
    self_weight = (self_exp / denom_sum).astype(jnp.bfloat16)
    value_self = new_values.astype(jnp.float32).reshape(row_count, kv_local, 1, HEAD_DIM)
    mixed = (
        jnp.einsum("bgql,blgd->bgqd", weights, values_all, preferred_element_type=jnp.float32)
        + self_weight.astype(jnp.float32)[..., None] * value_self
    )
    return mixed.astype(jnp.bfloat16).reshape(row_count, kv_local * group_size * HEAD_DIM)


def shards_general(
    resid,
    queries,
    new_keys,
    new_values,
    k_cache,
    v_cache,
    lengths,
    w_out,
    norm_gain,
    w_router,
    routes,
    w_gate,
    w_up,
    w_down,
):
    req_dev = resid.shape[0]
    width_local = resid.shape[1]
    slot_dev = w_gate.shape[0]
    req_count = lax.axis_size("req")
    shard_count = max(1, req_count // EXPERTS)
    attention = attend_local(queries, new_keys, new_values, k_cache, v_cache, lengths)
    partial_value = jnp.dot(attention, w_out, preferred_element_type=jnp.float32)
    projected = lax.psum_scatter(partial_value, "tp", scatter_dimension=1, tiled=True)
    attended = (resid.astype(jnp.float32) + projected).astype(jnp.bfloat16)
    attended_f = attended.astype(jnp.float32)
    scaled = attended_f * norm_gain[None, :]
    square_sum, logit_part = lax.psum(
        (
            jnp.sum(attended_f * attended_f, axis=1),
            jnp.dot(scaled, w_router, precision=lax.Precision.HIGHEST),
        ),
        "tp",
    )
    inv_rms = 1.0 / jnp.sqrt(square_sum / D + 1e-06)
    normed = (scaled * inv_rms[:, None]).astype(jnp.bfloat16)
    logits = logit_part * inv_rms[:, None]
    expert_ids = jnp.arange(EXPERTS, dtype=jnp.int32)
    first_logit = jnp.sum(jnp.where(routes[:, 0:1] == expert_ids[None, :], logits, 0.0), axis=1)
    second_logit = jnp.sum(jnp.where(routes[:, 1:2] == expert_ids[None, :], logits, 0.0), axis=1)
    first_weight = jax.nn.sigmoid(first_logit - second_logit)
    second_weight = 1.0 - first_weight
    flat_routes = routes.reshape(req_dev * TOP)
    one_hot = (flat_routes[None, :] == expert_ids[:, None]).astype(jnp.int32)
    rank_in = jnp.cumsum(one_hot, axis=1) - one_hot
    slot_ids = jnp.arange(CAP, dtype=jnp.int32)
    chosen = (one_hot[:, None, :] == 1) & (rank_in[:, None, :] == slot_ids[None, :, None])
    token_pick = jnp.sum(
        chosen.reshape(EXPERTS, CAP, req_dev, TOP).astype(jnp.int32), axis=-1
    ).astype(jnp.bfloat16)
    per_expert = jnp.einsum(
        "ecb,bd->ecd", token_pick, normed, preferred_element_type=jnp.float32
    ).astype(jnp.bfloat16)
    outgoing = jnp.broadcast_to(
        per_expert[:, None], (EXPERTS, shard_count, CAP, width_local)
    ).reshape(req_count, slot_dev, CAP, width_local)
    incoming = lax.all_to_all(outgoing, "req", split_axis=0, concat_axis=0, tiled=True)
    gate_pre = jnp.einsum("nscd,sdf->nscf", incoming, w_gate, preferred_element_type=jnp.float32)
    up_pre = jnp.einsum("nscd,sdf->nscf", incoming, w_up, preferred_element_type=jnp.float32)
    gate_sum, up_sum = lax.psum((gate_pre, up_pre), "tp")
    hidden = (jax.nn.silu(gate_sum) * up_sum).astype(jnp.bfloat16)
    computed = jnp.einsum("nscf,sfd->nscd", hidden, w_down, preferred_element_type=jnp.float32)
    returned = lax.all_to_all(computed, "req", split_axis=0, concat_axis=0, tiled=True)
    combined = jnp.sum(returned.reshape(EXPERTS, shard_count, CAP, width_local), axis=1)
    route_out = jnp.einsum(
        "ecr,ecd->rd", chosen.astype(jnp.float32), combined, precision=lax.Precision.HIGHEST
    ).reshape(req_dev, TOP, width_local)
    moe = first_weight[:, None] * route_out[:, 0] + second_weight[:, None] * route_out[:, 1]
    layer_out = (attended_f + moe).astype(jnp.bfloat16)
    return (attended, layer_out)


TP_ORDER = (0, 2, 3, 1)


def spec(space=pltpu.VMEM):
    return pl.BlockSpec(memory_space=space)


def call(kernel, outs, ins, operands, scratch=(), mebibytes=8, flops=100_000, moved=100_000):
    return pl.pallas_call(
        kernel,
        out_shape=[jax.ShapeDtypeStruct(shape, dtype) for shape, dtype in outs],
        in_specs=ins,
        out_specs=[spec() for _ in outs],
        scratch_shapes=scratch,
        compiler_params=pltpu.CompilerParams(vmem_limit_bytes=mebibytes << 20),
        cost_estimate=pl.CostEstimate(flops=flops, bytes_accessed=moved, transcendentals=0),
    )(*operands)


def partner_permute(block, axis, distance):
    count = lax.axis_size(axis)
    return lax.ppermute(block, axis, [(i, i ^ distance) for i in range(count)])


def attend_kernel(
    lengths_hbm, queries_hbm, keys_hbm, values_hbm, k_hbm, v_hbm, w_hbm, own, sent1, sent2, sent3,
    lengths, queries, new_keys, new_values, k_buf, v_buf, w_buf,
    query_s, self_s, score_s, weight_s, small_sems, sems,
):
    row_count = queries.shape[0]
    width = own.shape[1]
    lanes = 2 * HEAD_DIM
    cache_len = k_hbm.shape[1]
    chunks = 4
    small = [
        pltpu.make_async_copy(source, target, small_sems.at[index])
        for index, (source, target) in enumerate(
            (
                (queries_hbm, queries),
                (keys_hbm, new_keys),
                (values_hbm, new_values),
                (lengths_hbm, lengths),
            )
        )
    ]
    copies = []
    for source, target in ((k_hbm, k_buf), (v_hbm, v_buf), (w_hbm, w_buf)):
        size = source.shape[0] // chunks
        for chunk in range(chunks):
            part = pl.ds(chunk * size, size)
            copies.append(
                pltpu.make_async_copy(source.at[part], target.at[part], sems.at[len(copies)])
            )
    for copy in small + copies:
        copy.start()
    per_chunk = row_count // chunks

    for copy in small:
        copy.wait()

    low = lax.broadcasted_iota(jnp.int32, (row_count, lanes), 1) < HEAD_DIM
    tiles = [queries[:, i * lanes : (i + 1) * lanes].astype(jnp.float32) for i in range(3)]
    heads = [
        jnp.where(low, tiles[0], 0.0),
        jnp.where(low, pltpu.roll(tiles[0], HEAD_DIM, 1), 0.0),
        jnp.where(low, tiles[1], 0.0),
        jnp.where(low, 0.0, tiles[1]),
        jnp.where(low, 0.0, pltpu.roll(tiles[2], HEAD_DIM, 1)),
        jnp.where(low, 0.0, tiles[2]),
    ]
    scale = 1.0 / math.sqrt(HEAD_DIM)
    keys_new = new_keys[...].astype(jnp.float32)
    zeros = jnp.zeros((row_count, lanes), jnp.float32)
    for head in range(8):
        rows = pl.ds(head, row_count, stride=8)
        if head < 6:
            own_score = jnp.sum(heads[head] * keys_new, axis=1, keepdims=True) * scale
            query_s[rows, :] = heads[head]
            self_s[rows, :] = jnp.broadcast_to(own_score, zeros.shape)
        else:
            query_s[rows, :] = zeros
            self_s[rows, :] = zeros

    pair_row = lax.broadcasted_iota(jnp.int32, (16, 2 * cache_len), 0)
    pair_lane = lax.broadcasted_iota(jnp.int32, (16, 2 * cache_len), 1)
    upper = pair_row < 8
    place = jnp.where(upper, pair_lane, pair_lane - cache_len)
    place = jnp.where(place < 0, cache_len, place)
    for pair in range(row_count // 2):
        if pair % (per_chunk // 2) == 0:
            copies[pair // (per_chunk // 2)].wait()
        pair_rows = slice(16 * pair, 16 * pair + 16)
        keys = k_buf[2 * pair : 2 * pair + 2].reshape(2 * cache_len, lanes)
        raw = lax.dot_general(
            query_s[pair_rows, :].astype(jnp.bfloat16), keys, (((1,), (1,)), ((), ())),
            preferred_element_type=jnp.float32,
        )
        limit = jnp.where(upper, lengths[2 * pair], lengths[2 * pair + 1])
        score_s[pair_rows, :] = jnp.where(place < limit, raw * scale, -1e30)

    own_score = self_s[:, 0:1]
    scores = score_s[...]
    peak = jnp.maximum(jnp.max(scores, axis=1, keepdims=True), own_score)
    terms = jnp.exp(scores - peak)
    own_term = jnp.exp(own_score - peak)
    inverse = 1.0 / (jnp.sum(terms, axis=1, keepdims=True) + own_term)
    weight_s[...] = (terms * inverse).astype(jnp.bfloat16)
    own_weight = (own_term * inverse).astype(jnp.bfloat16).astype(jnp.float32)
    self_s[...] = jnp.broadcast_to(own_weight, self_s.shape)
    for pair in range(row_count // 2):
        if pair % (per_chunk // 2) == 0:
            copies[chunks + pair // (per_chunk // 2)].wait()
        pair_rows = slice(16 * pair, 16 * pair + 16)
        values = v_buf[2 * pair : 2 * pair + 2].reshape(2 * cache_len, lanes)
        query_s[pair_rows, :] = jnp.dot(
            weight_s[pair_rows, :], values, preferred_element_type=jnp.float32
        )

    values_new = new_values[...].astype(jnp.float32)
    mixed = []
    for head in range(6):
        rows = pl.ds(head, row_count, stride=8)
        mixed.append(query_s[rows, :] + self_s[rows, :] * values_new)
    attention = jnp.concatenate(
        [
            jnp.where(low, mixed[0], pltpu.roll(mixed[1], HEAD_DIM, 1)),
            jnp.where(low, mixed[2], mixed[3]),
            jnp.where(low, pltpu.roll(mixed[4], HEAD_DIM, 1), mixed[5]),
        ],
        axis=1,
    ).astype(jnp.bfloat16)
    for copy in copies[2 * chunks :]:
        copy.wait()
    place_tp = lax.axis_index("tp")
    for shift, out in zip(TP_ORDER, (own, sent1, sent2, sent3)):
        columns = pl.ds(pl.multiple_of((place_tp ^ shift) * width, width), width)
        out[...] = jnp.dot(
            attention, w_buf[:, columns], preferred_element_type=jnp.float32
        ).astype(out.dtype)


def ready_kernel(
    slot_dev, own, resid, routes, w_router, base, pick_rows, pick0, pick1, router_rows
):
    base[...] = own[...] + resid[...].astype(jnp.float32)
    packed_count, row_count = pick_rows.shape

    route0, route1 = routes[0:1, :], routes[1:2, :]
    place = lax.broadcasted_iota(jnp.int32, (packed_count, row_count), 0)
    named0 = jnp.where(place == route0, 1.0, 0.0)
    named1 = jnp.where(place == route1, 1.0, 0.0)
    row_of = lax.broadcasted_iota(jnp.int32, (row_count, row_count), 0)
    col_of = lax.broadcasted_iota(jnp.int32, (row_count, row_count), 1)
    earlier = jnp.where(row_of < col_of, 1.0, 0.0).astype(jnp.bfloat16)
    before = jnp.dot(
        (named0 + named1).astype(jnp.bfloat16), earlier, preferred_element_type=jnp.float32
    )
    place_req = lax.axis_index("req")

    def pick(route, named, mine):
        rank = jnp.sum(named * before, axis=0, keepdims=True).astype(jnp.int32)
        block = ((route // slot_dev) ^ mine) * slot_dev + lax.rem(route, slot_dev)
        return jnp.where(place == block * CAP + rank, 1.0, 0.0)

    sent_rows = pick(route0, named0, place_req) + pick(route1, named1, place_req)
    pick_rows[...] = sent_rows.astype(jnp.bfloat16)
    pick0[...] = jnp.transpose(pick(route0, named0, 0)).astype(jnp.bfloat16)
    pick1[...] = jnp.transpose(pick(route1, named1, 0)).astype(jnp.bfloat16)
    signed = jnp.transpose(named0 - named1)
    router_rows[...] = jnp.dot(
        signed[:, :EXPERTS], w_router[...],
        precision=lax.Precision.HIGHEST, preferred_element_type=jnp.float32,
    )


def pack_kernel(base, part1, part2, part3, pick_rows, attended, home, sent1, sent2, sent3):
    total = base[...]
    for part in (part1, part2, part3):
        total = total + part[...].astype(jnp.float32)
    rows = total.astype(jnp.bfloat16)
    attended[...] = rows
    packed = jnp.dot(pick_rows[...], rows, preferred_element_type=jnp.float32)
    size = home.shape[0]
    for distance, out in enumerate((home, sent1, sent2, sent3)):
        out[...] = packed[distance * size : (distance + 1) * size].astype(out.dtype)


def stats_kernel(attended, gain, router_rows, stats, result):
    result[...] = attended[...]
    rows = attended[...].astype(jnp.float32)
    square = jnp.sum(rows * rows, axis=1, keepdims=True)
    logit = jnp.sum(rows * gain[...] * router_rows[...], axis=1, keepdims=True)
    lane = lax.broadcasted_iota(jnp.int32, stats.shape, 1)
    stats[...] = jnp.where(lane == 0, square, jnp.where(lane == 1, logit, 0.0))


def turn_kernel(home, part1, part2, part3, along):
    half = home.shape[0] // 2
    for index, part in enumerate((home, part1, part2, part3)):
        along[index * half : (index + 1) * half, :] = part[half:, :]


def slot_masks(row_count, slot_dev):
    slot = lax.rem(lax.broadcasted_iota(jnp.int32, (row_count, 1), 0) // CAP, slot_dev)
    return [slot == index for index in range(slot_dev)]


def split_high(column):
    high = column.astype(jnp.bfloat16).astype(jnp.float32)
    return high, column - high


def gate_terms(slot_dev, blocks, gain, stats, w_gate, w_up, kept, sent, lhs):
    size = kept.shape[0] // 2
    width = blocks.shape[1]
    hidden = w_gate.shape[1]
    place_tp = lax.axis_index("tp")
    masks = slot_masks(size, slot_dev)
    lane = lax.broadcasted_iota(jnp.int32, (size, 128), 1)
    for order, shift in enumerate((0, 2, 1, 3)):
        out, first_row = (kept, sent)[order // 2], order % 2 * size
        rows = blocks[
            pl.ds(pl.multiple_of((place_tp ^ shift) * size, size), size), :
        ].astype(jnp.float32)
        columns = [jnp.sum(rows * rows, axis=1, keepdims=True)]
        if stats is not None:
            for first in range(0, stats.shape[0], size):
                columns += [stats[first : first + size, 0:1], stats[first : first + size, 1:2]]
        extra = jnp.zeros((size, 128), jnp.float32)
        for index, column in enumerate(columns):
            high, low = split_high(column)
            extra = jnp.where(lane == 2 * index, high, extra)
            extra = jnp.where(lane == 2 * index + 1, low, extra)
        out[first_row : first_row + size, 2 * hidden :] = extra.astype(out.dtype)
        scaled = rows * gain[...]
        for index, mask in enumerate(masks):
            lhs[order * size : (order + 1) * size, index * width : (index + 1) * width] = (
                jnp.where(mask, scaled, 0.0).astype(jnp.bfloat16)
            )
    left = lhs[...]
    for first, weight in ((0, w_gate), (hidden, w_up)):
        product = jnp.dot(left, weight[...], preferred_element_type=jnp.float32)
        kept[:, first : first + hidden] = product[: 2 * size]
        sent[:, first : first + hidden] = product[2 * size :].astype(sent.dtype)


def early_kernel(
    slot_dev, in0, in1, in2, in3, gain, stats, w_gate, w_up, kept, sent, blocks, lhs
):
    half = kept.shape[0] // 2
    for index, part in enumerate((in0, in1, in2, in3)):
        blocks[index * half : (index + 1) * half, :] = part[:half, :]
    gate_terms(slot_dev, blocks, gain, stats, w_gate, w_up, kept, sent, lhs)


def late_kernel(slot_dev, blocks, gain, w_gate, w_up, kept, sent, lhs):
    gate_terms(slot_dev, blocks, gain, None, w_gate, w_up, kept, sent, lhs)


def chip_kernel(kept, part, own, sent):
    size, width = own.shape
    own[...] = kept[:size, :] + part[:size, :].astype(jnp.float32)
    total = kept[size:, :] + part[size:, :].astype(jnp.float32)
    extra = total[:, width - 128 :]
    lane = lax.broadcasted_iota(jnp.int32, extra.shape, 1)
    high, low = split_high(extra + pltpu.roll(extra, 127, 1))
    sent[:, : width - 128] = total[:, : width - 128].astype(sent.dtype)
    sent[:, width - 128 :] = jnp.where(
        lax.rem(lane, 2) == 0, high, pltpu.roll(low, 1, 1)
    ).astype(sent.dtype)


def hidden_kernel(*refs):
    late, early, (hidden, first_weight) = refs[:2], refs[2:4], refs[4:]
    width = hidden.shape[1]
    half = hidden.shape[0] // 2

    def total(parts, columns):
        result = parts[0][:, columns]
        for part in parts[1:]:
            result = result + part[:, columns].astype(jnp.float32)
        return result

    def inverse_rms(columns, index):
        square = columns[:, index : index + 1] + columns[:, index + 1 : index + 2]
        return 1.0 / jnp.sqrt(square / D + 1e-06)

    for index, parts in ((1, late), (0, early)):
        extra = total(parts, slice(2 * width, 2 * width + 128))
        row_inv = inverse_rms(extra, 0)
        gate = total(parts, slice(0, width)) * row_inv
        up = total(parts, slice(width, 2 * width)) * row_inv
        hidden[index * half : (index + 1) * half, :] = (
            gate / (1.0 + jnp.exp(-gate)) * up
        ).astype(jnp.bfloat16)
    for index in range(first_weight.shape[0] // half):
        place = 2 + 4 * index
        logit = extra[:, place + 2 : place + 3] + extra[:, place + 3 : place + 4]
        weight = 1.0 / (1.0 + jnp.exp(-logit * inverse_rms(extra, place)))
        first_weight[index * half : (index + 1) * half, :] = jnp.broadcast_to(weight, (half, 128))


def down_kernel(slot_dev, own, part1, part2, part3, w_down, computed, lhs):
    quarter, width = own.shape
    block = computed.shape[1]
    place_tp = lax.axis_index("tp")
    place_req = lax.axis_index("req")
    masks = slot_masks(quarter, slot_dev)
    for shift, part in enumerate((own, part1, part2, part3)):
        rows = part[...].astype(jnp.float32)
        place = pl.ds(pl.multiple_of((place_tp ^ shift) * quarter, quarter), quarter)
        for index, mask in enumerate(masks):
            lhs[place, index * width : (index + 1) * width] = jnp.where(mask, rows, 0.0).astype(
                jnp.bfloat16
            )
    product = jnp.dot(lhs[...], w_down[...], preferred_element_type=jnp.float32)
    for index in range(computed.shape[0]):
        computed[place_req ^ index] = product[index * block : (index + 1) * block].astype(
            computed.dtype
        )


def combine_kernel(returned, pick0, pick1, first_weight, attended, layer_out):
    rows = returned[...]
    out0 = jnp.dot(pick0[...], rows, preferred_element_type=jnp.float32)
    out1 = jnp.dot(pick1[...], rows, preferred_element_type=jnp.float32)
    weight = first_weight[:, 0:1]
    moe = weight * out0 + (1.0 - weight) * out1
    layer_out[...] = (attended[...].astype(jnp.float32) + moe).astype(jnp.bfloat16)


def shards(
    resid,
    queries,
    new_keys,
    new_values,
    k_cache,
    v_cache,
    lengths,
    w_out,
    norm_gain,
    w_router,
    routes,
    w_gate,
    w_up,
    w_down,
):
    row_count, width = resid.shape
    slot_dev, _, hidden = w_gate.shape
    cache_len, lanes = k_cache.shape[1:]
    packed_count = EXPERTS * CAP
    quarter = packed_count // lax.axis_size("tp")
    if not (
        lax.axis_size("tp") == 4
        and lax.axis_size("req") == 8
        and 8 * slot_dev == EXPERTS
        and row_count == quarter
        and lanes == 2 * HEAD_DIM
        and queries.shape[1] == 6 * HEAD_DIM
    ):
        return shards_general(
            resid, queries, new_keys, new_values, k_cache, v_cache, lengths, w_out,
            norm_gain, w_router, routes, w_gate, w_up, w_down,
        )
    bf16, f32 = jnp.bfloat16, jnp.float32
    gain = norm_gain.reshape(1, width)
    own, *sents = call(
        attend_kernel,
        [((row_count, width), f32)] + [((row_count, width), bf16)] * 3,
        [spec(pl.ANY)] * 7,
        (lengths, queries, new_keys, new_values, k_cache, v_cache, w_out),
        scratch=[
            pltpu.SMEM(lengths.shape, jnp.int32),
            pltpu.VMEM(queries.shape, bf16),
            pltpu.VMEM(new_keys.shape, bf16),
            pltpu.VMEM(new_values.shape, bf16),
            pltpu.VMEM(k_cache.shape, bf16),
            pltpu.VMEM(v_cache.shape, bf16),
            pltpu.VMEM(w_out.shape, bf16),
            pltpu.VMEM((8 * row_count, lanes), f32),
            pltpu.VMEM((8 * row_count, lanes), f32),
            pltpu.VMEM((8 * row_count, 2 * cache_len), f32),
            pltpu.VMEM((8 * row_count, 2 * cache_len), bf16),
            pltpu.SemaphoreType.DMA((4,)),
            pltpu.SemaphoreType.DMA((12,)),
        ],
        mebibytes=56,
        flops=200_000_000,
        moved=3_400_000,
    )
    def sum_exchange(sents):
        return [partner_permute(block, "tp", k) for k, block in zip(TP_ORDER[1:], sents)]

    parts = sum_exchange(sents)
    base, pick_rows, pick0, pick1, router_rows = call(
        functools.partial(ready_kernel, slot_dev),
        [
            ((row_count, width), f32),
            ((packed_count, row_count), bf16),
            ((row_count, packed_count), bf16),
            ((row_count, packed_count), bf16),
            ((row_count, width), f32),
        ],
        [spec()] * 4,
        (own, resid, routes.T, w_router.T),
    )
    attended, home, *sents = call(
        pack_kernel,
        [((row_count, width), bf16)] + [((quarter, width), bf16)] * 4,
        [spec()] * 5,
        (base, *parts, pick_rows),
    )
    stats, result = call(
        stats_kernel,
        [((row_count, 128), f32), ((row_count, width), bf16)],
        [spec()] * 3,
        (attended, gain, router_rows),
    )
    parts = [partner_permute(block, "req", 2 * k) for k, block in enumerate(sents, 1)]
    (along,) = call(
        turn_kernel, [((2 * quarter, width), bf16)], [spec()] * 4, (home, *parts)
    )
    along = partner_permute(along, "req", 1)
    weights = (w_gate.reshape(slot_dev * width, hidden), w_up.reshape(slot_dev * width, hidden))
    half = quarter // 2
    message = (half, 2 * hidden + 128)
    lhs = pltpu.VMEM((packed_count // 2, slot_dev * width), bf16)

    def chip_sums(kept, sent):
        own, sent = call(
            chip_kernel, [(message, f32), (message, bf16)], [spec()] * 2,
            (kept, partner_permute(sent, "tp", 1)),
        )
        return own, partner_permute(sent, "tp", 2)

    pair = (quarter, message[1])
    early = call(
        functools.partial(early_kernel, slot_dev),
        [(pair, f32), (pair, bf16)],
        [spec()] * 8,
        (home, *parts, gain, stats, *weights),
        scratch=[pltpu.VMEM((2 * quarter, width), bf16), lhs],
        flops=400_000_000,
        moved=3_500_000,
    )
    late = call(
        functools.partial(late_kernel, slot_dev),
        [(pair, f32), (pair, bf16)],
        [spec()] * 4,
        (along, gain, *weights),
        scratch=[lhs],
        flops=400_000_000,
        moved=3_500_000,
    )
    early = chip_sums(*early)
    late = chip_sums(*late)
    own, first_weight = call(
        hidden_kernel,
        [((quarter, hidden), bf16), ((row_count, 128), f32)],
        [spec()] * 4,
        (*late, *early),
    )
    across = partner_permute(own, "tp", 2)
    parts = [partner_permute(own, "tp", 1), across, partner_permute(across, "tp", 1)]
    (computed,) = call(
        functools.partial(down_kernel, slot_dev),
        [((8, packed_count // 8, width), bf16)],
        [spec()] * 5,
        (own, *parts, w_down.reshape(slot_dev * hidden, width)),
        scratch=[pltpu.VMEM((packed_count, slot_dev * hidden), bf16)],
        flops=200_000_000,
        moved=2_000_000,
    )
    returned = lax.all_to_all(computed, "req", split_axis=0, concat_axis=0, tiled=True)
    (layer_out,) = call(
        combine_kernel,
        [((row_count, width), bf16)],
        [spec()] * 5,
        (returned.reshape(packed_count, width), pick0, pick1, first_weight, attended),
    )
    return (result, layer_out)


def solution(mesh):
    placed = (
        P("req", "tp"),
        P("req", "tp"),
        P("req", "tp"),
        P("req", "tp"),
        P("req", None, "tp"),
        P("req", None, "tp"),
        P("req"),
        P("tp", None),
        P("tp"),
        P("tp", None),
        P("req", None),
        P("req", "tp", None),
        P("req", "tp", None),
        P("req", None, "tp"),
    )
    return jax.shard_map(
        shards,
        mesh=mesh,
        in_specs=placed,
        out_specs=(P("req", "tp"), P("req", "tp")),
        check_vma=False,
    )
```

```python
import functools
import math

import jax
import jax.numpy as jnp
from jax import lax
from jax.experimental import pallas as pl
from jax.experimental.pallas import tpu as pltpu
from jax.sharding import PartitionSpec as P

D = 1536
HEAD_DIM = 64
EXPERTS = 16
TOP = 2
CAP = 8


def attend_local(queries, new_keys, new_values, k_cache, v_cache, lengths):
    row_count = queries.shape[0]
    kv_local = new_keys.shape[1] // HEAD_DIM
    group_size = queries.shape[1] // HEAD_DIM // kv_local
    cache_len = k_cache.shape[1]
    score_scale = 1.0 / math.sqrt(HEAD_DIM)
    query = queries.reshape(row_count, kv_local, group_size, HEAD_DIM)
    keys_all = k_cache.reshape(row_count, cache_len, kv_local, HEAD_DIM)
    values_all = v_cache.reshape(row_count, cache_len, kv_local, HEAD_DIM)
    scores = (
        jnp.einsum("bgqd,blgd->bgql", query, keys_all, preferred_element_type=jnp.float32)
        * score_scale
    )
    self_score = (
        jnp.einsum(
            "bgqd,bgd->bgq",
            query,
            new_keys.reshape(row_count, kv_local, HEAD_DIM),
            preferred_element_type=jnp.float32,
        )
        * score_scale
    )
    valid_mask = (jnp.arange(cache_len, dtype=jnp.int32)[None, :] < lengths[:, None])[
        :, None, None, :
    ]
    peak_score = jnp.maximum(jnp.max(jnp.where(valid_mask, scores, -1e30), axis=-1), self_score)
    exp_terms = jnp.where(valid_mask, jnp.exp(scores - peak_score[..., None]), 0.0)
    self_exp = jnp.exp(self_score - peak_score)
    denom_sum = jnp.sum(exp_terms, axis=-1) + self_exp
    weights = (exp_terms / denom_sum[..., None]).astype(jnp.bfloat16)
    self_weight = (self_exp / denom_sum).astype(jnp.bfloat16)
    value_self = new_values.astype(jnp.float32).reshape(row_count, kv_local, 1, HEAD_DIM)
    mixed = (
        jnp.einsum("bgql,blgd->bgqd", weights, values_all, preferred_element_type=jnp.float32)
        + self_weight.astype(jnp.float32)[..., None] * value_self
    )
    return mixed.astype(jnp.bfloat16).reshape(row_count, kv_local * group_size * HEAD_DIM)


def shards_general(
    resid,
    queries,
    new_keys,
    new_values,
    k_cache,
    v_cache,
    lengths,
    w_out,
    norm_gain,
    w_router,
    routes,
    w_gate,
    w_up,
    w_down,
):
    req_dev = resid.shape[0]
    width_local = resid.shape[1]
    slot_dev = w_gate.shape[0]
    req_count = lax.axis_size("req")
    shard_count = max(1, req_count // EXPERTS)
    attention = attend_local(queries, new_keys, new_values, k_cache, v_cache, lengths)
    partial_value = jnp.dot(attention, w_out, preferred_element_type=jnp.float32)
    projected = lax.psum_scatter(partial_value, "tp", scatter_dimension=1, tiled=True)
    attended = (resid.astype(jnp.float32) + projected).astype(jnp.bfloat16)
    attended_f = attended.astype(jnp.float32)
    scaled = attended_f * norm_gain[None, :]
    square_sum, logit_part = lax.psum(
        (
            jnp.sum(attended_f * attended_f, axis=1),
            jnp.dot(scaled, w_router, precision=lax.Precision.HIGHEST),
        ),
        "tp",
    )
    inv_rms = 1.0 / jnp.sqrt(square_sum / D + 1e-06)
    normed = (scaled * inv_rms[:, None]).astype(jnp.bfloat16)
    logits = logit_part * inv_rms[:, None]
    expert_ids = jnp.arange(EXPERTS, dtype=jnp.int32)
    first_logit = jnp.sum(jnp.where(routes[:, 0:1] == expert_ids[None, :], logits, 0.0), axis=1)
    second_logit = jnp.sum(jnp.where(routes[:, 1:2] == expert_ids[None, :], logits, 0.0), axis=1)
    first_weight = jax.nn.sigmoid(first_logit - second_logit)
    second_weight = 1.0 - first_weight
    flat_routes = routes.reshape(req_dev * TOP)
    one_hot = (flat_routes[None, :] == expert_ids[:, None]).astype(jnp.int32)
    rank_in = jnp.cumsum(one_hot, axis=1) - one_hot
    slot_ids = jnp.arange(CAP, dtype=jnp.int32)
    chosen = (one_hot[:, None, :] == 1) & (rank_in[:, None, :] == slot_ids[None, :, None])
    token_pick = jnp.sum(
        chosen.reshape(EXPERTS, CAP, req_dev, TOP).astype(jnp.int32), axis=-1
    ).astype(jnp.bfloat16)
    per_expert = jnp.einsum(
        "ecb,bd->ecd", token_pick, normed, preferred_element_type=jnp.float32
    ).astype(jnp.bfloat16)
    outgoing = jnp.broadcast_to(
        per_expert[:, None], (EXPERTS, shard_count, CAP, width_local)
    ).reshape(req_count, slot_dev, CAP, width_local)
    incoming = lax.all_to_all(outgoing, "req", split_axis=0, concat_axis=0, tiled=True)
    gate_pre = jnp.einsum("nscd,sdf->nscf", incoming, w_gate, preferred_element_type=jnp.float32)
    up_pre = jnp.einsum("nscd,sdf->nscf", incoming, w_up, preferred_element_type=jnp.float32)
    gate_sum, up_sum = lax.psum((gate_pre, up_pre), "tp")
    hidden = (jax.nn.silu(gate_sum) * up_sum).astype(jnp.bfloat16)
    computed = jnp.einsum("nscf,sfd->nscd", hidden, w_down, preferred_element_type=jnp.float32)
    returned = lax.all_to_all(computed, "req", split_axis=0, concat_axis=0, tiled=True)
    combined = jnp.sum(returned.reshape(EXPERTS, shard_count, CAP, width_local), axis=1)
    route_out = jnp.einsum(
        "ecr,ecd->rd", chosen.astype(jnp.float32), combined, precision=lax.Precision.HIGHEST
    ).reshape(req_dev, TOP, width_local)
    moe = first_weight[:, None] * route_out[:, 0] + second_weight[:, None] * route_out[:, 1]
    layer_out = (attended_f + moe).astype(jnp.bfloat16)
    return (attended, layer_out)


TP_ORDER = (0, 2, 3, 1)


def spec(space=pltpu.VMEM):
    return pl.BlockSpec(memory_space=space)


def call(kernel, outs, ins, operands, scratch=(), mebibytes=8, flops=100_000, moved=100_000):
    return pl.pallas_call(
        kernel,
        out_shape=[jax.ShapeDtypeStruct(shape, dtype) for shape, dtype in outs],
        in_specs=ins,
        out_specs=[spec() for _ in outs],
        scratch_shapes=scratch,
        compiler_params=pltpu.CompilerParams(vmem_limit_bytes=mebibytes << 20),
        cost_estimate=pl.CostEstimate(flops=flops, bytes_accessed=moved, transcendentals=0),
    )(*operands)


def partner_permute(block, axis, distance):
    count = lax.axis_size(axis)
    return lax.ppermute(block, axis, [(i, i ^ distance) for i in range(count)])


def attend_kernel(
    lengths_hbm, queries_hbm, keys_hbm, values_hbm, k_hbm, v_hbm, w_hbm, own, sent1, sent2, sent3,
    lengths, queries, new_keys, new_values, k_buf, v_buf, w_buf,
    query_s, self_s, score_s, weight_s, small_sems, sems,
):
    row_count = queries.shape[0]
    width = own.shape[1]
    lanes = 2 * HEAD_DIM
    cache_len = k_hbm.shape[1]
    chunks = 4
    small = [
        pltpu.make_async_copy(source, target, small_sems.at[index])
        for index, (source, target) in enumerate(
            (
                (queries_hbm, queries),
                (keys_hbm, new_keys),
                (values_hbm, new_values),
                (lengths_hbm, lengths),
            )
        )
    ]
    copies = []
    for source, target in ((k_hbm, k_buf), (v_hbm, v_buf), (w_hbm, w_buf)):
        size = source.shape[0] // chunks
        for chunk in range(chunks):
            part = pl.ds(chunk * size, size)
            copies.append(
                pltpu.make_async_copy(source.at[part], target.at[part], sems.at[len(copies)])
            )
    for copy in small + copies:
        copy.start()
    per_chunk = row_count // chunks

    for copy in small:
        copy.wait()

    low = lax.broadcasted_iota(jnp.int32, (row_count, lanes), 1) < HEAD_DIM
    tiles = [queries[:, i * lanes : (i + 1) * lanes].astype(jnp.float32) for i in range(3)]
    heads = [
        jnp.where(low, tiles[0], 0.0),
        jnp.where(low, pltpu.roll(tiles[0], HEAD_DIM, 1), 0.0),
        jnp.where(low, tiles[1], 0.0),
        jnp.where(low, 0.0, tiles[1]),
        jnp.where(low, 0.0, pltpu.roll(tiles[2], HEAD_DIM, 1)),
        jnp.where(low, 0.0, tiles[2]),
    ]
    scale = 1.0 / math.sqrt(HEAD_DIM)
    keys_new = new_keys[...].astype(jnp.float32)
    zeros = jnp.zeros((row_count, lanes), jnp.float32)
    for head in range(8):
        rows = pl.ds(head, row_count, stride=8)
        if head < 6:
            own_score = jnp.sum(heads[head] * keys_new, axis=1, keepdims=True) * scale
            query_s[rows, :] = heads[head]
            self_s[rows, :] = jnp.broadcast_to(own_score, zeros.shape)
        else:
            query_s[rows, :] = zeros
            self_s[rows, :] = zeros

    pair_row = lax.broadcasted_iota(jnp.int32, (16, 2 * cache_len), 0)
    pair_lane = lax.broadcasted_iota(jnp.int32, (16, 2 * cache_len), 1)
    upper = pair_row < 8
    place = jnp.where(upper, pair_lane, pair_lane - cache_len)
    place = jnp.where(place < 0, cache_len, place)
    for pair in range(row_count // 2):
        if pair % (per_chunk // 2) == 0:
            copies[pair // (per_chunk // 2)].wait()
        pair_rows = slice(16 * pair, 16 * pair + 16)
        keys = k_buf[2 * pair : 2 * pair + 2].reshape(2 * cache_len, lanes)
        raw = lax.dot_general(
            query_s[pair_rows, :].astype(jnp.bfloat16), keys, (((1,), (1,)), ((), ())),
            preferred_element_type=jnp.float32,
        )
        limit = jnp.where(upper, lengths[2 * pair], lengths[2 * pair + 1])
        score_s[pair_rows, :] = jnp.where(place < limit, raw * scale, -1e30)

    own_score = self_s[:, 0:1]
    scores = score_s[...]
    peak = jnp.maximum(jnp.max(scores, axis=1, keepdims=True), own_score)
    terms = jnp.exp(scores - peak)
    own_term = jnp.exp(own_score - peak)
    inverse = 1.0 / (jnp.sum(terms, axis=1, keepdims=True) + own_term)
    weight_s[...] = (terms * inverse).astype(jnp.bfloat16)
    own_weight = (own_term * inverse).astype(jnp.bfloat16).astype(jnp.float32)
    self_s[...] = jnp.broadcast_to(own_weight, self_s.shape)
    for pair in range(row_count // 2):
        if pair % (per_chunk // 2) == 0:
            copies[chunks + pair // (per_chunk // 2)].wait()
        pair_rows = slice(16 * pair, 16 * pair + 16)
        values = v_buf[2 * pair : 2 * pair + 2].reshape(2 * cache_len, lanes)
        query_s[pair_rows, :] = jnp.dot(
            weight_s[pair_rows, :], values, preferred_element_type=jnp.float32
        )

    values_new = new_values[...].astype(jnp.float32)
    mixed = []
    for head in range(6):
        rows = pl.ds(head, row_count, stride=8)
        mixed.append(query_s[rows, :] + self_s[rows, :] * values_new)
    attention = jnp.concatenate(
        [
            jnp.where(low, mixed[0], pltpu.roll(mixed[1], HEAD_DIM, 1)),
            jnp.where(low, mixed[2], mixed[3]),
            jnp.where(low, pltpu.roll(mixed[4], HEAD_DIM, 1), mixed[5]),
        ],
        axis=1,
    ).astype(jnp.bfloat16)
    for copy in copies[2 * chunks :]:
        copy.wait()
    place_tp = lax.axis_index("tp")
    for shift, out in zip(TP_ORDER, (own, sent1, sent2, sent3)):
        columns = pl.ds(pl.multiple_of((place_tp ^ shift) * width, width), width)
        out[...] = jnp.dot(
            attention, w_buf[:, columns], preferred_element_type=jnp.float32
        ).astype(out.dtype)


def ready_kernel(
    slot_dev, own, resid, routes, w_router, base, pick_rows, pick0, pick1, router_rows
):
    base[...] = own[...] + resid[...].astype(jnp.float32)
    packed_count, row_count = pick_rows.shape

    route0, route1 = routes[0:1, :], routes[1:2, :]
    place = lax.broadcasted_iota(jnp.int32, (packed_count, row_count), 0)
    named0 = jnp.where(place == route0, 1.0, 0.0)
    named1 = jnp.where(place == route1, 1.0, 0.0)
    row_of = lax.broadcasted_iota(jnp.int32, (row_count, row_count), 0)
    col_of = lax.broadcasted_iota(jnp.int32, (row_count, row_count), 1)
    earlier = jnp.where(row_of < col_of, 1.0, 0.0).astype(jnp.bfloat16)
    before = jnp.dot(
        (named0 + named1).astype(jnp.bfloat16), earlier, preferred_element_type=jnp.float32
    )
    row_req = lax.rem(lax.axis_index("req"), 2)

    def pick(route, named):
        rank = jnp.sum(named * before, axis=0, keepdims=True).astype(jnp.int32)
        block = ((route // slot_dev) ^ row_req) * slot_dev + lax.rem(route, slot_dev)
        return jnp.where(place == block * CAP + rank, 1.0, 0.0)

    first, second = pick(route0, named0), pick(route1, named1)
    pick_rows[...] = (first + second).astype(jnp.bfloat16)
    pick0[...] = jnp.transpose(first).astype(jnp.bfloat16)
    pick1[...] = jnp.transpose(second).astype(jnp.bfloat16)
    signed = jnp.transpose(named0 - named1)
    router_rows[...] = jnp.dot(
        signed[:, :EXPERTS], w_router[...],
        precision=lax.Precision.HIGHEST, preferred_element_type=jnp.float32,
    )


def pack_kernel(base, part1, part2, part3, pick_rows, attended, packed):
    total = base[...]
    for part in (part1, part2, part3):
        total = total + part[...].astype(jnp.float32)
    rows = total.astype(jnp.bfloat16)
    attended[...] = rows
    product = jnp.dot(pick_rows[...], rows, preferred_element_type=jnp.float32)
    size = packed.shape[1]
    for index in range(packed.shape[0]):
        packed[index] = product[index * size : (index + 1) * size].astype(packed.dtype)


def result_kernel(attended, result):
    result[...] = attended[...]


def stats_kernel(attended, gain, router_rows, stats):
    rows = attended[...].astype(jnp.float32)
    square = jnp.sum(rows * rows, axis=1, keepdims=True)
    logit = jnp.sum(rows * gain[...] * router_rows[...], axis=1, keepdims=True)
    lane = lax.broadcasted_iota(jnp.int32, stats.shape, 1)
    stats[...] = jnp.where(lane == 0, square, jnp.where(lane == 1, logit, 0.0))


def turn_kernel(blocks, along):
    half = blocks.shape[1] // 2
    for index in range(blocks.shape[0]):
        along[index * half : (index + 1) * half, :] = blocks[index, half:, :]


def hop_along_z(packed):
    count = lax.axis_size("req")
    near = lax.all_to_all(
        packed, "req", split_axis=0, concat_axis=0, tiled=True,
        axis_index_groups=[list(range(row, count, 2)) for row in range(2)],
    )
    depth, size, width = packed.shape
    (along,) = call(
        turn_kernel, [((depth * size // 2, width), packed.dtype)], [spec()], (near,)
    )
    return near, partner_permute(along, "req", 1)


def slot_masks(row_count, slot_dev):
    slot = lax.rem(lax.broadcasted_iota(jnp.int32, (row_count, 1), 0) // CAP, slot_dev)
    return [slot == index for index in range(slot_dev)]


def split_high(column):
    high = column.astype(jnp.bfloat16).astype(jnp.float32)
    return high, column - high


def gate_terms(slot_dev, blocks, gain, stats, w_gate, w_up, kept, sent, lhs):
    size = kept.shape[0] // 2
    width = blocks.shape[1]
    hidden = w_gate.shape[1]
    place_tp = lax.axis_index("tp")
    masks = slot_masks(size, slot_dev)
    lane = lax.broadcasted_iota(jnp.int32, (size, 128), 1)
    for order, shift in enumerate((0, 2, 1, 3)):
        out, first_row = (kept, sent)[order // 2], order % 2 * size
        rows = blocks[
            pl.ds(pl.multiple_of((place_tp ^ shift) * size, size), size), :
        ].astype(jnp.float32)
        columns = [jnp.sum(rows * rows, axis=1, keepdims=True)]
        if stats is not None:
            for first in range(0, stats.shape[0], size):
                columns += [stats[first : first + size, 0:1], stats[first : first + size, 1:2]]
        extra = jnp.zeros((size, 128), jnp.float32)
        for index, column in enumerate(columns):
            high, low = split_high(column)
            extra = jnp.where(lane == 2 * index, high, extra)
            extra = jnp.where(lane == 2 * index + 1, low, extra)
        out[first_row : first_row + size, 2 * hidden :] = extra.astype(out.dtype)
        scaled = rows * gain[...]
        for index, mask in enumerate(masks):
            lhs[order * size : (order + 1) * size, index * width : (index + 1) * width] = (
                jnp.where(mask, scaled, 0.0).astype(jnp.bfloat16)
            )
    left = lhs[...]
    for first, weight in ((0, w_gate), (hidden, w_up)):
        product = jnp.dot(left, weight[...], preferred_element_type=jnp.float32)
        kept[:, first : first + hidden] = product[: 2 * size]
        sent[:, first : first + hidden] = product[2 * size :].astype(sent.dtype)


def early_kernel(
    slot_dev, near, gain, stats, w_gate, w_up, kept, sent, blocks, lhs
):
    half = kept.shape[0] // 2
    for index in range(near.shape[0]):
        blocks[index * half : (index + 1) * half, :] = near[index, :half, :]
    gate_terms(slot_dev, blocks, gain, stats, w_gate, w_up, kept, sent, lhs)


def late_kernel(slot_dev, blocks, gain, w_gate, w_up, kept, sent, lhs):
    gate_terms(slot_dev, blocks, gain, None, w_gate, w_up, kept, sent, lhs)


def chip_kernel(kept, part, own, sent):
    size, width = own.shape
    own[...] = kept[:size, :] + part[:size, :].astype(jnp.float32)
    total = kept[size:, :] + part[size:, :].astype(jnp.float32)
    extra = total[:, width - 128 :]
    lane = lax.broadcasted_iota(jnp.int32, extra.shape, 1)
    high, low = split_high(extra + pltpu.roll(extra, 127, 1))
    sent[:, : width - 128] = total[:, : width - 128].astype(sent.dtype)
    sent[:, width - 128 :] = jnp.where(
        lax.rem(lane, 2) == 0, high, pltpu.roll(low, 1, 1)
    ).astype(sent.dtype)


def hidden_kernel(*refs):
    late, early, (hidden, first_weight) = refs[:2], refs[2:4], refs[4:]
    width = hidden.shape[1]
    half = hidden.shape[0] // 2

    def total(parts, columns):
        result = parts[0][:, columns]
        for part in parts[1:]:
            result = result + part[:, columns].astype(jnp.float32)
        return result

    def inverse_rms(columns, index):
        square = columns[:, index : index + 1] + columns[:, index + 1 : index + 2]
        return 1.0 / jnp.sqrt(square / D + 1e-06)

    for index, parts in ((1, late), (0, early)):
        extra = total(parts, slice(2 * width, 2 * width + 128))
        row_inv = inverse_rms(extra, 0)
        gate = total(parts, slice(0, width)) * row_inv
        up = total(parts, slice(width, 2 * width)) * row_inv
        hidden[index * half : (index + 1) * half, :] = (
            gate / (1.0 + jnp.exp(-gate)) * up
        ).astype(jnp.bfloat16)
    for index in range(first_weight.shape[0] // half):
        place = 2 + 4 * index
        logit = extra[:, place + 2 : place + 3] + extra[:, place + 3 : place + 4]
        weight = 1.0 / (1.0 + jnp.exp(-logit * inverse_rms(extra, place)))
        first_weight[index * half : (index + 1) * half, :] = jnp.broadcast_to(weight, (half, 128))


def down_kernel(slot_dev, own, part1, part2, part3, w_down, computed, lhs):
    quarter, width = own.shape
    place_tp = lax.axis_index("tp")
    masks = slot_masks(quarter, slot_dev)
    for shift, part in enumerate((own, part1, part2, part3)):
        rows = part[...].astype(jnp.float32)
        place = pl.ds(pl.multiple_of((place_tp ^ shift) * quarter, quarter), quarter)
        for index, mask in enumerate(masks):
            lhs[place, index * width : (index + 1) * width] = jnp.where(mask, rows, 0.0).astype(
                jnp.bfloat16
            )
    product = jnp.dot(lhs[...], w_down[...], preferred_element_type=jnp.float32)
    for index in range(computed.shape[0]):
        computed[index] = product[index * quarter : (index + 1) * quarter].astype(computed.dtype)


def combine_kernel(near, far, pick0, pick1, first_weight, attended, layer_out, returned):
    half = near.shape[1] // 2
    for index in range(near.shape[0]):
        start = 2 * index * half
        returned[start : start + half, :] = near[index, :half, :]
        returned[start + half : start + 2 * half, :] = far[index * half : (index + 1) * half, :]
    rows = returned[...]
    out0 = jnp.dot(pick0[...], rows, preferred_element_type=jnp.float32)
    out1 = jnp.dot(pick1[...], rows, preferred_element_type=jnp.float32)
    weight = first_weight[:, 0:1]
    moe = weight * out0 + (1.0 - weight) * out1
    layer_out[...] = (attended[...].astype(jnp.float32) + moe).astype(jnp.bfloat16)


def shards(
    resid,
    queries,
    new_keys,
    new_values,
    k_cache,
    v_cache,
    lengths,
    w_out,
    norm_gain,
    w_router,
    routes,
    w_gate,
    w_up,
    w_down,
):
    row_count, width = resid.shape
    slot_dev, _, hidden = w_gate.shape
    cache_len, lanes = k_cache.shape[1:]
    packed_count = EXPERTS * CAP
    quarter = packed_count // lax.axis_size("tp")
    if not (
        lax.axis_size("tp") == 4
        and lax.axis_size("req") == 8
        and 8 * slot_dev == EXPERTS
        and row_count == quarter
        and lanes == 2 * HEAD_DIM
        and queries.shape[1] == 6 * HEAD_DIM
    ):
        return shards_general(
            resid, queries, new_keys, new_values, k_cache, v_cache, lengths, w_out,
            norm_gain, w_router, routes, w_gate, w_up, w_down,
        )
    bf16, f32 = jnp.bfloat16, jnp.float32
    gain = norm_gain.reshape(1, width)
    own, *sents = call(
        attend_kernel,
        [((row_count, width), f32)] + [((row_count, width), bf16)] * 3,
        [spec(pl.ANY)] * 7,
        [
            pltpu.with_memory_space_constraint(operand, pltpu.HBM)
            for operand in (lengths, queries, new_keys, new_values, k_cache, v_cache, w_out)
        ],
        scratch=[
            pltpu.SMEM(lengths.shape, jnp.int32),
            pltpu.VMEM(queries.shape, bf16),
            pltpu.VMEM(new_keys.shape, bf16),
            pltpu.VMEM(new_values.shape, bf16),
            pltpu.VMEM(k_cache.shape, bf16),
            pltpu.VMEM(v_cache.shape, bf16),
            pltpu.VMEM(w_out.shape, bf16),
            pltpu.VMEM((8 * row_count, lanes), f32),
            pltpu.VMEM((8 * row_count, lanes), f32),
            pltpu.VMEM((8 * row_count, 2 * cache_len), f32),
            pltpu.VMEM((8 * row_count, 2 * cache_len), bf16),
            pltpu.SemaphoreType.DMA((4,)),
            pltpu.SemaphoreType.DMA((12,)),
        ],
        mebibytes=16,
        flops=200_000_000,
        moved=3_400_000,
    )
    def sum_exchange(sents):
        return [partner_permute(block, "tp", k) for k, block in zip(TP_ORDER[1:], sents)]

    parts = sum_exchange(sents)
    base, pick_rows, pick0, pick1, router_rows = call(
        functools.partial(ready_kernel, slot_dev),
        [
            ((row_count, width), f32),
            ((packed_count, row_count), bf16),
            ((row_count, packed_count), bf16),
            ((row_count, packed_count), bf16),
            ((row_count, width), f32),
        ],
        [spec()] * 4,
        (own, resid, routes.T, w_router.T),
    )
    attended, packed = call(
        pack_kernel,
        [((row_count, width), bf16), ((4, quarter, width), bf16)],
        [spec()] * 5,
        (base, *parts, pick_rows),
    )
    (stats,) = call(
        stats_kernel, [((row_count, 128), f32)], [spec()] * 3, (attended, gain, router_rows)
    )
    (result,) = call(result_kernel, [((row_count, width), bf16)], [spec()], (attended,))
    near, along = hop_along_z(packed)
    weights = (w_gate.reshape(slot_dev * width, hidden), w_up.reshape(slot_dev * width, hidden))
    half = quarter // 2
    message = (half, 2 * hidden + 128)
    lhs = pltpu.VMEM((packed_count // 2, slot_dev * width), bf16)

    def chip_sums(kept, sent):
        own, sent = call(
            chip_kernel, [(message, f32), (message, bf16)], [spec()] * 2,
            (kept, partner_permute(sent, "tp", 1)),
        )
        return own, partner_permute(sent, "tp", 2)

    pair = (quarter, message[1])
    early = call(
        functools.partial(early_kernel, slot_dev),
        [(pair, f32), (pair, bf16)],
        [spec()] * 5,
        (near, gain, stats, *weights),
        scratch=[pltpu.VMEM((2 * quarter, width), bf16), lhs],
        flops=400_000_000,
        moved=3_500_000,
    )
    late = call(
        functools.partial(late_kernel, slot_dev),
        [(pair, f32), (pair, bf16)],
        [spec()] * 4,
        (along, gain, *weights),
        scratch=[lhs],
        flops=400_000_000,
        moved=3_500_000,
    )
    early = chip_sums(*early)
    late = chip_sums(*late)
    own, first_weight = call(
        hidden_kernel,
        [((quarter, hidden), bf16), ((row_count, 128), f32)],
        [spec()] * 4,
        (*late, *early),
    )
    across = partner_permute(own, "tp", 2)
    parts = [partner_permute(own, "tp", 1), across, partner_permute(across, "tp", 1)]
    (computed,) = call(
        functools.partial(down_kernel, slot_dev),
        [((4, quarter, width), bf16)],
        [spec()] * 5,
        (own, *parts, w_down.reshape(slot_dev * hidden, width)),
        scratch=[pltpu.VMEM((packed_count, slot_dev * hidden), bf16)],
        flops=200_000_000,
        moved=2_000_000,
    )
    (layer_out,) = call(
        combine_kernel,
        [((row_count, width), bf16)],
        [spec()] * 6,
        (*hop_along_z(computed), pick0, pick1, first_weight, attended),
        scratch=[pltpu.VMEM((packed_count, width), bf16)],
    )
    return (result, layer_out)


def solution(mesh):
    placed = (
        P("req", "tp"),
        P("req", "tp"),
        P("req", "tp"),
        P("req", "tp"),
        P("req", None, "tp"),
        P("req", None, "tp"),
        P("req"),
        P("tp", None),
        P("tp"),
        P("tp", None),
        P("req", None),
        P("req", "tp", None),
        P("req", "tp", None),
        P("req", None, "tp"),
    )
    return jax.shard_map(
        shards,
        mesh=mesh,
        in_specs=placed,
        out_specs=(P("req", "tp"), P("req", "tp")),
        check_vma=False,
    )
```

```python
import functools
import math

import jax
import jax.numpy as jnp
from jax import lax
from jax.experimental import pallas as pl
from jax.experimental.pallas import tpu as pltpu
from jax.sharding import PartitionSpec as P

D = 1536
HEAD_DIM = 64
EXPERTS = 16
TOP = 2
CAP = 8


def attend_local(queries, new_keys, new_values, k_cache, v_cache, lengths):
    row_count = queries.shape[0]
    kv_local = new_keys.shape[1] // HEAD_DIM
    group_size = queries.shape[1] // HEAD_DIM // kv_local
    cache_len = k_cache.shape[1]
    score_scale = 1.0 / math.sqrt(HEAD_DIM)
    query = queries.reshape(row_count, kv_local, group_size, HEAD_DIM)
    keys_all = k_cache.reshape(row_count, cache_len, kv_local, HEAD_DIM)
    values_all = v_cache.reshape(row_count, cache_len, kv_local, HEAD_DIM)
    scores = (
        jnp.einsum("bgqd,blgd->bgql", query, keys_all, preferred_element_type=jnp.float32)
        * score_scale
    )
    self_score = (
        jnp.einsum(
            "bgqd,bgd->bgq",
            query,
            new_keys.reshape(row_count, kv_local, HEAD_DIM),
            preferred_element_type=jnp.float32,
        )
        * score_scale
    )
    valid_mask = (jnp.arange(cache_len, dtype=jnp.int32)[None, :] < lengths[:, None])[
        :, None, None, :
    ]
    peak_score = jnp.maximum(jnp.max(jnp.where(valid_mask, scores, -1e30), axis=-1), self_score)
    exp_terms = jnp.where(valid_mask, jnp.exp(scores - peak_score[..., None]), 0.0)
    self_exp = jnp.exp(self_score - peak_score)
    denom_sum = jnp.sum(exp_terms, axis=-1) + self_exp
    weights = (exp_terms / denom_sum[..., None]).astype(jnp.bfloat16)
    self_weight = (self_exp / denom_sum).astype(jnp.bfloat16)
    value_self = new_values.astype(jnp.float32).reshape(row_count, kv_local, 1, HEAD_DIM)
    mixed = (
        jnp.einsum("bgql,blgd->bgqd", weights, values_all, preferred_element_type=jnp.float32)
        + self_weight.astype(jnp.float32)[..., None] * value_self
    )
    return mixed.astype(jnp.bfloat16).reshape(row_count, kv_local * group_size * HEAD_DIM)


def shards_general(
    resid,
    queries,
    new_keys,
    new_values,
    k_cache,
    v_cache,
    lengths,
    w_out,
    norm_gain,
    w_router,
    routes,
    w_gate,
    w_up,
    w_down,
):
    req_dev = resid.shape[0]
    width_local = resid.shape[1]
    slot_dev = w_gate.shape[0]
    req_count = lax.axis_size("req")
    shard_count = max(1, req_count // EXPERTS)
    attention = attend_local(queries, new_keys, new_values, k_cache, v_cache, lengths)
    partial_value = jnp.dot(attention, w_out, preferred_element_type=jnp.float32)
    projected = lax.psum_scatter(partial_value, "tp", scatter_dimension=1, tiled=True)
    attended = (resid.astype(jnp.float32) + projected).astype(jnp.bfloat16)
    attended_f = attended.astype(jnp.float32)
    scaled = attended_f * norm_gain[None, :]
    square_sum, logit_part = lax.psum(
        (
            jnp.sum(attended_f * attended_f, axis=1),
            jnp.dot(scaled, w_router, precision=lax.Precision.HIGHEST),
        ),
        "tp",
    )
    inv_rms = 1.0 / jnp.sqrt(square_sum / D + 1e-06)
    normed = (scaled * inv_rms[:, None]).astype(jnp.bfloat16)
    logits = logit_part * inv_rms[:, None]
    expert_ids = jnp.arange(EXPERTS, dtype=jnp.int32)
    first_logit = jnp.sum(jnp.where(routes[:, 0:1] == expert_ids[None, :], logits, 0.0), axis=1)
    second_logit = jnp.sum(jnp.where(routes[:, 1:2] == expert_ids[None, :], logits, 0.0), axis=1)
    first_weight = jax.nn.sigmoid(first_logit - second_logit)
    second_weight = 1.0 - first_weight
    flat_routes = routes.reshape(req_dev * TOP)
    one_hot = (flat_routes[None, :] == expert_ids[:, None]).astype(jnp.int32)
    rank_in = jnp.cumsum(one_hot, axis=1) - one_hot
    slot_ids = jnp.arange(CAP, dtype=jnp.int32)
    chosen = (one_hot[:, None, :] == 1) & (rank_in[:, None, :] == slot_ids[None, :, None])
    token_pick = jnp.sum(
        chosen.reshape(EXPERTS, CAP, req_dev, TOP).astype(jnp.int32), axis=-1
    ).astype(jnp.bfloat16)
    per_expert = jnp.einsum(
        "ecb,bd->ecd", token_pick, normed, preferred_element_type=jnp.float32
    ).astype(jnp.bfloat16)
    outgoing = jnp.broadcast_to(
        per_expert[:, None], (EXPERTS, shard_count, CAP, width_local)
    ).reshape(req_count, slot_dev, CAP, width_local)
    incoming = lax.all_to_all(outgoing, "req", split_axis=0, concat_axis=0, tiled=True)
    gate_pre = jnp.einsum("nscd,sdf->nscf", incoming, w_gate, preferred_element_type=jnp.float32)
    up_pre = jnp.einsum("nscd,sdf->nscf", incoming, w_up, preferred_element_type=jnp.float32)
    gate_sum, up_sum = lax.psum((gate_pre, up_pre), "tp")
    hidden = (jax.nn.silu(gate_sum) * up_sum).astype(jnp.bfloat16)
    computed = jnp.einsum("nscf,sfd->nscd", hidden, w_down, preferred_element_type=jnp.float32)
    returned = lax.all_to_all(computed, "req", split_axis=0, concat_axis=0, tiled=True)
    combined = jnp.sum(returned.reshape(EXPERTS, shard_count, CAP, width_local), axis=1)
    route_out = jnp.einsum(
        "ecr,ecd->rd", chosen.astype(jnp.float32), combined, precision=lax.Precision.HIGHEST
    ).reshape(req_dev, TOP, width_local)
    moe = first_weight[:, None] * route_out[:, 0] + second_weight[:, None] * route_out[:, 1]
    layer_out = (attended_f + moe).astype(jnp.bfloat16)
    return (attended, layer_out)


TP_ORDER = (0, 2, 3, 1)


def spec(space=pltpu.VMEM):
    return pl.BlockSpec(memory_space=space)


def call(kernel, outs, ins, operands, scratch=(), mebibytes=8, flops=100_000, moved=100_000):
    return pl.pallas_call(
        kernel,
        out_shape=[jax.ShapeDtypeStruct(shape, dtype) for shape, dtype in outs],
        in_specs=ins,
        out_specs=[spec() for _ in outs],
        scratch_shapes=scratch,
        compiler_params=pltpu.CompilerParams(vmem_limit_bytes=mebibytes << 20),
        cost_estimate=pl.CostEstimate(flops=flops, bytes_accessed=moved, transcendentals=0),
    )(*operands)


def partner_permute(block, axis, distance):
    count = lax.axis_size(axis)
    return lax.ppermute(block, axis, [(i, i ^ distance) for i in range(count)])


def attend_kernel(
    lengths_hbm, queries_hbm, keys_hbm, values_hbm, k_hbm, v_hbm, w_hbm, own, sent1, sent2, sent3,
    lengths, queries, new_keys, new_values, k_buf, v_buf, w_buf,
    query_s, self_s, score_s, weight_s, small_sems, sems,
):
    row_count = queries.shape[0]
    width = own.shape[1]
    lanes = 2 * HEAD_DIM
    cache_len = k_hbm.shape[1]
    chunks = 4
    small = [
        pltpu.make_async_copy(source, target, small_sems.at[index])
        for index, (source, target) in enumerate(
            (
                (queries_hbm, queries),
                (keys_hbm, new_keys),
                (values_hbm, new_values),
                (lengths_hbm, lengths),
            )
        )
    ]
    copies = []
    for source, target in ((k_hbm, k_buf), (v_hbm, v_buf), (w_hbm, w_buf)):
        size = source.shape[0] // chunks
        for chunk in range(chunks):
            part = pl.ds(chunk * size, size)
            copies.append(
                pltpu.make_async_copy(source.at[part], target.at[part], sems.at[len(copies)])
            )
    for copy in small + copies:
        copy.start()
    per_chunk = row_count // chunks

    for copy in small:
        copy.wait()

    low = lax.broadcasted_iota(jnp.int32, (row_count, lanes), 1) < HEAD_DIM
    tiles = [queries[:, i * lanes : (i + 1) * lanes].astype(jnp.float32) for i in range(3)]
    heads = [
        jnp.where(low, tiles[0], 0.0),
        jnp.where(low, pltpu.roll(tiles[0], HEAD_DIM, 1), 0.0),
        jnp.where(low, tiles[1], 0.0),
        jnp.where(low, 0.0, tiles[1]),
        jnp.where(low, 0.0, pltpu.roll(tiles[2], HEAD_DIM, 1)),
        jnp.where(low, 0.0, tiles[2]),
    ]
    scale = 1.0 / math.sqrt(HEAD_DIM)
    for head in range(8):
        rows = pl.ds(head, row_count, stride=8)
        query_s[rows, :] = heads[head] if head < 6 else jnp.zeros((row_count, lanes), jnp.float32)

    row_of = lax.broadcasted_iota(jnp.int32, (8 * row_count, row_count), 0)
    request_of = lax.broadcasted_iota(jnp.int32, (8 * row_count, row_count), 1)
    spread = jnp.where(row_of // 8 == request_of, 1.0, 0.0).astype(jnp.bfloat16)
    keys_new = jnp.dot(spread, new_keys[...], preferred_element_type=jnp.float32)
    values_new = jnp.dot(spread, new_values[...], preferred_element_type=jnp.float32)
    own_score = jnp.sum(query_s[...] * keys_new, axis=1, keepdims=True) * scale

    upper = lax.broadcasted_iota(jnp.int32, (16, lanes), 0) < 8
    position = lax.broadcasted_iota(jnp.int32, (16, cache_len), 1)
    for pair in range(row_count // 2):
        if pair % (per_chunk // 2) == 0:
            copies[pair // (per_chunk // 2)].wait()
        pair_rows = slice(16 * pair, 16 * pair + 16)
        keys = k_buf[2 * pair : 2 * pair + 2].reshape(2 * cache_len, lanes)
        raw = lax.dot_general(
            query_s[pair_rows, :].astype(jnp.bfloat16), keys, (((1,), (1,)), ((), ())),
            preferred_element_type=jnp.float32,
        )
        limit = jnp.where(upper, lengths[2 * pair], lengths[2 * pair + 1])
        score_s[pair_rows, :] = jnp.where(
            position < limit,
            jnp.where(upper, raw[:, :cache_len], raw[:, cache_len:]) * scale,
            -1e30,
        )

    scores = score_s[...]
    peak = jnp.maximum(jnp.max(scores, axis=1, keepdims=True), own_score)
    terms = jnp.exp(scores - peak)
    own_term = jnp.exp(own_score - peak)
    inverse = 1.0 / (jnp.sum(terms, axis=1, keepdims=True) + own_term)
    weight_s[...] = (terms * inverse).astype(jnp.bfloat16)
    own_weight = (own_term * inverse).astype(jnp.bfloat16).astype(jnp.float32)
    self_s[...] = own_weight * values_new
    for pair in range(row_count // 2):
        if pair % (per_chunk // 2) == 0:
            copies[chunks + pair // (per_chunk // 2)].wait()
        pair_rows = slice(16 * pair, 16 * pair + 16)
        values = jnp.concatenate([v_buf[2 * pair], v_buf[2 * pair + 1]], axis=1)
        mixed = jnp.dot(weight_s[pair_rows, :], values, preferred_element_type=jnp.float32)
        query_s[pair_rows, :] = (
            jnp.where(upper, mixed[:, :lanes], mixed[:, lanes:]) + self_s[pair_rows, :]
        )

    mixed = [query_s[pl.ds(head, row_count, stride=8), :] for head in range(6)]
    attention = jnp.concatenate(
        [
            jnp.where(low, mixed[0], pltpu.roll(mixed[1], HEAD_DIM, 1)),
            jnp.where(low, mixed[2], mixed[3]),
            jnp.where(low, pltpu.roll(mixed[4], HEAD_DIM, 1), mixed[5]),
        ],
        axis=1,
    ).astype(jnp.bfloat16)
    for copy in copies[2 * chunks :]:
        copy.wait()
    place_tp = lax.axis_index("tp")
    for shift, out in zip(TP_ORDER, (own, sent1, sent2, sent3)):
        columns = pl.ds(pl.multiple_of((place_tp ^ shift) * width, width), width)
        out[...] = jnp.dot(
            attention, w_buf[:, columns], preferred_element_type=jnp.float32
        ).astype(out.dtype)


def ready_kernel(
    slot_dev, own, resid, routes, w_router, base, pick_rows, pick0, pick1, router_rows
):
    base[...] = own[...] + resid[...].astype(jnp.float32)
    packed_count, row_count = pick_rows.shape

    route0, route1 = routes[0:1, :], routes[1:2, :]
    place = lax.broadcasted_iota(jnp.int32, (packed_count, row_count), 0)
    named0 = jnp.where(place == route0, 1.0, 0.0)
    named1 = jnp.where(place == route1, 1.0, 0.0)
    row_of = lax.broadcasted_iota(jnp.int32, (row_count, row_count), 0)
    col_of = lax.broadcasted_iota(jnp.int32, (row_count, row_count), 1)
    earlier = jnp.where(row_of < col_of, 1.0, 0.0).astype(jnp.bfloat16)
    before = jnp.dot(
        (named0 + named1).astype(jnp.bfloat16), earlier, preferred_element_type=jnp.float32
    )
    place_req = lax.axis_index("req")

    def pick(route, named, mine):
        rank = jnp.sum(named * before, axis=0, keepdims=True).astype(jnp.int32)
        block = ((route // slot_dev) ^ mine) * slot_dev + lax.rem(route, slot_dev)
        return jnp.where(place == block * CAP + rank, 1.0, 0.0)

    sent_rows = pick(route0, named0, place_req) + pick(route1, named1, place_req)
    pick_rows[...] = sent_rows.astype(jnp.bfloat16)
    pick0[...] = jnp.transpose(pick(route0, named0, 0)).astype(jnp.bfloat16)
    pick1[...] = jnp.transpose(pick(route1, named1, 0)).astype(jnp.bfloat16)
    signed = jnp.transpose(named0 - named1)
    router_rows[...] = jnp.dot(
        signed[:, :EXPERTS], w_router[...],
        precision=lax.Precision.HIGHEST, preferred_element_type=jnp.float32,
    )


def pack_kernel(base, part1, part2, part3, pick_rows, attended, home, sent1, sent2, sent3):
    total = base[...]
    for part in (part1, part2, part3):
        total = total + part[...].astype(jnp.float32)
    rows = total.astype(jnp.bfloat16)
    attended[...] = rows
    packed = jnp.dot(pick_rows[...], rows, preferred_element_type=jnp.float32)
    size = home.shape[0]
    for distance, out in enumerate((home, sent1, sent2, sent3)):
        out[...] = packed[distance * size : (distance + 1) * size].astype(out.dtype)


def result_kernel(attended, result):
    result[...] = attended[...]


def stats_kernel(attended, gain, router_rows, stats):
    rows = attended[...].astype(jnp.float32)
    square = jnp.sum(rows * rows, axis=1, keepdims=True)
    logit = jnp.sum(rows * gain[...] * router_rows[...], axis=1, keepdims=True)
    lane = lax.broadcasted_iota(jnp.int32, stats.shape, 1)
    stats[...] = jnp.where(lane == 0, square, jnp.where(lane == 1, logit, 0.0))


def turn_kernel(home, part1, part2, part3, along):
    half = home.shape[0] // 2
    for index, part in enumerate((home, part1, part2, part3)):
        along[index * half : (index + 1) * half, :] = part[half:, :]


def slot_masks(row_count, slot_dev):
    slot = lax.rem(lax.broadcasted_iota(jnp.int32, (row_count, 1), 0) // CAP, slot_dev)
    return [slot == index for index in range(slot_dev)]


def split_high(column):
    high = column.astype(jnp.bfloat16).astype(jnp.float32)
    return high, column - high


def gate_terms(slot_dev, blocks, gain, stats, w_gate, w_up, kept, sent, lhs):
    size = kept.shape[0] // 2
    width = blocks.shape[1]
    hidden = w_gate.shape[1]
    place_tp = lax.axis_index("tp")
    masks = slot_masks(size, slot_dev)
    lane = lax.broadcasted_iota(jnp.int32, (size, 128), 1)
    for order, shift in enumerate((0, 2, 1, 3)):
        out, first_row = (kept, sent)[order // 2], order % 2 * size
        rows = blocks[
            pl.ds(pl.multiple_of((place_tp ^ shift) * size, size), size), :
        ].astype(jnp.float32)
        columns = [jnp.sum(rows * rows, axis=1, keepdims=True)]
        if stats is not None:
            for first in range(0, stats.shape[0], size):
                columns += [stats[first : first + size, 0:1], stats[first : first + size, 1:2]]
        extra = jnp.zeros((size, 128), jnp.float32)
        for index, column in enumerate(columns):
            high, low = split_high(column)
            extra = jnp.where(lane == 2 * index, high, extra)
            extra = jnp.where(lane == 2 * index + 1, low, extra)
        out[first_row : first_row + size, 2 * hidden :] = extra.astype(out.dtype)
        scaled = rows * gain[...]
        for index, mask in enumerate(masks):
            lhs[order * size : (order + 1) * size, index * width : (index + 1) * width] = (
                jnp.where(mask, scaled, 0.0).astype(jnp.bfloat16)
            )
    left = lhs[...]
    for first, weight in ((0, w_gate), (hidden, w_up)):
        product = jnp.dot(left, weight[...], preferred_element_type=jnp.float32)
        kept[:, first : first + hidden] = product[: 2 * size]
        sent[:, first : first + hidden] = product[2 * size :].astype(sent.dtype)


def early_kernel(
    slot_dev, in0, in1, in2, in3, gain, stats, w_gate, w_up, kept, sent, blocks, lhs
):
    half = kept.shape[0] // 2
    for index, part in enumerate((in0, in1, in2, in3)):
        blocks[index * half : (index + 1) * half, :] = part[:half, :]
    gate_terms(slot_dev, blocks, gain, stats, w_gate, w_up, kept, sent, lhs)


def late_kernel(slot_dev, blocks, gain, w_gate, w_up, kept, sent, lhs):
    gate_terms(slot_dev, blocks, gain, None, w_gate, w_up, kept, sent, lhs)


def chip_kernel(kept, part, own, sent):
    size, width = own.shape
    own[...] = kept[:size, :] + part[:size, :].astype(jnp.float32)
    total = kept[size:, :] + part[size:, :].astype(jnp.float32)
    extra = total[:, width - 128 :]
    lane = lax.broadcasted_iota(jnp.int32, extra.shape, 1)
    high, low = split_high(extra + pltpu.roll(extra, 127, 1))
    sent[:, : width - 128] = total[:, : width - 128].astype(sent.dtype)
    sent[:, width - 128 :] = jnp.where(
        lax.rem(lane, 2) == 0, high, pltpu.roll(low, 1, 1)
    ).astype(sent.dtype)


def hidden_kernel(*refs):
    late, early, (hidden, first_weight) = refs[:2], refs[2:4], refs[4:]
    width = hidden.shape[1]
    half = hidden.shape[0] // 2

    def total(parts, columns):
        result = parts[0][:, columns]
        for part in parts[1:]:
            result = result + part[:, columns].astype(jnp.float32)
        return result

    def inverse_rms(columns, index):
        square = columns[:, index : index + 1] + columns[:, index + 1 : index + 2]
        return 1.0 / jnp.sqrt(square / D + 1e-06)

    for index, parts in ((1, late), (0, early)):
        extra = total(parts, slice(2 * width, 2 * width + 128))
        row_inv = inverse_rms(extra, 0)
        gate = total(parts, slice(0, width)) * row_inv
        up = total(parts, slice(width, 2 * width)) * row_inv
        hidden[index * half : (index + 1) * half, :] = (
            gate / (1.0 + jnp.exp(-gate)) * up
        ).astype(jnp.bfloat16)
    for index in range(first_weight.shape[0] // half):
        place = 2 + 4 * index
        logit = extra[:, place + 2 : place + 3] + extra[:, place + 3 : place + 4]
        weight = 1.0 / (1.0 + jnp.exp(-logit * inverse_rms(extra, place)))
        first_weight[index * half : (index + 1) * half, :] = jnp.broadcast_to(weight, (half, 128))


def down_kernel(slot_dev, own, part1, part2, part3, w_down, computed, lhs):
    quarter, width = own.shape
    block = computed.shape[1]
    place_tp = lax.axis_index("tp")
    place_req = lax.axis_index("req")
    masks = slot_masks(quarter, slot_dev)
    for shift, part in enumerate((own, part1, part2, part3)):
        rows = part[...].astype(jnp.float32)
        place = pl.ds(pl.multiple_of((place_tp ^ shift) * quarter, quarter), quarter)
        for index, mask in enumerate(masks):
            lhs[place, index * width : (index + 1) * width] = jnp.where(mask, rows, 0.0).astype(
                jnp.bfloat16
            )
    product = jnp.dot(lhs[...], w_down[...], preferred_element_type=jnp.float32)
    for index in range(computed.shape[0]):
        computed[place_req ^ index] = product[index * block : (index + 1) * block].astype(
            computed.dtype
        )


def combine_kernel(returned, pick0, pick1, first_weight, attended, layer_out):
    rows = returned[...]
    out0 = jnp.dot(pick0[...], rows, preferred_element_type=jnp.float32)
    out1 = jnp.dot(pick1[...], rows, preferred_element_type=jnp.float32)
    weight = first_weight[:, 0:1]
    moe = weight * out0 + (1.0 - weight) * out1
    layer_out[...] = (attended[...].astype(jnp.float32) + moe).astype(jnp.bfloat16)


def shards(
    resid,
    queries,
    new_keys,
    new_values,
    k_cache,
    v_cache,
    lengths,
    w_out,
    norm_gain,
    w_router,
    routes,
    w_gate,
    w_up,
    w_down,
):
    row_count, width = resid.shape
    slot_dev, _, hidden = w_gate.shape
    cache_len, lanes = k_cache.shape[1:]
    packed_count = EXPERTS * CAP
    quarter = packed_count // lax.axis_size("tp")
    if not (
        lax.axis_size("tp") == 4
        and lax.axis_size("req") == 8
        and 8 * slot_dev == EXPERTS
        and row_count == quarter
        and cache_len == lanes == 2 * HEAD_DIM
        and queries.shape[1] == 6 * HEAD_DIM
    ):
        return shards_general(
            resid, queries, new_keys, new_values, k_cache, v_cache, lengths, w_out,
            norm_gain, w_router, routes, w_gate, w_up, w_down,
        )
    bf16, f32 = jnp.bfloat16, jnp.float32
    gain = norm_gain.reshape(1, width)
    own, *sents = call(
        attend_kernel,
        [((row_count, width), f32)] + [((row_count, width), bf16)] * 3,
        [spec(pl.ANY)] * 7,
        [
            pltpu.with_memory_space_constraint(operand, pltpu.HBM)
            for operand in (lengths, queries, new_keys, new_values, k_cache, v_cache, w_out)
        ],
        scratch=[
            pltpu.SMEM(lengths.shape, jnp.int32),
            pltpu.VMEM(queries.shape, bf16),
            pltpu.VMEM(new_keys.shape, bf16),
            pltpu.VMEM(new_values.shape, bf16),
            pltpu.VMEM(k_cache.shape, bf16),
            pltpu.VMEM(v_cache.shape, bf16),
            pltpu.VMEM(w_out.shape, bf16),
            pltpu.VMEM((8 * row_count, lanes), f32),
            pltpu.VMEM((8 * row_count, lanes), f32),
            pltpu.VMEM((8 * row_count, cache_len), f32),
            pltpu.VMEM((8 * row_count, cache_len), bf16),
            pltpu.SemaphoreType.DMA((4,)),
            pltpu.SemaphoreType.DMA((12,)),
        ],
        mebibytes=16,
        flops=200_000_000,
        moved=3_400_000,
    )
    def sum_exchange(sents):
        return [partner_permute(block, "tp", k) for k, block in zip(TP_ORDER[1:], sents)]

    parts = sum_exchange(sents)
    base, pick_rows, pick0, pick1, router_rows = call(
        functools.partial(ready_kernel, slot_dev),
        [
            ((row_count, width), f32),
            ((packed_count, row_count), bf16),
            ((row_count, packed_count), bf16),
            ((row_count, packed_count), bf16),
            ((row_count, width), f32),
        ],
        [spec()] * 4,
        (own, resid, routes.T, w_router.T),
    )
    attended, home, *sents = call(
        pack_kernel,
        [((row_count, width), bf16)] + [((quarter, width), bf16)] * 4,
        [spec()] * 5,
        (base, *parts, pick_rows),
    )
    (stats,) = call(
        stats_kernel, [((row_count, 128), f32)], [spec()] * 3, (attended, gain, router_rows)
    )
    (result,) = call(result_kernel, [((row_count, width), bf16)], [spec()], (attended,))
    parts = [partner_permute(block, "req", 2 * k) for k, block in enumerate(sents, 1)]
    (along,) = call(
        turn_kernel, [((2 * quarter, width), bf16)], [spec()] * 4, (home, *parts)
    )
    along = partner_permute(along, "req", 1)
    weights = (w_gate.reshape(slot_dev * width, hidden), w_up.reshape(slot_dev * width, hidden))
    half = quarter // 2
    message = (half, 2 * hidden + 128)
    lhs = pltpu.VMEM((packed_count // 2, slot_dev * width), bf16)

    def chip_sums(kept, sent):
        own, sent = call(
            chip_kernel, [(message, f32), (message, bf16)], [spec()] * 2,
            (kept, partner_permute(sent, "tp", 1)),
        )
        return own, partner_permute(sent, "tp", 2)

    pair = (quarter, message[1])
    early = call(
        functools.partial(early_kernel, slot_dev),
        [(pair, f32), (pair, bf16)],
        [spec()] * 8,
        (home, *parts, gain, stats, *weights),
        scratch=[pltpu.VMEM((2 * quarter, width), bf16), lhs],
        flops=400_000_000,
        moved=3_500_000,
    )
    late = call(
        functools.partial(late_kernel, slot_dev),
        [(pair, f32), (pair, bf16)],
        [spec()] * 4,
        (along, gain, *weights),
        scratch=[lhs],
        flops=400_000_000,
        moved=3_500_000,
    )
    early = chip_sums(*early)
    late = chip_sums(*late)
    own, first_weight = call(
        hidden_kernel,
        [((quarter, hidden), bf16), ((row_count, 128), f32)],
        [spec()] * 4,
        (*late, *early),
    )
    across = partner_permute(own, "tp", 2)
    parts = [partner_permute(own, "tp", 1), across, partner_permute(across, "tp", 1)]
    (computed,) = call(
        functools.partial(down_kernel, slot_dev),
        [((8, packed_count // 8, width), bf16)],
        [spec()] * 5,
        (own, *parts, w_down.reshape(slot_dev * hidden, width)),
        scratch=[pltpu.VMEM((packed_count, slot_dev * hidden), bf16)],
        flops=200_000_000,
        moved=2_000_000,
    )
    returned = lax.all_to_all(computed, "req", split_axis=0, concat_axis=0, tiled=True)
    (layer_out,) = call(
        combine_kernel,
        [((row_count, width), bf16)],
        [spec()] * 5,
        (returned.reshape(packed_count, width), pick0, pick1, first_weight, attended),
    )
    return (result, layer_out)


def solution(mesh):
    placed = (
        P("req", "tp"),
        P("req", "tp"),
        P("req", "tp"),
        P("req", "tp"),
        P("req", None, "tp"),
        P("req", None, "tp"),
        P("req"),
        P("tp", None),
        P("tp"),
        P("tp", None),
        P("req", None),
        P("req", "tp", None),
        P("req", "tp", None),
        P("req", None, "tp"),
    )
    return jax.shard_map(
        shards,
        mesh=mesh,
        in_specs=placed,
        out_specs=(P("req", "tp"), P("req", "tp")),
        check_vma=False,
    )
```

```python
import functools
import math

import jax
import jax.numpy as jnp
from jax import lax
from jax.experimental import pallas as pl
from jax.experimental.pallas import tpu as pltpu
from jax.sharding import PartitionSpec as P

D = 1536
HEAD_DIM = 64
EXPERTS = 16
TOP = 2
CAP = 8


def attend_local(queries, new_keys, new_values, k_cache, v_cache, lengths):
    row_count = queries.shape[0]
    kv_local = new_keys.shape[1] // HEAD_DIM
    group_size = queries.shape[1] // HEAD_DIM // kv_local
    cache_len = k_cache.shape[1]
    score_scale = 1.0 / math.sqrt(HEAD_DIM)
    query = queries.reshape(row_count, kv_local, group_size, HEAD_DIM)
    keys_all = k_cache.reshape(row_count, cache_len, kv_local, HEAD_DIM)
    values_all = v_cache.reshape(row_count, cache_len, kv_local, HEAD_DIM)
    scores = (
        jnp.einsum("bgqd,blgd->bgql", query, keys_all, preferred_element_type=jnp.float32)
        * score_scale
    )
    self_score = (
        jnp.einsum(
            "bgqd,bgd->bgq",
            query,
            new_keys.reshape(row_count, kv_local, HEAD_DIM),
            preferred_element_type=jnp.float32,
        )
        * score_scale
    )
    valid_mask = (jnp.arange(cache_len, dtype=jnp.int32)[None, :] < lengths[:, None])[
        :, None, None, :
    ]
    peak_score = jnp.maximum(jnp.max(jnp.where(valid_mask, scores, -1e30), axis=-1), self_score)
    exp_terms = jnp.where(valid_mask, jnp.exp(scores - peak_score[..., None]), 0.0)
    self_exp = jnp.exp(self_score - peak_score)
    denom_sum = jnp.sum(exp_terms, axis=-1) + self_exp
    weights = (exp_terms / denom_sum[..., None]).astype(jnp.bfloat16)
    self_weight = (self_exp / denom_sum).astype(jnp.bfloat16)
    value_self = new_values.astype(jnp.float32).reshape(row_count, kv_local, 1, HEAD_DIM)
    mixed = (
        jnp.einsum("bgql,blgd->bgqd", weights, values_all, preferred_element_type=jnp.float32)
        + self_weight.astype(jnp.float32)[..., None] * value_self
    )
    return mixed.astype(jnp.bfloat16).reshape(row_count, kv_local * group_size * HEAD_DIM)


def shards_general(
    resid,
    queries,
    new_keys,
    new_values,
    k_cache,
    v_cache,
    lengths,
    w_out,
    norm_gain,
    w_router,
    routes,
    w_gate,
    w_up,
    w_down,
):
    req_dev = resid.shape[0]
    width_local = resid.shape[1]
    slot_dev = w_gate.shape[0]
    req_count = lax.axis_size("req")
    shard_count = max(1, req_count // EXPERTS)
    attention = attend_local(queries, new_keys, new_values, k_cache, v_cache, lengths)
    partial_value = jnp.dot(attention, w_out, preferred_element_type=jnp.float32)
    projected = lax.psum_scatter(partial_value, "tp", scatter_dimension=1, tiled=True)
    attended = (resid.astype(jnp.float32) + projected).astype(jnp.bfloat16)
    attended_f = attended.astype(jnp.float32)
    scaled = attended_f * norm_gain[None, :]
    square_sum, logit_part = lax.psum(
        (
            jnp.sum(attended_f * attended_f, axis=1),
            jnp.dot(scaled, w_router, precision=lax.Precision.HIGHEST),
        ),
        "tp",
    )
    inv_rms = 1.0 / jnp.sqrt(square_sum / D + 1e-06)
    normed = (scaled * inv_rms[:, None]).astype(jnp.bfloat16)
    logits = logit_part * inv_rms[:, None]
    expert_ids = jnp.arange(EXPERTS, dtype=jnp.int32)
    first_logit = jnp.sum(jnp.where(routes[:, 0:1] == expert_ids[None, :], logits, 0.0), axis=1)
    second_logit = jnp.sum(jnp.where(routes[:, 1:2] == expert_ids[None, :], logits, 0.0), axis=1)
    first_weight = jax.nn.sigmoid(first_logit - second_logit)
    second_weight = 1.0 - first_weight
    flat_routes = routes.reshape(req_dev * TOP)
    one_hot = (flat_routes[None, :] == expert_ids[:, None]).astype(jnp.int32)
    rank_in = jnp.cumsum(one_hot, axis=1) - one_hot
    slot_ids = jnp.arange(CAP, dtype=jnp.int32)
    chosen = (one_hot[:, None, :] == 1) & (rank_in[:, None, :] == slot_ids[None, :, None])
    token_pick = jnp.sum(
        chosen.reshape(EXPERTS, CAP, req_dev, TOP).astype(jnp.int32), axis=-1
    ).astype(jnp.bfloat16)
    per_expert = jnp.einsum(
        "ecb,bd->ecd", token_pick, normed, preferred_element_type=jnp.float32
    ).astype(jnp.bfloat16)
    outgoing = jnp.broadcast_to(
        per_expert[:, None], (EXPERTS, shard_count, CAP, width_local)
    ).reshape(req_count, slot_dev, CAP, width_local)
    incoming = lax.all_to_all(outgoing, "req", split_axis=0, concat_axis=0, tiled=True)
    gate_pre = jnp.einsum("nscd,sdf->nscf", incoming, w_gate, preferred_element_type=jnp.float32)
    up_pre = jnp.einsum("nscd,sdf->nscf", incoming, w_up, preferred_element_type=jnp.float32)
    gate_sum, up_sum = lax.psum((gate_pre, up_pre), "tp")
    hidden = (jax.nn.silu(gate_sum) * up_sum).astype(jnp.bfloat16)
    computed = jnp.einsum("nscf,sfd->nscd", hidden, w_down, preferred_element_type=jnp.float32)
    returned = lax.all_to_all(computed, "req", split_axis=0, concat_axis=0, tiled=True)
    combined = jnp.sum(returned.reshape(EXPERTS, shard_count, CAP, width_local), axis=1)
    route_out = jnp.einsum(
        "ecr,ecd->rd", chosen.astype(jnp.float32), combined, precision=lax.Precision.HIGHEST
    ).reshape(req_dev, TOP, width_local)
    moe = first_weight[:, None] * route_out[:, 0] + second_weight[:, None] * route_out[:, 1]
    layer_out = (attended_f + moe).astype(jnp.bfloat16)
    return (attended, layer_out)


TP_ORDER = (0, 2, 3, 1)


def spec(space=pltpu.VMEM):
    return pl.BlockSpec(memory_space=space)


def call(kernel, outs, ins, operands, scratch=(), mebibytes=8, flops=100_000, moved=100_000):
    return pl.pallas_call(
        kernel,
        out_shape=[jax.ShapeDtypeStruct(shape, dtype) for shape, dtype in outs],
        in_specs=ins,
        out_specs=[spec() for _ in outs],
        scratch_shapes=scratch,
        compiler_params=pltpu.CompilerParams(vmem_limit_bytes=mebibytes << 20),
        cost_estimate=pl.CostEstimate(flops=flops, bytes_accessed=moved, transcendentals=0),
    )(*operands)


def partner_permute(block, axis, distance):
    count = lax.axis_size(axis)
    return lax.ppermute(block, axis, [(i, i ^ distance) for i in range(count)])


def attend_kernel(
    lengths_hbm, queries_hbm, keys_hbm, values_hbm, k_hbm, v_hbm, w_hbm, own, sent1, sent2, sent3,
    lengths, queries, new_keys, new_values, k_buf, v_buf, w_buf,
    query_s, self_s, score_s, weight_s, product_s, small_sems, sems,
):
    row_count = queries.shape[0]
    width = own.shape[1]
    lanes = 2 * HEAD_DIM
    cache_len = k_hbm.shape[1]
    chunks = 4
    small = [
        pltpu.make_async_copy(source, target, small_sems.at[index])
        for index, (source, target) in enumerate(
            (
                (queries_hbm, queries),
                (keys_hbm, new_keys),
                (values_hbm, new_values),
                (lengths_hbm, lengths),
            )
        )
    ]
    copies = []
    for source, target in ((k_hbm, k_buf), (v_hbm, v_buf), (w_hbm, w_buf)):
        size = source.shape[0] // chunks
        for chunk in range(chunks):
            part = pl.ds(chunk * size, size)
            copies.append(
                pltpu.make_async_copy(source.at[part], target.at[part], sems.at[len(copies)])
            )
    for copy in small + copies:
        copy.start()
    per_chunk = row_count // chunks

    for copy in small:
        copy.wait()

    low = lax.broadcasted_iota(jnp.int32, (row_count, lanes), 1) < HEAD_DIM
    tiles = [queries[:, i * lanes : (i + 1) * lanes].astype(jnp.float32) for i in range(3)]
    heads = [
        jnp.where(low, tiles[0], 0.0),
        jnp.where(low, pltpu.roll(tiles[0], HEAD_DIM, 1), 0.0),
        jnp.where(low, tiles[1], 0.0),
        jnp.where(low, 0.0, tiles[1]),
        jnp.where(low, 0.0, pltpu.roll(tiles[2], HEAD_DIM, 1)),
        jnp.where(low, 0.0, tiles[2]),
    ]
    scale = 1.0 / math.sqrt(HEAD_DIM)
    for head in range(8):
        rows = pl.ds(head, row_count, stride=8)
        query_s[rows, :] = heads[head] if head < 6 else jnp.zeros((row_count, lanes), jnp.float32)

    row_of = lax.broadcasted_iota(jnp.int32, (8 * row_count, row_count), 0)
    request_of = lax.broadcasted_iota(jnp.int32, (8 * row_count, row_count), 1)
    spread = jnp.where(row_of // 8 == request_of, 1.0, 0.0).astype(jnp.bfloat16)
    keys_new = jnp.dot(spread, new_keys[...], preferred_element_type=jnp.float32)
    values_new = jnp.dot(spread, new_values[...], preferred_element_type=jnp.float32)
    own_score = jnp.sum(query_s[...] * keys_new, axis=1, keepdims=True) * scale

    upper = lax.broadcasted_iota(jnp.int32, (16, lanes), 0) < 8
    position = lax.broadcasted_iota(jnp.int32, (16, cache_len), 1)
    for pair in range(row_count // 2):
        if pair % (per_chunk // 2) == 0:
            copies[pair // (per_chunk // 2)].wait()
        pair_rows = slice(16 * pair, 16 * pair + 16)
        keys = k_buf[2 * pair : 2 * pair + 2].reshape(2 * cache_len, lanes)
        raw = lax.dot_general(
            query_s[pair_rows, :].astype(jnp.bfloat16), keys, (((1,), (1,)), ((), ())),
            preferred_element_type=jnp.float32,
        )
        limit = jnp.where(upper, lengths[2 * pair], lengths[2 * pair + 1])
        score_s[pair_rows, :] = jnp.where(
            position < limit,
            jnp.where(upper, raw[:, :cache_len], raw[:, cache_len:]) * scale,
            -1e30,
        )

    scores = score_s[...]
    peak = jnp.maximum(jnp.max(scores, axis=1, keepdims=True), own_score)
    terms = jnp.exp(scores - peak)
    own_term = jnp.exp(own_score - peak)
    inverse = 1.0 / (jnp.sum(terms, axis=1, keepdims=True) + own_term)
    weight_s[...] = (terms * inverse).astype(jnp.bfloat16)
    own_weight = (own_term * inverse).astype(jnp.bfloat16).astype(jnp.float32)
    self_s[...] = own_weight * values_new
    for pair in range(row_count // 2):
        if pair % (per_chunk // 2) == 0:
            copies[chunks + pair // (per_chunk // 2)].wait()
        pair_rows = slice(16 * pair, 16 * pair + 16)
        values = jnp.concatenate([v_buf[2 * pair], v_buf[2 * pair + 1]], axis=1)
        mixed = jnp.dot(weight_s[pair_rows, :], values, preferred_element_type=jnp.float32)
        query_s[pair_rows, :] = (
            jnp.where(upper, mixed[:, :lanes], mixed[:, lanes:]) + self_s[pair_rows, :]
        )

    mixed = [query_s[pl.ds(head, row_count, stride=8), :] for head in range(6)]
    attention = jnp.concatenate(
        [
            jnp.where(low, mixed[0], pltpu.roll(mixed[1], HEAD_DIM, 1)),
            jnp.where(low, mixed[2], mixed[3]),
            jnp.where(low, pltpu.roll(mixed[4], HEAD_DIM, 1), mixed[5]),
        ],
        axis=1,
    ).astype(jnp.bfloat16)
    for copy in copies[2 * chunks :]:
        copy.wait()
    place_tp = lax.axis_index("tp")
    product_s[...] = jnp.dot(attention, w_buf[...], preferred_element_type=jnp.float32)
    for shift, out in zip(TP_ORDER, (own, sent1, sent2, sent3)):
        columns = pl.ds(pl.multiple_of((place_tp ^ shift) * width, width), width)
        out[...] = product_s[:, columns].astype(out.dtype)


def ready_kernel(
    slot_dev, own, resid, routes, w_router, gate_hbm, up_hbm,
    base, pick_rows, pick0, pick1, router_rows, w_gate, w_up, sems,
):
    copies = []
    for source, target in ((gate_hbm, w_gate), (up_hbm, w_up)):
        size = source.shape[0] // 4
        for chunk in range(4):
            part = pl.ds(chunk * size, size)
            copies.append(
                pltpu.make_async_copy(source.at[part], target.at[part], sems.at[len(copies)])
            )
    for copy in copies:
        copy.start()
    base[...] = own[...] + resid[...].astype(jnp.float32)
    packed_count, row_count = pick_rows.shape

    route0, route1 = routes[0:1, :], routes[1:2, :]
    place = lax.broadcasted_iota(jnp.int32, (packed_count, row_count), 0)
    named0 = jnp.where(place == route0, 1.0, 0.0)
    named1 = jnp.where(place == route1, 1.0, 0.0)
    row_of = lax.broadcasted_iota(jnp.int32, (row_count, row_count), 0)
    col_of = lax.broadcasted_iota(jnp.int32, (row_count, row_count), 1)
    earlier = jnp.where(row_of < col_of, 1.0, 0.0).astype(jnp.bfloat16)
    before = jnp.dot(
        (named0 + named1).astype(jnp.bfloat16), earlier, preferred_element_type=jnp.float32
    )
    place_req = lax.axis_index("req")

    def pick(route, named, mine):
        rank = jnp.sum(named * before, axis=0, keepdims=True).astype(jnp.int32)
        block = ((route // slot_dev) ^ mine) * slot_dev + lax.rem(route, slot_dev)
        return jnp.where(place == block * CAP + rank, 1.0, 0.0)

    sent_rows = pick(route0, named0, place_req) + pick(route1, named1, place_req)
    pick_rows[...] = sent_rows.astype(jnp.bfloat16)
    pick0[...] = jnp.transpose(pick(route0, named0, 0)).astype(jnp.bfloat16)
    pick1[...] = jnp.transpose(pick(route1, named1, 0)).astype(jnp.bfloat16)
    signed = jnp.transpose(named0 - named1)
    router_rows[...] = jnp.dot(
        signed[:, :EXPERTS], w_router[...],
        precision=lax.Precision.HIGHEST, preferred_element_type=jnp.float32,
    )
    for copy in copies:
        copy.wait()


def pack_kernel(base, part1, part2, part3, pick_rows, attended, home, sent1, sent2, sent3):
    total = base[...]
    for part in (part1, part2, part3):
        total = total + part[...].astype(jnp.float32)
    rows = total.astype(jnp.bfloat16)
    attended[...] = rows
    packed = jnp.dot(pick_rows[...], rows, preferred_element_type=jnp.float32)
    size = home.shape[0]
    for distance, out in enumerate((home, sent1, sent2, sent3)):
        out[...] = packed[distance * size : (distance + 1) * size].astype(out.dtype)


def result_kernel(attended, result):
    result[...] = attended[...]


def stats_kernel(attended, gain, router_rows, stats):
    rows = attended[...].astype(jnp.float32)
    square = jnp.sum(rows * rows, axis=1, keepdims=True)
    logit = jnp.sum(rows * gain[...] * router_rows[...], axis=1, keepdims=True)
    lane = lax.broadcasted_iota(jnp.int32, stats.shape, 1)
    stats[...] = jnp.where(lane == 0, square, jnp.where(lane == 1, logit, 0.0))


def turn_kernel(home, part1, part2, part3, along):
    half = home.shape[0] // 2
    for index, part in enumerate((home, part1, part2, part3)):
        along[index * half : (index + 1) * half, :] = part[half:, :]


def slot_masks(row_count, slot_dev):
    slot = lax.rem(lax.broadcasted_iota(jnp.int32, (row_count, 1), 0) // CAP, slot_dev)
    return [slot == index for index in range(slot_dev)]


def split_high(column):
    high = column.astype(jnp.bfloat16).astype(jnp.float32)
    return high, column - high


def gate_terms(slot_dev, blocks, gain, stats, w_gate, w_up, kept, sent, lhs):
    size = kept.shape[0] // 2
    width = blocks.shape[1]
    hidden = w_gate.shape[1]
    place_tp = lax.axis_index("tp")
    masks = slot_masks(size, slot_dev)
    lane = lax.broadcasted_iota(jnp.int32, (size, 128), 1)
    for order, shift in enumerate((0, 2, 1, 3)):
        out, first_row = (kept, sent)[order // 2], order % 2 * size
        rows = blocks[
            pl.ds(pl.multiple_of((place_tp ^ shift) * size, size), size), :
        ].astype(jnp.float32)
        columns = [jnp.sum(rows * rows, axis=1, keepdims=True)]
        if stats is not None:
            for first in range(0, stats.shape[0], size):
                columns += [stats[first : first + size, 0:1], stats[first : first + size, 1:2]]
        extra = jnp.zeros((size, 128), jnp.float32)
        for index, column in enumerate(columns):
            high, low = split_high(column)
            extra = jnp.where(lane == 2 * index, high, extra)
            extra = jnp.where(lane == 2 * index + 1, low, extra)
        out[first_row : first_row + size, 2 * hidden :] = extra.astype(out.dtype)
        scaled = rows * gain[...]
        for index, mask in enumerate(masks):
            lhs[order * size : (order + 1) * size, index * width : (index + 1) * width] = (
                jnp.where(mask, scaled, 0.0).astype(jnp.bfloat16)
            )
    left = lhs[...]
    for first, weight in ((0, w_gate), (hidden, w_up)):
        product = jnp.dot(left, weight[...], preferred_element_type=jnp.float32)
        kept[:, first : first + hidden] = product[: 2 * size]
        sent[:, first : first + hidden] = product[2 * size :].astype(sent.dtype)


def early_kernel(
    slot_dev, in0, in1, in2, in3, gain, stats, w_gate, w_up, kept, sent, blocks, lhs
):
    half = kept.shape[0] // 2
    for index, part in enumerate((in0, in1, in2, in3)):
        blocks[index * half : (index + 1) * half, :] = part[:half, :]
    gate_terms(slot_dev, blocks, gain, stats, w_gate, w_up, kept, sent, lhs)


def late_kernel(slot_dev, blocks, gain, w_gate, w_up, kept, sent, lhs):
    gate_terms(slot_dev, blocks, gain, None, w_gate, w_up, kept, sent, lhs)


def chip_kernel(kept, part, own, sent):
    size, width = own.shape
    own[...] = kept[:size, :] + part[:size, :].astype(jnp.float32)
    total = kept[size:, :] + part[size:, :].astype(jnp.float32)
    extra = total[:, width - 128 :]
    lane = lax.broadcasted_iota(jnp.int32, extra.shape, 1)
    high, low = split_high(extra + pltpu.roll(extra, 127, 1))
    sent[:, : width - 128] = total[:, : width - 128].astype(sent.dtype)
    sent[:, width - 128 :] = jnp.where(
        lax.rem(lane, 2) == 0, high, pltpu.roll(low, 1, 1)
    ).astype(sent.dtype)


def hidden_kernel(*refs):
    late, early, (hidden, first_weight) = refs[:2], refs[2:4], refs[4:]
    width = hidden.shape[1]
    half = hidden.shape[0] // 2

    def total(parts, columns):
        result = parts[0][:, columns]
        for part in parts[1:]:
            result = result + part[:, columns].astype(jnp.float32)
        return result

    def inverse_rms(columns, index):
        square = columns[:, index : index + 1] + columns[:, index + 1 : index + 2]
        return 1.0 / jnp.sqrt(square / D + 1e-06)

    for index, parts in ((1, late), (0, early)):
        extra = total(parts, slice(2 * width, 2 * width + 128))
        row_inv = inverse_rms(extra, 0)
        gate = total(parts, slice(0, width)) * row_inv
        up = total(parts, slice(width, 2 * width)) * row_inv
        hidden[index * half : (index + 1) * half, :] = (
            gate / (1.0 + jnp.exp(-gate)) * up
        ).astype(jnp.bfloat16)
    for index in range(first_weight.shape[0] // half):
        place = 2 + 4 * index
        logit = extra[:, place + 2 : place + 3] + extra[:, place + 3 : place + 4]
        weight = 1.0 / (1.0 + jnp.exp(-logit * inverse_rms(extra, place)))
        first_weight[index * half : (index + 1) * half, :] = jnp.broadcast_to(weight, (half, 128))


def down_kernel(slot_dev, own, part1, part2, part3, w_down, computed, lhs):
    quarter, width = own.shape
    block = computed.shape[1]
    place_tp = lax.axis_index("tp")
    place_req = lax.axis_index("req")
    masks = slot_masks(quarter, slot_dev)
    for shift, part in enumerate((own, part1, part2, part3)):
        rows = part[...].astype(jnp.float32)
        place = pl.ds(pl.multiple_of((place_tp ^ shift) * quarter, quarter), quarter)
        for index, mask in enumerate(masks):
            lhs[place, index * width : (index + 1) * width] = jnp.where(mask, rows, 0.0).astype(
                jnp.bfloat16
            )
    product = jnp.dot(lhs[...], w_down[...], preferred_element_type=jnp.float32)
    for index in range(computed.shape[0]):
        computed[place_req ^ index] = product[index * block : (index + 1) * block].astype(
            computed.dtype
        )


def combine_kernel(returned, pick0, pick1, first_weight, attended, layer_out):
    rows = returned[...]
    out0 = jnp.dot(pick0[...], rows, preferred_element_type=jnp.float32)
    out1 = jnp.dot(pick1[...], rows, preferred_element_type=jnp.float32)
    weight = first_weight[:, 0:1]
    moe = weight * out0 + (1.0 - weight) * out1
    layer_out[...] = (attended[...].astype(jnp.float32) + moe).astype(jnp.bfloat16)


def shards(
    resid,
    queries,
    new_keys,
    new_values,
    k_cache,
    v_cache,
    lengths,
    w_out,
    norm_gain,
    w_router,
    routes,
    w_gate,
    w_up,
    w_down,
):
    row_count, width = resid.shape
    slot_dev, _, hidden = w_gate.shape
    cache_len, lanes = k_cache.shape[1:]
    packed_count = EXPERTS * CAP
    quarter = packed_count // lax.axis_size("tp")
    if not (
        lax.axis_size("tp") == 4
        and lax.axis_size("req") == 8
        and 8 * slot_dev == EXPERTS
        and row_count == quarter
        and cache_len == lanes == 2 * HEAD_DIM
        and queries.shape[1] == 6 * HEAD_DIM
    ):
        return shards_general(
            resid, queries, new_keys, new_values, k_cache, v_cache, lengths, w_out,
            norm_gain, w_router, routes, w_gate, w_up, w_down,
        )
    bf16, f32 = jnp.bfloat16, jnp.float32
    gain = norm_gain.reshape(1, width)
    own, *sents = call(
        attend_kernel,
        [((row_count, width), f32)] + [((row_count, width), bf16)] * 3,
        [spec(pl.ANY)] * 7,
        [
            pltpu.with_memory_space_constraint(operand, pltpu.HBM)
            for operand in (lengths, queries, new_keys, new_values, k_cache, v_cache, w_out)
        ],
        scratch=[
            pltpu.SMEM(lengths.shape, jnp.int32),
            pltpu.VMEM(queries.shape, bf16),
            pltpu.VMEM(new_keys.shape, bf16),
            pltpu.VMEM(new_values.shape, bf16),
            pltpu.VMEM(k_cache.shape, bf16),
            pltpu.VMEM(v_cache.shape, bf16),
            pltpu.VMEM(w_out.shape, bf16),
            pltpu.VMEM((8 * row_count, lanes), f32),
            pltpu.VMEM((8 * row_count, lanes), f32),
            pltpu.VMEM((8 * row_count, cache_len), f32),
            pltpu.VMEM((8 * row_count, cache_len), bf16),
            pltpu.VMEM((row_count, w_out.shape[1]), f32),
            pltpu.SemaphoreType.DMA((4,)),
            pltpu.SemaphoreType.DMA((12,)),
        ],
        mebibytes=16,
        flops=200_000_000,
        moved=3_400_000,
    )
    def sum_exchange(sents):
        return [partner_permute(block, "tp", k) for k, block in zip(TP_ORDER[1:], sents)]

    parts = sum_exchange(sents)
    weight = (slot_dev * width, hidden)
    base, pick_rows, pick0, pick1, router_rows, *weights = call(
        functools.partial(ready_kernel, slot_dev),
        [
            ((row_count, width), f32),
            ((packed_count, row_count), bf16),
            ((row_count, packed_count), bf16),
            ((row_count, packed_count), bf16),
            ((row_count, width), f32),
            (weight, bf16),
            (weight, bf16),
        ],
        [spec()] * 4 + [spec(pl.ANY)] * 2,
        (
            own,
            resid,
            routes.T,
            w_router.T,
            pltpu.with_memory_space_constraint(w_gate.reshape(weight), pltpu.HBM),
            pltpu.with_memory_space_constraint(w_up.reshape(weight), pltpu.HBM),
        ),
        scratch=[pltpu.SemaphoreType.DMA((8,))],
        mebibytes=12,
        moved=3_300_000,
    )
    attended, home, *sents = call(
        pack_kernel,
        [((row_count, width), bf16)] + [((quarter, width), bf16)] * 4,
        [spec()] * 5,
        (base, *parts, pick_rows),
    )
    (stats,) = call(
        stats_kernel, [((row_count, 128), f32)], [spec()] * 3, (attended, gain, router_rows)
    )
    (result,) = call(result_kernel, [((row_count, width), bf16)], [spec()], (attended,))
    stats, result = lax.optimization_barrier((stats, result))
    parts = [partner_permute(block, "req", 2 * k) for k, block in enumerate(sents, 1)]
    (along,) = call(
        turn_kernel, [((2 * quarter, width), bf16)], [spec()] * 4, (home, *parts)
    )
    along = partner_permute(along, "req", 1)
    half = quarter // 2
    message = (half, 2 * hidden + 128)
    lhs = pltpu.VMEM((packed_count // 2, slot_dev * width), bf16)

    def chip_sums(kept, sent):
        own, sent = call(
            chip_kernel, [(message, f32), (message, bf16)], [spec()] * 2,
            (kept, partner_permute(sent, "tp", 1)),
        )
        return own, partner_permute(sent, "tp", 2)

    pair = (quarter, message[1])
    early = call(
        functools.partial(early_kernel, slot_dev),
        [(pair, f32), (pair, bf16)],
        [spec()] * 8,
        (home, *parts, gain, stats, *weights),
        scratch=[pltpu.VMEM((2 * quarter, width), bf16), lhs],
        flops=400_000_000,
        moved=3_500_000,
    )
    late = call(
        functools.partial(late_kernel, slot_dev),
        [(pair, f32), (pair, bf16)],
        [spec()] * 4,
        (along, gain, *weights),
        scratch=[lhs],
        flops=400_000_000,
        moved=3_500_000,
    )
    early = chip_sums(*early)
    late = chip_sums(*late)
    own, first_weight = call(
        hidden_kernel,
        [((quarter, hidden), bf16), ((row_count, 128), f32)],
        [spec()] * 4,
        (*late, *early),
    )
    across = partner_permute(own, "tp", 2)
    parts = [partner_permute(own, "tp", 1), across, partner_permute(across, "tp", 1)]
    (computed,) = call(
        functools.partial(down_kernel, slot_dev),
        [((8, packed_count // 8, width), bf16)],
        [spec()] * 5,
        (own, *parts, w_down.reshape(slot_dev * hidden, width)),
        scratch=[pltpu.VMEM((packed_count, slot_dev * hidden), bf16)],
        flops=200_000_000,
        moved=2_000_000,
    )
    returned = lax.all_to_all(computed, "req", split_axis=0, concat_axis=0, tiled=True)
    (layer_out,) = call(
        combine_kernel,
        [((row_count, width), bf16)],
        [spec()] * 5,
        (returned.reshape(packed_count, width), pick0, pick1, first_weight, attended),
    )
    return (result, layer_out)


def solution(mesh):
    placed = (
        P("req", "tp"),
        P("req", "tp"),
        P("req", "tp"),
        P("req", "tp"),
        P("req", None, "tp"),
        P("req", None, "tp"),
        P("req"),
        P("tp", None),
        P("tp"),
        P("tp", None),
        P("req", None),
        P("req", "tp", None),
        P("req", "tp", None),
        P("req", None, "tp"),
    )
    return jax.shard_map(
        shards,
        mesh=mesh,
        in_specs=placed,
        out_specs=(P("req", "tp"), P("req", "tp")),
        check_vma=False,
    )
```

```python
import functools
import math

import jax
import jax.numpy as jnp
from jax import lax
from jax.experimental import pallas as pl
from jax.experimental.pallas import tpu as pltpu
from jax.sharding import PartitionSpec as P

D = 1536
HEAD_DIM = 64
EXPERTS = 16
TOP = 2
CAP = 8


def attend_local(queries, new_keys, new_values, k_cache, v_cache, lengths):
    row_count = queries.shape[0]
    kv_local = new_keys.shape[1] // HEAD_DIM
    group_size = queries.shape[1] // HEAD_DIM // kv_local
    cache_len = k_cache.shape[1]
    score_scale = 1.0 / math.sqrt(HEAD_DIM)
    query = queries.reshape(row_count, kv_local, group_size, HEAD_DIM)
    keys_all = k_cache.reshape(row_count, cache_len, kv_local, HEAD_DIM)
    values_all = v_cache.reshape(row_count, cache_len, kv_local, HEAD_DIM)
    scores = (
        jnp.einsum("bgqd,blgd->bgql", query, keys_all, preferred_element_type=jnp.float32)
        * score_scale
    )
    self_score = (
        jnp.einsum(
            "bgqd,bgd->bgq",
            query,
            new_keys.reshape(row_count, kv_local, HEAD_DIM),
            preferred_element_type=jnp.float32,
        )
        * score_scale
    )
    valid_mask = (jnp.arange(cache_len, dtype=jnp.int32)[None, :] < lengths[:, None])[
        :, None, None, :
    ]
    peak_score = jnp.maximum(jnp.max(jnp.where(valid_mask, scores, -1e30), axis=-1), self_score)
    exp_terms = jnp.where(valid_mask, jnp.exp(scores - peak_score[..., None]), 0.0)
    self_exp = jnp.exp(self_score - peak_score)
    denom_sum = jnp.sum(exp_terms, axis=-1) + self_exp
    weights = (exp_terms / denom_sum[..., None]).astype(jnp.bfloat16)
    self_weight = (self_exp / denom_sum).astype(jnp.bfloat16)
    value_self = new_values.astype(jnp.float32).reshape(row_count, kv_local, 1, HEAD_DIM)
    mixed = (
        jnp.einsum("bgql,blgd->bgqd", weights, values_all, preferred_element_type=jnp.float32)
        + self_weight.astype(jnp.float32)[..., None] * value_self
    )
    return mixed.astype(jnp.bfloat16).reshape(row_count, kv_local * group_size * HEAD_DIM)


def shards_general(
    resid,
    queries,
    new_keys,
    new_values,
    k_cache,
    v_cache,
    lengths,
    w_out,
    norm_gain,
    w_router,
    routes,
    w_gate,
    w_up,
    w_down,
):
    req_dev = resid.shape[0]
    width_local = resid.shape[1]
    slot_dev = w_gate.shape[0]
    req_count = lax.axis_size("req")
    shard_count = max(1, req_count // EXPERTS)
    attention = attend_local(queries, new_keys, new_values, k_cache, v_cache, lengths)
    partial_value = jnp.dot(attention, w_out, preferred_element_type=jnp.float32)
    projected = lax.psum_scatter(partial_value, "tp", scatter_dimension=1, tiled=True)
    attended = (resid.astype(jnp.float32) + projected).astype(jnp.bfloat16)
    attended_f = attended.astype(jnp.float32)
    scaled = attended_f * norm_gain[None, :]
    square_sum, logit_part = lax.psum(
        (
            jnp.sum(attended_f * attended_f, axis=1),
            jnp.dot(scaled, w_router, precision=lax.Precision.HIGHEST),
        ),
        "tp",
    )
    inv_rms = 1.0 / jnp.sqrt(square_sum / D + 1e-06)
    normed = (scaled * inv_rms[:, None]).astype(jnp.bfloat16)
    logits = logit_part * inv_rms[:, None]
    expert_ids = jnp.arange(EXPERTS, dtype=jnp.int32)
    first_logit = jnp.sum(jnp.where(routes[:, 0:1] == expert_ids[None, :], logits, 0.0), axis=1)
    second_logit = jnp.sum(jnp.where(routes[:, 1:2] == expert_ids[None, :], logits, 0.0), axis=1)
    first_weight = jax.nn.sigmoid(first_logit - second_logit)
    second_weight = 1.0 - first_weight
    flat_routes = routes.reshape(req_dev * TOP)
    one_hot = (flat_routes[None, :] == expert_ids[:, None]).astype(jnp.int32)
    rank_in = jnp.cumsum(one_hot, axis=1) - one_hot
    slot_ids = jnp.arange(CAP, dtype=jnp.int32)
    chosen = (one_hot[:, None, :] == 1) & (rank_in[:, None, :] == slot_ids[None, :, None])
    token_pick = jnp.sum(
        chosen.reshape(EXPERTS, CAP, req_dev, TOP).astype(jnp.int32), axis=-1
    ).astype(jnp.bfloat16)
    per_expert = jnp.einsum(
        "ecb,bd->ecd", token_pick, normed, preferred_element_type=jnp.float32
    ).astype(jnp.bfloat16)
    outgoing = jnp.broadcast_to(
        per_expert[:, None], (EXPERTS, shard_count, CAP, width_local)
    ).reshape(req_count, slot_dev, CAP, width_local)
    incoming = lax.all_to_all(outgoing, "req", split_axis=0, concat_axis=0, tiled=True)
    gate_pre = jnp.einsum("nscd,sdf->nscf", incoming, w_gate, preferred_element_type=jnp.float32)
    up_pre = jnp.einsum("nscd,sdf->nscf", incoming, w_up, preferred_element_type=jnp.float32)
    gate_sum, up_sum = lax.psum((gate_pre, up_pre), "tp")
    hidden = (jax.nn.silu(gate_sum) * up_sum).astype(jnp.bfloat16)
    computed = jnp.einsum("nscf,sfd->nscd", hidden, w_down, preferred_element_type=jnp.float32)
    returned = lax.all_to_all(computed, "req", split_axis=0, concat_axis=0, tiled=True)
    combined = jnp.sum(returned.reshape(EXPERTS, shard_count, CAP, width_local), axis=1)
    route_out = jnp.einsum(
        "ecr,ecd->rd", chosen.astype(jnp.float32), combined, precision=lax.Precision.HIGHEST
    ).reshape(req_dev, TOP, width_local)
    moe = first_weight[:, None] * route_out[:, 0] + second_weight[:, None] * route_out[:, 1]
    layer_out = (attended_f + moe).astype(jnp.bfloat16)
    return (attended, layer_out)


FAR_FIRST = (0, 2, 3, 1)


def spec(space=pltpu.VMEM):
    return pl.BlockSpec(memory_space=space)


def call(kernel, outs, ins, operands, scratch=(), mebibytes=8, flops=100_000, moved=100_000):
    return pl.pallas_call(
        kernel,
        out_shape=[jax.ShapeDtypeStruct(shape, dtype) for shape, dtype in outs],
        in_specs=ins,
        out_specs=[spec() for _ in outs],
        scratch_shapes=scratch,
        compiler_params=pltpu.CompilerParams(vmem_limit_bytes=mebibytes << 20),
        cost_estimate=pl.CostEstimate(flops=flops, bytes_accessed=moved, transcendentals=0),
    )(*operands)


def partner_permute(block, axis, distance):
    count = lax.axis_size(axis)
    return lax.ppermute(block, axis, [(i, i ^ distance) for i in range(count)])


def attend_kernel(
    lengths_hbm, queries_hbm, keys_hbm, values_hbm, k_hbm, v_hbm, w_hbm, own, sent1, sent2, sent3,
    lengths, queries, new_keys, new_values, k_buf, v_buf, w_buf,
    query_s, mixed_s, product_s, small_sems, sems,
):
    row_count = queries.shape[0]
    width = own.shape[1]
    lanes = 2 * HEAD_DIM
    cache_len = k_hbm.shape[1]
    chunks = 4
    small = [
        pltpu.make_async_copy(source, target, small_sems.at[index])
        for index, (source, target) in enumerate(
            (
                (queries_hbm, queries),
                (keys_hbm, new_keys),
                (values_hbm, new_values),
                (lengths_hbm, lengths),
            )
        )
    ]
    copies = []
    for source, target in ((k_hbm, k_buf), (v_hbm, v_buf), (w_hbm, w_buf)):
        size = source.shape[0] // chunks
        for chunk in range(chunks):
            part = pl.ds(chunk * size, size)
            copies.append(
                pltpu.make_async_copy(source.at[part], target.at[part], sems.at[len(copies)])
            )
    for copy in small + copies:
        copy.start()
    per_chunk = row_count // chunks

    for copy in small:
        copy.wait()

    low = lax.broadcasted_iota(jnp.int32, (row_count, lanes), 1) < HEAD_DIM
    tiles = [queries[:, i * lanes : (i + 1) * lanes].astype(jnp.float32) for i in range(3)]
    heads = [
        jnp.where(low, tiles[0], 0.0),
        jnp.where(low, pltpu.roll(tiles[0], HEAD_DIM, 1), 0.0),
        jnp.where(low, tiles[1], 0.0),
        jnp.where(low, 0.0, tiles[1]),
        jnp.where(low, 0.0, pltpu.roll(tiles[2], HEAD_DIM, 1)),
        jnp.where(low, 0.0, tiles[2]),
    ]
    scale = 1.0 / math.sqrt(HEAD_DIM)
    for head in range(8):
        rows = pl.ds(head, row_count, stride=8)
        query_s[rows, :] = heads[head] if head < 6 else jnp.zeros((row_count, lanes), jnp.float32)

    row_of = lax.broadcasted_iota(jnp.int32, (8 * row_count, row_count), 0)
    request_of = lax.broadcasted_iota(jnp.int32, (8 * row_count, row_count), 1)
    spread = jnp.where(row_of // 8 == request_of, 1.0, 0.0).astype(jnp.bfloat16)
    keys_new = jnp.dot(spread, new_keys[...], preferred_element_type=jnp.float32)
    values_new = jnp.dot(spread, new_values[...], preferred_element_type=jnp.float32)
    own_score = jnp.sum(query_s[...] * keys_new, axis=1, keepdims=True) * scale

    position = lax.broadcasted_iota(jnp.int32, (8, cache_len), 1)
    group = 4
    query_rows = query_s[...].astype(jnp.bfloat16)

    def own_tiles(product):
        return [
            product[8 * index : 8 * index + 8, lanes * index : lanes * (index + 1)]
            for index in range(group)
        ]

    def attend(chunk):
        start = chunk * per_chunk
        chunk_rows = slice(8 * start, 8 * (start + per_chunk))
        copies[chunk].wait()
        tiles = []
        for first in range(start, start + per_chunk, group):
            raw = lax.dot_general(
                query_rows[8 * first : 8 * (first + group)],
                k_buf[first : first + group].reshape(group * cache_len, lanes),
                (((1,), (1,)), ((), ())),
                preferred_element_type=jnp.float32,
            )
            for index, tile in enumerate(own_tiles(raw)):
                tiles.append(jnp.where(position < lengths[first + index], tile * scale, -1e30))
        scores = jnp.concatenate(tiles, axis=0)
        own = own_score[chunk_rows]
        peak = jnp.maximum(jnp.max(scores, axis=1, keepdims=True), own)
        terms = jnp.exp(scores - peak)
        own_term = jnp.exp(own - peak)
        inverse = 1.0 / (jnp.sum(terms, axis=1, keepdims=True) + own_term)
        own_weight = (own_term * inverse).astype(jnp.bfloat16).astype(jnp.float32)
        return (terms * inverse).astype(jnp.bfloat16), own_weight * values_new[chunk_rows]

    def mix(chunk, weights, own):
        start = chunk * per_chunk
        copies[chunks + chunk].wait()
        tiles = []
        for first in range(start, start + per_chunk, group):
            values = jnp.concatenate([v_buf[first + index] for index in range(group)], axis=1)
            rows = slice(8 * (first - start), 8 * (first - start + group))
            tiles += own_tiles(jnp.dot(weights[rows], values, preferred_element_type=jnp.float32))
        mixed_s[8 * start : 8 * (start + per_chunk), :] = jnp.concatenate(tiles, axis=0) + own

    ready = attend(0)
    for chunk in range(1, chunks):
        following = attend(chunk)
        mix(chunk - 1, *ready)
        ready = following
    mix(chunks - 1, *ready)

    mixed = [mixed_s[pl.ds(head, row_count, stride=8), :] for head in range(6)]
    attention = jnp.concatenate(
        [
            jnp.where(low, mixed[0], pltpu.roll(mixed[1], HEAD_DIM, 1)),
            jnp.where(low, mixed[2], mixed[3]),
            jnp.where(low, pltpu.roll(mixed[4], HEAD_DIM, 1), mixed[5]),
        ],
        axis=1,
    ).astype(jnp.bfloat16)
    for copy in copies[2 * chunks :]:
        copy.wait()
    place_tp = lax.axis_index("tp")
    product_s[...] = jnp.dot(attention, w_buf[...], preferred_element_type=jnp.float32)
    for shift, out in zip(FAR_FIRST, (own, sent1, sent2, sent3)):
        columns = pl.ds(pl.multiple_of((place_tp ^ shift) * width, width), width)
        out[...] = product_s[:, columns].astype(out.dtype)


def ready_kernel(
    slot_dev, own, resid, routes, w_router, gate_hbm, up_hbm,
    base, pick_rows, pick0, pick1, router_rows, w_gate, w_up, sems,
):
    copies = []
    for source, target in ((gate_hbm, w_gate), (up_hbm, w_up)):
        size = source.shape[0] // 4
        for chunk in range(4):
            part = pl.ds(chunk * size, size)
            copies.append(
                pltpu.make_async_copy(source.at[part], target.at[part], sems.at[len(copies)])
            )
    for copy in copies:
        copy.start()
    base[...] = own[...] + resid[...].astype(jnp.float32)
    packed_count, row_count = pick_rows.shape

    route0, route1 = routes[0:1, :], routes[1:2, :]
    place = lax.broadcasted_iota(jnp.int32, (packed_count, row_count), 0)
    named0 = jnp.where(place == route0, 1.0, 0.0)
    named1 = jnp.where(place == route1, 1.0, 0.0)
    row_of = lax.broadcasted_iota(jnp.int32, (row_count, row_count), 0)
    col_of = lax.broadcasted_iota(jnp.int32, (row_count, row_count), 1)
    earlier = jnp.where(row_of < col_of, 1.0, 0.0).astype(jnp.bfloat16)
    before = jnp.dot(
        (named0 + named1).astype(jnp.bfloat16), earlier, preferred_element_type=jnp.float32
    )
    place_req = lax.axis_index("req")

    def pick(route, named, mine):
        rank = jnp.sum(named * before, axis=0, keepdims=True).astype(jnp.int32)
        block = ((route // slot_dev) ^ mine) * slot_dev + lax.rem(route, slot_dev)
        return jnp.where(place == block * CAP + rank, 1.0, 0.0)

    sent_rows = pick(route0, named0, place_req) + pick(route1, named1, place_req)
    pick_rows[...] = sent_rows.astype(jnp.bfloat16)
    pick0[...] = jnp.transpose(pick(route0, named0, 0)).astype(jnp.bfloat16)
    pick1[...] = jnp.transpose(pick(route1, named1, 0)).astype(jnp.bfloat16)
    signed = jnp.transpose(named0 - named1)
    router_rows[...] = jnp.dot(
        signed[:, :EXPERTS], w_router[...],
        precision=lax.Precision.HIGHEST, preferred_element_type=jnp.float32,
    )
    for copy in copies:
        copy.wait()


def pack_kernel(base, part1, part2, part3, pick_rows, attended, home, sent1, sent2, sent3):
    total = base[...]
    for part in (part1, part2, part3):
        total = total + part[...].astype(jnp.float32)
    rows = total.astype(jnp.bfloat16)
    attended[...] = rows
    packed = jnp.dot(pick_rows[...], rows, preferred_element_type=jnp.float32)
    size = home.shape[0]
    for distance, out in zip(FAR_FIRST, (home, sent1, sent2, sent3)):
        out[...] = packed[distance * size : (distance + 1) * size].astype(out.dtype)


def result_kernel(attended, result):
    result[...] = attended[...]


def stats_kernel(attended, gain, router_rows, stats):
    rows = attended[...].astype(jnp.float32)
    square = jnp.sum(rows * rows, axis=1, keepdims=True)
    logit = jnp.sum(rows * gain[...] * router_rows[...], axis=1, keepdims=True)
    lane = lax.broadcasted_iota(jnp.int32, stats.shape, 1)
    stats[...] = jnp.where(lane == 0, square, jnp.where(lane == 1, logit, 0.0))


def turn_kernel(home, part1, part2, part3, along):
    half = home.shape[0] // 2
    for index, part in enumerate((home, part1, part2, part3)):
        along[index * half : (index + 1) * half, :] = part[half:, :]


def slot_masks(row_count, slot_dev):
    slot = lax.rem(lax.broadcasted_iota(jnp.int32, (row_count, 1), 0) // CAP, slot_dev)
    return [slot == index for index in range(slot_dev)]


def split_high(column):
    high = column.astype(jnp.bfloat16).astype(jnp.float32)
    return high, column - high


def gate_terms(slot_dev, blocks, gain, stats, w_gate, w_up, kept, sent, lhs):
    size = kept.shape[0] // 2
    width = blocks.shape[1]
    hidden = w_gate.shape[1]
    place_tp = lax.axis_index("tp")
    masks = slot_masks(size, slot_dev)
    lane = lax.broadcasted_iota(jnp.int32, (size, 128), 1)
    for order, shift in enumerate((0, 2, 1, 3)):
        out, first_row = (kept, sent)[order // 2], order % 2 * size
        rows = blocks[
            pl.ds(pl.multiple_of((place_tp ^ shift) * size, size), size), :
        ].astype(jnp.float32)
        columns = [jnp.sum(rows * rows, axis=1, keepdims=True)]
        if stats is not None:
            for first in range(0, stats.shape[0], size):
                columns += [stats[first : first + size, 0:1], stats[first : first + size, 1:2]]
        extra = jnp.zeros((size, 128), jnp.float32)
        for index, column in enumerate(columns):
            high, low = split_high(column)
            extra = jnp.where(lane == 2 * index, high, extra)
            extra = jnp.where(lane == 2 * index + 1, low, extra)
        out[first_row : first_row + size, 2 * hidden :] = extra.astype(out.dtype)
        scaled = rows * gain[...]
        for index, mask in enumerate(masks):
            lhs[order * size : (order + 1) * size, index * width : (index + 1) * width] = (
                jnp.where(mask, scaled, 0.0).astype(jnp.bfloat16)
            )
    left = lhs[...]
    for first, weight in ((0, w_gate), (hidden, w_up)):
        product = jnp.dot(left, weight[...], preferred_element_type=jnp.float32)
        kept[:, first : first + hidden] = product[: 2 * size]
        sent[:, first : first + hidden] = product[2 * size :].astype(sent.dtype)


def early_kernel(
    slot_dev, in0, in1, in2, in3, gain, stats, w_gate, w_up, kept, sent, blocks, lhs
):
    half = kept.shape[0] // 2
    for index, part in enumerate((in0, in1, in2, in3)):
        blocks[index * half : (index + 1) * half, :] = part[:half, :]
    gate_terms(slot_dev, blocks, gain, stats, w_gate, w_up, kept, sent, lhs)


def late_kernel(slot_dev, blocks, gain, w_gate, w_up, kept, sent, lhs):
    gate_terms(slot_dev, blocks, gain, None, w_gate, w_up, kept, sent, lhs)


def chip_kernel(kept, part, own, sent):
    size, width = own.shape
    own[...] = kept[:size, :] + part[:size, :].astype(jnp.float32)
    total = kept[size:, :] + part[size:, :].astype(jnp.float32)
    extra = total[:, width - 128 :]
    lane = lax.broadcasted_iota(jnp.int32, extra.shape, 1)
    high, low = split_high(extra + pltpu.roll(extra, 127, 1))
    sent[:, : width - 128] = total[:, : width - 128].astype(sent.dtype)
    sent[:, width - 128 :] = jnp.where(
        lax.rem(lane, 2) == 0, high, pltpu.roll(low, 1, 1)
    ).astype(sent.dtype)


def hidden_kernel(*refs):
    late, early, (hidden, first_weight) = refs[:2], refs[2:4], refs[4:]
    width = hidden.shape[1]
    half = hidden.shape[0] // 2

    def total(parts, columns):
        result = parts[0][:, columns]
        for part in parts[1:]:
            result = result + part[:, columns].astype(jnp.float32)
        return result

    def inverse_rms(columns, index):
        square = columns[:, index : index + 1] + columns[:, index + 1 : index + 2]
        return 1.0 / jnp.sqrt(square / D + 1e-06)

    for index, parts in ((1, late), (0, early)):
        extra = total(parts, slice(2 * width, 2 * width + 128))
        row_inv = inverse_rms(extra, 0)
        gate = total(parts, slice(0, width)) * row_inv
        up = total(parts, slice(width, 2 * width)) * row_inv
        hidden[index * half : (index + 1) * half, :] = (
            gate / (1.0 + jnp.exp(-gate)) * up
        ).astype(jnp.bfloat16)
    for index in range(first_weight.shape[0] // half):
        place = 2 + 4 * index
        logit = extra[:, place + 2 : place + 3] + extra[:, place + 3 : place + 4]
        weight = 1.0 / (1.0 + jnp.exp(-logit * inverse_rms(extra, place)))
        first_weight[index * half : (index + 1) * half, :] = jnp.broadcast_to(weight, (half, 128))


def down_kernel(slot_dev, own, part1, part2, part3, w_down, computed, lhs):
    quarter, width = own.shape
    block = computed.shape[1]
    place_tp = lax.axis_index("tp")
    place_req = lax.axis_index("req")
    masks = slot_masks(quarter, slot_dev)
    for shift, part in enumerate((own, part1, part2, part3)):
        rows = part[...].astype(jnp.float32)
        place = pl.ds(pl.multiple_of((place_tp ^ shift) * quarter, quarter), quarter)
        for index, mask in enumerate(masks):
            lhs[place, index * width : (index + 1) * width] = jnp.where(mask, rows, 0.0).astype(
                jnp.bfloat16
            )
    product = jnp.dot(lhs[...], w_down[...], preferred_element_type=jnp.float32)
    for index in range(computed.shape[0]):
        computed[place_req ^ index] = product[index * block : (index + 1) * block].astype(
            computed.dtype
        )


def combine_kernel(returned, pick0, pick1, first_weight, attended, layer_out):
    rows = returned[...]
    out0 = jnp.dot(pick0[...], rows, preferred_element_type=jnp.float32)
    out1 = jnp.dot(pick1[...], rows, preferred_element_type=jnp.float32)
    weight = first_weight[:, 0:1]
    moe = weight * out0 + (1.0 - weight) * out1
    layer_out[...] = (attended[...].astype(jnp.float32) + moe).astype(jnp.bfloat16)


def shards(
    resid,
    queries,
    new_keys,
    new_values,
    k_cache,
    v_cache,
    lengths,
    w_out,
    norm_gain,
    w_router,
    routes,
    w_gate,
    w_up,
    w_down,
):
    row_count, width = resid.shape
    slot_dev, _, hidden = w_gate.shape
    cache_len, lanes = k_cache.shape[1:]
    packed_count = EXPERTS * CAP
    quarter = packed_count // lax.axis_size("tp")
    if not (
        lax.axis_size("tp") == 4
        and lax.axis_size("req") == 8
        and 8 * slot_dev == EXPERTS
        and row_count == quarter
        and cache_len == lanes == 2 * HEAD_DIM
        and queries.shape[1] == 6 * HEAD_DIM
    ):
        return shards_general(
            resid, queries, new_keys, new_values, k_cache, v_cache, lengths, w_out,
            norm_gain, w_router, routes, w_gate, w_up, w_down,
        )
    bf16, f32 = jnp.bfloat16, jnp.float32
    gain = norm_gain.reshape(1, width)
    own, *sents = call(
        attend_kernel,
        [((row_count, width), f32)] + [((row_count, width), bf16)] * 3,
        [spec(pl.ANY)] * 7,
        [
            pltpu.with_memory_space_constraint(operand, pltpu.HBM)
            for operand in (lengths, queries, new_keys, new_values, k_cache, v_cache, w_out)
        ],
        scratch=[
            pltpu.SMEM(lengths.shape, jnp.int32),
            pltpu.VMEM(queries.shape, bf16),
            pltpu.VMEM(new_keys.shape, bf16),
            pltpu.VMEM(new_values.shape, bf16),
            pltpu.VMEM(k_cache.shape, bf16),
            pltpu.VMEM(v_cache.shape, bf16),
            pltpu.VMEM(w_out.shape, bf16),
            pltpu.VMEM((8 * row_count, lanes), f32),
            pltpu.VMEM((8 * row_count, lanes), f32),
            pltpu.VMEM((row_count, w_out.shape[1]), f32),
            pltpu.SemaphoreType.DMA((4,)),
            pltpu.SemaphoreType.DMA((12,)),
        ],
        mebibytes=16,
        flops=200_000_000,
        moved=3_400_000,
    )
    def sum_exchange(sents):
        return [partner_permute(block, "tp", k) for k, block in zip(FAR_FIRST[1:], sents)]

    parts = sum_exchange(sents)
    weight = (slot_dev * width, hidden)
    base, pick_rows, pick0, pick1, router_rows, *weights = call(
        functools.partial(ready_kernel, slot_dev),
        [
            ((row_count, width), f32),
            ((packed_count, row_count), bf16),
            ((row_count, packed_count), bf16),
            ((row_count, packed_count), bf16),
            ((row_count, width), f32),
            (weight, bf16),
            (weight, bf16),
        ],
        [spec()] * 4 + [spec(pl.ANY)] * 2,
        (
            own,
            resid,
            routes.T,
            w_router.T,
            pltpu.with_memory_space_constraint(w_gate.reshape(weight), pltpu.HBM),
            pltpu.with_memory_space_constraint(w_up.reshape(weight), pltpu.HBM),
        ),
        scratch=[pltpu.SemaphoreType.DMA((8,))],
        mebibytes=12,
        moved=3_300_000,
    )
    attended, home, *sents = call(
        pack_kernel,
        [((row_count, width), bf16)] + [((quarter, width), bf16)] * 4,
        [spec()] * 5,
        (base, *parts, pick_rows),
    )
    (stats,) = call(
        stats_kernel, [((row_count, 128), f32)], [spec()] * 3, (attended, gain, router_rows)
    )
    (result,) = call(result_kernel, [((row_count, width), bf16)], [spec()], (attended,))
    stats, result = lax.optimization_barrier((stats, result))
    hops = {
        k: partner_permute(block, "req", 2 * k) for k, block in zip(FAR_FIRST[1:], sents)
    }
    parts = [hops[k] for k in (1, 2, 3)]
    (along,) = call(
        turn_kernel, [((2 * quarter, width), bf16)], [spec()] * 4, (home, *parts)
    )
    along = partner_permute(along, "req", 1)
    half = quarter // 2
    message = (half, 2 * hidden + 128)
    lhs = pltpu.VMEM((packed_count // 2, slot_dev * width), bf16)

    def chip_sums(kept, sent):
        own, sent = call(
            chip_kernel, [(message, f32), (message, bf16)], [spec()] * 2,
            (kept, partner_permute(sent, "tp", 1)),
        )
        return own, partner_permute(sent, "tp", 2)

    pair = (quarter, message[1])
    early = call(
        functools.partial(early_kernel, slot_dev),
        [(pair, f32), (pair, bf16)],
        [spec()] * 8,
        (home, *parts, gain, stats, *weights),
        scratch=[pltpu.VMEM((2 * quarter, width), bf16), lhs],
        flops=400_000_000,
        moved=3_500_000,
    )
    late = call(
        functools.partial(late_kernel, slot_dev),
        [(pair, f32), (pair, bf16)],
        [spec()] * 4,
        (along, gain, *weights),
        scratch=[lhs],
        flops=400_000_000,
        moved=3_500_000,
    )
    early = chip_sums(*early)
    late = chip_sums(*late)
    own, first_weight = call(
        hidden_kernel,
        [((quarter, hidden), bf16), ((row_count, 128), f32)],
        [spec()] * 4,
        (*late, *early),
    )
    across = partner_permute(own, "tp", 2)
    parts = [partner_permute(own, "tp", 1), across, partner_permute(across, "tp", 1)]
    (computed,) = call(
        functools.partial(down_kernel, slot_dev),
        [((8, packed_count // 8, width), bf16)],
        [spec()] * 5,
        (own, *parts, w_down.reshape(slot_dev * hidden, width)),
        scratch=[pltpu.VMEM((packed_count, slot_dev * hidden), bf16)],
        flops=200_000_000,
        moved=2_000_000,
    )
    returned = lax.all_to_all(computed, "req", split_axis=0, concat_axis=0, tiled=True)
    (layer_out,) = call(
        combine_kernel,
        [((row_count, width), bf16)],
        [spec()] * 5,
        (returned.reshape(packed_count, width), pick0, pick1, first_weight, attended),
    )
    return (result, layer_out)


def solution(mesh):
    placed = (
        P("req", "tp"),
        P("req", "tp"),
        P("req", "tp"),
        P("req", "tp"),
        P("req", None, "tp"),
        P("req", None, "tp"),
        P("req"),
        P("tp", None),
        P("tp"),
        P("tp", None),
        P("req", None),
        P("req", "tp", None),
        P("req", "tp", None),
        P("req", None, "tp"),
    )
    return jax.shard_map(
        shards,
        mesh=mesh,
        in_specs=placed,
        out_specs=(P("req", "tp"), P("req", "tp")),
        check_vma=False,
    )
```

```python
import functools
import math

import jax
import jax.numpy as jnp
from jax import lax
from jax.experimental import pallas as pl
from jax.experimental.pallas import tpu as pltpu
from jax.sharding import PartitionSpec as P

D = 1536
HEAD_DIM = 64
EXPERTS = 16
TOP = 2
CAP = 8


def attend_local(queries, new_keys, new_values, k_cache, v_cache, lengths):
    row_count = queries.shape[0]
    kv_local = new_keys.shape[1] // HEAD_DIM
    group_size = queries.shape[1] // HEAD_DIM // kv_local
    cache_len = k_cache.shape[1]
    score_scale = 1.0 / math.sqrt(HEAD_DIM)
    query = queries.reshape(row_count, kv_local, group_size, HEAD_DIM)
    keys_all = k_cache.reshape(row_count, cache_len, kv_local, HEAD_DIM)
    values_all = v_cache.reshape(row_count, cache_len, kv_local, HEAD_DIM)
    scores = (
        jnp.einsum("bgqd,blgd->bgql", query, keys_all, preferred_element_type=jnp.float32)
        * score_scale
    )
    self_score = (
        jnp.einsum(
            "bgqd,bgd->bgq",
            query,
            new_keys.reshape(row_count, kv_local, HEAD_DIM),
            preferred_element_type=jnp.float32,
        )
        * score_scale
    )
    valid_mask = (jnp.arange(cache_len, dtype=jnp.int32)[None, :] < lengths[:, None])[
        :, None, None, :
    ]
    peak_score = jnp.maximum(jnp.max(jnp.where(valid_mask, scores, -1e30), axis=-1), self_score)
    exp_terms = jnp.where(valid_mask, jnp.exp(scores - peak_score[..., None]), 0.0)
    self_exp = jnp.exp(self_score - peak_score)
    denom_sum = jnp.sum(exp_terms, axis=-1) + self_exp
    weights = (exp_terms / denom_sum[..., None]).astype(jnp.bfloat16)
    self_weight = (self_exp / denom_sum).astype(jnp.bfloat16)
    value_self = new_values.astype(jnp.float32).reshape(row_count, kv_local, 1, HEAD_DIM)
    mixed = (
        jnp.einsum("bgql,blgd->bgqd", weights, values_all, preferred_element_type=jnp.float32)
        + self_weight.astype(jnp.float32)[..., None] * value_self
    )
    return mixed.astype(jnp.bfloat16).reshape(row_count, kv_local * group_size * HEAD_DIM)


def shards_general(
    resid,
    queries,
    new_keys,
    new_values,
    k_cache,
    v_cache,
    lengths,
    w_out,
    norm_gain,
    w_router,
    routes,
    w_gate,
    w_up,
    w_down,
):
    req_dev = resid.shape[0]
    width_local = resid.shape[1]
    slot_dev = w_gate.shape[0]
    req_count = lax.axis_size("req")
    shard_count = max(1, req_count // EXPERTS)
    attention = attend_local(queries, new_keys, new_values, k_cache, v_cache, lengths)
    partial_value = jnp.dot(attention, w_out, preferred_element_type=jnp.float32)
    projected = lax.psum_scatter(partial_value, "tp", scatter_dimension=1, tiled=True)
    attended = (resid.astype(jnp.float32) + projected).astype(jnp.bfloat16)
    attended_f = attended.astype(jnp.float32)
    scaled = attended_f * norm_gain[None, :]
    square_sum, logit_part = lax.psum(
        (
            jnp.sum(attended_f * attended_f, axis=1),
            jnp.dot(scaled, w_router, precision=lax.Precision.HIGHEST),
        ),
        "tp",
    )
    inv_rms = 1.0 / jnp.sqrt(square_sum / D + 1e-06)
    normed = (scaled * inv_rms[:, None]).astype(jnp.bfloat16)
    logits = logit_part * inv_rms[:, None]
    expert_ids = jnp.arange(EXPERTS, dtype=jnp.int32)
    first_logit = jnp.sum(jnp.where(routes[:, 0:1] == expert_ids[None, :], logits, 0.0), axis=1)
    second_logit = jnp.sum(jnp.where(routes[:, 1:2] == expert_ids[None, :], logits, 0.0), axis=1)
    first_weight = jax.nn.sigmoid(first_logit - second_logit)
    second_weight = 1.0 - first_weight
    flat_routes = routes.reshape(req_dev * TOP)
    one_hot = (flat_routes[None, :] == expert_ids[:, None]).astype(jnp.int32)
    rank_in = jnp.cumsum(one_hot, axis=1) - one_hot
    slot_ids = jnp.arange(CAP, dtype=jnp.int32)
    chosen = (one_hot[:, None, :] == 1) & (rank_in[:, None, :] == slot_ids[None, :, None])
    token_pick = jnp.sum(
        chosen.reshape(EXPERTS, CAP, req_dev, TOP).astype(jnp.int32), axis=-1
    ).astype(jnp.bfloat16)
    per_expert = jnp.einsum(
        "ecb,bd->ecd", token_pick, normed, preferred_element_type=jnp.float32
    ).astype(jnp.bfloat16)
    outgoing = jnp.broadcast_to(
        per_expert[:, None], (EXPERTS, shard_count, CAP, width_local)
    ).reshape(req_count, slot_dev, CAP, width_local)
    incoming = lax.all_to_all(outgoing, "req", split_axis=0, concat_axis=0, tiled=True)
    gate_pre = jnp.einsum("nscd,sdf->nscf", incoming, w_gate, preferred_element_type=jnp.float32)
    up_pre = jnp.einsum("nscd,sdf->nscf", incoming, w_up, preferred_element_type=jnp.float32)
    gate_sum, up_sum = lax.psum((gate_pre, up_pre), "tp")
    hidden = (jax.nn.silu(gate_sum) * up_sum).astype(jnp.bfloat16)
    computed = jnp.einsum("nscf,sfd->nscd", hidden, w_down, preferred_element_type=jnp.float32)
    returned = lax.all_to_all(computed, "req", split_axis=0, concat_axis=0, tiled=True)
    combined = jnp.sum(returned.reshape(EXPERTS, shard_count, CAP, width_local), axis=1)
    route_out = jnp.einsum(
        "ecr,ecd->rd", chosen.astype(jnp.float32), combined, precision=lax.Precision.HIGHEST
    ).reshape(req_dev, TOP, width_local)
    moe = first_weight[:, None] * route_out[:, 0] + second_weight[:, None] * route_out[:, 1]
    layer_out = (attended_f + moe).astype(jnp.bfloat16)
    return (attended, layer_out)


FAR_FIRST = (0, 2, 3, 1)


def spec(space=pltpu.VMEM):
    return pl.BlockSpec(memory_space=space)


def call(kernel, outs, ins, operands, scratch=(), mebibytes=8, flops=100_000, moved=100_000):
    return pl.pallas_call(
        kernel,
        out_shape=[jax.ShapeDtypeStruct(shape, dtype) for shape, dtype in outs],
        in_specs=ins,
        out_specs=[spec() for _ in outs],
        scratch_shapes=scratch,
        compiler_params=pltpu.CompilerParams(vmem_limit_bytes=mebibytes << 20),
        cost_estimate=pl.CostEstimate(flops=flops, bytes_accessed=moved, transcendentals=0),
    )(*operands)


def partner_permute(block, axis, distance):
    count = lax.axis_size(axis)
    return lax.ppermute(block, axis, [(i, i ^ distance) for i in range(count)])


def attend_kernel(
    lengths_hbm, queries_hbm, keys_hbm, values_hbm, k_hbm, v_hbm, w_hbm, own, sent1, sent2, sent3,
    lengths, queries, new_keys, new_values, k_buf, v_buf, w_buf,
    query_s, self_s, score_s, weight_s, product_s, small_sems, sems,
):
    row_count = queries.shape[0]
    width = own.shape[1]
    lanes = 2 * HEAD_DIM
    cache_len = k_hbm.shape[1]
    chunks = 4
    small = [
        pltpu.make_async_copy(source, target, small_sems.at[index])
        for index, (source, target) in enumerate(
            (
                (queries_hbm, queries),
                (keys_hbm, new_keys),
                (values_hbm, new_values),
                (lengths_hbm, lengths),
            )
        )
    ]
    copies = []
    for source, target in ((k_hbm, k_buf), (v_hbm, v_buf), (w_hbm, w_buf)):
        size = source.shape[0] // chunks
        for chunk in range(chunks):
            part = pl.ds(chunk * size, size)
            copies.append(
                pltpu.make_async_copy(source.at[part], target.at[part], sems.at[len(copies)])
            )
    for copy in small + copies:
        copy.start()
    per_chunk = row_count // chunks

    for copy in small:
        copy.wait()

    low = lax.broadcasted_iota(jnp.int32, (row_count, lanes), 1) < HEAD_DIM
    tiles = [queries[:, i * lanes : (i + 1) * lanes].astype(jnp.float32) for i in range(3)]
    heads = [
        jnp.where(low, tiles[0], 0.0),
        jnp.where(low, pltpu.roll(tiles[0], HEAD_DIM, 1), 0.0),
        jnp.where(low, tiles[1], 0.0),
        jnp.where(low, 0.0, tiles[1]),
        jnp.where(low, 0.0, pltpu.roll(tiles[2], HEAD_DIM, 1)),
        jnp.where(low, 0.0, tiles[2]),
    ]
    scale = 1.0 / math.sqrt(HEAD_DIM)
    for head in range(8):
        rows = pl.ds(head, row_count, stride=8)
        query_s[rows, :] = heads[head] if head < 6 else jnp.zeros((row_count, lanes), jnp.float32)

    row_of = lax.broadcasted_iota(jnp.int32, (8 * row_count, row_count), 0)
    request_of = lax.broadcasted_iota(jnp.int32, (8 * row_count, row_count), 1)
    spread = jnp.where(row_of // 8 == request_of, 1.0, 0.0).astype(jnp.bfloat16)
    keys_new = jnp.dot(spread, new_keys[...], preferred_element_type=jnp.float32)
    values_new = jnp.dot(spread, new_values[...], preferred_element_type=jnp.float32)
    own_score = jnp.sum(query_s[...] * keys_new, axis=1, keepdims=True) * scale

    upper = lax.broadcasted_iota(jnp.int32, (16, lanes), 0) < 8
    position = lax.broadcasted_iota(jnp.int32, (16, cache_len), 1)
    for pair in range(row_count // 2):
        if pair % (per_chunk // 2) == 0:
            copies[pair // (per_chunk // 2)].wait()
        pair_rows = slice(16 * pair, 16 * pair + 16)
        keys = k_buf[2 * pair : 2 * pair + 2].reshape(2 * cache_len, lanes)
        raw = lax.dot_general(
            query_s[pair_rows, :].astype(jnp.bfloat16), keys, (((1,), (1,)), ((), ())),
            preferred_element_type=jnp.float32,
        )
        limit = jnp.where(upper, lengths[2 * pair], lengths[2 * pair + 1])
        score_s[pair_rows, :] = jnp.where(
            position < limit,
            jnp.where(upper, raw[:, :cache_len], raw[:, cache_len:]) * scale,
            -1e30,
        )

    scores = score_s[...]
    peak = jnp.maximum(jnp.max(scores, axis=1, keepdims=True), own_score)
    terms = jnp.exp(scores - peak)
    own_term = jnp.exp(own_score - peak)
    inverse = 1.0 / (jnp.sum(terms, axis=1, keepdims=True) + own_term)
    weight_s[...] = (terms * inverse).astype(jnp.bfloat16)
    own_weight = (own_term * inverse).astype(jnp.bfloat16).astype(jnp.float32)
    self_s[...] = own_weight * values_new
    for pair in range(row_count // 2):
        if pair % (per_chunk // 2) == 0:
            copies[chunks + pair // (per_chunk // 2)].wait()
        pair_rows = slice(16 * pair, 16 * pair + 16)
        values = jnp.concatenate([v_buf[2 * pair], v_buf[2 * pair + 1]], axis=1)
        mixed = jnp.dot(weight_s[pair_rows, :], values, preferred_element_type=jnp.float32)
        query_s[pair_rows, :] = (
            jnp.where(upper, mixed[:, :lanes], mixed[:, lanes:]) + self_s[pair_rows, :]
        )

    mixed = [query_s[pl.ds(head, row_count, stride=8), :] for head in range(6)]
    attention = jnp.concatenate(
        [
            jnp.where(low, mixed[0], pltpu.roll(mixed[1], HEAD_DIM, 1)),
            jnp.where(low, mixed[2], mixed[3]),
            jnp.where(low, pltpu.roll(mixed[4], HEAD_DIM, 1), mixed[5]),
        ],
        axis=1,
    ).astype(jnp.bfloat16)
    for copy in copies[2 * chunks :]:
        copy.wait()
    place_tp = lax.axis_index("tp")
    product_s[...] = jnp.dot(attention, w_buf[...], preferred_element_type=jnp.float32)
    for shift, out in zip(FAR_FIRST, (own, sent1, sent2, sent3)):
        columns = pl.ds(pl.multiple_of((place_tp ^ shift) * width, width), width)
        out[...] = product_s[:, columns].astype(out.dtype)


def ready_kernel(
    slot_dev, own, resid, routes, w_router, gate_hbm, up_hbm,
    base, pick_rows, pick0, pick1, router_rows, w_gate, w_up, sems,
):
    copies = []
    for source, target in ((gate_hbm, w_gate), (up_hbm, w_up)):
        size = source.shape[0] // 4
        for chunk in range(4):
            part = pl.ds(chunk * size, size)
            copies.append(
                pltpu.make_async_copy(source.at[part], target.at[part], sems.at[len(copies)])
            )
    for copy in copies:
        copy.start()
    base[...] = own[...] + resid[...].astype(jnp.float32)
    packed_count, row_count = pick_rows.shape

    route0, route1 = routes[0:1, :], routes[1:2, :]
    place = lax.broadcasted_iota(jnp.int32, (packed_count, row_count), 0)
    named0 = jnp.where(place == route0, 1.0, 0.0)
    named1 = jnp.where(place == route1, 1.0, 0.0)
    row_of = lax.broadcasted_iota(jnp.int32, (row_count, row_count), 0)
    col_of = lax.broadcasted_iota(jnp.int32, (row_count, row_count), 1)
    earlier = jnp.where(row_of < col_of, 1.0, 0.0).astype(jnp.bfloat16)
    before = jnp.dot(
        (named0 + named1).astype(jnp.bfloat16), earlier, preferred_element_type=jnp.float32
    )
    place_req = lax.axis_index("req")

    def pick(route, named, mine):
        rank = jnp.sum(named * before, axis=0, keepdims=True).astype(jnp.int32)
        block = ((route // slot_dev) ^ mine) * slot_dev + lax.rem(route, slot_dev)
        return jnp.where(place == block * CAP + rank, 1.0, 0.0)

    sent_rows = pick(route0, named0, place_req) + pick(route1, named1, place_req)
    pick_rows[...] = sent_rows.astype(jnp.bfloat16)
    pick0[...] = jnp.transpose(pick(route0, named0, 0)).astype(jnp.bfloat16)
    pick1[...] = jnp.transpose(pick(route1, named1, 0)).astype(jnp.bfloat16)
    signed = jnp.transpose(named0 - named1)
    router_rows[...] = jnp.dot(
        signed[:, :EXPERTS], w_router[...],
        precision=lax.Precision.HIGHEST, preferred_element_type=jnp.float32,
    )
    for copy in copies:
        copy.wait()


def pack_kernel(base, part1, part2, part3, pick_rows, attended, home, sent1, sent2, sent3):
    total = base[...]
    for part in (part1, part2, part3):
        total = total + part[...].astype(jnp.float32)
    rows = total.astype(jnp.bfloat16)
    attended[...] = rows
    packed = jnp.dot(pick_rows[...], rows, preferred_element_type=jnp.float32)
    size = home.shape[0]
    for distance, out in zip(FAR_FIRST, (home, sent1, sent2, sent3)):
        out[...] = packed[distance * size : (distance + 1) * size].astype(out.dtype)


def result_kernel(attended, result):
    result[...] = attended[...]


def stats_kernel(attended, gain, router_rows, stats):
    rows = attended[...].astype(jnp.float32)
    square = jnp.sum(rows * rows, axis=1, keepdims=True)
    logit = jnp.sum(rows * gain[...] * router_rows[...], axis=1, keepdims=True)
    lane = lax.broadcasted_iota(jnp.int32, stats.shape, 1)
    stats[...] = jnp.where(lane == 0, square, jnp.where(lane == 1, logit, 0.0))


def turn_kernel(home, part1, part2, part3, along):
    half = home.shape[0] // 2
    for index, part in zip(FAR_FIRST, (home, part1, part2, part3)):
        along[index * half : (index + 1) * half, :] = part[half:, :]


def slot_masks(row_count, slot_dev):
    slot = lax.rem(lax.broadcasted_iota(jnp.int32, (row_count, 1), 0) // CAP, slot_dev)
    return [slot == index for index in range(slot_dev)]


def split_high(column):
    high = column.astype(jnp.bfloat16).astype(jnp.float32)
    return high, column - high


def gate_terms(slot_dev, blocks, gain, stats, w_gate, w_up, kept, sent, lhs):
    size = kept.shape[0] // 2
    width = blocks.shape[1]
    hidden = w_gate.shape[1]
    place_tp = lax.axis_index("tp")
    masks = slot_masks(size, slot_dev)
    lane = lax.broadcasted_iota(jnp.int32, (size, 128), 1)
    for order, shift in enumerate((0, 2, 1, 3)):
        out, first_row = (kept, sent)[order // 2], order % 2 * size
        rows = blocks[
            pl.ds(pl.multiple_of((place_tp ^ shift) * size, size), size), :
        ].astype(jnp.float32)
        columns = [jnp.sum(rows * rows, axis=1, keepdims=True)]
        if stats is not None:
            for first in range(0, stats.shape[0], size):
                columns += [stats[first : first + size, 0:1], stats[first : first + size, 1:2]]
        extra = jnp.zeros((size, 128), jnp.float32)
        for index, column in enumerate(columns):
            high, low = split_high(column)
            extra = jnp.where(lane == 2 * index, high, extra)
            extra = jnp.where(lane == 2 * index + 1, low, extra)
        out[first_row : first_row + size, 2 * hidden :] = extra.astype(out.dtype)
        scaled = rows * gain[...]
        for index, mask in enumerate(masks):
            lhs[order * size : (order + 1) * size, index * width : (index + 1) * width] = (
                jnp.where(mask, scaled, 0.0).astype(jnp.bfloat16)
            )
    left = lhs[...]
    for first, weight in ((0, w_gate), (hidden, w_up)):
        product = jnp.dot(left, weight[...], preferred_element_type=jnp.float32)
        kept[:, first : first + hidden] = product[: 2 * size]
        sent[:, first : first + hidden] = product[2 * size :].astype(sent.dtype)


def early_kernel(
    slot_dev, in0, in1, in2, in3, gain, stats, w_gate, w_up, turned, kept, sent, blocks, lhs
):
    del turned
    half = kept.shape[0] // 2
    for index, part in zip(FAR_FIRST, (in0, in1, in2, in3)):
        blocks[index * half : (index + 1) * half, :] = part[:half, :]
    gate_terms(slot_dev, blocks, gain, stats, w_gate, w_up, kept, sent, lhs)


def late_kernel(slot_dev, blocks, gain, w_gate, w_up, kept, sent, lhs):
    gate_terms(slot_dev, blocks, gain, None, w_gate, w_up, kept, sent, lhs)


def chip_kernel(kept, part, own, sent):
    size, width = own.shape[0] // 2, own.shape[1]
    total = kept[...] + part[...].astype(jnp.float32)
    own[...] = total
    extra = total[:, width - 128 :]
    lane = lax.broadcasted_iota(jnp.int32, extra.shape, 1)
    high, low = split_high(extra + pltpu.roll(extra, 127, 1))
    extra = jnp.where(lax.rem(lane, 2) == 0, high, pltpu.roll(low, 1, 1))
    for target, source in ((0, size), (size, 0)):
        sent[target : target + size, : width - 128] = total[
            source : source + size, : width - 128
        ].astype(sent.dtype)
        sent[target : target + size, width - 128 :] = extra[source : source + size].astype(
            sent.dtype
        )


def hidden_kernel(*refs):
    late, early, (hidden, first_weight) = refs[:2], refs[2:4], refs[4:]
    width = hidden.shape[1]
    half = hidden.shape[0] // 4

    def total(parts, columns):
        result = parts[0][:, columns]
        for part in parts[1:]:
            result = result + part[:, columns].astype(jnp.float32)
        return result

    def inverse_rms(columns, index):
        square = columns[:, index : index + 1] + columns[:, index + 1 : index + 2]
        return 1.0 / jnp.sqrt(square / D + 1e-06)

    for index, parts in ((1, late), (0, early)):
        extra = total(parts, slice(2 * width, 2 * width + 128))
        row_inv = inverse_rms(extra, 0)
        gate = total(parts, slice(0, width)) * row_inv
        up = total(parts, slice(width, 2 * width)) * row_inv
        rows = (gate / (1.0 + jnp.exp(-gate)) * up).astype(jnp.bfloat16)
        for block in range(2):
            start = (2 * block + index) * half
            hidden[start : start + half, :] = rows[block * half : (block + 1) * half]
    extra = extra[:half]
    for index in range(first_weight.shape[0] // half):
        place = 2 + 4 * index
        logit = extra[:, place + 2 : place + 3] + extra[:, place + 3 : place + 4]
        weight = 1.0 / (1.0 + jnp.exp(-logit * inverse_rms(extra, place)))
        first_weight[index * half : (index + 1) * half, :] = jnp.broadcast_to(weight, (half, 128))


def down_kernel(slot_dev, own, part, w_down, computed, lhs):
    quarter, width = own.shape[0] // 2, own.shape[1]
    block = computed.shape[1]
    place_tp = lax.axis_index("tp")
    place_req = lax.axis_index("req")
    masks = slot_masks(quarter, slot_dev)
    for shift in range(4):
        first = shift // 2 * quarter
        rows = (own, part)[shift % 2][first : first + quarter, :].astype(jnp.float32)
        place = pl.ds(pl.multiple_of((place_tp ^ shift) * quarter, quarter), quarter)
        for index, mask in enumerate(masks):
            lhs[place, index * width : (index + 1) * width] = jnp.where(mask, rows, 0.0).astype(
                jnp.bfloat16
            )
    product = jnp.dot(lhs[...], w_down[...], preferred_element_type=jnp.float32)
    for index in range(computed.shape[0]):
        computed[place_req ^ index] = product[index * block : (index + 1) * block].astype(
            computed.dtype
        )


def combine_kernel(returned, pick0, pick1, first_weight, attended, layer_out):
    rows = returned[...]
    out0 = jnp.dot(pick0[...], rows, preferred_element_type=jnp.float32)
    out1 = jnp.dot(pick1[...], rows, preferred_element_type=jnp.float32)
    weight = first_weight[:, 0:1]
    moe = weight * out0 + (1.0 - weight) * out1
    layer_out[...] = (attended[...].astype(jnp.float32) + moe).astype(jnp.bfloat16)


def shards(
    resid,
    queries,
    new_keys,
    new_values,
    k_cache,
    v_cache,
    lengths,
    w_out,
    norm_gain,
    w_router,
    routes,
    w_gate,
    w_up,
    w_down,
):
    row_count, width = resid.shape
    slot_dev, _, hidden = w_gate.shape
    cache_len, lanes = k_cache.shape[1:]
    packed_count = EXPERTS * CAP
    quarter = packed_count // lax.axis_size("tp")
    if not (
        lax.axis_size("tp") == 4
        and lax.axis_size("req") == 8
        and 8 * slot_dev == EXPERTS
        and row_count == quarter
        and cache_len == lanes == 2 * HEAD_DIM
        and queries.shape[1] == 6 * HEAD_DIM
    ):
        return shards_general(
            resid, queries, new_keys, new_values, k_cache, v_cache, lengths, w_out,
            norm_gain, w_router, routes, w_gate, w_up, w_down,
        )
    bf16, f32 = jnp.bfloat16, jnp.float32
    gain = norm_gain.reshape(1, width)
    own, *sents = call(
        attend_kernel,
        [((row_count, width), f32)] + [((row_count, width), bf16)] * 3,
        [spec(pl.ANY)] * 7,
        [
            pltpu.with_memory_space_constraint(operand, pltpu.HBM)
            for operand in (lengths, queries, new_keys, new_values, k_cache, v_cache, w_out)
        ],
        scratch=[
            pltpu.SMEM(lengths.shape, jnp.int32),
            pltpu.VMEM(queries.shape, bf16),
            pltpu.VMEM(new_keys.shape, bf16),
            pltpu.VMEM(new_values.shape, bf16),
            pltpu.VMEM(k_cache.shape, bf16),
            pltpu.VMEM(v_cache.shape, bf16),
            pltpu.VMEM(w_out.shape, bf16),
            pltpu.VMEM((8 * row_count, lanes), f32),
            pltpu.VMEM((8 * row_count, lanes), f32),
            pltpu.VMEM((8 * row_count, cache_len), f32),
            pltpu.VMEM((8 * row_count, cache_len), bf16),
            pltpu.VMEM((row_count, w_out.shape[1]), f32),
            pltpu.SemaphoreType.DMA((4,)),
            pltpu.SemaphoreType.DMA((12,)),
        ],
        mebibytes=16,
        flops=200_000_000,
        moved=3_400_000,
    )
    def sum_exchange(sents):
        return [partner_permute(block, "tp", k) for k, block in zip(FAR_FIRST[1:], sents)]

    parts = sum_exchange(sents)
    weight = (slot_dev * width, hidden)
    base, pick_rows, pick0, pick1, router_rows, *weights = call(
        functools.partial(ready_kernel, slot_dev),
        [
            ((row_count, width), f32),
            ((packed_count, row_count), bf16),
            ((row_count, packed_count), bf16),
            ((row_count, packed_count), bf16),
            ((row_count, width), f32),
            (weight, bf16),
            (weight, bf16),
        ],
        [spec()] * 4 + [spec(pl.ANY)] * 2,
        (
            own,
            resid,
            routes.T,
            w_router.T,
            pltpu.with_memory_space_constraint(w_gate.reshape(weight), pltpu.HBM),
            pltpu.with_memory_space_constraint(w_up.reshape(weight), pltpu.HBM),
        ),
        scratch=[pltpu.SemaphoreType.DMA((8,))],
        mebibytes=12,
        moved=3_300_000,
    )
    attended, home, *sents = call(
        pack_kernel,
        [((row_count, width), bf16)] + [((quarter, width), bf16)] * 4,
        [spec()] * 5,
        (base, *parts, pick_rows),
    )
    (stats,) = call(
        stats_kernel, [((row_count, 128), f32)], [spec()] * 3, (attended, gain, router_rows)
    )
    (result,) = call(result_kernel, [((row_count, width), bf16)], [spec()], (attended,))
    stats, result = lax.optimization_barrier((stats, result))
    parts = [
        partner_permute(block, "req", 2 * k) for k, block in zip(FAR_FIRST[1:], sents)
    ]
    (turned,) = call(
        turn_kernel, [((2 * quarter, width), bf16)], [spec()] * 4, (home, *parts)
    )
    along = partner_permute(turned, "req", 1)
    lhs = pltpu.VMEM((packed_count // 2, slot_dev * width), bf16)

    pair = (quarter, 2 * hidden + 128)

    def chip_sums(kept, sent):
        return call(
            chip_kernel, [(pair, f32), (pair, bf16)], [spec()] * 2,
            (kept, partner_permute(sent, "tp", 1)),
        )

    kept, sent = call(
        functools.partial(early_kernel, slot_dev),
        [(pair, f32), (pair, bf16)],
        [spec()] * 9,
        (home, *parts, gain, stats, *weights, turned),
        scratch=[pltpu.VMEM((2 * quarter, width), bf16), lhs],
        flops=400_000_000,
        moved=3_500_000,
    )
    early, sent = chip_sums(kept, sent)
    early = (early, partner_permute(sent, "tp", 2))
    kept, sent = call(
        functools.partial(late_kernel, slot_dev),
        [(pair, f32), (pair, bf16)],
        [spec()] * 4,
        (along, gain, *weights),
        scratch=[lhs],
        flops=400_000_000,
        moved=3_500_000,
    )
    late, sent = chip_sums(kept, sent)
    late = (late, partner_permute(sent, "tp", 2))
    own, first_weight = call(
        hidden_kernel,
        [((2 * quarter, hidden), bf16), ((row_count, 128), f32)],
        [spec()] * 4,
        (*late, *early),
    )
    (computed,) = call(
        functools.partial(down_kernel, slot_dev),
        [((8, packed_count // 8, width), bf16)],
        [spec()] * 3,
        (own, partner_permute(own, "tp", 1), w_down.reshape(slot_dev * hidden, width)),
        scratch=[pltpu.VMEM((packed_count, slot_dev * hidden), bf16)],
        flops=200_000_000,
        moved=2_000_000,
    )
    returned = lax.all_to_all(computed, "req", split_axis=0, concat_axis=0, tiled=True)
    (layer_out,) = call(
        combine_kernel,
        [((row_count, width), bf16)],
        [spec()] * 5,
        (returned.reshape(packed_count, width), pick0, pick1, first_weight, attended),
    )
    return (result, layer_out)


def solution(mesh):
    placed = (
        P("req", "tp"),
        P("req", "tp"),
        P("req", "tp"),
        P("req", "tp"),
        P("req", None, "tp"),
        P("req", None, "tp"),
        P("req"),
        P("tp", None),
        P("tp"),
        P("tp", None),
        P("req", None),
        P("req", "tp", None),
        P("req", "tp", None),
        P("req", None, "tp"),
    )
    return jax.shard_map(
        shards,
        mesh=mesh,
        in_specs=placed,
        out_specs=(P("req", "tp"), P("req", "tp")),
        check_vma=False,
    )
```

```python
import functools
import math

import jax
import jax.numpy as jnp
from jax import lax
from jax.experimental import pallas as pl
from jax.experimental.pallas import tpu as pltpu
from jax.sharding import PartitionSpec as P

D = 1536
HEAD_DIM = 64
EXPERTS = 16
TOP = 2
CAP = 8


def attend_local(queries, new_keys, new_values, k_cache, v_cache, lengths):
    row_count = queries.shape[0]
    kv_local = new_keys.shape[1] // HEAD_DIM
    group_size = queries.shape[1] // HEAD_DIM // kv_local
    cache_len = k_cache.shape[1]
    score_scale = 1.0 / math.sqrt(HEAD_DIM)
    query = queries.reshape(row_count, kv_local, group_size, HEAD_DIM)
    keys_all = k_cache.reshape(row_count, cache_len, kv_local, HEAD_DIM)
    values_all = v_cache.reshape(row_count, cache_len, kv_local, HEAD_DIM)
    scores = (
        jnp.einsum("bgqd,blgd->bgql", query, keys_all, preferred_element_type=jnp.float32)
        * score_scale
    )
    self_score = (
        jnp.einsum(
            "bgqd,bgd->bgq",
            query,
            new_keys.reshape(row_count, kv_local, HEAD_DIM),
            preferred_element_type=jnp.float32,
        )
        * score_scale
    )
    valid_mask = (jnp.arange(cache_len, dtype=jnp.int32)[None, :] < lengths[:, None])[
        :, None, None, :
    ]
    peak_score = jnp.maximum(jnp.max(jnp.where(valid_mask, scores, -1e30), axis=-1), self_score)
    exp_terms = jnp.where(valid_mask, jnp.exp(scores - peak_score[..., None]), 0.0)
    self_exp = jnp.exp(self_score - peak_score)
    denom_sum = jnp.sum(exp_terms, axis=-1) + self_exp
    weights = (exp_terms / denom_sum[..., None]).astype(jnp.bfloat16)
    self_weight = (self_exp / denom_sum).astype(jnp.bfloat16)
    value_self = new_values.astype(jnp.float32).reshape(row_count, kv_local, 1, HEAD_DIM)
    mixed = (
        jnp.einsum("bgql,blgd->bgqd", weights, values_all, preferred_element_type=jnp.float32)
        + self_weight.astype(jnp.float32)[..., None] * value_self
    )
    return mixed.astype(jnp.bfloat16).reshape(row_count, kv_local * group_size * HEAD_DIM)


def shards_general(
    resid,
    queries,
    new_keys,
    new_values,
    k_cache,
    v_cache,
    lengths,
    w_out,
    norm_gain,
    w_router,
    routes,
    w_gate,
    w_up,
    w_down,
):
    req_dev = resid.shape[0]
    width_local = resid.shape[1]
    slot_dev = w_gate.shape[0]
    req_count = lax.axis_size("req")
    shard_count = max(1, req_count // EXPERTS)
    attention = attend_local(queries, new_keys, new_values, k_cache, v_cache, lengths)
    partial_value = jnp.dot(attention, w_out, preferred_element_type=jnp.float32)
    projected = lax.psum_scatter(partial_value, "tp", scatter_dimension=1, tiled=True)
    attended = (resid.astype(jnp.float32) + projected).astype(jnp.bfloat16)
    attended_f = attended.astype(jnp.float32)
    scaled = attended_f * norm_gain[None, :]
    square_sum, logit_part = lax.psum(
        (
            jnp.sum(attended_f * attended_f, axis=1),
            jnp.dot(scaled, w_router, precision=lax.Precision.HIGHEST),
        ),
        "tp",
    )
    inv_rms = 1.0 / jnp.sqrt(square_sum / D + 1e-06)
    normed = (scaled * inv_rms[:, None]).astype(jnp.bfloat16)
    logits = logit_part * inv_rms[:, None]
    expert_ids = jnp.arange(EXPERTS, dtype=jnp.int32)
    first_logit = jnp.sum(jnp.where(routes[:, 0:1] == expert_ids[None, :], logits, 0.0), axis=1)
    second_logit = jnp.sum(jnp.where(routes[:, 1:2] == expert_ids[None, :], logits, 0.0), axis=1)
    first_weight = jax.nn.sigmoid(first_logit - second_logit)
    second_weight = 1.0 - first_weight
    flat_routes = routes.reshape(req_dev * TOP)
    one_hot = (flat_routes[None, :] == expert_ids[:, None]).astype(jnp.int32)
    rank_in = jnp.cumsum(one_hot, axis=1) - one_hot
    slot_ids = jnp.arange(CAP, dtype=jnp.int32)
    chosen = (one_hot[:, None, :] == 1) & (rank_in[:, None, :] == slot_ids[None, :, None])
    token_pick = jnp.sum(
        chosen.reshape(EXPERTS, CAP, req_dev, TOP).astype(jnp.int32), axis=-1
    ).astype(jnp.bfloat16)
    per_expert = jnp.einsum(
        "ecb,bd->ecd", token_pick, normed, preferred_element_type=jnp.float32
    ).astype(jnp.bfloat16)
    outgoing = jnp.broadcast_to(
        per_expert[:, None], (EXPERTS, shard_count, CAP, width_local)
    ).reshape(req_count, slot_dev, CAP, width_local)
    incoming = lax.all_to_all(outgoing, "req", split_axis=0, concat_axis=0, tiled=True)
    gate_pre = jnp.einsum("nscd,sdf->nscf", incoming, w_gate, preferred_element_type=jnp.float32)
    up_pre = jnp.einsum("nscd,sdf->nscf", incoming, w_up, preferred_element_type=jnp.float32)
    gate_sum, up_sum = lax.psum((gate_pre, up_pre), "tp")
    hidden = (jax.nn.silu(gate_sum) * up_sum).astype(jnp.bfloat16)
    computed = jnp.einsum("nscf,sfd->nscd", hidden, w_down, preferred_element_type=jnp.float32)
    returned = lax.all_to_all(computed, "req", split_axis=0, concat_axis=0, tiled=True)
    combined = jnp.sum(returned.reshape(EXPERTS, shard_count, CAP, width_local), axis=1)
    route_out = jnp.einsum(
        "ecr,ecd->rd", chosen.astype(jnp.float32), combined, precision=lax.Precision.HIGHEST
    ).reshape(req_dev, TOP, width_local)
    moe = first_weight[:, None] * route_out[:, 0] + second_weight[:, None] * route_out[:, 1]
    layer_out = (attended_f + moe).astype(jnp.bfloat16)
    return (attended, layer_out)


FAR_FIRST = (0, 2, 3, 1)


def spec(space=pltpu.VMEM):
    return pl.BlockSpec(memory_space=space)


def call(kernel, outs, ins, operands, scratch=(), mebibytes=8, flops=100_000, moved=100_000):
    return pl.pallas_call(
        kernel,
        out_shape=[jax.ShapeDtypeStruct(shape, dtype) for shape, dtype in outs],
        in_specs=ins,
        out_specs=[spec() for _ in outs],
        scratch_shapes=scratch,
        compiler_params=pltpu.CompilerParams(vmem_limit_bytes=mebibytes << 20),
        cost_estimate=pl.CostEstimate(flops=flops, bytes_accessed=moved, transcendentals=0),
    )(*operands)


def partner_permute(block, axis, distance):
    count = lax.axis_size(axis)
    return lax.ppermute(block, axis, [(i, i ^ distance) for i in range(count)])


def attend_kernel(
    lengths_hbm, queries_hbm, keys_hbm, values_hbm, k_hbm, v_hbm, w_hbm, own, sent1, sent2, sent3,
    lengths, queries, new_keys, new_values, k_buf, v_buf, w_buf,
    query_s, self_s, score_s, weight_s, product_s, small_sems, sems,
):
    row_count = queries.shape[0]
    width = own.shape[1]
    lanes = 2 * HEAD_DIM
    cache_len = k_hbm.shape[1]
    chunks = 2
    small = [
        pltpu.make_async_copy(source, target, small_sems.at[index])
        for index, (source, target) in enumerate(
            (
                (queries_hbm, queries),
                (keys_hbm, new_keys),
                (values_hbm, new_values),
                (lengths_hbm, lengths),
            )
        )
    ]
    copies = []
    for source, target in ((k_hbm, k_buf), (v_hbm, v_buf), (w_hbm, w_buf)):
        size = source.shape[0] // chunks
        for chunk in range(chunks):
            part = pl.ds(chunk * size, size)
            copies.append(
                pltpu.make_async_copy(source.at[part], target.at[part], sems.at[len(copies)])
            )
    for copy in small + copies:
        copy.start()

    for copy in small:
        copy.wait()

    low = lax.broadcasted_iota(jnp.int32, (row_count, lanes), 1) < HEAD_DIM
    tiles = [queries[:, i * lanes : (i + 1) * lanes].astype(jnp.float32) for i in range(3)]
    heads = [
        jnp.where(low, tiles[0], 0.0),
        jnp.where(low, pltpu.roll(tiles[0], HEAD_DIM, 1), 0.0),
        jnp.where(low, tiles[1], 0.0),
        jnp.where(low, 0.0, tiles[1]),
        jnp.where(low, 0.0, pltpu.roll(tiles[2], HEAD_DIM, 1)),
        jnp.where(low, 0.0, tiles[2]),
    ]
    scale = 1.0 / math.sqrt(HEAD_DIM)
    for head in range(8):
        rows = pl.ds(head, row_count, stride=8)
        query_s[rows, :] = heads[head] if head < 6 else jnp.zeros((row_count, lanes), jnp.float32)

    row_of = lax.broadcasted_iota(jnp.int32, (8 * row_count, row_count), 0)
    request_of = lax.broadcasted_iota(jnp.int32, (8 * row_count, row_count), 1)
    spread = jnp.where(row_of // 8 == request_of, 1.0, 0.0).astype(jnp.bfloat16)
    keys_new = jnp.dot(spread, new_keys[...], preferred_element_type=jnp.float32)
    values_new = jnp.dot(spread, new_values[...], preferred_element_type=jnp.float32)
    own_score = jnp.sum(query_s[...] * keys_new, axis=1, keepdims=True) * scale

    upper = lax.broadcasted_iota(jnp.int32, (16, lanes), 0) < 8
    position = lax.broadcasted_iota(jnp.int32, (16, cache_len), 1)
    for copy in copies[:chunks]:
        copy.wait()
    for pair in range(row_count // 2):
        pair_rows = slice(16 * pair, 16 * pair + 16)
        keys = k_buf[2 * pair : 2 * pair + 2].reshape(2 * cache_len, lanes)
        raw = lax.dot_general(
            query_s[pair_rows, :].astype(jnp.bfloat16), keys, (((1,), (1,)), ((), ())),
            preferred_element_type=jnp.float32,
        )
        limit = jnp.where(upper, lengths[2 * pair], lengths[2 * pair + 1])
        score_s[pair_rows, :] = jnp.where(
            position < limit,
            jnp.where(upper, raw[:, :cache_len], raw[:, cache_len:]) * scale,
            -1e30,
        )

    scores = score_s[...]
    peak = jnp.maximum(jnp.max(scores, axis=1, keepdims=True), own_score)
    terms = jnp.exp(scores - peak)
    own_term = jnp.exp(own_score - peak)
    inverse = 1.0 / (jnp.sum(terms, axis=1, keepdims=True) + own_term)
    weight_s[...] = (terms * inverse).astype(jnp.bfloat16)
    own_weight = (own_term * inverse).astype(jnp.bfloat16).astype(jnp.float32)
    self_s[...] = own_weight * values_new
    for copy in copies[chunks : 2 * chunks]:
        copy.wait()
    for pair in range(row_count // 2):
        pair_rows = slice(16 * pair, 16 * pair + 16)
        values = jnp.concatenate([v_buf[2 * pair], v_buf[2 * pair + 1]], axis=1)
        mixed = jnp.dot(weight_s[pair_rows, :], values, preferred_element_type=jnp.float32)
        query_s[pair_rows, :] = (
            jnp.where(upper, mixed[:, :lanes], mixed[:, lanes:]) + self_s[pair_rows, :]
        )

    mixed = [query_s[pl.ds(head, row_count, stride=8), :] for head in range(6)]
    attention = jnp.concatenate(
        [
            jnp.where(low, mixed[0], pltpu.roll(mixed[1], HEAD_DIM, 1)),
            jnp.where(low, mixed[2], mixed[3]),
            jnp.where(low, pltpu.roll(mixed[4], HEAD_DIM, 1), mixed[5]),
        ],
        axis=1,
    ).astype(jnp.bfloat16)
    for copy in copies[2 * chunks :]:
        copy.wait()
    place_tp = lax.axis_index("tp")
    product_s[...] = jnp.dot(attention, w_buf[...], preferred_element_type=jnp.float32)
    for shift, out in zip(FAR_FIRST, (own, sent1, sent2, sent3)):
        columns = pl.ds(pl.multiple_of((place_tp ^ shift) * width, width), width)
        out[...] = product_s[:, columns].astype(out.dtype)


def ready_kernel(
    slot_dev, own, resid, routes, w_router, gate_hbm, up_hbm,
    base, pick_rows, pick0, pick1, router_rows, w_gate, w_up, sems,
):
    copies = []
    for source, target in ((gate_hbm, w_gate), (up_hbm, w_up)):
        size = source.shape[0] // 4
        for chunk in range(4):
            part = pl.ds(chunk * size, size)
            copies.append(
                pltpu.make_async_copy(source.at[part], target.at[part], sems.at[len(copies)])
            )
    for copy in copies:
        copy.start()
    base[...] = own[...] + resid[...].astype(jnp.float32)
    packed_count, row_count = pick_rows.shape

    route0, route1 = routes[0:1, :], routes[1:2, :]
    place = lax.broadcasted_iota(jnp.int32, (packed_count, row_count), 0)
    named0 = jnp.where(place == route0, 1.0, 0.0)
    named1 = jnp.where(place == route1, 1.0, 0.0)
    row_of = lax.broadcasted_iota(jnp.int32, (row_count, row_count), 0)
    col_of = lax.broadcasted_iota(jnp.int32, (row_count, row_count), 1)
    earlier = jnp.where(row_of < col_of, 1.0, 0.0).astype(jnp.bfloat16)
    before = jnp.dot(
        (named0 + named1).astype(jnp.bfloat16), earlier, preferred_element_type=jnp.float32
    )
    place_req = lax.axis_index("req")

    def pick(route, named, mine):
        rank = jnp.sum(named * before, axis=0, keepdims=True).astype(jnp.int32)
        block = ((route // slot_dev) ^ mine) * slot_dev + lax.rem(route, slot_dev)
        return jnp.where(place == block * CAP + rank, 1.0, 0.0)

    sent_rows = pick(route0, named0, place_req) + pick(route1, named1, place_req)
    pick_rows[...] = sent_rows.astype(jnp.bfloat16)
    pick0[...] = jnp.transpose(pick(route0, named0, 0)).astype(jnp.bfloat16)
    pick1[...] = jnp.transpose(pick(route1, named1, 0)).astype(jnp.bfloat16)
    signed = jnp.transpose(named0 - named1)
    router_rows[...] = jnp.dot(
        signed[:, :EXPERTS], w_router[...],
        precision=lax.Precision.HIGHEST, preferred_element_type=jnp.float32,
    )
    for copy in copies:
        copy.wait()


def pack_kernel(base, part1, part2, part3, pick_rows, attended, home, sent1, sent2, sent3):
    total = base[...]
    for part in (part1, part2, part3):
        total = total + part[...].astype(jnp.float32)
    rows = total.astype(jnp.bfloat16)
    attended[...] = rows
    packed = jnp.dot(pick_rows[...], rows, preferred_element_type=jnp.float32)
    size = home.shape[0]
    for distance, out in zip(FAR_FIRST, (home, sent1, sent2, sent3)):
        out[...] = packed[distance * size : (distance + 1) * size].astype(out.dtype)


def result_kernel(attended, result):
    result[...] = attended[...]


def stats_kernel(attended, gain, router_rows, stats):
    rows = attended[...].astype(jnp.float32)
    square = jnp.sum(rows * rows, axis=1, keepdims=True)
    logit = jnp.sum(rows * gain[...] * router_rows[...], axis=1, keepdims=True)
    lane = lax.broadcasted_iota(jnp.int32, stats.shape, 1)
    stats[...] = jnp.where(lane == 0, square, jnp.where(lane == 1, logit, 0.0))


def turn_kernel(home, part1, part2, part3, along):
    half = home.shape[0] // 2
    for index, part in zip(FAR_FIRST, (home, part1, part2, part3)):
        along[index * half : (index + 1) * half, :] = part[half:, :]


def slot_masks(row_count, slot_dev):
    slot = lax.rem(lax.broadcasted_iota(jnp.int32, (row_count, 1), 0) // CAP, slot_dev)
    return [slot == index for index in range(slot_dev)]


def split_high(column):
    high = column.astype(jnp.bfloat16).astype(jnp.float32)
    return high, column - high


def gate_terms(slot_dev, blocks, gain, stats, w_gate, w_up, kept, sent, lhs):
    size = kept.shape[0] // 2
    width = blocks.shape[1]
    hidden = w_gate.shape[1]
    place_tp = lax.axis_index("tp")
    masks = slot_masks(size, slot_dev)
    lane = lax.broadcasted_iota(jnp.int32, (size, 128), 1)
    for order, shift in enumerate((0, 2, 1, 3)):
        out, first_row = (kept, sent)[order // 2], order % 2 * size
        rows = blocks[
            pl.ds(pl.multiple_of((place_tp ^ shift) * size, size), size), :
        ].astype(jnp.float32)
        columns = [jnp.sum(rows * rows, axis=1, keepdims=True)]
        if stats is not None:
            for first in range(0, stats.shape[0], size):
                columns += [stats[first : first + size, 0:1], stats[first : first + size, 1:2]]
        extra = jnp.zeros((size, 128), jnp.float32)
        for index, column in enumerate(columns):
            high, low = split_high(column)
            extra = jnp.where(lane == 2 * index, high, extra)
            extra = jnp.where(lane == 2 * index + 1, low, extra)
        out[first_row : first_row + size, 2 * hidden :] = extra.astype(out.dtype)
        scaled = rows * gain[...]
        for index, mask in enumerate(masks):
            lhs[order * size : (order + 1) * size, index * width : (index + 1) * width] = (
                jnp.where(mask, scaled, 0.0).astype(jnp.bfloat16)
            )
    left = lhs[...]
    for first, weight in ((0, w_gate), (hidden, w_up)):
        product = jnp.dot(left, weight[...], preferred_element_type=jnp.float32)
        kept[:, first : first + hidden] = product[: 2 * size]
        sent[:, first : first + hidden] = product[2 * size :].astype(sent.dtype)


def early_kernel(
    slot_dev, in0, in1, in2, in3, gain, stats, w_gate, w_up, turned, kept, sent, blocks, lhs
):
    del turned
    half = kept.shape[0] // 2
    for index, part in zip(FAR_FIRST, (in0, in1, in2, in3)):
        blocks[index * half : (index + 1) * half, :] = part[:half, :]
    gate_terms(slot_dev, blocks, gain, stats, w_gate, w_up, kept, sent, lhs)


def late_kernel(slot_dev, blocks, gain, w_gate, w_up, kept, sent, lhs):
    gate_terms(slot_dev, blocks, gain, None, w_gate, w_up, kept, sent, lhs)


def chip_kernel(kept, part, own, sent):
    size, width = own.shape[0] // 2, own.shape[1]
    total = kept[...] + part[...].astype(jnp.float32)
    own[...] = total
    extra = total[:, width - 128 :]
    lane = lax.broadcasted_iota(jnp.int32, extra.shape, 1)
    high, low = split_high(extra + pltpu.roll(extra, 127, 1))
    extra = jnp.where(lax.rem(lane, 2) == 0, high, pltpu.roll(low, 1, 1))
    for target, source in ((0, size), (size, 0)):
        sent[target : target + size, : width - 128] = total[
            source : source + size, : width - 128
        ].astype(sent.dtype)
        sent[target : target + size, width - 128 :] = extra[source : source + size].astype(
            sent.dtype
        )


def hidden_kernel(*refs):
    late, early, (hidden, first_weight) = refs[:2], refs[2:4], refs[4:]
    width = hidden.shape[1]
    half = hidden.shape[0] // 4

    def total(parts, columns):
        result = parts[0][:, columns]
        for part in parts[1:]:
            result = result + part[:, columns].astype(jnp.float32)
        return result

    def inverse_rms(columns, index):
        square = columns[:, index : index + 1] + columns[:, index + 1 : index + 2]
        return 1.0 / jnp.sqrt(square / D + 1e-06)

    for index, parts in ((1, late), (0, early)):
        extra = total(parts, slice(2 * width, 2 * width + 128))
        row_inv = inverse_rms(extra, 0)
        gate = total(parts, slice(0, width)) * row_inv
        up = total(parts, slice(width, 2 * width)) * row_inv
        rows = (gate / (1.0 + jnp.exp(-gate)) * up).astype(jnp.bfloat16)
        for block in range(2):
            start = (2 * block + index) * half
            hidden[start : start + half, :] = rows[block * half : (block + 1) * half]
    extra = extra[:half]
    for index in range(first_weight.shape[0] // half):
        place = 2 + 4 * index
        logit = extra[:, place + 2 : place + 3] + extra[:, place + 3 : place + 4]
        weight = 1.0 / (1.0 + jnp.exp(-logit * inverse_rms(extra, place)))
        first_weight[index * half : (index + 1) * half, :] = jnp.broadcast_to(weight, (half, 128))


def down_kernel(slot_dev, own, part, w_down, computed, lhs):
    quarter, width = own.shape[0] // 2, own.shape[1]
    block = computed.shape[1]
    place_tp = lax.axis_index("tp")
    place_req = lax.axis_index("req")
    masks = slot_masks(quarter, slot_dev)
    for shift in range(4):
        first = shift // 2 * quarter
        rows = (own, part)[shift % 2][first : first + quarter, :].astype(jnp.float32)
        place = pl.ds(pl.multiple_of((place_tp ^ shift) * quarter, quarter), quarter)
        for index, mask in enumerate(masks):
            lhs[place, index * width : (index + 1) * width] = jnp.where(mask, rows, 0.0).astype(
                jnp.bfloat16
            )
    product = jnp.dot(lhs[...], w_down[...], preferred_element_type=jnp.float32)
    for index in range(computed.shape[0]):
        computed[place_req ^ index] = product[index * block : (index + 1) * block].astype(
            computed.dtype
        )


def combine_kernel(returned, pick0, pick1, first_weight, attended, layer_out):
    rows = returned[...]
    out0 = jnp.dot(pick0[...], rows, preferred_element_type=jnp.float32)
    out1 = jnp.dot(pick1[...], rows, preferred_element_type=jnp.float32)
    weight = first_weight[:, 0:1]
    moe = weight * out0 + (1.0 - weight) * out1
    layer_out[...] = (attended[...].astype(jnp.float32) + moe).astype(jnp.bfloat16)


def shards(
    resid,
    queries,
    new_keys,
    new_values,
    k_cache,
    v_cache,
    lengths,
    w_out,
    norm_gain,
    w_router,
    routes,
    w_gate,
    w_up,
    w_down,
):
    row_count, width = resid.shape
    slot_dev, _, hidden = w_gate.shape
    cache_len, lanes = k_cache.shape[1:]
    packed_count = EXPERTS * CAP
    quarter = packed_count // lax.axis_size("tp")
    if not (
        lax.axis_size("tp") == 4
        and lax.axis_size("req") == 8
        and 8 * slot_dev == EXPERTS
        and row_count == quarter
        and cache_len == lanes == 2 * HEAD_DIM
        and queries.shape[1] == 6 * HEAD_DIM
    ):
        return shards_general(
            resid, queries, new_keys, new_values, k_cache, v_cache, lengths, w_out,
            norm_gain, w_router, routes, w_gate, w_up, w_down,
        )
    bf16, f32 = jnp.bfloat16, jnp.float32
    gain = norm_gain.reshape(1, width)
    own, *sents = call(
        attend_kernel,
        [((row_count, width), f32)] + [((row_count, width), bf16)] * 3,
        [spec(pl.ANY)] * 7,
        [
            pltpu.with_memory_space_constraint(operand, pltpu.HBM)
            for operand in (lengths, queries, new_keys, new_values, k_cache, v_cache, w_out)
        ],
        scratch=[
            pltpu.SMEM(lengths.shape, jnp.int32),
            pltpu.VMEM(queries.shape, bf16),
            pltpu.VMEM(new_keys.shape, bf16),
            pltpu.VMEM(new_values.shape, bf16),
            pltpu.VMEM(k_cache.shape, bf16),
            pltpu.VMEM(v_cache.shape, bf16),
            pltpu.VMEM(w_out.shape, bf16),
            pltpu.VMEM((8 * row_count, lanes), f32),
            pltpu.VMEM((8 * row_count, lanes), f32),
            pltpu.VMEM((8 * row_count, cache_len), f32),
            pltpu.VMEM((8 * row_count, cache_len), bf16),
            pltpu.VMEM((row_count, w_out.shape[1]), f32),
            pltpu.SemaphoreType.DMA((4,)),
            pltpu.SemaphoreType.DMA((6,)),
        ],
        mebibytes=16,
        flops=200_000_000,
        moved=3_400_000,
    )
    def sum_exchange(sents):
        return [partner_permute(block, "tp", k) for k, block in zip(FAR_FIRST[1:], sents)]

    parts = sum_exchange(sents)
    weight = (slot_dev * width, hidden)
    base, pick_rows, pick0, pick1, router_rows, *weights = call(
        functools.partial(ready_kernel, slot_dev),
        [
            ((row_count, width), f32),
            ((packed_count, row_count), bf16),
            ((row_count, packed_count), bf16),
            ((row_count, packed_count), bf16),
            ((row_count, width), f32),
            (weight, bf16),
            (weight, bf16),
        ],
        [spec()] * 4 + [spec(pl.ANY)] * 2,
        (
            own,
            resid,
            routes.T,
            w_router.T,
            pltpu.with_memory_space_constraint(w_gate.reshape(weight), pltpu.HBM),
            pltpu.with_memory_space_constraint(w_up.reshape(weight), pltpu.HBM),
        ),
        scratch=[pltpu.SemaphoreType.DMA((8,))],
        mebibytes=12,
        moved=3_300_000,
    )
    attended, home, *sents = call(
        pack_kernel,
        [((row_count, width), bf16)] + [((quarter, width), bf16)] * 4,
        [spec()] * 5,
        (base, *parts, pick_rows),
    )
    (stats,) = call(
        stats_kernel, [((row_count, 128), f32)], [spec()] * 3, (attended, gain, router_rows)
    )
    (result,) = call(result_kernel, [((row_count, width), bf16)], [spec()], (attended,))
    stats, result = lax.optimization_barrier((stats, result))
    parts = [
        partner_permute(block, "req", 2 * k) for k, block in zip(FAR_FIRST[1:], sents)
    ]
    (turned,) = call(
        turn_kernel, [((2 * quarter, width), bf16)], [spec()] * 4, (home, *parts)
    )
    along = partner_permute(turned, "req", 1)
    lhs = pltpu.VMEM((packed_count // 2, slot_dev * width), bf16)

    pair = (quarter, 2 * hidden + 128)

    def chip_sums(kept, sent):
        return call(
            chip_kernel, [(pair, f32), (pair, bf16)], [spec()] * 2,
            (kept, partner_permute(sent, "tp", 1)),
        )

    kept, sent = call(
        functools.partial(early_kernel, slot_dev),
        [(pair, f32), (pair, bf16)],
        [spec()] * 9,
        (home, *parts, gain, stats, *weights, turned),
        scratch=[pltpu.VMEM((2 * quarter, width), bf16), lhs],
        flops=400_000_000,
        moved=3_500_000,
    )
    early, sent = chip_sums(kept, sent)
    early = (early, partner_permute(sent, "tp", 2))
    kept, sent = call(
        functools.partial(late_kernel, slot_dev),
        [(pair, f32), (pair, bf16)],
        [spec()] * 4,
        (along, gain, *weights),
        scratch=[lhs],
        flops=400_000_000,
        moved=3_500_000,
    )
    late, sent = chip_sums(kept, sent)
    late = (late, partner_permute(sent, "tp", 2))
    own, first_weight = call(
        hidden_kernel,
        [((2 * quarter, hidden), bf16), ((row_count, 128), f32)],
        [spec()] * 4,
        (*late, *early),
    )
    (computed,) = call(
        functools.partial(down_kernel, slot_dev),
        [((8, packed_count // 8, width), bf16)],
        [spec()] * 3,
        (own, partner_permute(own, "tp", 1), w_down.reshape(slot_dev * hidden, width)),
        scratch=[pltpu.VMEM((packed_count, slot_dev * hidden), bf16)],
        flops=200_000_000,
        moved=2_000_000,
    )
    returned = lax.all_to_all(computed, "req", split_axis=0, concat_axis=0, tiled=True)
    (layer_out,) = call(
        combine_kernel,
        [((row_count, width), bf16)],
        [spec()] * 5,
        (returned.reshape(packed_count, width), pick0, pick1, first_weight, attended),
    )
    return (result, layer_out)


def solution(mesh):
    placed = (
        P("req", "tp"),
        P("req", "tp"),
        P("req", "tp"),
        P("req", "tp"),
        P("req", None, "tp"),
        P("req", None, "tp"),
        P("req"),
        P("tp", None),
        P("tp"),
        P("tp", None),
        P("req", None),
        P("req", "tp", None),
        P("req", "tp", None),
        P("req", None, "tp"),
    )
    return jax.shard_map(
        shards,
        mesh=mesh,
        in_specs=placed,
        out_specs=(P("req", "tp"), P("req", "tp")),
        check_vma=False,
    )
```

```python
import functools
import math

import jax
import jax.numpy as jnp
from jax import lax
from jax.experimental import pallas as pl
from jax.experimental.pallas import tpu as pltpu
from jax.sharding import PartitionSpec as P

D = 1536
HEAD_DIM = 64
EXPERTS = 16
TOP = 2
CAP = 8


def attend_local(queries, new_keys, new_values, k_cache, v_cache, lengths):
    row_count = queries.shape[0]
    kv_local = new_keys.shape[1] // HEAD_DIM
    group_size = queries.shape[1] // HEAD_DIM // kv_local
    cache_len = k_cache.shape[1]
    score_scale = 1.0 / math.sqrt(HEAD_DIM)
    query = queries.reshape(row_count, kv_local, group_size, HEAD_DIM)
    keys_all = k_cache.reshape(row_count, cache_len, kv_local, HEAD_DIM)
    values_all = v_cache.reshape(row_count, cache_len, kv_local, HEAD_DIM)
    scores = (
        jnp.einsum("bgqd,blgd->bgql", query, keys_all, preferred_element_type=jnp.float32)
        * score_scale
    )
    self_score = (
        jnp.einsum(
            "bgqd,bgd->bgq",
            query,
            new_keys.reshape(row_count, kv_local, HEAD_DIM),
            preferred_element_type=jnp.float32,
        )
        * score_scale
    )
    valid_mask = (jnp.arange(cache_len, dtype=jnp.int32)[None, :] < lengths[:, None])[
        :, None, None, :
    ]
    peak_score = jnp.maximum(jnp.max(jnp.where(valid_mask, scores, -1e30), axis=-1), self_score)
    exp_terms = jnp.where(valid_mask, jnp.exp(scores - peak_score[..., None]), 0.0)
    self_exp = jnp.exp(self_score - peak_score)
    denom_sum = jnp.sum(exp_terms, axis=-1) + self_exp
    weights = (exp_terms / denom_sum[..., None]).astype(jnp.bfloat16)
    self_weight = (self_exp / denom_sum).astype(jnp.bfloat16)
    value_self = new_values.astype(jnp.float32).reshape(row_count, kv_local, 1, HEAD_DIM)
    mixed = (
        jnp.einsum("bgql,blgd->bgqd", weights, values_all, preferred_element_type=jnp.float32)
        + self_weight.astype(jnp.float32)[..., None] * value_self
    )
    return mixed.astype(jnp.bfloat16).reshape(row_count, kv_local * group_size * HEAD_DIM)


def shards_general(
    resid,
    queries,
    new_keys,
    new_values,
    k_cache,
    v_cache,
    lengths,
    w_out,
    norm_gain,
    w_router,
    routes,
    w_gate,
    w_up,
    w_down,
):
    req_dev = resid.shape[0]
    width_local = resid.shape[1]
    slot_dev = w_gate.shape[0]
    req_count = lax.axis_size("req")
    shard_count = max(1, req_count // EXPERTS)
    attention = attend_local(queries, new_keys, new_values, k_cache, v_cache, lengths)
    partial_value = jnp.dot(attention, w_out, preferred_element_type=jnp.float32)
    projected = lax.psum_scatter(partial_value, "tp", scatter_dimension=1, tiled=True)
    attended = (resid.astype(jnp.float32) + projected).astype(jnp.bfloat16)
    attended_f = attended.astype(jnp.float32)
    scaled = attended_f * norm_gain[None, :]
    square_sum, logit_part = lax.psum(
        (
            jnp.sum(attended_f * attended_f, axis=1),
            jnp.dot(scaled, w_router, precision=lax.Precision.HIGHEST),
        ),
        "tp",
    )
    inv_rms = 1.0 / jnp.sqrt(square_sum / D + 1e-06)
    normed = (scaled * inv_rms[:, None]).astype(jnp.bfloat16)
    logits = logit_part * inv_rms[:, None]
    expert_ids = jnp.arange(EXPERTS, dtype=jnp.int32)
    first_logit = jnp.sum(jnp.where(routes[:, 0:1] == expert_ids[None, :], logits, 0.0), axis=1)
    second_logit = jnp.sum(jnp.where(routes[:, 1:2] == expert_ids[None, :], logits, 0.0), axis=1)
    first_weight = jax.nn.sigmoid(first_logit - second_logit)
    second_weight = 1.0 - first_weight
    flat_routes = routes.reshape(req_dev * TOP)
    one_hot = (flat_routes[None, :] == expert_ids[:, None]).astype(jnp.int32)
    rank_in = jnp.cumsum(one_hot, axis=1) - one_hot
    slot_ids = jnp.arange(CAP, dtype=jnp.int32)
    chosen = (one_hot[:, None, :] == 1) & (rank_in[:, None, :] == slot_ids[None, :, None])
    token_pick = jnp.sum(
        chosen.reshape(EXPERTS, CAP, req_dev, TOP).astype(jnp.int32), axis=-1
    ).astype(jnp.bfloat16)
    per_expert = jnp.einsum(
        "ecb,bd->ecd", token_pick, normed, preferred_element_type=jnp.float32
    ).astype(jnp.bfloat16)
    outgoing = jnp.broadcast_to(
        per_expert[:, None], (EXPERTS, shard_count, CAP, width_local)
    ).reshape(req_count, slot_dev, CAP, width_local)
    incoming = lax.all_to_all(outgoing, "req", split_axis=0, concat_axis=0, tiled=True)
    gate_pre = jnp.einsum("nscd,sdf->nscf", incoming, w_gate, preferred_element_type=jnp.float32)
    up_pre = jnp.einsum("nscd,sdf->nscf", incoming, w_up, preferred_element_type=jnp.float32)
    gate_sum, up_sum = lax.psum((gate_pre, up_pre), "tp")
    hidden = (jax.nn.silu(gate_sum) * up_sum).astype(jnp.bfloat16)
    computed = jnp.einsum("nscf,sfd->nscd", hidden, w_down, preferred_element_type=jnp.float32)
    returned = lax.all_to_all(computed, "req", split_axis=0, concat_axis=0, tiled=True)
    combined = jnp.sum(returned.reshape(EXPERTS, shard_count, CAP, width_local), axis=1)
    route_out = jnp.einsum(
        "ecr,ecd->rd", chosen.astype(jnp.float32), combined, precision=lax.Precision.HIGHEST
    ).reshape(req_dev, TOP, width_local)
    moe = first_weight[:, None] * route_out[:, 0] + second_weight[:, None] * route_out[:, 1]
    layer_out = (attended_f + moe).astype(jnp.bfloat16)
    return (attended, layer_out)


FAR_FIRST = (0, 2, 3, 1)


def spec(space=pltpu.VMEM):
    return pl.BlockSpec(memory_space=space)


def call(kernel, outs, ins, operands, scratch=(), mebibytes=8, flops=100_000, moved=100_000):
    return pl.pallas_call(
        kernel,
        out_shape=[jax.ShapeDtypeStruct(shape, dtype) for shape, dtype in outs],
        in_specs=ins,
        out_specs=[spec() for _ in outs],
        scratch_shapes=scratch,
        compiler_params=pltpu.CompilerParams(vmem_limit_bytes=mebibytes << 20),
        cost_estimate=pl.CostEstimate(flops=flops, bytes_accessed=moved, transcendentals=0),
    )(*operands)


def partner_permute(block, axis, distance):
    count = lax.axis_size(axis)
    return lax.ppermute(block, axis, [(i, i ^ distance) for i in range(count)])


def attend_kernel(
    lengths_hbm, queries_hbm, keys_hbm, values_hbm, k_hbm, v_hbm, w_hbm, own, sent1, sent2, sent3,
    lengths, queries, new_keys, new_values, k_buf, v_buf, w_buf,
    query_s, score_s, product_s, small_sems, sems,
):
    row_count = queries.shape[0]
    width = own.shape[1]
    lanes = 2 * HEAD_DIM
    cache_len = k_hbm.shape[1]
    chunks = 2
    small = [
        pltpu.make_async_copy(source, target, small_sems.at[index])
        for index, (source, target) in enumerate(
            (
                (queries_hbm, queries),
                (keys_hbm, new_keys),
                (values_hbm, new_values),
                (lengths_hbm, lengths),
            )
        )
    ]
    copies = []
    for source, target in ((k_hbm, k_buf), (v_hbm, v_buf), (w_hbm, w_buf)):
        size = source.shape[0] // chunks
        for chunk in range(chunks):
            part = pl.ds(chunk * size, size)
            copies.append(
                pltpu.make_async_copy(source.at[part], target.at[part], sems.at[len(copies)])
            )
    for copy in small + copies:
        copy.start()

    for copy in small:
        copy.wait()

    low = lax.broadcasted_iota(jnp.int32, (row_count, lanes), 1) < HEAD_DIM
    tiles = [queries[:, i * lanes : (i + 1) * lanes].astype(jnp.float32) for i in range(3)]
    heads = [
        jnp.where(low, tiles[0], 0.0),
        jnp.where(low, pltpu.roll(tiles[0], HEAD_DIM, 1), 0.0),
        jnp.where(low, tiles[1], 0.0),
        jnp.where(low, 0.0, tiles[1]),
        jnp.where(low, 0.0, pltpu.roll(tiles[2], HEAD_DIM, 1)),
        jnp.where(low, 0.0, tiles[2]),
    ]
    scale = 1.0 / math.sqrt(HEAD_DIM)
    for head in range(8):
        rows = pl.ds(head, row_count, stride=8)
        query_s[rows, :] = heads[head] if head < 6 else jnp.zeros((row_count, lanes), jnp.float32)

    row_of = lax.broadcasted_iota(jnp.int32, (8 * row_count, row_count), 0)
    request_of = lax.broadcasted_iota(jnp.int32, (8 * row_count, row_count), 1)
    spread = jnp.where(row_of // 8 == request_of, 1.0, 0.0).astype(jnp.bfloat16)
    keys_new = jnp.dot(spread, new_keys[...], preferred_element_type=jnp.float32)
    values_new = jnp.dot(spread, new_values[...], preferred_element_type=jnp.float32)
    own_score = jnp.sum(query_s[...] * keys_new, axis=1, keepdims=True) * scale

    upper = lax.broadcasted_iota(jnp.int32, (16, lanes), 0) < 8
    position = lax.broadcasted_iota(jnp.int32, (16, cache_len), 1)
    for copy in copies[:chunks]:
        copy.wait()
    for pair in range(row_count // 2):
        pair_rows = slice(16 * pair, 16 * pair + 16)
        keys = k_buf[2 * pair : 2 * pair + 2].reshape(2 * cache_len, lanes)
        raw = lax.dot_general(
            query_s[pair_rows, :].astype(jnp.bfloat16), keys, (((1,), (1,)), ((), ())),
            preferred_element_type=jnp.float32,
        )
        limit = jnp.where(upper, lengths[2 * pair], lengths[2 * pair + 1])
        score_s[pair_rows, :] = jnp.where(
            position < limit,
            jnp.where(upper, raw[:, :cache_len], raw[:, cache_len:]) * scale,
            -1e30,
        )

    for copy in copies[chunks : 2 * chunks]:
        copy.wait()
    for first in range(0, row_count, 8):
        chunk_rows = slice(8 * first, 8 * first + 64)
        scores = score_s[chunk_rows, :]
        own_rows = own_score[chunk_rows]
        peak = jnp.maximum(jnp.max(scores, axis=1, keepdims=True), own_rows)
        terms = jnp.exp(scores - peak)
        own_term = jnp.exp(own_rows - peak)
        inverse = 1.0 / (jnp.sum(terms, axis=1, keepdims=True) + own_term)
        weights = (terms * inverse).astype(jnp.bfloat16)
        own_weight = (own_term * inverse).astype(jnp.bfloat16).astype(jnp.float32)
        own_part = own_weight * values_new[chunk_rows]
        for index in range(0, 8, 2):
            values = jnp.concatenate([v_buf[first + index], v_buf[first + index + 1]], axis=1)
            rows = slice(8 * index, 8 * index + 16)
            mixed = jnp.dot(weights[rows], values, preferred_element_type=jnp.float32)
            query_s[8 * (first + index) : 8 * (first + index) + 16, :] = (
                jnp.where(upper, mixed[:, :lanes], mixed[:, lanes:]) + own_part[rows]
            )

    mixed = [query_s[pl.ds(head, row_count, stride=8), :] for head in range(6)]
    attention = jnp.concatenate(
        [
            jnp.where(low, mixed[0], pltpu.roll(mixed[1], HEAD_DIM, 1)),
            jnp.where(low, mixed[2], mixed[3]),
            jnp.where(low, pltpu.roll(mixed[4], HEAD_DIM, 1), mixed[5]),
        ],
        axis=1,
    ).astype(jnp.bfloat16)
    for copy in copies[2 * chunks :]:
        copy.wait()
    place_tp = lax.axis_index("tp")
    product_s[...] = jnp.dot(attention, w_buf[...], preferred_element_type=jnp.float32)
    for shift, out in zip(FAR_FIRST, (own, sent1, sent2, sent3)):
        columns = pl.ds(pl.multiple_of((place_tp ^ shift) * width, width), width)
        out[...] = product_s[:, columns].astype(out.dtype)


def ready_kernel(
    slot_dev, own, resid, routes, w_router, gate_hbm, up_hbm,
    base, pick_rows, pick0, pick1, router_rows, w_gate, w_up, sems,
):
    copies = []
    for source, target in ((gate_hbm, w_gate), (up_hbm, w_up)):
        size = source.shape[0] // 4
        for chunk in range(4):
            part = pl.ds(chunk * size, size)
            copies.append(
                pltpu.make_async_copy(source.at[part], target.at[part], sems.at[len(copies)])
            )
    for copy in copies:
        copy.start()
    base[...] = own[...] + resid[...].astype(jnp.float32)
    packed_count, row_count = pick_rows.shape

    route0, route1 = routes[0:1, :], routes[1:2, :]
    place = lax.broadcasted_iota(jnp.int32, (packed_count, row_count), 0)
    named0 = jnp.where(place == route0, 1.0, 0.0)
    named1 = jnp.where(place == route1, 1.0, 0.0)
    row_of = lax.broadcasted_iota(jnp.int32, (row_count, row_count), 0)
    col_of = lax.broadcasted_iota(jnp.int32, (row_count, row_count), 1)
    earlier = jnp.where(row_of < col_of, 1.0, 0.0).astype(jnp.bfloat16)
    before = jnp.dot(
        (named0 + named1).astype(jnp.bfloat16), earlier, preferred_element_type=jnp.float32
    )
    place_req = lax.axis_index("req")

    def pick(route, named, mine):
        rank = jnp.sum(named * before, axis=0, keepdims=True).astype(jnp.int32)
        block = ((route // slot_dev) ^ mine) * slot_dev + lax.rem(route, slot_dev)
        return jnp.where(place == block * CAP + rank, 1.0, 0.0)

    sent_rows = pick(route0, named0, place_req) + pick(route1, named1, place_req)
    pick_rows[...] = sent_rows.astype(jnp.bfloat16)
    pick0[...] = jnp.transpose(pick(route0, named0, 0)).astype(jnp.bfloat16)
    pick1[...] = jnp.transpose(pick(route1, named1, 0)).astype(jnp.bfloat16)
    signed = jnp.transpose(named0 - named1)
    router_rows[...] = jnp.dot(
        signed[:, :EXPERTS], w_router[...],
        precision=lax.Precision.HIGHEST, preferred_element_type=jnp.float32,
    )
    for copy in copies:
        copy.wait()


def pack_kernel(base, part1, part2, part3, pick_rows, attended, home, sent1, sent2, sent3):
    total = base[...]
    for part in (part1, part2, part3):
        total = total + part[...].astype(jnp.float32)
    rows = total.astype(jnp.bfloat16)
    attended[...] = rows
    packed = jnp.dot(pick_rows[...], rows, preferred_element_type=jnp.float32)
    size = home.shape[0]
    for distance, out in zip(FAR_FIRST, (home, sent1, sent2, sent3)):
        out[...] = packed[distance * size : (distance + 1) * size].astype(out.dtype)


def result_kernel(attended, result):
    result[...] = attended[...]


def stats_kernel(attended, gain, router_rows, stats):
    rows = attended[...].astype(jnp.float32)
    square = jnp.sum(rows * rows, axis=1, keepdims=True)
    logit = jnp.sum(rows * gain[...] * router_rows[...], axis=1, keepdims=True)
    lane = lax.broadcasted_iota(jnp.int32, stats.shape, 1)
    stats[...] = jnp.where(lane == 0, square, jnp.where(lane == 1, logit, 0.0))


def turn_kernel(home, part1, part2, part3, along):
    half = home.shape[0] // 2
    for index, part in zip(FAR_FIRST, (home, part1, part2, part3)):
        along[index * half : (index + 1) * half, :] = part[half:, :]


def slot_masks(row_count, slot_dev):
    slot = lax.rem(lax.broadcasted_iota(jnp.int32, (row_count, 1), 0) // CAP, slot_dev)
    return [slot == index for index in range(slot_dev)]


def split_high(column):
    high = column.astype(jnp.bfloat16).astype(jnp.float32)
    return high, column - high


def gate_terms(slot_dev, blocks, gain, stats, w_gate, w_up, kept, sent, lhs):
    size = kept.shape[0] // 2
    width = blocks.shape[1]
    hidden = w_gate.shape[1]
    place_tp = lax.axis_index("tp")
    masks = slot_masks(size, slot_dev)
    lane = lax.broadcasted_iota(jnp.int32, (size, 128), 1)
    for order, shift in enumerate((0, 2, 1, 3)):
        out, first_row = (kept, sent)[order // 2], order % 2 * size
        rows = blocks[
            pl.ds(pl.multiple_of((place_tp ^ shift) * size, size), size), :
        ].astype(jnp.float32)
        columns = [jnp.sum(rows * rows, axis=1, keepdims=True)]
        if stats is not None:
            for first in range(0, stats.shape[0], size):
                columns += [stats[first : first + size, 0:1], stats[first : first + size, 1:2]]
        extra = jnp.zeros((size, 128), jnp.float32)
        for index, column in enumerate(columns):
            high, low = split_high(column)
            extra = jnp.where(lane == 2 * index, high, extra)
            extra = jnp.where(lane == 2 * index + 1, low, extra)
        out[first_row : first_row + size, 2 * hidden :] = extra.astype(out.dtype)
        scaled = rows * gain[...]
        for index, mask in enumerate(masks):
            lhs[order * size : (order + 1) * size, index * width : (index + 1) * width] = (
                jnp.where(mask, scaled, 0.0).astype(jnp.bfloat16)
            )
    left = lhs[...]
    for first, weight in ((0, w_gate), (hidden, w_up)):
        product = jnp.dot(left, weight[...], preferred_element_type=jnp.float32)
        kept[:, first : first + hidden] = product[: 2 * size]
        sent[:, first : first + hidden] = product[2 * size :].astype(sent.dtype)


def early_kernel(
    slot_dev, in0, in1, in2, in3, gain, stats, w_gate, w_up, turned, kept, sent, blocks, lhs
):
    del turned
    half = kept.shape[0] // 2
    for index, part in zip(FAR_FIRST, (in0, in1, in2, in3)):
        blocks[index * half : (index + 1) * half, :] = part[:half, :]
    gate_terms(slot_dev, blocks, gain, stats, w_gate, w_up, kept, sent, lhs)


def late_kernel(slot_dev, blocks, gain, w_gate, w_up, kept, sent, lhs):
    gate_terms(slot_dev, blocks, gain, None, w_gate, w_up, kept, sent, lhs)


def chip_kernel(kept, part, own, sent):
    size, width = own.shape[0] // 2, own.shape[1]
    total = kept[...] + part[...].astype(jnp.float32)
    own[...] = total
    extra = total[:, width - 128 :]
    lane = lax.broadcasted_iota(jnp.int32, extra.shape, 1)
    high, low = split_high(extra + pltpu.roll(extra, 127, 1))
    extra = jnp.where(lax.rem(lane, 2) == 0, high, pltpu.roll(low, 1, 1))
    for target, source in ((0, size), (size, 0)):
        sent[target : target + size, : width - 128] = total[
            source : source + size, : width - 128
        ].astype(sent.dtype)
        sent[target : target + size, width - 128 :] = extra[source : source + size].astype(
            sent.dtype
        )


def hidden_kernel(*refs):
    late, early, (hidden, first_weight) = refs[:2], refs[2:4], refs[4:]
    width = hidden.shape[1]
    half = hidden.shape[0] // 4

    def total(parts, columns):
        result = parts[0][:, columns]
        for part in parts[1:]:
            result = result + part[:, columns].astype(jnp.float32)
        return result

    def inverse_rms(columns, index):
        square = columns[:, index : index + 1] + columns[:, index + 1 : index + 2]
        return 1.0 / jnp.sqrt(square / D + 1e-06)

    for index, parts in ((1, late), (0, early)):
        extra = total(parts, slice(2 * width, 2 * width + 128))
        row_inv = inverse_rms(extra, 0)
        gate = total(parts, slice(0, width)) * row_inv
        up = total(parts, slice(width, 2 * width)) * row_inv
        rows = (gate / (1.0 + jnp.exp(-gate)) * up).astype(jnp.bfloat16)
        for block in range(2):
            start = (2 * block + index) * half
            hidden[start : start + half, :] = rows[block * half : (block + 1) * half]
    extra = extra[:half]
    for index in range(first_weight.shape[0] // half):
        place = 2 + 4 * index
        logit = extra[:, place + 2 : place + 3] + extra[:, place + 3 : place + 4]
        weight = 1.0 / (1.0 + jnp.exp(-logit * inverse_rms(extra, place)))
        first_weight[index * half : (index + 1) * half, :] = jnp.broadcast_to(weight, (half, 128))


def down_kernel(slot_dev, own, part, w_down, computed, lhs):
    quarter, width = own.shape[0] // 2, own.shape[1]
    block = computed.shape[1]
    place_tp = lax.axis_index("tp")
    place_req = lax.axis_index("req")
    masks = slot_masks(quarter, slot_dev)
    for shift in range(4):
        first = shift // 2 * quarter
        rows = (own, part)[shift % 2][first : first + quarter, :].astype(jnp.float32)
        place = pl.ds(pl.multiple_of((place_tp ^ shift) * quarter, quarter), quarter)
        for index, mask in enumerate(masks):
            lhs[place, index * width : (index + 1) * width] = jnp.where(mask, rows, 0.0).astype(
                jnp.bfloat16
            )
    product = jnp.dot(lhs[...], w_down[...], preferred_element_type=jnp.float32)
    for index in range(computed.shape[0]):
        computed[place_req ^ index] = product[index * block : (index + 1) * block].astype(
            computed.dtype
        )


def combine_kernel(returned, pick0, pick1, first_weight, attended, layer_out):
    rows = returned[...]
    out0 = jnp.dot(pick0[...], rows, preferred_element_type=jnp.float32)
    out1 = jnp.dot(pick1[...], rows, preferred_element_type=jnp.float32)
    weight = first_weight[:, 0:1]
    moe = weight * out0 + (1.0 - weight) * out1
    layer_out[...] = (attended[...].astype(jnp.float32) + moe).astype(jnp.bfloat16)


def shards(
    resid,
    queries,
    new_keys,
    new_values,
    k_cache,
    v_cache,
    lengths,
    w_out,
    norm_gain,
    w_router,
    routes,
    w_gate,
    w_up,
    w_down,
):
    row_count, width = resid.shape
    slot_dev, _, hidden = w_gate.shape
    cache_len, lanes = k_cache.shape[1:]
    packed_count = EXPERTS * CAP
    quarter = packed_count // lax.axis_size("tp")
    if not (
        lax.axis_size("tp") == 4
        and lax.axis_size("req") == 8
        and 8 * slot_dev == EXPERTS
        and row_count == quarter
        and cache_len == lanes == 2 * HEAD_DIM
        and queries.shape[1] == 6 * HEAD_DIM
    ):
        return shards_general(
            resid, queries, new_keys, new_values, k_cache, v_cache, lengths, w_out,
            norm_gain, w_router, routes, w_gate, w_up, w_down,
        )
    bf16, f32 = jnp.bfloat16, jnp.float32
    gain = norm_gain.reshape(1, width)
    own, *sents = call(
        attend_kernel,
        [((row_count, width), f32)] + [((row_count, width), bf16)] * 3,
        [spec(pl.ANY)] * 7,
        [
            pltpu.with_memory_space_constraint(operand, pltpu.HBM)
            for operand in (lengths, queries, new_keys, new_values, k_cache, v_cache, w_out)
        ],
        scratch=[
            pltpu.SMEM(lengths.shape, jnp.int32),
            pltpu.VMEM(queries.shape, bf16),
            pltpu.VMEM(new_keys.shape, bf16),
            pltpu.VMEM(new_values.shape, bf16),
            pltpu.VMEM(k_cache.shape, bf16),
            pltpu.VMEM(v_cache.shape, bf16),
            pltpu.VMEM(w_out.shape, bf16),
            pltpu.VMEM((8 * row_count, lanes), f32),
            pltpu.VMEM((8 * row_count, cache_len), f32),
            pltpu.VMEM((row_count, w_out.shape[1]), f32),
            pltpu.SemaphoreType.DMA((4,)),
            pltpu.SemaphoreType.DMA((6,)),
        ],
        mebibytes=16,
        flops=200_000_000,
        moved=3_400_000,
    )
    def sum_exchange(sents):
        return [partner_permute(block, "tp", k) for k, block in zip(FAR_FIRST[1:], sents)]

    parts = sum_exchange(sents)
    weight = (slot_dev * width, hidden)
    base, pick_rows, pick0, pick1, router_rows, *weights = call(
        functools.partial(ready_kernel, slot_dev),
        [
            ((row_count, width), f32),
            ((packed_count, row_count), bf16),
            ((row_count, packed_count), bf16),
            ((row_count, packed_count), bf16),
            ((row_count, width), f32),
            (weight, bf16),
            (weight, bf16),
        ],
        [spec()] * 4 + [spec(pl.ANY)] * 2,
        (
            own,
            resid,
            routes.T,
            w_router.T,
            pltpu.with_memory_space_constraint(w_gate.reshape(weight), pltpu.HBM),
            pltpu.with_memory_space_constraint(w_up.reshape(weight), pltpu.HBM),
        ),
        scratch=[pltpu.SemaphoreType.DMA((8,))],
        mebibytes=12,
        moved=3_300_000,
    )
    attended, home, *sents = call(
        pack_kernel,
        [((row_count, width), bf16)] + [((quarter, width), bf16)] * 4,
        [spec()] * 5,
        (base, *parts, pick_rows),
    )
    (stats,) = call(
        stats_kernel, [((row_count, 128), f32)], [spec()] * 3, (attended, gain, router_rows)
    )
    (result,) = call(result_kernel, [((row_count, width), bf16)], [spec()], (attended,))
    stats, result = lax.optimization_barrier((stats, result))
    parts = [
        partner_permute(block, "req", 2 * k) for k, block in zip(FAR_FIRST[1:], sents)
    ]
    (turned,) = call(
        turn_kernel, [((2 * quarter, width), bf16)], [spec()] * 4, (home, *parts)
    )
    along = partner_permute(turned, "req", 1)
    lhs = pltpu.VMEM((packed_count // 2, slot_dev * width), bf16)

    pair = (quarter, 2 * hidden + 128)

    def chip_sums(kept, sent):
        return call(
            chip_kernel, [(pair, f32), (pair, bf16)], [spec()] * 2,
            (kept, partner_permute(sent, "tp", 1)),
        )

    kept, sent = call(
        functools.partial(early_kernel, slot_dev),
        [(pair, f32), (pair, bf16)],
        [spec()] * 9,
        (home, *parts, gain, stats, *weights, turned),
        scratch=[pltpu.VMEM((2 * quarter, width), bf16), lhs],
        flops=400_000_000,
        moved=3_500_000,
    )
    early, sent = chip_sums(kept, sent)
    early = (early, partner_permute(sent, "tp", 2))
    kept, sent = call(
        functools.partial(late_kernel, slot_dev),
        [(pair, f32), (pair, bf16)],
        [spec()] * 4,
        (along, gain, *weights),
        scratch=[lhs],
        flops=400_000_000,
        moved=3_500_000,
    )
    late, sent = chip_sums(kept, sent)
    late = (late, partner_permute(sent, "tp", 2))
    own, first_weight = call(
        hidden_kernel,
        [((2 * quarter, hidden), bf16), ((row_count, 128), f32)],
        [spec()] * 4,
        (*late, *early),
    )
    (computed,) = call(
        functools.partial(down_kernel, slot_dev),
        [((8, packed_count // 8, width), bf16)],
        [spec()] * 3,
        (own, partner_permute(own, "tp", 1), w_down.reshape(slot_dev * hidden, width)),
        scratch=[pltpu.VMEM((packed_count, slot_dev * hidden), bf16)],
        flops=200_000_000,
        moved=2_000_000,
    )
    returned = lax.all_to_all(computed, "req", split_axis=0, concat_axis=0, tiled=True)
    (layer_out,) = call(
        combine_kernel,
        [((row_count, width), bf16)],
        [spec()] * 5,
        (returned.reshape(packed_count, width), pick0, pick1, first_weight, attended),
    )
    return (result, layer_out)


def solution(mesh):
    placed = (
        P("req", "tp"),
        P("req", "tp"),
        P("req", "tp"),
        P("req", "tp"),
        P("req", None, "tp"),
        P("req", None, "tp"),
        P("req"),
        P("tp", None),
        P("tp"),
        P("tp", None),
        P("req", None),
        P("req", "tp", None),
        P("req", "tp", None),
        P("req", None, "tp"),
    )
    return jax.shard_map(
        shards,
        mesh=mesh,
        in_specs=placed,
        out_specs=(P("req", "tp"), P("req", "tp")),
        check_vma=False,
    )
```

```python
import functools
import math

import jax
import jax.numpy as jnp
from jax import lax
from jax.experimental import pallas as pl
from jax.experimental.pallas import tpu as pltpu
from jax.sharding import PartitionSpec as P

D = 1536
HEAD_DIM = 64
EXPERTS = 16
TOP = 2
CAP = 8


def attend_local(queries, new_keys, new_values, k_cache, v_cache, lengths):
    row_count = queries.shape[0]
    kv_local = new_keys.shape[1] // HEAD_DIM
    group_size = queries.shape[1] // HEAD_DIM // kv_local
    cache_len = k_cache.shape[1]
    score_scale = 1.0 / math.sqrt(HEAD_DIM)
    query = queries.reshape(row_count, kv_local, group_size, HEAD_DIM)
    keys_all = k_cache.reshape(row_count, cache_len, kv_local, HEAD_DIM)
    values_all = v_cache.reshape(row_count, cache_len, kv_local, HEAD_DIM)
    scores = (
        jnp.einsum("bgqd,blgd->bgql", query, keys_all, preferred_element_type=jnp.float32)
        * score_scale
    )
    self_score = (
        jnp.einsum(
            "bgqd,bgd->bgq",
            query,
            new_keys.reshape(row_count, kv_local, HEAD_DIM),
            preferred_element_type=jnp.float32,
        )
        * score_scale
    )
    valid_mask = (jnp.arange(cache_len, dtype=jnp.int32)[None, :] < lengths[:, None])[
        :, None, None, :
    ]
    peak_score = jnp.maximum(jnp.max(jnp.where(valid_mask, scores, -1e30), axis=-1), self_score)
    exp_terms = jnp.where(valid_mask, jnp.exp(scores - peak_score[..., None]), 0.0)
    self_exp = jnp.exp(self_score - peak_score)
    denom_sum = jnp.sum(exp_terms, axis=-1) + self_exp
    weights = (exp_terms / denom_sum[..., None]).astype(jnp.bfloat16)
    self_weight = (self_exp / denom_sum).astype(jnp.bfloat16)
    value_self = new_values.astype(jnp.float32).reshape(row_count, kv_local, 1, HEAD_DIM)
    mixed = (
        jnp.einsum("bgql,blgd->bgqd", weights, values_all, preferred_element_type=jnp.float32)
        + self_weight.astype(jnp.float32)[..., None] * value_self
    )
    return mixed.astype(jnp.bfloat16).reshape(row_count, kv_local * group_size * HEAD_DIM)


def shards_general(
    resid,
    queries,
    new_keys,
    new_values,
    k_cache,
    v_cache,
    lengths,
    w_out,
    norm_gain,
    w_router,
    routes,
    w_gate,
    w_up,
    w_down,
):
    req_dev = resid.shape[0]
    width_local = resid.shape[1]
    slot_dev = w_gate.shape[0]
    req_count = lax.axis_size("req")
    shard_count = max(1, req_count // EXPERTS)
    attention = attend_local(queries, new_keys, new_values, k_cache, v_cache, lengths)
    partial_value = jnp.dot(attention, w_out, preferred_element_type=jnp.float32)
    projected = lax.psum_scatter(partial_value, "tp", scatter_dimension=1, tiled=True)
    attended = (resid.astype(jnp.float32) + projected).astype(jnp.bfloat16)
    attended_f = attended.astype(jnp.float32)
    scaled = attended_f * norm_gain[None, :]
    square_sum, logit_part = lax.psum(
        (
            jnp.sum(attended_f * attended_f, axis=1),
            jnp.dot(scaled, w_router, precision=lax.Precision.HIGHEST),
        ),
        "tp",
    )
    inv_rms = 1.0 / jnp.sqrt(square_sum / D + 1e-06)
    normed = (scaled * inv_rms[:, None]).astype(jnp.bfloat16)
    logits = logit_part * inv_rms[:, None]
    expert_ids = jnp.arange(EXPERTS, dtype=jnp.int32)
    first_logit = jnp.sum(jnp.where(routes[:, 0:1] == expert_ids[None, :], logits, 0.0), axis=1)
    second_logit = jnp.sum(jnp.where(routes[:, 1:2] == expert_ids[None, :], logits, 0.0), axis=1)
    first_weight = jax.nn.sigmoid(first_logit - second_logit)
    second_weight = 1.0 - first_weight
    flat_routes = routes.reshape(req_dev * TOP)
    one_hot = (flat_routes[None, :] == expert_ids[:, None]).astype(jnp.int32)
    rank_in = jnp.cumsum(one_hot, axis=1) - one_hot
    slot_ids = jnp.arange(CAP, dtype=jnp.int32)
    chosen = (one_hot[:, None, :] == 1) & (rank_in[:, None, :] == slot_ids[None, :, None])
    token_pick = jnp.sum(
        chosen.reshape(EXPERTS, CAP, req_dev, TOP).astype(jnp.int32), axis=-1
    ).astype(jnp.bfloat16)
    per_expert = jnp.einsum(
        "ecb,bd->ecd", token_pick, normed, preferred_element_type=jnp.float32
    ).astype(jnp.bfloat16)
    outgoing = jnp.broadcast_to(
        per_expert[:, None], (EXPERTS, shard_count, CAP, width_local)
    ).reshape(req_count, slot_dev, CAP, width_local)
    incoming = lax.all_to_all(outgoing, "req", split_axis=0, concat_axis=0, tiled=True)
    gate_pre = jnp.einsum("nscd,sdf->nscf", incoming, w_gate, preferred_element_type=jnp.float32)
    up_pre = jnp.einsum("nscd,sdf->nscf", incoming, w_up, preferred_element_type=jnp.float32)
    gate_sum, up_sum = lax.psum((gate_pre, up_pre), "tp")
    hidden = (jax.nn.silu(gate_sum) * up_sum).astype(jnp.bfloat16)
    computed = jnp.einsum("nscf,sfd->nscd", hidden, w_down, preferred_element_type=jnp.float32)
    returned = lax.all_to_all(computed, "req", split_axis=0, concat_axis=0, tiled=True)
    combined = jnp.sum(returned.reshape(EXPERTS, shard_count, CAP, width_local), axis=1)
    route_out = jnp.einsum(
        "ecr,ecd->rd", chosen.astype(jnp.float32), combined, precision=lax.Precision.HIGHEST
    ).reshape(req_dev, TOP, width_local)
    moe = first_weight[:, None] * route_out[:, 0] + second_weight[:, None] * route_out[:, 1]
    layer_out = (attended_f + moe).astype(jnp.bfloat16)
    return (attended, layer_out)


FAR_FIRST = (0, 2, 3, 1)


def spec(space=pltpu.VMEM):
    return pl.BlockSpec(memory_space=space)


def call(kernel, outs, ins, operands, scratch=(), mebibytes=8, flops=100_000, moved=100_000):
    return pl.pallas_call(
        kernel,
        out_shape=[jax.ShapeDtypeStruct(shape, dtype) for shape, dtype in outs],
        in_specs=ins,
        out_specs=[spec() for _ in outs],
        scratch_shapes=scratch,
        compiler_params=pltpu.CompilerParams(vmem_limit_bytes=mebibytes << 20),
        cost_estimate=pl.CostEstimate(flops=flops, bytes_accessed=moved, transcendentals=0),
    )(*operands)


def partner_permute(block, axis, distance):
    count = lax.axis_size(axis)
    return lax.ppermute(block, axis, [(i, i ^ distance) for i in range(count)])


def attend_kernel(
    lengths_hbm, queries_hbm, keys_hbm, values_hbm, k_hbm, v_hbm, w_hbm, own, sent1, sent2, sent3,
    lengths, queries, new_keys, new_values, k_buf, v_buf, w_buf,
    query_s, self_s, score_s, weight_s, product_s, small_sems, sems,
):
    row_count = queries.shape[0]
    width = own.shape[1]
    lanes = 2 * HEAD_DIM
    cache_len = k_hbm.shape[1]
    chunks = 2
    small = [
        pltpu.make_async_copy(source, target, small_sems.at[index])
        for index, (source, target) in enumerate(
            (
                (queries_hbm, queries),
                (keys_hbm, new_keys),
                (values_hbm, new_values),
                (lengths_hbm, lengths),
            )
        )
    ]
    copies = []
    for source, target in ((k_hbm, k_buf), (v_hbm, v_buf), (w_hbm, w_buf)):
        size = source.shape[0] // chunks
        for chunk in range(chunks):
            part = pl.ds(chunk * size, size)
            copies.append(
                pltpu.make_async_copy(source.at[part], target.at[part], sems.at[len(copies)])
            )
    for copy in small + copies:
        copy.start()

    for copy in small:
        copy.wait()

    low = lax.broadcasted_iota(jnp.int32, (row_count, lanes), 1) < HEAD_DIM
    tiles = [queries[:, i * lanes : (i + 1) * lanes].astype(jnp.float32) for i in range(3)]
    heads = [
        jnp.where(low, tiles[0], 0.0),
        jnp.where(low, pltpu.roll(tiles[0], HEAD_DIM, 1), 0.0),
        jnp.where(low, tiles[1], 0.0),
        jnp.where(low, 0.0, tiles[1]),
        jnp.where(low, 0.0, pltpu.roll(tiles[2], HEAD_DIM, 1)),
        jnp.where(low, 0.0, tiles[2]),
    ]
    scale = 1.0 / math.sqrt(HEAD_DIM)
    for head in range(8):
        rows = pl.ds(head, row_count, stride=8)
        query_s[rows, :] = heads[head] if head < 6 else jnp.zeros((row_count, lanes), jnp.float32)

    row_of = lax.broadcasted_iota(jnp.int32, (8 * row_count, row_count), 0)
    request_of = lax.broadcasted_iota(jnp.int32, (8 * row_count, row_count), 1)
    spread = jnp.where(row_of // 8 == request_of, 1.0, 0.0).astype(jnp.bfloat16)
    keys_new = jnp.dot(spread, new_keys[...], preferred_element_type=jnp.float32)
    values_new = jnp.dot(spread, new_values[...], preferred_element_type=jnp.float32)
    own_score = jnp.sum(query_s[...] * keys_new, axis=1, keepdims=True) * scale

    upper = lax.broadcasted_iota(jnp.int32, (16, lanes), 0) < 8
    position = lax.broadcasted_iota(jnp.int32, (16, cache_len), 1)
    for copy in copies[:chunks]:
        copy.wait()
    for pair in range(row_count // 2):
        pair_rows = slice(16 * pair, 16 * pair + 16)
        keys = k_buf[2 * pair : 2 * pair + 2].reshape(2 * cache_len, lanes)
        raw = lax.dot_general(
            query_s[pair_rows, :].astype(jnp.bfloat16), keys, (((1,), (1,)), ((), ())),
            preferred_element_type=jnp.float32,
        )
        limit = jnp.where(upper, lengths[2 * pair], lengths[2 * pair + 1])
        score_s[pair_rows, :] = jnp.where(
            position < limit,
            jnp.where(upper, raw[:, :cache_len], raw[:, cache_len:]) * scale,
            -1e30,
        )

    scores = score_s[...]
    peak = jnp.maximum(jnp.max(scores, axis=1, keepdims=True), own_score)
    terms = jnp.exp(scores - peak)
    own_term = jnp.exp(own_score - peak)
    inverse = 1.0 / (jnp.sum(terms, axis=1, keepdims=True) + own_term)
    weight_s[...] = (terms * inverse).astype(jnp.bfloat16)
    own_weight = (own_term * inverse).astype(jnp.bfloat16).astype(jnp.float32)
    self_s[...] = own_weight * values_new
    for copy in copies[chunks : 2 * chunks]:
        copy.wait()
    for pair in range(row_count // 2):
        pair_rows = slice(16 * pair, 16 * pair + 16)
        values = jnp.concatenate([v_buf[2 * pair], v_buf[2 * pair + 1]], axis=1)
        mixed = jnp.dot(weight_s[pair_rows, :], values, preferred_element_type=jnp.float32)
        query_s[pair_rows, :] = (
            jnp.where(upper, mixed[:, :lanes], mixed[:, lanes:]) + self_s[pair_rows, :]
        )

    mixed = [query_s[pl.ds(head, row_count, stride=8), :] for head in range(6)]
    attention = jnp.concatenate(
        [
            jnp.where(low, mixed[0], pltpu.roll(mixed[1], HEAD_DIM, 1)),
            jnp.where(low, mixed[2], mixed[3]),
            jnp.where(low, pltpu.roll(mixed[4], HEAD_DIM, 1), mixed[5]),
        ],
        axis=1,
    ).astype(jnp.bfloat16)
    for copy in copies[2 * chunks :]:
        copy.wait()
    place_tp = lax.axis_index("tp")
    product_s[...] = jnp.dot(attention, w_buf[...], preferred_element_type=jnp.float32)
    for shift, out in zip(FAR_FIRST, (own, sent1, sent2, sent3)):
        columns = pl.ds(pl.multiple_of((place_tp ^ shift) * width, width), width)
        out[...] = product_s[:, columns].astype(out.dtype)


def ready_kernel(
    slot_dev, own, resid, routes, w_router, gate_hbm, up_hbm,
    base, pick_rows, pick0, pick1, router_rows, w_gate, w_up, sems,
):
    copies = []
    for source, target in ((gate_hbm, w_gate), (up_hbm, w_up)):
        size = source.shape[0] // 4
        for chunk in range(4):
            part = pl.ds(chunk * size, size)
            copies.append(
                pltpu.make_async_copy(source.at[part], target.at[part], sems.at[len(copies)])
            )
    for copy in copies:
        copy.start()
    base[...] = own[...] + resid[...].astype(jnp.float32)
    packed_count, row_count = pick_rows.shape

    route0, route1 = routes[0:1, :], routes[1:2, :]
    place = lax.broadcasted_iota(jnp.int32, (packed_count, row_count), 0)
    named0 = jnp.where(place == route0, 1.0, 0.0)
    named1 = jnp.where(place == route1, 1.0, 0.0)
    row_of = lax.broadcasted_iota(jnp.int32, (row_count, row_count), 0)
    col_of = lax.broadcasted_iota(jnp.int32, (row_count, row_count), 1)
    earlier = jnp.where(row_of < col_of, 1.0, 0.0).astype(jnp.bfloat16)
    before = jnp.dot(
        (named0 + named1).astype(jnp.bfloat16), earlier, preferred_element_type=jnp.float32
    )
    place_req = lax.axis_index("req")

    def pick(route, named):
        rank = jnp.sum(named * before, axis=0, keepdims=True).astype(jnp.int32)
        block = ((route // slot_dev) ^ place_req) * slot_dev + lax.rem(route, slot_dev)
        return jnp.where(place == block * CAP + rank, 1.0, 0.0)

    first, second = pick(route0, named0), pick(route1, named1)
    pick_rows[...] = (first + second).astype(jnp.bfloat16)
    pick0[...] = jnp.transpose(first).astype(jnp.bfloat16)
    pick1[...] = jnp.transpose(second).astype(jnp.bfloat16)
    signed = jnp.transpose(named0 - named1)
    router_rows[...] = jnp.dot(
        signed[:, :EXPERTS], w_router[...],
        precision=lax.Precision.HIGHEST, preferred_element_type=jnp.float32,
    )
    for copy in copies:
        copy.wait()


def pack_kernel(base, part1, part2, part3, pick_rows, attended, home, sent1, sent2, sent3):
    total = base[...]
    for part in (part1, part2, part3):
        total = total + part[...].astype(jnp.float32)
    rows = total.astype(jnp.bfloat16)
    attended[...] = rows
    packed = jnp.dot(pick_rows[...], rows, preferred_element_type=jnp.float32)
    size = home.shape[0]
    for distance, out in zip(FAR_FIRST, (home, sent1, sent2, sent3)):
        out[...] = packed[distance * size : (distance + 1) * size].astype(out.dtype)


def result_kernel(attended, result):
    result[...] = attended[...]


def stats_kernel(attended, gain, router_rows, stats):
    rows = attended[...].astype(jnp.float32)
    square = jnp.sum(rows * rows, axis=1, keepdims=True)
    logit = jnp.sum(rows * gain[...] * router_rows[...], axis=1, keepdims=True)
    lane = lax.broadcasted_iota(jnp.int32, stats.shape, 1)
    stats[...] = jnp.where(lane == 0, square, jnp.where(lane == 1, logit, 0.0))


def turn_kernel(home, part1, part2, part3, along):
    half = home.shape[0] // 2
    for index, part in zip(FAR_FIRST, (home, part1, part2, part3)):
        along[index * half : (index + 1) * half, :] = part[half:, :]


def slot_masks(row_count, slot_dev):
    slot = lax.rem(lax.broadcasted_iota(jnp.int32, (row_count, 1), 0) // CAP, slot_dev)
    return [slot == index for index in range(slot_dev)]


def split_high(column):
    high = column.astype(jnp.bfloat16).astype(jnp.float32)
    return high, column - high


def gate_terms(slot_dev, blocks, gain, stats, w_gate, w_up, kept, sent, lhs):
    size = kept.shape[0] // 2
    width = blocks.shape[1]
    hidden = w_gate.shape[1]
    place_tp = lax.axis_index("tp")
    masks = slot_masks(size, slot_dev)
    lane = lax.broadcasted_iota(jnp.int32, (size, 128), 1)
    for order, shift in enumerate((0, 2, 1, 3)):
        out, first_row = (kept, sent)[order // 2], order % 2 * size
        rows = blocks[
            pl.ds(pl.multiple_of((place_tp ^ shift) * size, size), size), :
        ].astype(jnp.float32)
        columns = [jnp.sum(rows * rows, axis=1, keepdims=True)]
        if stats is not None:
            for first in range(0, stats.shape[0], size):
                columns += [stats[first : first + size, 0:1], stats[first : first + size, 1:2]]
        extra = jnp.zeros((size, 128), jnp.float32)
        for index, column in enumerate(columns):
            high, low = split_high(column)
            extra = jnp.where(lane == 2 * index, high, extra)
            extra = jnp.where(lane == 2 * index + 1, low, extra)
        out[first_row : first_row + size, 2 * hidden :] = extra.astype(out.dtype)
        scaled = rows * gain[...]
        for index, mask in enumerate(masks):
            lhs[order * size : (order + 1) * size, index * width : (index + 1) * width] = (
                jnp.where(mask, scaled, 0.0).astype(jnp.bfloat16)
            )
    left = lhs[...]
    for first, weight in ((0, w_gate), (hidden, w_up)):
        product = jnp.dot(left, weight[...], preferred_element_type=jnp.float32)
        kept[:, first : first + hidden] = product[: 2 * size]
        sent[:, first : first + hidden] = product[2 * size :].astype(sent.dtype)


def early_kernel(
    slot_dev, in0, in1, in2, in3, gain, stats, w_gate, w_up, turned, kept, sent, blocks, lhs
):
    del turned
    half = kept.shape[0] // 2
    for index, part in zip(FAR_FIRST, (in0, in1, in2, in3)):
        blocks[index * half : (index + 1) * half, :] = part[:half, :]
    gate_terms(slot_dev, blocks, gain, stats, w_gate, w_up, kept, sent, lhs)


def late_kernel(slot_dev, blocks, gain, w_gate, w_up, kept, sent, lhs):
    gate_terms(slot_dev, blocks, gain, None, w_gate, w_up, kept, sent, lhs)


def chip_kernel(kept, part, own, sent):
    size, width = own.shape[0] // 2, own.shape[1]
    total = kept[...] + part[...].astype(jnp.float32)
    own[...] = total
    extra = total[:, width - 128 :]
    lane = lax.broadcasted_iota(jnp.int32, extra.shape, 1)
    high, low = split_high(extra + pltpu.roll(extra, 127, 1))
    extra = jnp.where(lax.rem(lane, 2) == 0, high, pltpu.roll(low, 1, 1))
    for target, source in ((0, size), (size, 0)):
        sent[target : target + size, : width - 128] = total[
            source : source + size, : width - 128
        ].astype(sent.dtype)
        sent[target : target + size, width - 128 :] = extra[source : source + size].astype(
            sent.dtype
        )


def hidden_kernel(*refs):
    late, early, (hidden, first_weight) = refs[:2], refs[2:4], refs[4:]
    width = hidden.shape[1]
    half = hidden.shape[0] // 4

    def total(parts, columns):
        result = parts[0][:, columns]
        for part in parts[1:]:
            result = result + part[:, columns].astype(jnp.float32)
        return result

    def inverse_rms(columns, index):
        square = columns[:, index : index + 1] + columns[:, index + 1 : index + 2]
        return 1.0 / jnp.sqrt(square / D + 1e-06)

    for index, parts in ((1, late), (0, early)):
        extra = total(parts, slice(2 * width, 2 * width + 128))
        row_inv = inverse_rms(extra, 0)
        gate = total(parts, slice(0, width)) * row_inv
        up = total(parts, slice(width, 2 * width)) * row_inv
        rows = (gate / (1.0 + jnp.exp(-gate)) * up).astype(jnp.bfloat16)
        for block in range(2):
            start = (2 * block + index) * half
            hidden[start : start + half, :] = rows[block * half : (block + 1) * half]
    extra = extra[:half]
    for index in range(first_weight.shape[0] // half):
        place = 2 + 4 * index
        logit = extra[:, place + 2 : place + 3] + extra[:, place + 3 : place + 4]
        weight = 1.0 / (1.0 + jnp.exp(-logit * inverse_rms(extra, place)))
        first_weight[index * half : (index + 1) * half, :] = jnp.broadcast_to(weight, (half, 128))


BACK = ((0, 2, 3, 1), (0, 3, 1, 2))


def down_rows(slot_dev, hidden, w_down, lhs, product):
    count, width = hidden.shape
    rows = hidden[...].astype(jnp.float32)
    for index, mask in enumerate(slot_masks(count, slot_dev)):
        lhs[:, index * width : (index + 1) * width] = jnp.where(mask, rows, 0.0).astype(
            jnp.bfloat16
        )
    product[...] = jnp.dot(lhs[...], w_down[...], preferred_element_type=jnp.float32)
    half = count // 2
    upper = lax.axis_index("tp") // 2
    near = pl.ds(pl.multiple_of(upper * half, half), half)
    far = pl.ds(pl.multiple_of((1 - upper) * half, half), half)
    return product[near, :], product[far, :]


def own_down_kernel(slot_dev, hidden, w_down, near, far, lhs, product):
    results = down_rows(slot_dev, hidden, w_down, lhs, product)
    for out, rows in zip((near, far), results):
        out[...] = rows.astype(out.dtype)


def other_down_kernel(slot_dev, hidden, w_down, own_near, home, second, third, lhs, product):
    near, far = down_rows(slot_dev, hidden, w_down, lhs, product)
    own = own_near[...].astype(jnp.float32)
    first_core = lax.rem(lax.axis_index("tp"), 2) == 0
    home[...] = jnp.where(first_core, own, near).astype(home.dtype)
    second[...] = jnp.where(first_core, far, own).astype(second.dtype)
    third[...] = jnp.where(first_core, near, far).astype(third.dtype)


def back_permute(block, order):
    reqs, tps = lax.axis_size("req"), lax.axis_size("tp")
    pairs = [
        (req * tps + tp, (req ^ (2 * BACK[tp % 2][order])) * tps + tp)
        for req in range(reqs)
        for tp in range(tps)
    ]
    return lax.ppermute(block, ("req", "tp"), pairs)


def back_turn_kernel(home, part1, part2, part3, along):
    half = home.shape[0] // 2
    for index, part in enumerate((home, part1, part2, part3)):
        along[index * half : (index + 1) * half, :] = part[half:, :]


def combine_kernel(
    home, part1, part2, part3, along, pick0, pick1, first_weight, attended, layer_out, returned
):
    half = home.shape[0] // 2
    core = lax.rem(lax.axis_index("tp"), 2)
    for index, part in enumerate((home, part1, part2, part3)):
        distance = jnp.where(core == 0, BACK[0][index], BACK[1][index])
        start = pl.multiple_of(distance * 2 * half, 2 * half)
        returned[pl.ds(start, half), :] = part[:half, :]
        returned[pl.ds(start + half, half), :] = along[index * half : (index + 1) * half, :]
    rows = returned[...]
    out0 = jnp.dot(pick0[...], rows, preferred_element_type=jnp.float32)
    out1 = jnp.dot(pick1[...], rows, preferred_element_type=jnp.float32)
    weight = first_weight[:, 0:1]
    moe = weight * out0 + (1.0 - weight) * out1
    layer_out[...] = (attended[...].astype(jnp.float32) + moe).astype(jnp.bfloat16)


def shards(
    resid,
    queries,
    new_keys,
    new_values,
    k_cache,
    v_cache,
    lengths,
    w_out,
    norm_gain,
    w_router,
    routes,
    w_gate,
    w_up,
    w_down,
):
    row_count, width = resid.shape
    slot_dev, _, hidden = w_gate.shape
    cache_len, lanes = k_cache.shape[1:]
    packed_count = EXPERTS * CAP
    quarter = packed_count // lax.axis_size("tp")
    if not (
        lax.axis_size("tp") == 4
        and lax.axis_size("req") == 8
        and 8 * slot_dev == EXPERTS
        and row_count == quarter
        and cache_len == lanes == 2 * HEAD_DIM
        and queries.shape[1] == 6 * HEAD_DIM
    ):
        return shards_general(
            resid, queries, new_keys, new_values, k_cache, v_cache, lengths, w_out,
            norm_gain, w_router, routes, w_gate, w_up, w_down,
        )
    bf16, f32 = jnp.bfloat16, jnp.float32
    gain = norm_gain.reshape(1, width)
    own, *sents = call(
        attend_kernel,
        [((row_count, width), f32)] + [((row_count, width), bf16)] * 3,
        [spec(pl.ANY)] * 7,
        [
            pltpu.with_memory_space_constraint(operand, pltpu.HBM)
            for operand in (lengths, queries, new_keys, new_values, k_cache, v_cache, w_out)
        ],
        scratch=[
            pltpu.SMEM(lengths.shape, jnp.int32),
            pltpu.VMEM(queries.shape, bf16),
            pltpu.VMEM(new_keys.shape, bf16),
            pltpu.VMEM(new_values.shape, bf16),
            pltpu.VMEM(k_cache.shape, bf16),
            pltpu.VMEM(v_cache.shape, bf16),
            pltpu.VMEM(w_out.shape, bf16),
            pltpu.VMEM((8 * row_count, lanes), f32),
            pltpu.VMEM((8 * row_count, lanes), f32),
            pltpu.VMEM((8 * row_count, cache_len), f32),
            pltpu.VMEM((8 * row_count, cache_len), bf16),
            pltpu.VMEM((row_count, w_out.shape[1]), f32),
            pltpu.SemaphoreType.DMA((4,)),
            pltpu.SemaphoreType.DMA((6,)),
        ],
        mebibytes=16,
        flops=200_000_000,
        moved=3_400_000,
    )
    def sum_exchange(sents):
        return [partner_permute(block, "tp", k) for k, block in zip(FAR_FIRST[1:], sents)]

    parts = sum_exchange(sents)
    weight = (slot_dev * width, hidden)
    base, pick_rows, pick0, pick1, router_rows, *weights = call(
        functools.partial(ready_kernel, slot_dev),
        [
            ((row_count, width), f32),
            ((packed_count, row_count), bf16),
            ((row_count, packed_count), bf16),
            ((row_count, packed_count), bf16),
            ((row_count, width), f32),
            (weight, bf16),
            (weight, bf16),
        ],
        [spec()] * 4 + [spec(pl.ANY)] * 2,
        (
            own,
            resid,
            routes.T,
            w_router.T,
            pltpu.with_memory_space_constraint(w_gate.reshape(weight), pltpu.HBM),
            pltpu.with_memory_space_constraint(w_up.reshape(weight), pltpu.HBM),
        ),
        scratch=[pltpu.SemaphoreType.DMA((8,))],
        mebibytes=12,
        moved=3_300_000,
    )
    attended, home, *sents = call(
        pack_kernel,
        [((row_count, width), bf16)] + [((quarter, width), bf16)] * 4,
        [spec()] * 5,
        (base, *parts, pick_rows),
    )
    (stats,) = call(
        stats_kernel, [((row_count, 128), f32)], [spec()] * 3, (attended, gain, router_rows)
    )
    (result,) = call(result_kernel, [((row_count, width), bf16)], [spec()], (attended,))
    stats, result = lax.optimization_barrier((stats, result))
    parts = [
        partner_permute(block, "req", 2 * k) for k, block in zip(FAR_FIRST[1:], sents)
    ]
    (turned,) = call(
        turn_kernel, [((2 * quarter, width), bf16)], [spec()] * 4, (home, *parts)
    )
    along = partner_permute(turned, "req", 1)
    lhs = pltpu.VMEM((packed_count // 2, slot_dev * width), bf16)

    pair = (quarter, 2 * hidden + 128)

    def chip_sums(kept, sent):
        return call(
            chip_kernel, [(pair, f32), (pair, bf16)], [spec()] * 2,
            (kept, partner_permute(sent, "tp", 1)),
        )

    kept, sent = call(
        functools.partial(early_kernel, slot_dev),
        [(pair, f32), (pair, bf16)],
        [spec()] * 9,
        (home, *parts, gain, stats, *weights, turned),
        scratch=[pltpu.VMEM((2 * quarter, width), bf16), lhs],
        flops=400_000_000,
        moved=3_500_000,
    )
    early, sent = chip_sums(kept, sent)
    early = (early, partner_permute(sent, "tp", 2))
    kept, sent = call(
        functools.partial(late_kernel, slot_dev),
        [(pair, f32), (pair, bf16)],
        [spec()] * 4,
        (along, gain, *weights),
        scratch=[lhs],
        flops=400_000_000,
        moved=3_500_000,
    )
    late, sent = chip_sums(kept, sent)
    late = (late, partner_permute(sent, "tp", 2))
    own, first_weight = call(
        hidden_kernel,
        [((2 * quarter, hidden), bf16), ((row_count, 128), f32)],
        [spec()] * 4,
        (*late, *early),
    )
    w_down = w_down.reshape(slot_dev * hidden, width)
    block = ((quarter, width), bf16)
    down_scratch = [
        pltpu.VMEM((2 * quarter, slot_dev * hidden), bf16),
        pltpu.VMEM((2 * quarter, width), f32),
    ]
    near, far = call(
        functools.partial(own_down_kernel, slot_dev), [block] * 2, [spec()] * 2, (own, w_down),
        scratch=down_scratch, flops=100_000_000, moved=2_000_000,
    )
    home, second, third = call(
        functools.partial(other_down_kernel, slot_dev), [block] * 3, [spec()] * 3,
        (partner_permute(own, "tp", 1), w_down, near),
        scratch=down_scratch, flops=100_000_000, moved=2_000_000,
    )
    parts = [back_permute(rows, order) for order, rows in enumerate((far, second, third), 1)]
    (along,) = call(
        back_turn_kernel, [((2 * quarter, width), bf16)], [spec()] * 4, (home, *parts)
    )
    (layer_out,) = call(
        combine_kernel,
        [((row_count, width), bf16)],
        [spec()] * 9,
        (
            home, *parts, partner_permute(along, "req", 1), pick0, pick1, first_weight, attended,
        ),
        scratch=[pltpu.VMEM((packed_count, width), bf16)],
    )
    return (result, layer_out)


def solution(mesh):
    placed = (
        P("req", "tp"),
        P("req", "tp"),
        P("req", "tp"),
        P("req", "tp"),
        P("req", None, "tp"),
        P("req", None, "tp"),
        P("req"),
        P("tp", None),
        P("tp"),
        P("tp", None),
        P("req", None),
        P("req", "tp", None),
        P("req", "tp", None),
        P("req", None, "tp"),
    )
    return jax.shard_map(
        shards,
        mesh=mesh,
        in_specs=placed,
        out_specs=(P("req", "tp"), P("req", "tp")),
        check_vma=False,
    )
```

```python
import functools
import math

import jax
import jax.numpy as jnp
from jax import lax
from jax.experimental import pallas as pl
from jax.experimental.pallas import tpu as pltpu
from jax.sharding import PartitionSpec as P

D = 1536
HEAD_DIM = 64
EXPERTS = 16
TOP = 2
CAP = 8


def attend_local(queries, new_keys, new_values, k_cache, v_cache, lengths):
    row_count = queries.shape[0]
    kv_local = new_keys.shape[1] // HEAD_DIM
    group_size = queries.shape[1] // HEAD_DIM // kv_local
    cache_len = k_cache.shape[1]
    score_scale = 1.0 / math.sqrt(HEAD_DIM)
    query = queries.reshape(row_count, kv_local, group_size, HEAD_DIM)
    keys_all = k_cache.reshape(row_count, cache_len, kv_local, HEAD_DIM)
    values_all = v_cache.reshape(row_count, cache_len, kv_local, HEAD_DIM)
    scores = (
        jnp.einsum("bgqd,blgd->bgql", query, keys_all, preferred_element_type=jnp.float32)
        * score_scale
    )
    self_score = (
        jnp.einsum(
            "bgqd,bgd->bgq",
            query,
            new_keys.reshape(row_count, kv_local, HEAD_DIM),
            preferred_element_type=jnp.float32,
        )
        * score_scale
    )
    valid_mask = (jnp.arange(cache_len, dtype=jnp.int32)[None, :] < lengths[:, None])[
        :, None, None, :
    ]
    peak_score = jnp.maximum(jnp.max(jnp.where(valid_mask, scores, -1e30), axis=-1), self_score)
    exp_terms = jnp.where(valid_mask, jnp.exp(scores - peak_score[..., None]), 0.0)
    self_exp = jnp.exp(self_score - peak_score)
    denom_sum = jnp.sum(exp_terms, axis=-1) + self_exp
    weights = (exp_terms / denom_sum[..., None]).astype(jnp.bfloat16)
    self_weight = (self_exp / denom_sum).astype(jnp.bfloat16)
    value_self = new_values.astype(jnp.float32).reshape(row_count, kv_local, 1, HEAD_DIM)
    mixed = (
        jnp.einsum("bgql,blgd->bgqd", weights, values_all, preferred_element_type=jnp.float32)
        + self_weight.astype(jnp.float32)[..., None] * value_self
    )
    return mixed.astype(jnp.bfloat16).reshape(row_count, kv_local * group_size * HEAD_DIM)


def shards_general(
    resid,
    queries,
    new_keys,
    new_values,
    k_cache,
    v_cache,
    lengths,
    w_out,
    norm_gain,
    w_router,
    routes,
    w_gate,
    w_up,
    w_down,
):
    req_dev = resid.shape[0]
    width_local = resid.shape[1]
    slot_dev = w_gate.shape[0]
    req_count = lax.axis_size("req")
    shard_count = max(1, req_count // EXPERTS)
    attention = attend_local(queries, new_keys, new_values, k_cache, v_cache, lengths)
    partial_value = jnp.dot(attention, w_out, preferred_element_type=jnp.float32)
    projected = lax.psum_scatter(partial_value, "tp", scatter_dimension=1, tiled=True)
    attended = (resid.astype(jnp.float32) + projected).astype(jnp.bfloat16)
    attended_f = attended.astype(jnp.float32)
    scaled = attended_f * norm_gain[None, :]
    square_sum, logit_part = lax.psum(
        (
            jnp.sum(attended_f * attended_f, axis=1),
            jnp.dot(scaled, w_router, precision=lax.Precision.HIGHEST),
        ),
        "tp",
    )
    inv_rms = 1.0 / jnp.sqrt(square_sum / D + 1e-06)
    normed = (scaled * inv_rms[:, None]).astype(jnp.bfloat16)
    logits = logit_part * inv_rms[:, None]
    expert_ids = jnp.arange(EXPERTS, dtype=jnp.int32)
    first_logit = jnp.sum(jnp.where(routes[:, 0:1] == expert_ids[None, :], logits, 0.0), axis=1)
    second_logit = jnp.sum(jnp.where(routes[:, 1:2] == expert_ids[None, :], logits, 0.0), axis=1)
    first_weight = jax.nn.sigmoid(first_logit - second_logit)
    second_weight = 1.0 - first_weight
    flat_routes = routes.reshape(req_dev * TOP)
    one_hot = (flat_routes[None, :] == expert_ids[:, None]).astype(jnp.int32)
    rank_in = jnp.cumsum(one_hot, axis=1) - one_hot
    slot_ids = jnp.arange(CAP, dtype=jnp.int32)
    chosen = (one_hot[:, None, :] == 1) & (rank_in[:, None, :] == slot_ids[None, :, None])
    token_pick = jnp.sum(
        chosen.reshape(EXPERTS, CAP, req_dev, TOP).astype(jnp.int32), axis=-1
    ).astype(jnp.bfloat16)
    per_expert = jnp.einsum(
        "ecb,bd->ecd", token_pick, normed, preferred_element_type=jnp.float32
    ).astype(jnp.bfloat16)
    outgoing = jnp.broadcast_to(
        per_expert[:, None], (EXPERTS, shard_count, CAP, width_local)
    ).reshape(req_count, slot_dev, CAP, width_local)
    incoming = lax.all_to_all(outgoing, "req", split_axis=0, concat_axis=0, tiled=True)
    gate_pre = jnp.einsum("nscd,sdf->nscf", incoming, w_gate, preferred_element_type=jnp.float32)
    up_pre = jnp.einsum("nscd,sdf->nscf", incoming, w_up, preferred_element_type=jnp.float32)
    gate_sum, up_sum = lax.psum((gate_pre, up_pre), "tp")
    hidden = (jax.nn.silu(gate_sum) * up_sum).astype(jnp.bfloat16)
    computed = jnp.einsum("nscf,sfd->nscd", hidden, w_down, preferred_element_type=jnp.float32)
    returned = lax.all_to_all(computed, "req", split_axis=0, concat_axis=0, tiled=True)
    combined = jnp.sum(returned.reshape(EXPERTS, shard_count, CAP, width_local), axis=1)
    route_out = jnp.einsum(
        "ecr,ecd->rd", chosen.astype(jnp.float32), combined, precision=lax.Precision.HIGHEST
    ).reshape(req_dev, TOP, width_local)
    moe = first_weight[:, None] * route_out[:, 0] + second_weight[:, None] * route_out[:, 1]
    layer_out = (attended_f + moe).astype(jnp.bfloat16)
    return (attended, layer_out)


FAR_FIRST = (0, 2, 3, 1)


def spec(space=pltpu.VMEM):
    return pl.BlockSpec(memory_space=space)


def call(kernel, outs, ins, operands, scratch=(), mebibytes=8, flops=100_000, moved=100_000):
    return pl.pallas_call(
        kernel,
        out_shape=[jax.ShapeDtypeStruct(shape, dtype) for shape, dtype in outs],
        in_specs=ins,
        out_specs=[spec() for _ in outs],
        scratch_shapes=scratch,
        compiler_params=pltpu.CompilerParams(vmem_limit_bytes=mebibytes << 20),
        cost_estimate=pl.CostEstimate(flops=flops, bytes_accessed=moved, transcendentals=0),
    )(*operands)


def partner_permute(block, axis, distance):
    count = lax.axis_size(axis)
    return lax.ppermute(block, axis, [(i, i ^ distance) for i in range(count)])


def attend_kernel(
    lengths_hbm, queries_hbm, keys_hbm, values_hbm, k_hbm, v_hbm, w_hbm, own, sent1, sent2, sent3,
    lengths, queries, new_keys, new_values, k_buf, v_buf, w_buf,
    query_s, self_s, score_s, weight_s, product_s, small_sems, sems,
):
    row_count = queries.shape[0]
    width = own.shape[1]
    lanes = 2 * HEAD_DIM
    cache_len = k_hbm.shape[1]
    chunks = 1
    small = [
        pltpu.make_async_copy(source, target, small_sems.at[index])
        for index, (source, target) in enumerate(
            (
                (queries_hbm, queries),
                (keys_hbm, new_keys),
                (values_hbm, new_values),
                (lengths_hbm, lengths),
            )
        )
    ]
    copies = []
    for source, target in ((k_hbm, k_buf), (v_hbm, v_buf), (w_hbm, w_buf)):
        size = source.shape[0] // chunks
        for chunk in range(chunks):
            part = pl.ds(chunk * size, size)
            copies.append(
                pltpu.make_async_copy(source.at[part], target.at[part], sems.at[len(copies)])
            )
    for copy in small + copies:
        copy.start()

    for copy in small:
        copy.wait()

    low = lax.broadcasted_iota(jnp.int32, (row_count, lanes), 1) < HEAD_DIM
    tiles = [queries[:, i * lanes : (i + 1) * lanes].astype(jnp.float32) for i in range(3)]
    heads = [
        jnp.where(low, tiles[0], 0.0),
        jnp.where(low, pltpu.roll(tiles[0], HEAD_DIM, 1), 0.0),
        jnp.where(low, tiles[1], 0.0),
        jnp.where(low, 0.0, tiles[1]),
        jnp.where(low, 0.0, pltpu.roll(tiles[2], HEAD_DIM, 1)),
        jnp.where(low, 0.0, tiles[2]),
    ]
    scale = 1.0 / math.sqrt(HEAD_DIM)
    for head in range(8):
        rows = pl.ds(head, row_count, stride=8)
        query_s[rows, :] = heads[head] if head < 6 else jnp.zeros((row_count, lanes), jnp.float32)

    row_of = lax.broadcasted_iota(jnp.int32, (8 * row_count, row_count), 0)
    request_of = lax.broadcasted_iota(jnp.int32, (8 * row_count, row_count), 1)
    spread = jnp.where(row_of // 8 == request_of, 1.0, 0.0).astype(jnp.bfloat16)
    keys_new = jnp.dot(spread, new_keys[...], preferred_element_type=jnp.float32)
    values_new = jnp.dot(spread, new_values[...], preferred_element_type=jnp.float32)
    own_score = jnp.sum(query_s[...] * keys_new, axis=1, keepdims=True) * scale

    upper = lax.broadcasted_iota(jnp.int32, (16, lanes), 0) < 8
    position = lax.broadcasted_iota(jnp.int32, (16, cache_len), 1)
    for copy in copies[:chunks]:
        copy.wait()
    for pair in range(row_count // 2):
        pair_rows = slice(16 * pair, 16 * pair + 16)
        keys = k_buf[2 * pair : 2 * pair + 2].reshape(2 * cache_len, lanes)
        raw = lax.dot_general(
            query_s[pair_rows, :].astype(jnp.bfloat16), keys, (((1,), (1,)), ((), ())),
            preferred_element_type=jnp.float32,
        )
        limit = jnp.where(upper, lengths[2 * pair], lengths[2 * pair + 1])
        score_s[pair_rows, :] = jnp.where(
            position < limit,
            jnp.where(upper, raw[:, :cache_len], raw[:, cache_len:]) * scale,
            -1e30,
        )

    for copy in copies[chunks:]:
        copy.wait()
    scores = score_s[...]
    peak = jnp.maximum(jnp.max(scores, axis=1, keepdims=True), own_score)
    terms = jnp.exp(scores - peak)
    own_term = jnp.exp(own_score - peak)
    inverse = 1.0 / (jnp.sum(terms, axis=1, keepdims=True) + own_term)
    weight_s[...] = (terms * inverse).astype(jnp.bfloat16)
    own_weight = (own_term * inverse).astype(jnp.bfloat16).astype(jnp.float32)
    self_s[...] = own_weight * values_new
    for pair in range(row_count // 2):
        pair_rows = slice(16 * pair, 16 * pair + 16)
        values = jnp.concatenate([v_buf[2 * pair], v_buf[2 * pair + 1]], axis=1)
        mixed = jnp.dot(weight_s[pair_rows, :], values, preferred_element_type=jnp.float32)
        query_s[pair_rows, :] = (
            jnp.where(upper, mixed[:, :lanes], mixed[:, lanes:]) + self_s[pair_rows, :]
        )

    mixed = [query_s[pl.ds(head, row_count, stride=8), :] for head in range(6)]
    attention = jnp.concatenate(
        [
            jnp.where(low, mixed[0], pltpu.roll(mixed[1], HEAD_DIM, 1)),
            jnp.where(low, mixed[2], mixed[3]),
            jnp.where(low, pltpu.roll(mixed[4], HEAD_DIM, 1), mixed[5]),
        ],
        axis=1,
    ).astype(jnp.bfloat16)
    place_tp = lax.axis_index("tp")
    product_s[...] = jnp.dot(attention, w_buf[...], preferred_element_type=jnp.float32)
    for shift, out in zip(FAR_FIRST, (own, sent1, sent2, sent3)):
        columns = pl.ds(pl.multiple_of((place_tp ^ shift) * width, width), width)
        out[...] = product_s[:, columns].astype(out.dtype)


def ready_kernel(
    slot_dev, own, resid, routes, w_router, gate_hbm, up_hbm,
    base, pick_rows, pick0, pick1, router_rows, w_gate, w_up, sems,
):
    copies = []
    for source, target in ((gate_hbm, w_gate), (up_hbm, w_up)):
        size = source.shape[0] // 4
        for chunk in range(4):
            part = pl.ds(chunk * size, size)
            copies.append(
                pltpu.make_async_copy(source.at[part], target.at[part], sems.at[len(copies)])
            )
    for copy in copies:
        copy.start()
    base[...] = own[...] + resid[...].astype(jnp.float32)
    packed_count, row_count = pick_rows.shape

    route0, route1 = routes[0:1, :], routes[1:2, :]
    place = lax.broadcasted_iota(jnp.int32, (packed_count, row_count), 0)
    named0 = jnp.where(place == route0, 1.0, 0.0)
    named1 = jnp.where(place == route1, 1.0, 0.0)
    row_of = lax.broadcasted_iota(jnp.int32, (row_count, row_count), 0)
    col_of = lax.broadcasted_iota(jnp.int32, (row_count, row_count), 1)
    earlier = jnp.where(row_of < col_of, 1.0, 0.0).astype(jnp.bfloat16)
    before = jnp.dot(
        (named0 + named1).astype(jnp.bfloat16), earlier, preferred_element_type=jnp.float32
    )
    place_req = lax.axis_index("req")

    def pick(route, named):
        rank = jnp.sum(named * before, axis=0, keepdims=True).astype(jnp.int32)
        block = ((route // slot_dev) ^ place_req) * slot_dev + lax.rem(route, slot_dev)
        return jnp.where(place == block * CAP + rank, 1.0, 0.0)

    first, second = pick(route0, named0), pick(route1, named1)
    pick_rows[...] = (first + second).astype(jnp.bfloat16)
    pick0[...] = jnp.transpose(first).astype(jnp.bfloat16)
    pick1[...] = jnp.transpose(second).astype(jnp.bfloat16)
    signed = jnp.transpose(named0 - named1)
    router_rows[...] = jnp.dot(
        signed[:, :EXPERTS], w_router[...],
        precision=lax.Precision.HIGHEST, preferred_element_type=jnp.float32,
    )
    for copy in copies:
        copy.wait()


def pack_kernel(base, part1, part2, part3, pick_rows, attended, home, sent1, sent2, sent3):
    total = base[...]
    for part in (part1, part2, part3):
        total = total + part[...].astype(jnp.float32)
    rows = total.astype(jnp.bfloat16)
    attended[...] = rows
    packed = jnp.dot(pick_rows[...], rows, preferred_element_type=jnp.float32)
    size = home.shape[0]
    for distance, out in zip(FAR_FIRST, (home, sent1, sent2, sent3)):
        out[...] = packed[distance * size : (distance + 1) * size].astype(out.dtype)


def result_kernel(attended, result):
    result[...] = attended[...]


def stats_kernel(attended, gain, router_rows, stats):
    rows = attended[...].astype(jnp.float32)
    square = jnp.sum(rows * rows, axis=1, keepdims=True)
    logit = jnp.sum(rows * gain[...] * router_rows[...], axis=1, keepdims=True)
    lane = lax.broadcasted_iota(jnp.int32, stats.shape, 1)
    stats[...] = jnp.where(lane == 0, square, jnp.where(lane == 1, logit, 0.0))


def turn_kernel(home, part1, part2, part3, along):
    half = home.shape[0] // 2
    for index, part in zip(FAR_FIRST, (home, part1, part2, part3)):
        along[index * half : (index + 1) * half, :] = part[half:, :]


def slot_masks(row_count, slot_dev):
    slot = lax.rem(lax.broadcasted_iota(jnp.int32, (row_count, 1), 0) // CAP, slot_dev)
    return [slot == index for index in range(slot_dev)]


def split_high(column):
    high = column.astype(jnp.bfloat16).astype(jnp.float32)
    return high, column - high


def gate_terms(slot_dev, blocks, gain, stats, w_gate, w_up, kept, sent, lhs):
    size = kept.shape[0] // 2
    width = blocks.shape[1]
    hidden = w_gate.shape[1]
    place_tp = lax.axis_index("tp")
    masks = slot_masks(size, slot_dev)
    lane = lax.broadcasted_iota(jnp.int32, (size, 128), 1)
    for order, shift in enumerate((0, 2, 1, 3)):
        out, first_row = (kept, sent)[order // 2], order % 2 * size
        rows = blocks[
            pl.ds(pl.multiple_of((place_tp ^ shift) * size, size), size), :
        ].astype(jnp.float32)
        columns = [jnp.sum(rows * rows, axis=1, keepdims=True)]
        if stats is not None:
            for first in range(0, stats.shape[0], size):
                columns += [stats[first : first + size, 0:1], stats[first : first + size, 1:2]]
        extra = jnp.zeros((size, 128), jnp.float32)
        for index, column in enumerate(columns):
            high, low = split_high(column)
            extra = jnp.where(lane == 2 * index, high, extra)
            extra = jnp.where(lane == 2 * index + 1, low, extra)
        out[first_row : first_row + size, 2 * hidden :] = extra.astype(out.dtype)
        scaled = rows * gain[...]
        for index, mask in enumerate(masks):
            lhs[order * size : (order + 1) * size, index * width : (index + 1) * width] = (
                jnp.where(mask, scaled, 0.0).astype(jnp.bfloat16)
            )
    left = lhs[...]
    for first, weight in ((0, w_gate), (hidden, w_up)):
        product = jnp.dot(left, weight[...], preferred_element_type=jnp.float32)
        kept[:, first : first + hidden] = product[: 2 * size]
        sent[:, first : first + hidden] = product[2 * size :].astype(sent.dtype)


def early_kernel(
    slot_dev, in0, in1, in2, in3, gain, stats, w_gate, w_up, turned, kept, sent, blocks, lhs
):
    del turned
    half = kept.shape[0] // 2
    for index, part in zip(FAR_FIRST, (in0, in1, in2, in3)):
        blocks[index * half : (index + 1) * half, :] = part[:half, :]
    gate_terms(slot_dev, blocks, gain, stats, w_gate, w_up, kept, sent, lhs)


def late_kernel(slot_dev, blocks, gain, w_gate, w_up, kept, sent, lhs):
    gate_terms(slot_dev, blocks, gain, None, w_gate, w_up, kept, sent, lhs)


def chip_kernel(kept, part, own, sent):
    size, width = own.shape[0] // 2, own.shape[1]
    total = kept[...] + part[...].astype(jnp.float32)
    own[...] = total
    extra = total[:, width - 128 :]
    lane = lax.broadcasted_iota(jnp.int32, extra.shape, 1)
    high, low = split_high(extra + pltpu.roll(extra, 127, 1))
    extra = jnp.where(lax.rem(lane, 2) == 0, high, pltpu.roll(low, 1, 1))
    for target, source in ((0, size), (size, 0)):
        sent[target : target + size, : width - 128] = total[
            source : source + size, : width - 128
        ].astype(sent.dtype)
        sent[target : target + size, width - 128 :] = extra[source : source + size].astype(
            sent.dtype
        )


def hidden_kernel(*refs):
    late, early, (hidden, first_weight) = refs[:2], refs[2:4], refs[4:]
    width = hidden.shape[1]
    half = hidden.shape[0] // 4

    def total(parts, columns):
        result = parts[0][:, columns]
        for part in parts[1:]:
            result = result + part[:, columns].astype(jnp.float32)
        return result

    def inverse_rms(columns, index):
        square = columns[:, index : index + 1] + columns[:, index + 1 : index + 2]
        return 1.0 / jnp.sqrt(square / D + 1e-06)

    for index, parts in ((1, late), (0, early)):
        extra = total(parts, slice(2 * width, 2 * width + 128))
        row_inv = inverse_rms(extra, 0)
        gate = total(parts, slice(0, width)) * row_inv
        up = total(parts, slice(width, 2 * width)) * row_inv
        rows = (gate / (1.0 + jnp.exp(-gate)) * up).astype(jnp.bfloat16)
        for block in range(2):
            start = (2 * block + index) * half
            hidden[start : start + half, :] = rows[block * half : (block + 1) * half]
    extra = extra[:half]
    for index in range(first_weight.shape[0] // half):
        place = 2 + 4 * index
        logit = extra[:, place + 2 : place + 3] + extra[:, place + 3 : place + 4]
        weight = 1.0 / (1.0 + jnp.exp(-logit * inverse_rms(extra, place)))
        first_weight[index * half : (index + 1) * half, :] = jnp.broadcast_to(weight, (half, 128))


BACK = ((0, 2, 3, 1), (0, 3, 1, 2))


def down_rows(slot_dev, hidden, w_down, lhs, product):
    count, width = hidden.shape
    rows = hidden[...].astype(jnp.float32)
    for index, mask in enumerate(slot_masks(count, slot_dev)):
        lhs[:, index * width : (index + 1) * width] = jnp.where(mask, rows, 0.0).astype(
            jnp.bfloat16
        )
    product[...] = jnp.dot(lhs[...], w_down[...], preferred_element_type=jnp.float32)
    half = count // 2
    upper = lax.axis_index("tp") // 2
    near = pl.ds(pl.multiple_of(upper * half, half), half)
    far = pl.ds(pl.multiple_of((1 - upper) * half, half), half)
    return product[near, :], product[far, :]


def own_down_kernel(slot_dev, hidden, w_down, near, far, lhs, product):
    results = down_rows(slot_dev, hidden, w_down, lhs, product)
    for out, rows in zip((near, far), results):
        out[...] = rows.astype(out.dtype)


def other_down_kernel(slot_dev, hidden, w_down, own_near, home, second, third, lhs, product):
    near, far = down_rows(slot_dev, hidden, w_down, lhs, product)
    own = own_near[...].astype(jnp.float32)
    first_core = lax.rem(lax.axis_index("tp"), 2) == 0
    home[...] = jnp.where(first_core, own, near).astype(home.dtype)
    second[...] = jnp.where(first_core, far, own).astype(second.dtype)
    third[...] = jnp.where(first_core, near, far).astype(third.dtype)


def back_permute(block, order):
    reqs, tps = lax.axis_size("req"), lax.axis_size("tp")
    pairs = [
        (req * tps + tp, (req ^ (2 * BACK[tp % 2][order])) * tps + tp)
        for req in range(reqs)
        for tp in range(tps)
    ]
    return lax.ppermute(block, ("req", "tp"), pairs)


def back_turn_kernel(home, part1, part2, part3, along):
    half = home.shape[0] // 2
    for index, part in enumerate((home, part1, part2, part3)):
        along[index * half : (index + 1) * half, :] = part[half:, :]


def combine_kernel(
    home, part1, part2, part3, along, pick0, pick1, first_weight, attended, layer_out, returned
):
    half = home.shape[0] // 2
    core = lax.rem(lax.axis_index("tp"), 2)
    for index, part in enumerate((home, part1, part2, part3)):
        distance = jnp.where(core == 0, BACK[0][index], BACK[1][index])
        start = pl.multiple_of(distance * 2 * half, 2 * half)
        returned[pl.ds(start, half), :] = part[:half, :]
        returned[pl.ds(start + half, half), :] = along[index * half : (index + 1) * half, :]
    rows = returned[...]
    out0 = jnp.dot(pick0[...], rows, preferred_element_type=jnp.float32)
    out1 = jnp.dot(pick1[...], rows, preferred_element_type=jnp.float32)
    weight = first_weight[:, 0:1]
    moe = weight * out0 + (1.0 - weight) * out1
    layer_out[...] = (attended[...].astype(jnp.float32) + moe).astype(jnp.bfloat16)


def shards(
    resid,
    queries,
    new_keys,
    new_values,
    k_cache,
    v_cache,
    lengths,
    w_out,
    norm_gain,
    w_router,
    routes,
    w_gate,
    w_up,
    w_down,
):
    row_count, width = resid.shape
    slot_dev, _, hidden = w_gate.shape
    cache_len, lanes = k_cache.shape[1:]
    packed_count = EXPERTS * CAP
    quarter = packed_count // lax.axis_size("tp")
    if not (
        lax.axis_size("tp") == 4
        and lax.axis_size("req") == 8
        and 8 * slot_dev == EXPERTS
        and row_count == quarter
        and cache_len == lanes == 2 * HEAD_DIM
        and queries.shape[1] == 6 * HEAD_DIM
    ):
        return shards_general(
            resid, queries, new_keys, new_values, k_cache, v_cache, lengths, w_out,
            norm_gain, w_router, routes, w_gate, w_up, w_down,
        )
    bf16, f32 = jnp.bfloat16, jnp.float32
    gain = norm_gain.reshape(1, width)
    own, *sents = call(
        attend_kernel,
        [((row_count, width), f32)] + [((row_count, width), bf16)] * 3,
        [spec(pl.ANY)] * 7,
        [
            pltpu.with_memory_space_constraint(operand, pltpu.HBM)
            for operand in (lengths, queries, new_keys, new_values, k_cache, v_cache, w_out)
        ],
        scratch=[
            pltpu.SMEM(lengths.shape, jnp.int32),
            pltpu.VMEM(queries.shape, bf16),
            pltpu.VMEM(new_keys.shape, bf16),
            pltpu.VMEM(new_values.shape, bf16),
            pltpu.VMEM(k_cache.shape, bf16),
            pltpu.VMEM(v_cache.shape, bf16),
            pltpu.VMEM(w_out.shape, bf16),
            pltpu.VMEM((8 * row_count, lanes), f32),
            pltpu.VMEM((8 * row_count, lanes), f32),
            pltpu.VMEM((8 * row_count, cache_len), f32),
            pltpu.VMEM((8 * row_count, cache_len), bf16),
            pltpu.VMEM((row_count, w_out.shape[1]), f32),
            pltpu.SemaphoreType.DMA((4,)),
            pltpu.SemaphoreType.DMA((3,)),
        ],
        mebibytes=16,
        flops=200_000_000,
        moved=3_400_000,
    )
    def sum_exchange(sents):
        return [partner_permute(block, "tp", k) for k, block in zip(FAR_FIRST[1:], sents)]

    parts = sum_exchange(sents)
    weight = (slot_dev * width, hidden)
    base, pick_rows, pick0, pick1, router_rows, *weights = call(
        functools.partial(ready_kernel, slot_dev),
        [
            ((row_count, width), f32),
            ((packed_count, row_count), bf16),
            ((row_count, packed_count), bf16),
            ((row_count, packed_count), bf16),
            ((row_count, width), f32),
            (weight, bf16),
            (weight, bf16),
        ],
        [spec()] * 4 + [spec(pl.ANY)] * 2,
        (
            own,
            resid,
            routes.T,
            w_router.T,
            pltpu.with_memory_space_constraint(w_gate.reshape(weight), pltpu.HBM),
            pltpu.with_memory_space_constraint(w_up.reshape(weight), pltpu.HBM),
        ),
        scratch=[pltpu.SemaphoreType.DMA((8,))],
        mebibytes=12,
        moved=3_300_000,
    )
    attended, home, *sents = call(
        pack_kernel,
        [((row_count, width), bf16)] + [((quarter, width), bf16)] * 4,
        [spec()] * 5,
        (base, *parts, pick_rows),
    )
    (stats,) = call(
        stats_kernel, [((row_count, 128), f32)], [spec()] * 3, (attended, gain, router_rows)
    )
    (result,) = call(result_kernel, [((row_count, width), bf16)], [spec()], (attended,))
    stats, result = lax.optimization_barrier((stats, result))
    parts = [
        partner_permute(block, "req", 2 * k) for k, block in zip(FAR_FIRST[1:], sents)
    ]
    (turned,) = call(
        turn_kernel, [((2 * quarter, width), bf16)], [spec()] * 4, (home, *parts)
    )
    along = partner_permute(turned, "req", 1)
    lhs = pltpu.VMEM((packed_count // 2, slot_dev * width), bf16)

    pair = (quarter, 2 * hidden + 128)

    def chip_sums(kept, sent):
        return call(
            chip_kernel, [(pair, f32), (pair, bf16)], [spec()] * 2,
            (kept, partner_permute(sent, "tp", 1)),
        )

    kept, sent = call(
        functools.partial(early_kernel, slot_dev),
        [(pair, f32), (pair, bf16)],
        [spec()] * 9,
        (home, *parts, gain, stats, *weights, turned),
        scratch=[pltpu.VMEM((2 * quarter, width), bf16), lhs],
        flops=400_000_000,
        moved=3_500_000,
    )
    early, sent = chip_sums(kept, sent)
    early = (early, partner_permute(sent, "tp", 2))
    kept, sent = call(
        functools.partial(late_kernel, slot_dev),
        [(pair, f32), (pair, bf16)],
        [spec()] * 4,
        (along, gain, *weights),
        scratch=[lhs],
        flops=400_000_000,
        moved=3_500_000,
    )
    late, sent = chip_sums(kept, sent)
    late = (late, partner_permute(sent, "tp", 2))
    own, first_weight = call(
        hidden_kernel,
        [((2 * quarter, hidden), bf16), ((row_count, 128), f32)],
        [spec()] * 4,
        (*late, *early),
    )
    w_down = w_down.reshape(slot_dev * hidden, width)
    block = ((quarter, width), bf16)
    down_scratch = [
        pltpu.VMEM((2 * quarter, slot_dev * hidden), bf16),
        pltpu.VMEM((2 * quarter, width), f32),
    ]
    near, far = call(
        functools.partial(own_down_kernel, slot_dev), [block] * 2, [spec()] * 2, (own, w_down),
        scratch=down_scratch, flops=100_000_000, moved=2_000_000,
    )
    home, second, third = call(
        functools.partial(other_down_kernel, slot_dev), [block] * 3, [spec()] * 3,
        (partner_permute(own, "tp", 1), w_down, near),
        scratch=down_scratch, flops=100_000_000, moved=2_000_000,
    )
    parts = [back_permute(rows, order) for order, rows in enumerate((far, second, third), 1)]
    (along,) = call(
        back_turn_kernel, [((2 * quarter, width), bf16)], [spec()] * 4, (home, *parts)
    )
    (layer_out,) = call(
        combine_kernel,
        [((row_count, width), bf16)],
        [spec()] * 9,
        (
            home, *parts, partner_permute(along, "req", 1), pick0, pick1, first_weight, attended,
        ),
        scratch=[pltpu.VMEM((packed_count, width), bf16)],
    )
    return (result, layer_out)


def solution(mesh):
    placed = (
        P("req", "tp"),
        P("req", "tp"),
        P("req", "tp"),
        P("req", "tp"),
        P("req", None, "tp"),
        P("req", None, "tp"),
        P("req"),
        P("tp", None),
        P("tp"),
        P("tp", None),
        P("req", None),
        P("req", "tp", None),
        P("req", "tp", None),
        P("req", None, "tp"),
    )
    return jax.shard_map(
        shards,
        mesh=mesh,
        in_specs=placed,
        out_specs=(P("req", "tp"), P("req", "tp")),
        check_vma=False,
    )
```

```python
import functools
import math

import jax
import jax.numpy as jnp
from jax import lax
from jax.experimental import pallas as pl
from jax.experimental.pallas import tpu as pltpu
from jax.sharding import PartitionSpec as P

D = 1536
HEAD_DIM = 64
EXPERTS = 16
TOP = 2
CAP = 8


def attend_local(queries, new_keys, new_values, k_cache, v_cache, lengths):
    row_count = queries.shape[0]
    kv_local = new_keys.shape[1] // HEAD_DIM
    group_size = queries.shape[1] // HEAD_DIM // kv_local
    cache_len = k_cache.shape[1]
    score_scale = 1.0 / math.sqrt(HEAD_DIM)
    query = queries.reshape(row_count, kv_local, group_size, HEAD_DIM)
    keys_all = k_cache.reshape(row_count, cache_len, kv_local, HEAD_DIM)
    values_all = v_cache.reshape(row_count, cache_len, kv_local, HEAD_DIM)
    scores = (
        jnp.einsum("bgqd,blgd->bgql", query, keys_all, preferred_element_type=jnp.float32)
        * score_scale
    )
    self_score = (
        jnp.einsum(
            "bgqd,bgd->bgq",
            query,
            new_keys.reshape(row_count, kv_local, HEAD_DIM),
            preferred_element_type=jnp.float32,
        )
        * score_scale
    )
    valid_mask = (jnp.arange(cache_len, dtype=jnp.int32)[None, :] < lengths[:, None])[
        :, None, None, :
    ]
    peak_score = jnp.maximum(jnp.max(jnp.where(valid_mask, scores, -1e30), axis=-1), self_score)
    exp_terms = jnp.where(valid_mask, jnp.exp(scores - peak_score[..., None]), 0.0)
    self_exp = jnp.exp(self_score - peak_score)
    denom_sum = jnp.sum(exp_terms, axis=-1) + self_exp
    weights = (exp_terms / denom_sum[..., None]).astype(jnp.bfloat16)
    self_weight = (self_exp / denom_sum).astype(jnp.bfloat16)
    value_self = new_values.astype(jnp.float32).reshape(row_count, kv_local, 1, HEAD_DIM)
    mixed = (
        jnp.einsum("bgql,blgd->bgqd", weights, values_all, preferred_element_type=jnp.float32)
        + self_weight.astype(jnp.float32)[..., None] * value_self
    )
    return mixed.astype(jnp.bfloat16).reshape(row_count, kv_local * group_size * HEAD_DIM)


def shards_general(
    resid,
    queries,
    new_keys,
    new_values,
    k_cache,
    v_cache,
    lengths,
    w_out,
    norm_gain,
    w_router,
    routes,
    w_gate,
    w_up,
    w_down,
):
    req_dev = resid.shape[0]
    width_local = resid.shape[1]
    slot_dev = w_gate.shape[0]
    req_count = lax.axis_size("req")
    shard_count = max(1, req_count // EXPERTS)
    attention = attend_local(queries, new_keys, new_values, k_cache, v_cache, lengths)
    partial_value = jnp.dot(attention, w_out, preferred_element_type=jnp.float32)
    projected = lax.psum_scatter(partial_value, "tp", scatter_dimension=1, tiled=True)
    attended = (resid.astype(jnp.float32) + projected).astype(jnp.bfloat16)
    attended_f = attended.astype(jnp.float32)
    scaled = attended_f * norm_gain[None, :]
    square_sum, logit_part = lax.psum(
        (
            jnp.sum(attended_f * attended_f, axis=1),
            jnp.dot(scaled, w_router, precision=lax.Precision.HIGHEST),
        ),
        "tp",
    )
    inv_rms = 1.0 / jnp.sqrt(square_sum / D + 1e-06)
    normed = (scaled * inv_rms[:, None]).astype(jnp.bfloat16)
    logits = logit_part * inv_rms[:, None]
    expert_ids = jnp.arange(EXPERTS, dtype=jnp.int32)
    first_logit = jnp.sum(jnp.where(routes[:, 0:1] == expert_ids[None, :], logits, 0.0), axis=1)
    second_logit = jnp.sum(jnp.where(routes[:, 1:2] == expert_ids[None, :], logits, 0.0), axis=1)
    first_weight = jax.nn.sigmoid(first_logit - second_logit)
    second_weight = 1.0 - first_weight
    flat_routes = routes.reshape(req_dev * TOP)
    one_hot = (flat_routes[None, :] == expert_ids[:, None]).astype(jnp.int32)
    rank_in = jnp.cumsum(one_hot, axis=1) - one_hot
    slot_ids = jnp.arange(CAP, dtype=jnp.int32)
    chosen = (one_hot[:, None, :] == 1) & (rank_in[:, None, :] == slot_ids[None, :, None])
    token_pick = jnp.sum(
        chosen.reshape(EXPERTS, CAP, req_dev, TOP).astype(jnp.int32), axis=-1
    ).astype(jnp.bfloat16)
    per_expert = jnp.einsum(
        "ecb,bd->ecd", token_pick, normed, preferred_element_type=jnp.float32
    ).astype(jnp.bfloat16)
    outgoing = jnp.broadcast_to(
        per_expert[:, None], (EXPERTS, shard_count, CAP, width_local)
    ).reshape(req_count, slot_dev, CAP, width_local)
    incoming = lax.all_to_all(outgoing, "req", split_axis=0, concat_axis=0, tiled=True)
    gate_pre = jnp.einsum("nscd,sdf->nscf", incoming, w_gate, preferred_element_type=jnp.float32)
    up_pre = jnp.einsum("nscd,sdf->nscf", incoming, w_up, preferred_element_type=jnp.float32)
    gate_sum, up_sum = lax.psum((gate_pre, up_pre), "tp")
    hidden = (jax.nn.silu(gate_sum) * up_sum).astype(jnp.bfloat16)
    computed = jnp.einsum("nscf,sfd->nscd", hidden, w_down, preferred_element_type=jnp.float32)
    returned = lax.all_to_all(computed, "req", split_axis=0, concat_axis=0, tiled=True)
    combined = jnp.sum(returned.reshape(EXPERTS, shard_count, CAP, width_local), axis=1)
    route_out = jnp.einsum(
        "ecr,ecd->rd", chosen.astype(jnp.float32), combined, precision=lax.Precision.HIGHEST
    ).reshape(req_dev, TOP, width_local)
    moe = first_weight[:, None] * route_out[:, 0] + second_weight[:, None] * route_out[:, 1]
    layer_out = (attended_f + moe).astype(jnp.bfloat16)
    return (attended, layer_out)


FAR_FIRST = (0, 2, 3, 1)


def spec(space=pltpu.VMEM):
    return pl.BlockSpec(memory_space=space)


def call(kernel, outs, ins, operands, scratch=(), mebibytes=8, flops=100_000, moved=100_000):
    return pl.pallas_call(
        kernel,
        out_shape=[jax.ShapeDtypeStruct(shape, dtype) for shape, dtype in outs],
        in_specs=ins,
        out_specs=[spec() for _ in outs],
        scratch_shapes=scratch,
        compiler_params=pltpu.CompilerParams(vmem_limit_bytes=mebibytes << 20),
        cost_estimate=pl.CostEstimate(flops=flops, bytes_accessed=moved, transcendentals=0),
    )(*operands)


def partner_permute(block, axis, distance):
    count = lax.axis_size(axis)
    return lax.ppermute(block, axis, [(i, i ^ distance) for i in range(count)])


def attend_kernel(
    lengths_hbm, queries_hbm, keys_hbm, values_hbm, k_hbm, v_hbm, w_hbm, own, sent1, sent2, sent3,
    lengths, queries, new_keys, new_values, k_buf, v_buf, w_buf,
    query_s, self_s, score_s, weight_s, product_s, small_sems, sems,
):
    row_count = queries.shape[0]
    width = own.shape[1]
    lanes = 2 * HEAD_DIM
    cache_len = k_hbm.shape[1]
    chunks = 1
    small = [
        pltpu.make_async_copy(source, target, small_sems.at[index])
        for index, (source, target) in enumerate(
            (
                (queries_hbm, queries),
                (keys_hbm, new_keys),
                (values_hbm, new_values),
                (lengths_hbm, lengths),
            )
        )
    ]
    copies = []
    for source, target in ((k_hbm, k_buf), (v_hbm, v_buf), (w_hbm, w_buf)):
        size = source.shape[0] // chunks
        for chunk in range(chunks):
            part = pl.ds(chunk * size, size)
            copies.append(
                pltpu.make_async_copy(source.at[part], target.at[part], sems.at[len(copies)])
            )
    for copy in small + copies:
        copy.start()

    for copy in small:
        copy.wait()

    low = lax.broadcasted_iota(jnp.int32, (row_count, lanes), 1) < HEAD_DIM
    tiles = [queries[:, i * lanes : (i + 1) * lanes].astype(jnp.float32) for i in range(3)]
    heads = [
        jnp.where(low, tiles[0], 0.0),
        jnp.where(low, pltpu.roll(tiles[0], HEAD_DIM, 1), 0.0),
        jnp.where(low, tiles[1], 0.0),
        jnp.where(low, 0.0, tiles[1]),
        jnp.where(low, 0.0, pltpu.roll(tiles[2], HEAD_DIM, 1)),
        jnp.where(low, 0.0, tiles[2]),
    ]
    scale = 1.0 / math.sqrt(HEAD_DIM)
    for head in range(8):
        rows = pl.ds(head, row_count, stride=8)
        query_s[rows, :] = heads[head] if head < 6 else jnp.zeros((row_count, lanes), jnp.float32)

    row_of = lax.broadcasted_iota(jnp.int32, (8 * row_count, row_count), 0)
    request_of = lax.broadcasted_iota(jnp.int32, (8 * row_count, row_count), 1)
    spread = jnp.where(row_of // 8 == request_of, 1.0, 0.0).astype(jnp.bfloat16)
    keys_new = jnp.dot(spread, new_keys[...], preferred_element_type=jnp.float32)
    values_new = jnp.dot(spread, new_values[...], preferred_element_type=jnp.float32)
    own_score = jnp.sum(query_s[...] * keys_new, axis=1, keepdims=True) * scale

    upper = lax.broadcasted_iota(jnp.int32, (16, lanes), 0) < 8
    position = lax.broadcasted_iota(jnp.int32, (16, cache_len), 1)
    for copy in copies[:chunks]:
        copy.wait()
    for pair in range(row_count // 2):
        pair_rows = slice(16 * pair, 16 * pair + 16)
        keys = k_buf[2 * pair : 2 * pair + 2].reshape(2 * cache_len, lanes)
        raw = lax.dot_general(
            query_s[pair_rows, :].astype(jnp.bfloat16), keys, (((1,), (1,)), ((), ())),
            preferred_element_type=jnp.float32,
        )
        limit = jnp.where(upper, lengths[2 * pair], lengths[2 * pair + 1])
        score_s[pair_rows, :] = jnp.where(
            position < limit,
            jnp.where(upper, raw[:, :cache_len], raw[:, cache_len:]) * scale,
            -1e30,
        )

    scores = score_s[...]
    peak = jnp.maximum(jnp.max(scores, axis=1, keepdims=True), own_score)
    terms = jnp.exp(scores - peak)
    own_term = jnp.exp(own_score - peak)
    inverse = 1.0 / (jnp.sum(terms, axis=1, keepdims=True) + own_term)
    weight_s[...] = (terms * inverse).astype(jnp.bfloat16)
    own_weight = (own_term * inverse).astype(jnp.bfloat16).astype(jnp.float32)
    self_s[...] = own_weight * values_new
    for copy in copies[chunks:]:
        copy.wait()
    for pair in range(row_count // 2):
        pair_rows = slice(16 * pair, 16 * pair + 16)
        values = jnp.concatenate([v_buf[2 * pair], v_buf[2 * pair + 1]], axis=1)
        mixed = jnp.dot(weight_s[pair_rows, :], values, preferred_element_type=jnp.float32)
        query_s[pair_rows, :] = (
            jnp.where(upper, mixed[:, :lanes], mixed[:, lanes:]) + self_s[pair_rows, :]
        )

    mixed = [query_s[pl.ds(head, row_count, stride=8), :] for head in range(6)]
    attention = jnp.concatenate(
        [
            jnp.where(low, mixed[0], pltpu.roll(mixed[1], HEAD_DIM, 1)),
            jnp.where(low, mixed[2], mixed[3]),
            jnp.where(low, pltpu.roll(mixed[4], HEAD_DIM, 1), mixed[5]),
        ],
        axis=1,
    ).astype(jnp.bfloat16)
    place_tp = lax.axis_index("tp")
    product_s[...] = jnp.dot(attention, w_buf[...], preferred_element_type=jnp.float32)
    for shift, out in zip(FAR_FIRST, (own, sent1, sent2, sent3)):
        columns = pl.ds(pl.multiple_of((place_tp ^ shift) * width, width), width)
        out[...] = product_s[:, columns].astype(out.dtype)


def ready_kernel(
    slot_dev, own, resid, routes, w_router, gate_hbm, up_hbm,
    base, pick_rows, pick0, pick1, router_rows, w_gate, w_up, sems,
):
    copies = []
    for source, target in ((gate_hbm, w_gate), (up_hbm, w_up)):
        size = source.shape[0] // 4
        for chunk in range(4):
            part = pl.ds(chunk * size, size)
            copies.append(
                pltpu.make_async_copy(source.at[part], target.at[part], sems.at[len(copies)])
            )
    for copy in copies:
        copy.start()
    base[...] = own[...] + resid[...].astype(jnp.float32)
    packed_count, row_count = pick_rows.shape

    route0, route1 = routes[0:1, :], routes[1:2, :]
    place = lax.broadcasted_iota(jnp.int32, (packed_count, row_count), 0)
    named0 = jnp.where(place == route0, 1.0, 0.0)
    named1 = jnp.where(place == route1, 1.0, 0.0)
    row_of = lax.broadcasted_iota(jnp.int32, (row_count, row_count), 0)
    col_of = lax.broadcasted_iota(jnp.int32, (row_count, row_count), 1)
    earlier = jnp.where(row_of < col_of, 1.0, 0.0).astype(jnp.bfloat16)
    before = jnp.dot(
        (named0 + named1).astype(jnp.bfloat16), earlier, preferred_element_type=jnp.float32
    )
    place_req = lax.axis_index("req")

    def pick(route, named):
        rank = jnp.sum(named * before, axis=0, keepdims=True).astype(jnp.int32)
        block = ((route // slot_dev) ^ place_req) * slot_dev + lax.rem(route, slot_dev)
        return jnp.where(place == block * CAP + rank, 1.0, 0.0)

    first, second = pick(route0, named0), pick(route1, named1)
    pick_rows[...] = (first + second).astype(jnp.bfloat16)
    pick0[...] = jnp.transpose(first).astype(jnp.bfloat16)
    pick1[...] = jnp.transpose(second).astype(jnp.bfloat16)
    signed = jnp.transpose(named0 - named1)
    router_rows[...] = jnp.dot(
        signed[:, :EXPERTS], w_router[...],
        precision=lax.Precision.HIGHEST, preferred_element_type=jnp.float32,
    )
    for copy in copies:
        copy.wait()


def pack_kernel(base, part1, part2, part3, pick_rows, attended, home, sent1, sent2, sent3):
    total = base[...]
    for part in (part1, part2, part3):
        total = total + part[...].astype(jnp.float32)
    rows = total.astype(jnp.bfloat16)
    attended[...] = rows
    packed = jnp.dot(pick_rows[...], rows, preferred_element_type=jnp.float32)
    size = home.shape[0]
    for distance, out in zip(FAR_FIRST, (home, sent1, sent2, sent3)):
        out[...] = packed[distance * size : (distance + 1) * size].astype(out.dtype)


def result_kernel(attended, result):
    result[...] = attended[...]


def stats_kernel(attended, gain, router_rows, stats):
    rows = attended[...].astype(jnp.float32)
    square = jnp.sum(rows * rows, axis=1, keepdims=True)
    logit = jnp.sum(rows * gain[...] * router_rows[...], axis=1, keepdims=True)
    lane = lax.broadcasted_iota(jnp.int32, stats.shape, 1)
    stats[...] = jnp.where(lane == 0, square, jnp.where(lane == 1, logit, 0.0))


def turn_kernel(home, part1, part2, part3, along):
    half = home.shape[0] // 2
    for index, part in zip(FAR_FIRST, (home, part1, part2, part3)):
        along[index * half : (index + 1) * half, :] = part[half:, :]


def slot_masks(row_count, slot_dev):
    slot = lax.rem(lax.broadcasted_iota(jnp.int32, (row_count, 1), 0) // CAP, slot_dev)
    return [slot == index for index in range(slot_dev)]


def split_high(column):
    high = column.astype(jnp.bfloat16).astype(jnp.float32)
    return high, column - high


def gate_terms(slot_dev, blocks, gain, stats, w_gate, w_up, kept, sent, lhs):
    size = kept.shape[0] // 2
    width = blocks.shape[1]
    hidden = w_gate.shape[1]
    place_tp = lax.axis_index("tp")
    masks = slot_masks(size, slot_dev)
    lane = lax.broadcasted_iota(jnp.int32, (size, 128), 1)
    for order, shift in enumerate((0, 2, 1, 3)):
        out, first_row = (kept, sent)[order // 2], order % 2 * size
        rows = blocks[
            pl.ds(pl.multiple_of((place_tp ^ shift) * size, size), size), :
        ].astype(jnp.float32)
        columns = [jnp.sum(rows * rows, axis=1, keepdims=True)]
        if stats is not None:
            for first in range(0, stats.shape[0], size):
                columns += [stats[first : first + size, 0:1], stats[first : first + size, 1:2]]
        extra = jnp.zeros((size, 128), jnp.float32)
        for index, column in enumerate(columns):
            high, low = split_high(column)
            extra = jnp.where(lane == 2 * index, high, extra)
            extra = jnp.where(lane == 2 * index + 1, low, extra)
        out[first_row : first_row + size, 2 * hidden :] = extra.astype(out.dtype)
        scaled = rows * gain[...]
        for index, mask in enumerate(masks):
            lhs[order * size : (order + 1) * size, index * width : (index + 1) * width] = (
                jnp.where(mask, scaled, 0.0).astype(jnp.bfloat16)
            )
    left = lhs[...]
    for first, weight in ((0, w_gate), (hidden, w_up)):
        product = jnp.dot(left, weight[...], preferred_element_type=jnp.float32)
        kept[:, first : first + hidden] = product[: 2 * size]
        sent[:, first : first + hidden] = product[2 * size :].astype(sent.dtype)


def early_kernel(
    slot_dev, in0, in1, in2, in3, gain, stats, w_gate, w_up, turned, kept, sent, blocks, lhs
):
    del turned
    half = kept.shape[0] // 2
    for index, part in zip(FAR_FIRST, (in0, in1, in2, in3)):
        blocks[index * half : (index + 1) * half, :] = part[:half, :]
    gate_terms(slot_dev, blocks, gain, stats, w_gate, w_up, kept, sent, lhs)


def late_kernel(slot_dev, blocks, gain, w_gate, w_up, kept, sent, lhs):
    gate_terms(slot_dev, blocks, gain, None, w_gate, w_up, kept, sent, lhs)


def chip_kernel(kept, part, own, sent):
    size, width = own.shape[0] // 2, own.shape[1]
    total = kept[...] + part[...].astype(jnp.float32)
    own[...] = total
    extra = total[:, width - 128 :]
    lane = lax.broadcasted_iota(jnp.int32, extra.shape, 1)
    high, low = split_high(extra + pltpu.roll(extra, 127, 1))
    extra = jnp.where(lax.rem(lane, 2) == 0, high, pltpu.roll(low, 1, 1))
    for target, source in ((0, size), (size, 0)):
        sent[target : target + size, : width - 128] = total[
            source : source + size, : width - 128
        ].astype(sent.dtype)
        sent[target : target + size, width - 128 :] = extra[source : source + size].astype(
            sent.dtype
        )


def hidden_kernel(*refs):
    late, early, (hidden, first_weight) = refs[:2], refs[2:4], refs[4:]
    width = hidden.shape[1]
    half = hidden.shape[0] // 4

    def total(parts, columns):
        result = parts[0][:, columns]
        for part in parts[1:]:
            result = result + part[:, columns].astype(jnp.float32)
        return result

    def inverse_rms(columns, index):
        square = columns[:, index : index + 1] + columns[:, index + 1 : index + 2]
        return 1.0 / jnp.sqrt(square / D + 1e-06)

    for index, parts in ((1, late), (0, early)):
        extra = total(parts, slice(2 * width, 2 * width + 128))
        row_inv = inverse_rms(extra, 0)
        gate = total(parts, slice(0, width)) * row_inv
        up = total(parts, slice(width, 2 * width)) * row_inv
        rows = (gate / (1.0 + jnp.exp(-gate)) * up).astype(jnp.bfloat16)
        for block in range(2):
            start = (2 * block + index) * half
            hidden[start : start + half, :] = rows[block * half : (block + 1) * half]
    extra = extra[:half]
    for index in range(first_weight.shape[0] // half):
        place = 2 + 4 * index
        logit = extra[:, place + 2 : place + 3] + extra[:, place + 3 : place + 4]
        weight = 1.0 / (1.0 + jnp.exp(-logit * inverse_rms(extra, place)))
        first_weight[index * half : (index + 1) * half, :] = jnp.broadcast_to(weight, (half, 128))


BACK = ((0, 2, 3, 1), (0, 3, 1, 2))


def down_rows(slot_dev, hidden, w_down, lhs, product):
    count, width = hidden.shape
    rows = hidden[...].astype(jnp.float32)
    for index, mask in enumerate(slot_masks(count, slot_dev)):
        lhs[:, index * width : (index + 1) * width] = jnp.where(mask, rows, 0.0).astype(
            jnp.bfloat16
        )
    product[...] = jnp.dot(lhs[...], w_down[...], preferred_element_type=jnp.float32)
    half = count // 2
    upper = lax.axis_index("tp") // 2
    near = pl.ds(pl.multiple_of(upper * half, half), half)
    far = pl.ds(pl.multiple_of((1 - upper) * half, half), half)
    return product[near, :], product[far, :]


def own_down_kernel(slot_dev, hidden, w_down, near, far, lhs, product):
    results = down_rows(slot_dev, hidden, w_down, lhs, product)
    for out, rows in zip((near, far), results):
        out[...] = rows.astype(out.dtype)


def other_down_kernel(slot_dev, hidden, w_down, own_near, home, second, third, lhs, product):
    near, far = down_rows(slot_dev, hidden, w_down, lhs, product)
    own = own_near[...].astype(jnp.float32)
    first_core = lax.rem(lax.axis_index("tp"), 2) == 0
    home[...] = jnp.where(first_core, own, near).astype(home.dtype)
    second[...] = jnp.where(first_core, far, own).astype(second.dtype)
    third[...] = jnp.where(first_core, near, far).astype(third.dtype)


def back_permute(block, order):
    reqs, tps = lax.axis_size("req"), lax.axis_size("tp")
    pairs = [
        (req * tps + tp, (req ^ (2 * BACK[tp % 2][order])) * tps + tp)
        for req in range(reqs)
        for tp in range(tps)
    ]
    return lax.ppermute(block, ("req", "tp"), pairs)


def back_turn_kernel(home, part1, part2, part3, along):
    half = home.shape[0] // 2
    for index, part in enumerate((home, part1, part2, part3)):
        along[index * half : (index + 1) * half, :] = part[half:, :]


def combine_kernel(
    home, part1, part2, part3, along, pick0, pick1, first_weight, attended, layer_out, returned
):
    half = home.shape[0] // 2
    core = lax.rem(lax.axis_index("tp"), 2)
    for index, part in enumerate((home, part1, part2, part3)):
        distance = jnp.where(core == 0, BACK[0][index], BACK[1][index])
        start = pl.multiple_of(distance * 2 * half, 2 * half)
        returned[pl.ds(start, half), :] = part[:half, :]
        returned[pl.ds(start + half, half), :] = along[index * half : (index + 1) * half, :]
    rows = returned[...]
    out0 = jnp.dot(pick0[...], rows, preferred_element_type=jnp.float32)
    out1 = jnp.dot(pick1[...], rows, preferred_element_type=jnp.float32)
    weight = first_weight[:, 0:1]
    moe = weight * out0 + (1.0 - weight) * out1
    layer_out[...] = (attended[...].astype(jnp.float32) + moe).astype(jnp.bfloat16)


def shards(
    resid,
    queries,
    new_keys,
    new_values,
    k_cache,
    v_cache,
    lengths,
    w_out,
    norm_gain,
    w_router,
    routes,
    w_gate,
    w_up,
    w_down,
):
    row_count, width = resid.shape
    slot_dev, _, hidden = w_gate.shape
    cache_len, lanes = k_cache.shape[1:]
    packed_count = EXPERTS * CAP
    quarter = packed_count // lax.axis_size("tp")
    if not (
        lax.axis_size("tp") == 4
        and lax.axis_size("req") == 8
        and 8 * slot_dev == EXPERTS
        and row_count == quarter
        and cache_len == lanes == 2 * HEAD_DIM
        and queries.shape[1] == 6 * HEAD_DIM
    ):
        return shards_general(
            resid, queries, new_keys, new_values, k_cache, v_cache, lengths, w_out,
            norm_gain, w_router, routes, w_gate, w_up, w_down,
        )
    bf16, f32 = jnp.bfloat16, jnp.float32
    gain = norm_gain.reshape(1, width)
    own, *sents = call(
        attend_kernel,
        [((row_count, width), f32)] + [((row_count, width), bf16)] * 3,
        [spec(pl.ANY)] * 7,
        [
            pltpu.with_memory_space_constraint(operand, pltpu.HBM)
            for operand in (lengths, queries, new_keys, new_values, k_cache, v_cache, w_out)
        ],
        scratch=[
            pltpu.SMEM(lengths.shape, jnp.int32),
            pltpu.VMEM(queries.shape, bf16),
            pltpu.VMEM(new_keys.shape, bf16),
            pltpu.VMEM(new_values.shape, bf16),
            pltpu.VMEM(k_cache.shape, bf16),
            pltpu.VMEM(v_cache.shape, bf16),
            pltpu.VMEM(w_out.shape, bf16),
            pltpu.VMEM((8 * row_count, lanes), f32),
            pltpu.VMEM((8 * row_count, lanes), f32),
            pltpu.VMEM((8 * row_count, cache_len), f32),
            pltpu.VMEM((8 * row_count, cache_len), bf16),
            pltpu.VMEM((row_count, w_out.shape[1]), f32),
            pltpu.SemaphoreType.DMA((4,)),
            pltpu.SemaphoreType.DMA((3,)),
        ],
        mebibytes=16,
        flops=200_000_000,
        moved=3_400_000,
    )
    def sum_exchange(sents):
        return [partner_permute(block, "tp", k) for k, block in zip(FAR_FIRST[1:], sents)]

    parts = sum_exchange(sents)
    weight = (slot_dev * width, hidden)
    base, pick_rows, pick0, pick1, router_rows, *weights = call(
        functools.partial(ready_kernel, slot_dev),
        [
            ((row_count, width), f32),
            ((packed_count, row_count), bf16),
            ((row_count, packed_count), bf16),
            ((row_count, packed_count), bf16),
            ((row_count, width), f32),
            (weight, bf16),
            (weight, bf16),
        ],
        [spec()] * 4 + [spec(pl.ANY)] * 2,
        (
            own,
            resid,
            routes.T,
            w_router.T,
            pltpu.with_memory_space_constraint(w_gate.reshape(weight), pltpu.HBM),
            pltpu.with_memory_space_constraint(w_up.reshape(weight), pltpu.HBM),
        ),
        scratch=[pltpu.SemaphoreType.DMA((8,))],
        mebibytes=12,
        moved=3_300_000,
    )
    attended, home, *sents = call(
        pack_kernel,
        [((row_count, width), bf16)] + [((quarter, width), bf16)] * 4,
        [spec()] * 5,
        (base, *parts, pick_rows),
    )
    (stats,) = call(
        stats_kernel, [((row_count, 128), f32)], [spec()] * 3, (attended, gain, router_rows)
    )
    (result,) = call(result_kernel, [((row_count, width), bf16)], [spec()], (attended,))
    stats, result = lax.optimization_barrier((stats, result))
    parts = [
        partner_permute(block, "req", 2 * k) for k, block in zip(FAR_FIRST[1:], sents)
    ]
    (turned,) = call(
        turn_kernel, [((2 * quarter, width), bf16)], [spec()] * 4, (home, *parts)
    )
    along = partner_permute(turned, "req", 1)
    lhs = pltpu.VMEM((packed_count // 2, slot_dev * width), bf16)

    pair = (quarter, 2 * hidden + 128)

    def chip_sums(kept, sent):
        return call(
            chip_kernel, [(pair, f32), (pair, bf16)], [spec()] * 2,
            (kept, partner_permute(sent, "tp", 1)),
        )

    kept, sent = call(
        functools.partial(early_kernel, slot_dev),
        [(pair, f32), (pair, bf16)],
        [spec()] * 9,
        (home, *parts, gain, stats, *weights, turned),
        scratch=[pltpu.VMEM((2 * quarter, width), bf16), lhs],
        flops=400_000_000,
        moved=3_500_000,
    )
    early, sent = chip_sums(kept, sent)
    early = (early, partner_permute(sent, "tp", 2))
    kept, sent = call(
        functools.partial(late_kernel, slot_dev),
        [(pair, f32), (pair, bf16)],
        [spec()] * 4,
        (along, gain, *weights),
        scratch=[lhs],
        flops=400_000_000,
        moved=3_500_000,
    )
    late, sent = chip_sums(kept, sent)
    late = (late, partner_permute(sent, "tp", 2))
    own, first_weight = call(
        hidden_kernel,
        [((2 * quarter, hidden), bf16), ((row_count, 128), f32)],
        [spec()] * 4,
        (*late, *early),
    )
    w_down = w_down.reshape(slot_dev * hidden, width)
    block = ((quarter, width), bf16)
    down_scratch = [
        pltpu.VMEM((2 * quarter, slot_dev * hidden), bf16),
        pltpu.VMEM((2 * quarter, width), f32),
    ]
    near, far = call(
        functools.partial(own_down_kernel, slot_dev), [block] * 2, [spec()] * 2, (own, w_down),
        scratch=down_scratch, flops=100_000_000, moved=2_000_000,
    )
    home, second, third = call(
        functools.partial(other_down_kernel, slot_dev), [block] * 3, [spec()] * 3,
        (partner_permute(own, "tp", 1), w_down, near),
        scratch=down_scratch, flops=100_000_000, moved=2_000_000,
    )
    parts = [back_permute(rows, order) for order, rows in enumerate((far, second, third), 1)]
    (along,) = call(
        back_turn_kernel, [((2 * quarter, width), bf16)], [spec()] * 4, (home, *parts)
    )
    (layer_out,) = call(
        combine_kernel,
        [((row_count, width), bf16)],
        [spec()] * 9,
        (
            home, *parts, partner_permute(along, "req", 1), pick0, pick1, first_weight, attended,
        ),
        scratch=[pltpu.VMEM((packed_count, width), bf16)],
    )
    return (result, layer_out)


def solution(mesh):
    placed = (
        P("req", "tp"),
        P("req", "tp"),
        P("req", "tp"),
        P("req", "tp"),
        P("req", None, "tp"),
        P("req", None, "tp"),
        P("req"),
        P("tp", None),
        P("tp"),
        P("tp", None),
        P("req", None),
        P("req", "tp", None),
        P("req", "tp", None),
        P("req", None, "tp"),
    )
    return jax.shard_map(
        shards,
        mesh=mesh,
        in_specs=placed,
        out_specs=(P("req", "tp"), P("req", "tp")),
        check_vma=False,
    )
```

```python
import functools
import math

import jax
import jax.numpy as jnp
from jax import lax
from jax.experimental import pallas as pl
from jax.experimental.pallas import tpu as pltpu
from jax.sharding import PartitionSpec as P

D = 1536
HEAD_DIM = 64
EXPERTS = 16
TOP = 2
CAP = 8


def attend_local(queries, new_keys, new_values, k_cache, v_cache, lengths):
    row_count = queries.shape[0]
    kv_local = new_keys.shape[1] // HEAD_DIM
    group_size = queries.shape[1] // HEAD_DIM // kv_local
    cache_len = k_cache.shape[1]
    score_scale = 1.0 / math.sqrt(HEAD_DIM)
    query = queries.reshape(row_count, kv_local, group_size, HEAD_DIM)
    keys_all = k_cache.reshape(row_count, cache_len, kv_local, HEAD_DIM)
    values_all = v_cache.reshape(row_count, cache_len, kv_local, HEAD_DIM)
    scores = (
        jnp.einsum("bgqd,blgd->bgql", query, keys_all, preferred_element_type=jnp.float32)
        * score_scale
    )
    self_score = (
        jnp.einsum(
            "bgqd,bgd->bgq",
            query,
            new_keys.reshape(row_count, kv_local, HEAD_DIM),
            preferred_element_type=jnp.float32,
        )
        * score_scale
    )
    valid_mask = (jnp.arange(cache_len, dtype=jnp.int32)[None, :] < lengths[:, None])[
        :, None, None, :
    ]
    peak_score = jnp.maximum(jnp.max(jnp.where(valid_mask, scores, -1e30), axis=-1), self_score)
    exp_terms = jnp.where(valid_mask, jnp.exp(scores - peak_score[..., None]), 0.0)
    self_exp = jnp.exp(self_score - peak_score)
    denom_sum = jnp.sum(exp_terms, axis=-1) + self_exp
    weights = (exp_terms / denom_sum[..., None]).astype(jnp.bfloat16)
    self_weight = (self_exp / denom_sum).astype(jnp.bfloat16)
    value_self = new_values.astype(jnp.float32).reshape(row_count, kv_local, 1, HEAD_DIM)
    mixed = (
        jnp.einsum("bgql,blgd->bgqd", weights, values_all, preferred_element_type=jnp.float32)
        + self_weight.astype(jnp.float32)[..., None] * value_self
    )
    return mixed.astype(jnp.bfloat16).reshape(row_count, kv_local * group_size * HEAD_DIM)


def shards_general(
    resid,
    queries,
    new_keys,
    new_values,
    k_cache,
    v_cache,
    lengths,
    w_out,
    norm_gain,
    w_router,
    routes,
    w_gate,
    w_up,
    w_down,
):
    req_dev = resid.shape[0]
    width_local = resid.shape[1]
    slot_dev = w_gate.shape[0]
    req_count = lax.axis_size("req")
    shard_count = max(1, req_count // EXPERTS)
    attention = attend_local(queries, new_keys, new_values, k_cache, v_cache, lengths)
    partial_value = jnp.dot(attention, w_out, preferred_element_type=jnp.float32)
    projected = lax.psum_scatter(partial_value, "tp", scatter_dimension=1, tiled=True)
    attended = (resid.astype(jnp.float32) + projected).astype(jnp.bfloat16)
    attended_f = attended.astype(jnp.float32)
    scaled = attended_f * norm_gain[None, :]
    square_sum, logit_part = lax.psum(
        (
            jnp.sum(attended_f * attended_f, axis=1),
            jnp.dot(scaled, w_router, precision=lax.Precision.HIGHEST),
        ),
        "tp",
    )
    inv_rms = 1.0 / jnp.sqrt(square_sum / D + 1e-06)
    normed = (scaled * inv_rms[:, None]).astype(jnp.bfloat16)
    logits = logit_part * inv_rms[:, None]
    expert_ids = jnp.arange(EXPERTS, dtype=jnp.int32)
    first_logit = jnp.sum(jnp.where(routes[:, 0:1] == expert_ids[None, :], logits, 0.0), axis=1)
    second_logit = jnp.sum(jnp.where(routes[:, 1:2] == expert_ids[None, :], logits, 0.0), axis=1)
    first_weight = jax.nn.sigmoid(first_logit - second_logit)
    second_weight = 1.0 - first_weight
    flat_routes = routes.reshape(req_dev * TOP)
    one_hot = (flat_routes[None, :] == expert_ids[:, None]).astype(jnp.int32)
    rank_in = jnp.cumsum(one_hot, axis=1) - one_hot
    slot_ids = jnp.arange(CAP, dtype=jnp.int32)
    chosen = (one_hot[:, None, :] == 1) & (rank_in[:, None, :] == slot_ids[None, :, None])
    token_pick = jnp.sum(
        chosen.reshape(EXPERTS, CAP, req_dev, TOP).astype(jnp.int32), axis=-1
    ).astype(jnp.bfloat16)
    per_expert = jnp.einsum(
        "ecb,bd->ecd", token_pick, normed, preferred_element_type=jnp.float32
    ).astype(jnp.bfloat16)
    outgoing = jnp.broadcast_to(
        per_expert[:, None], (EXPERTS, shard_count, CAP, width_local)
    ).reshape(req_count, slot_dev, CAP, width_local)
    incoming = lax.all_to_all(outgoing, "req", split_axis=0, concat_axis=0, tiled=True)
    gate_pre = jnp.einsum("nscd,sdf->nscf", incoming, w_gate, preferred_element_type=jnp.float32)
    up_pre = jnp.einsum("nscd,sdf->nscf", incoming, w_up, preferred_element_type=jnp.float32)
    gate_sum, up_sum = lax.psum((gate_pre, up_pre), "tp")
    hidden = (jax.nn.silu(gate_sum) * up_sum).astype(jnp.bfloat16)
    computed = jnp.einsum("nscf,sfd->nscd", hidden, w_down, preferred_element_type=jnp.float32)
    returned = lax.all_to_all(computed, "req", split_axis=0, concat_axis=0, tiled=True)
    combined = jnp.sum(returned.reshape(EXPERTS, shard_count, CAP, width_local), axis=1)
    route_out = jnp.einsum(
        "ecr,ecd->rd", chosen.astype(jnp.float32), combined, precision=lax.Precision.HIGHEST
    ).reshape(req_dev, TOP, width_local)
    moe = first_weight[:, None] * route_out[:, 0] + second_weight[:, None] * route_out[:, 1]
    layer_out = (attended_f + moe).astype(jnp.bfloat16)
    return (attended, layer_out)


FAR_FIRST = (0, 2, 3, 1)


def spec(space=pltpu.VMEM):
    return pl.BlockSpec(memory_space=space)


def call(kernel, outs, ins, operands, scratch=(), mebibytes=8, flops=100_000, moved=100_000):
    return pl.pallas_call(
        kernel,
        out_shape=[jax.ShapeDtypeStruct(shape, dtype) for shape, dtype in outs],
        in_specs=ins,
        out_specs=[spec() for _ in outs],
        scratch_shapes=scratch,
        compiler_params=pltpu.CompilerParams(vmem_limit_bytes=mebibytes << 20),
        cost_estimate=pl.CostEstimate(flops=flops, bytes_accessed=moved, transcendentals=0),
    )(*operands)


def partner_permute(block, axis, distance):
    count = lax.axis_size(axis)
    return lax.ppermute(block, axis, [(i, i ^ distance) for i in range(count)])


def attend_kernel(
    lengths_hbm, queries_hbm, keys_hbm, values_hbm, k_hbm, v_hbm, w_hbm, own, sent1, sent2, sent3,
    lengths, queries, new_keys, new_values, k_buf, v_buf, w_buf,
    query_s, self_s, score_s, weight_s, product_s, small_sems, sems,
):
    row_count = queries.shape[0]
    width = own.shape[1]
    lanes = 2 * HEAD_DIM
    cache_len = k_hbm.shape[1]
    chunks = 1
    small = [
        pltpu.make_async_copy(source, target, small_sems.at[index])
        for index, (source, target) in enumerate(
            (
                (queries_hbm, queries),
                (keys_hbm, new_keys),
                (values_hbm, new_values),
                (lengths_hbm, lengths),
            )
        )
    ]
    copies = []
    for source, target in ((k_hbm, k_buf), (v_hbm, v_buf), (w_hbm, w_buf)):
        size = source.shape[0] // chunks
        for chunk in range(chunks):
            part = pl.ds(chunk * size, size)
            copies.append(
                pltpu.make_async_copy(source.at[part], target.at[part], sems.at[len(copies)])
            )
    for copy in copies[:chunks] + small + copies[chunks:]:
        copy.start()

    for copy in small:
        copy.wait()

    low = lax.broadcasted_iota(jnp.int32, (row_count, lanes), 1) < HEAD_DIM
    tiles = [queries[:, i * lanes : (i + 1) * lanes].astype(jnp.float32) for i in range(3)]
    heads = [
        jnp.where(low, tiles[0], 0.0),
        jnp.where(low, pltpu.roll(tiles[0], HEAD_DIM, 1), 0.0),
        jnp.where(low, tiles[1], 0.0),
        jnp.where(low, 0.0, tiles[1]),
        jnp.where(low, 0.0, pltpu.roll(tiles[2], HEAD_DIM, 1)),
        jnp.where(low, 0.0, tiles[2]),
    ]
    scale = 1.0 / math.sqrt(HEAD_DIM)
    for head in range(8):
        rows = pl.ds(head, row_count, stride=8)
        query_s[rows, :] = heads[head] if head < 6 else jnp.zeros((row_count, lanes), jnp.float32)

    row_of = lax.broadcasted_iota(jnp.int32, (8 * row_count, row_count), 0)
    request_of = lax.broadcasted_iota(jnp.int32, (8 * row_count, row_count), 1)
    spread = jnp.where(row_of // 8 == request_of, 1.0, 0.0).astype(jnp.bfloat16)
    keys_new = jnp.dot(spread, new_keys[...], preferred_element_type=jnp.float32)
    values_new = jnp.dot(spread, new_values[...], preferred_element_type=jnp.float32)
    own_score = jnp.sum(query_s[...] * keys_new, axis=1, keepdims=True) * scale

    upper = lax.broadcasted_iota(jnp.int32, (16, lanes), 0) < 8
    position = lax.broadcasted_iota(jnp.int32, (16, cache_len), 1)
    for copy in copies[:chunks]:
        copy.wait()
    for pair in range(row_count // 2):
        pair_rows = slice(16 * pair, 16 * pair + 16)
        keys = k_buf[2 * pair : 2 * pair + 2].reshape(2 * cache_len, lanes)
        raw = lax.dot_general(
            query_s[pair_rows, :].astype(jnp.bfloat16), keys, (((1,), (1,)), ((), ())),
            preferred_element_type=jnp.float32,
        )
        limit = jnp.where(upper, lengths[2 * pair], lengths[2 * pair + 1])
        score_s[pair_rows, :] = jnp.where(
            position < limit,
            jnp.where(upper, raw[:, :cache_len], raw[:, cache_len:]) * scale,
            -1e30,
        )

    scores = score_s[...]
    peak = jnp.maximum(jnp.max(scores, axis=1, keepdims=True), own_score)
    terms = jnp.exp(scores - peak)
    own_term = jnp.exp(own_score - peak)
    inverse = 1.0 / (jnp.sum(terms, axis=1, keepdims=True) + own_term)
    weight_s[...] = (terms * inverse).astype(jnp.bfloat16)
    own_weight = (own_term * inverse).astype(jnp.bfloat16).astype(jnp.float32)
    self_s[...] = own_weight * values_new
    for copy in copies[chunks:]:
        copy.wait()
    for pair in range(row_count // 2):
        pair_rows = slice(16 * pair, 16 * pair + 16)
        values = jnp.concatenate([v_buf[2 * pair], v_buf[2 * pair + 1]], axis=1)
        mixed = jnp.dot(weight_s[pair_rows, :], values, preferred_element_type=jnp.float32)
        query_s[pair_rows, :] = (
            jnp.where(upper, mixed[:, :lanes], mixed[:, lanes:]) + self_s[pair_rows, :]
        )

    mixed = [query_s[pl.ds(head, row_count, stride=8), :] for head in range(6)]
    attention = jnp.concatenate(
        [
            jnp.where(low, mixed[0], pltpu.roll(mixed[1], HEAD_DIM, 1)),
            jnp.where(low, mixed[2], mixed[3]),
            jnp.where(low, pltpu.roll(mixed[4], HEAD_DIM, 1), mixed[5]),
        ],
        axis=1,
    ).astype(jnp.bfloat16)
    place_tp = lax.axis_index("tp")
    product_s[...] = jnp.dot(attention, w_buf[...], preferred_element_type=jnp.float32)
    for shift, out in zip(FAR_FIRST, (own, sent1, sent2, sent3)):
        columns = pl.ds(pl.multiple_of((place_tp ^ shift) * width, width), width)
        out[...] = product_s[:, columns].astype(out.dtype)


def ready_kernel(
    slot_dev, own, resid, routes, w_router, gate_hbm, up_hbm,
    base, pick_rows, pick0, pick1, router_rows, w_gate, w_up, sems,
):
    copies = []
    for source, target in ((gate_hbm, w_gate), (up_hbm, w_up)):
        size = source.shape[0] // 4
        for chunk in range(4):
            part = pl.ds(chunk * size, size)
            copies.append(
                pltpu.make_async_copy(source.at[part], target.at[part], sems.at[len(copies)])
            )
    for copy in copies:
        copy.start()
    base[...] = own[...] + resid[...].astype(jnp.float32)
    packed_count, row_count = pick_rows.shape

    route0, route1 = routes[0:1, :], routes[1:2, :]
    place = lax.broadcasted_iota(jnp.int32, (packed_count, row_count), 0)
    named0 = jnp.where(place == route0, 1.0, 0.0)
    named1 = jnp.where(place == route1, 1.0, 0.0)
    row_of = lax.broadcasted_iota(jnp.int32, (row_count, row_count), 0)
    col_of = lax.broadcasted_iota(jnp.int32, (row_count, row_count), 1)
    earlier = jnp.where(row_of < col_of, 1.0, 0.0).astype(jnp.bfloat16)
    before = jnp.dot(
        (named0 + named1).astype(jnp.bfloat16), earlier, preferred_element_type=jnp.float32
    )
    place_req = lax.axis_index("req")

    def pick(route, named):
        rank = jnp.sum(named * before, axis=0, keepdims=True).astype(jnp.int32)
        block = ((route // slot_dev) ^ place_req) * slot_dev + lax.rem(route, slot_dev)
        return jnp.where(place == block * CAP + rank, 1.0, 0.0)

    first, second = pick(route0, named0), pick(route1, named1)
    pick_rows[...] = (first + second).astype(jnp.bfloat16)
    pick0[...] = jnp.transpose(first).astype(jnp.bfloat16)
    pick1[...] = jnp.transpose(second).astype(jnp.bfloat16)
    signed = jnp.transpose(named0 - named1)
    router_rows[...] = jnp.dot(
        signed[:, :EXPERTS], w_router[...],
        precision=lax.Precision.HIGHEST, preferred_element_type=jnp.float32,
    )
    for copy in copies:
        copy.wait()


def pack_kernel(base, part1, part2, part3, pick_rows, attended, home, sent1, sent2, sent3):
    total = base[...]
    for part in (part1, part2, part3):
        total = total + part[...].astype(jnp.float32)
    rows = total.astype(jnp.bfloat16)
    attended[...] = rows
    packed = jnp.dot(pick_rows[...], rows, preferred_element_type=jnp.float32)
    size = home.shape[0]
    for distance, out in zip(FAR_FIRST, (home, sent1, sent2, sent3)):
        out[...] = packed[distance * size : (distance + 1) * size].astype(out.dtype)


def result_kernel(attended, result):
    result[...] = attended[...]


def stats_kernel(attended, gain, router_rows, stats):
    rows = attended[...].astype(jnp.float32)
    square = jnp.sum(rows * rows, axis=1, keepdims=True)
    logit = jnp.sum(rows * gain[...] * router_rows[...], axis=1, keepdims=True)
    lane = lax.broadcasted_iota(jnp.int32, stats.shape, 1)
    stats[...] = jnp.where(lane == 0, square, jnp.where(lane == 1, logit, 0.0))


def turn_kernel(home, part1, part2, part3, along):
    half = home.shape[0] // 2
    for index, part in zip(FAR_FIRST, (home, part1, part2, part3)):
        along[index * half : (index + 1) * half, :] = part[half:, :]


def slot_masks(row_count, slot_dev):
    slot = lax.rem(lax.broadcasted_iota(jnp.int32, (row_count, 1), 0) // CAP, slot_dev)
    return [slot == index for index in range(slot_dev)]


def split_high(column):
    high = column.astype(jnp.bfloat16).astype(jnp.float32)
    return high, column - high


def gate_terms(slot_dev, blocks, gain, stats, w_gate, w_up, kept, sent, lhs):
    size = kept.shape[0] // 2
    width = blocks.shape[1]
    hidden = w_gate.shape[1]
    place_tp = lax.axis_index("tp")
    masks = slot_masks(size, slot_dev)
    lane = lax.broadcasted_iota(jnp.int32, (size, 128), 1)
    for order, shift in enumerate((0, 2, 1, 3)):
        out, first_row = (kept, sent)[order // 2], order % 2 * size
        rows = blocks[
            pl.ds(pl.multiple_of((place_tp ^ shift) * size, size), size), :
        ].astype(jnp.float32)
        columns = [jnp.sum(rows * rows, axis=1, keepdims=True)]
        if stats is not None:
            for first in range(0, stats.shape[0], size):
                columns += [stats[first : first + size, 0:1], stats[first : first + size, 1:2]]
        extra = jnp.zeros((size, 128), jnp.float32)
        for index, column in enumerate(columns):
            high, low = split_high(column)
            extra = jnp.where(lane == 2 * index, high, extra)
            extra = jnp.where(lane == 2 * index + 1, low, extra)
        out[first_row : first_row + size, 2 * hidden :] = extra.astype(out.dtype)
        scaled = rows * gain[...]
        for index, mask in enumerate(masks):
            lhs[order * size : (order + 1) * size, index * width : (index + 1) * width] = (
                jnp.where(mask, scaled, 0.0).astype(jnp.bfloat16)
            )
    left = lhs[...]
    for first, weight in ((0, w_gate), (hidden, w_up)):
        product = jnp.dot(left, weight[...], preferred_element_type=jnp.float32)
        kept[:, first : first + hidden] = product[: 2 * size]
        sent[:, first : first + hidden] = product[2 * size :].astype(sent.dtype)


def early_kernel(
    slot_dev, in0, in1, in2, in3, gain, stats, w_gate, w_up, turned, kept, sent, blocks, lhs
):
    del turned
    half = kept.shape[0] // 2
    for index, part in zip(FAR_FIRST, (in0, in1, in2, in3)):
        blocks[index * half : (index + 1) * half, :] = part[:half, :]
    gate_terms(slot_dev, blocks, gain, stats, w_gate, w_up, kept, sent, lhs)


def late_kernel(slot_dev, blocks, gain, w_gate, w_up, kept, sent, lhs):
    gate_terms(slot_dev, blocks, gain, None, w_gate, w_up, kept, sent, lhs)


def chip_kernel(kept, part, own, sent):
    size, width = own.shape[0] // 2, own.shape[1]
    total = kept[...] + part[...].astype(jnp.float32)
    own[...] = total
    extra = total[:, width - 128 :]
    lane = lax.broadcasted_iota(jnp.int32, extra.shape, 1)
    high, low = split_high(extra + pltpu.roll(extra, 127, 1))
    extra = jnp.where(lax.rem(lane, 2) == 0, high, pltpu.roll(low, 1, 1))
    for target, source in ((0, size), (size, 0)):
        sent[target : target + size, : width - 128] = total[
            source : source + size, : width - 128
        ].astype(sent.dtype)
        sent[target : target + size, width - 128 :] = extra[source : source + size].astype(
            sent.dtype
        )


def hidden_kernel(*refs):
    late, early, (hidden, first_weight) = refs[:2], refs[2:4], refs[4:]
    width = hidden.shape[1]
    half = hidden.shape[0] // 4

    def total(parts, columns):
        result = parts[0][:, columns]
        for part in parts[1:]:
            result = result + part[:, columns].astype(jnp.float32)
        return result

    def inverse_rms(columns, index):
        square = columns[:, index : index + 1] + columns[:, index + 1 : index + 2]
        return 1.0 / jnp.sqrt(square / D + 1e-06)

    for index, parts in ((1, late), (0, early)):
        extra = total(parts, slice(2 * width, 2 * width + 128))
        row_inv = inverse_rms(extra, 0)
        gate = total(parts, slice(0, width)) * row_inv
        up = total(parts, slice(width, 2 * width)) * row_inv
        rows = (gate / (1.0 + jnp.exp(-gate)) * up).astype(jnp.bfloat16)
        for block in range(2):
            start = (2 * block + index) * half
            hidden[start : start + half, :] = rows[block * half : (block + 1) * half]
    extra = extra[:half]
    for index in range(first_weight.shape[0] // half):
        place = 2 + 4 * index
        logit = extra[:, place + 2 : place + 3] + extra[:, place + 3 : place + 4]
        weight = 1.0 / (1.0 + jnp.exp(-logit * inverse_rms(extra, place)))
        first_weight[index * half : (index + 1) * half, :] = jnp.broadcast_to(weight, (half, 128))


BACK = ((0, 2, 3, 1), (0, 3, 1, 2))


def down_rows(slot_dev, hidden, w_down, lhs, product):
    count, width = hidden.shape
    rows = hidden[...].astype(jnp.float32)
    for index, mask in enumerate(slot_masks(count, slot_dev)):
        lhs[:, index * width : (index + 1) * width] = jnp.where(mask, rows, 0.0).astype(
            jnp.bfloat16
        )
    product[...] = jnp.dot(lhs[...], w_down[...], preferred_element_type=jnp.float32)
    half = count // 2
    upper = lax.axis_index("tp") // 2
    near = pl.ds(pl.multiple_of(upper * half, half), half)
    far = pl.ds(pl.multiple_of((1 - upper) * half, half), half)
    return product[near, :], product[far, :]


def own_down_kernel(slot_dev, hidden, w_down, near, far, lhs, product):
    results = down_rows(slot_dev, hidden, w_down, lhs, product)
    for out, rows in zip((near, far), results):
        out[...] = rows.astype(out.dtype)


def other_down_kernel(slot_dev, hidden, w_down, own_near, home, second, third, lhs, product):
    near, far = down_rows(slot_dev, hidden, w_down, lhs, product)
    own = own_near[...].astype(jnp.float32)
    first_core = lax.rem(lax.axis_index("tp"), 2) == 0
    home[...] = jnp.where(first_core, own, near).astype(home.dtype)
    second[...] = jnp.where(first_core, far, own).astype(second.dtype)
    third[...] = jnp.where(first_core, near, far).astype(third.dtype)


def back_permute(block, order):
    reqs, tps = lax.axis_size("req"), lax.axis_size("tp")
    pairs = [
        (req * tps + tp, (req ^ (2 * BACK[tp % 2][order])) * tps + tp)
        for req in range(reqs)
        for tp in range(tps)
    ]
    return lax.ppermute(block, ("req", "tp"), pairs)


def back_turn_kernel(home, part1, part2, part3, along):
    half = home.shape[0] // 2
    for index, part in enumerate((home, part1, part2, part3)):
        along[index * half : (index + 1) * half, :] = part[half:, :]


def combine_kernel(
    home, part1, part2, part3, along, pick0, pick1, first_weight, attended, layer_out, returned
):
    half = home.shape[0] // 2
    core = lax.rem(lax.axis_index("tp"), 2)
    for index, part in enumerate((home, part1, part2, part3)):
        distance = jnp.where(core == 0, BACK[0][index], BACK[1][index])
        start = pl.multiple_of(distance * 2 * half, 2 * half)
        returned[pl.ds(start, half), :] = part[:half, :]
        returned[pl.ds(start + half, half), :] = along[index * half : (index + 1) * half, :]
    rows = returned[...]
    out0 = jnp.dot(pick0[...], rows, preferred_element_type=jnp.float32)
    out1 = jnp.dot(pick1[...], rows, preferred_element_type=jnp.float32)
    weight = first_weight[:, 0:1]
    moe = weight * out0 + (1.0 - weight) * out1
    layer_out[...] = (attended[...].astype(jnp.float32) + moe).astype(jnp.bfloat16)


def shards(
    resid,
    queries,
    new_keys,
    new_values,
    k_cache,
    v_cache,
    lengths,
    w_out,
    norm_gain,
    w_router,
    routes,
    w_gate,
    w_up,
    w_down,
):
    row_count, width = resid.shape
    slot_dev, _, hidden = w_gate.shape
    cache_len, lanes = k_cache.shape[1:]
    packed_count = EXPERTS * CAP
    quarter = packed_count // lax.axis_size("tp")
    if not (
        lax.axis_size("tp") == 4
        and lax.axis_size("req") == 8
        and 8 * slot_dev == EXPERTS
        and row_count == quarter
        and cache_len == lanes == 2 * HEAD_DIM
        and queries.shape[1] == 6 * HEAD_DIM
    ):
        return shards_general(
            resid, queries, new_keys, new_values, k_cache, v_cache, lengths, w_out,
            norm_gain, w_router, routes, w_gate, w_up, w_down,
        )
    bf16, f32 = jnp.bfloat16, jnp.float32
    gain = norm_gain.reshape(1, width)
    own, *sents = call(
        attend_kernel,
        [((row_count, width), f32)] + [((row_count, width), bf16)] * 3,
        [spec(pl.ANY)] * 7,
        [
            pltpu.with_memory_space_constraint(operand, pltpu.HBM)
            for operand in (lengths, queries, new_keys, new_values, k_cache, v_cache, w_out)
        ],
        scratch=[
            pltpu.SMEM(lengths.shape, jnp.int32),
            pltpu.VMEM(queries.shape, bf16),
            pltpu.VMEM(new_keys.shape, bf16),
            pltpu.VMEM(new_values.shape, bf16),
            pltpu.VMEM(k_cache.shape, bf16),
            pltpu.VMEM(v_cache.shape, bf16),
            pltpu.VMEM(w_out.shape, bf16),
            pltpu.VMEM((8 * row_count, lanes), f32),
            pltpu.VMEM((8 * row_count, lanes), f32),
            pltpu.VMEM((8 * row_count, cache_len), f32),
            pltpu.VMEM((8 * row_count, cache_len), bf16),
            pltpu.VMEM((row_count, w_out.shape[1]), f32),
            pltpu.SemaphoreType.DMA((4,)),
            pltpu.SemaphoreType.DMA((3,)),
        ],
        mebibytes=16,
        flops=200_000_000,
        moved=3_400_000,
    )
    def sum_exchange(sents):
        return [partner_permute(block, "tp", k) for k, block in zip(FAR_FIRST[1:], sents)]

    parts = sum_exchange(sents)
    weight = (slot_dev * width, hidden)
    base, pick_rows, pick0, pick1, router_rows, *weights = call(
        functools.partial(ready_kernel, slot_dev),
        [
            ((row_count, width), f32),
            ((packed_count, row_count), bf16),
            ((row_count, packed_count), bf16),
            ((row_count, packed_count), bf16),
            ((row_count, width), f32),
            (weight, bf16),
            (weight, bf16),
        ],
        [spec()] * 4 + [spec(pl.ANY)] * 2,
        (
            own,
            resid,
            routes.T,
            w_router.T,
            pltpu.with_memory_space_constraint(w_gate.reshape(weight), pltpu.HBM),
            pltpu.with_memory_space_constraint(w_up.reshape(weight), pltpu.HBM),
        ),
        scratch=[pltpu.SemaphoreType.DMA((8,))],
        mebibytes=12,
        moved=3_300_000,
    )
    attended, home, *sents = call(
        pack_kernel,
        [((row_count, width), bf16)] + [((quarter, width), bf16)] * 4,
        [spec()] * 5,
        (base, *parts, pick_rows),
    )
    (stats,) = call(
        stats_kernel, [((row_count, 128), f32)], [spec()] * 3, (attended, gain, router_rows)
    )
    (result,) = call(result_kernel, [((row_count, width), bf16)], [spec()], (attended,))
    stats, result = lax.optimization_barrier((stats, result))
    parts = [
        partner_permute(block, "req", 2 * k) for k, block in zip(FAR_FIRST[1:], sents)
    ]
    (turned,) = call(
        turn_kernel, [((2 * quarter, width), bf16)], [spec()] * 4, (home, *parts)
    )
    along = partner_permute(turned, "req", 1)
    lhs = pltpu.VMEM((packed_count // 2, slot_dev * width), bf16)

    pair = (quarter, 2 * hidden + 128)

    def chip_sums(kept, sent):
        return call(
            chip_kernel, [(pair, f32), (pair, bf16)], [spec()] * 2,
            (kept, partner_permute(sent, "tp", 1)),
        )

    kept, sent = call(
        functools.partial(early_kernel, slot_dev),
        [(pair, f32), (pair, bf16)],
        [spec()] * 9,
        (home, *parts, gain, stats, *weights, turned),
        scratch=[pltpu.VMEM((2 * quarter, width), bf16), lhs],
        flops=400_000_000,
        moved=3_500_000,
    )
    early, sent = chip_sums(kept, sent)
    early = (early, partner_permute(sent, "tp", 2))
    kept, sent = call(
        functools.partial(late_kernel, slot_dev),
        [(pair, f32), (pair, bf16)],
        [spec()] * 4,
        (along, gain, *weights),
        scratch=[lhs],
        flops=400_000_000,
        moved=3_500_000,
    )
    late, sent = chip_sums(kept, sent)
    late = (late, partner_permute(sent, "tp", 2))
    own, first_weight = call(
        hidden_kernel,
        [((2 * quarter, hidden), bf16), ((row_count, 128), f32)],
        [spec()] * 4,
        (*late, *early),
    )
    w_down = w_down.reshape(slot_dev * hidden, width)
    block = ((quarter, width), bf16)
    down_scratch = [
        pltpu.VMEM((2 * quarter, slot_dev * hidden), bf16),
        pltpu.VMEM((2 * quarter, width), f32),
    ]
    near, far = call(
        functools.partial(own_down_kernel, slot_dev), [block] * 2, [spec()] * 2, (own, w_down),
        scratch=down_scratch, flops=100_000_000, moved=2_000_000,
    )
    home, second, third = call(
        functools.partial(other_down_kernel, slot_dev), [block] * 3, [spec()] * 3,
        (partner_permute(own, "tp", 1), w_down, near),
        scratch=down_scratch, flops=100_000_000, moved=2_000_000,
    )
    parts = [back_permute(rows, order) for order, rows in enumerate((far, second, third), 1)]
    (along,) = call(
        back_turn_kernel, [((2 * quarter, width), bf16)], [spec()] * 4, (home, *parts)
    )
    (layer_out,) = call(
        combine_kernel,
        [((row_count, width), bf16)],
        [spec()] * 9,
        (
            home, *parts, partner_permute(along, "req", 1), pick0, pick1, first_weight, attended,
        ),
        scratch=[pltpu.VMEM((packed_count, width), bf16)],
    )
    return (result, layer_out)


def solution(mesh):
    placed = (
        P("req", "tp"),
        P("req", "tp"),
        P("req", "tp"),
        P("req", "tp"),
        P("req", None, "tp"),
        P("req", None, "tp"),
        P("req"),
        P("tp", None),
        P("tp"),
        P("tp", None),
        P("req", None),
        P("req", "tp", None),
        P("req", "tp", None),
        P("req", None, "tp"),
    )
    return jax.shard_map(
        shards,
        mesh=mesh,
        in_specs=placed,
        out_specs=(P("req", "tp"), P("req", "tp")),
        check_vma=False,
    )
```
